32 devices in a mesh: expert: 8 (over z, y), tensor: 4 (over x, core).
Axes of the slice: x: 2, y: 2, z: 4, core: 2. Of those that a mesh axis runs over, the one named last changes fastest.
Arguments:
- tokens: bfloat16 [4096, 2048], P('expert'), may hold values from -15 to 15
- gain_attn: float32 [2048], replicated, may hold values from 0.5 to 1.5
- w_query: bfloat16 [2048, 2048], P(None, 'tensor'), may hold values from -0.125 to 0.125
- w_key: bfloat16 [2048, 2048], P(None, 'tensor'), may hold values from -0.125 to 0.125
- w_value: bfloat16 [2048, 2048], P(None, 'tensor'), may hold values from -0.125 to 0.125
- w_out: bfloat16 [2048, 2048], P('tensor'), may hold values from -2 to 2
- gain_moe: float32 [2048], replicated, may hold values from 0.5 to 1.5
- w_router: bfloat16 [2048, 64], replicated, may hold values from -0.0625 to 0.0625
- w_gate: bfloat16 [64, 2048, 1024], P('expert', None, 'tensor'), may hold values from -0.125 to 0.125
- w_up: bfloat16 [64, 2048, 1024], P('expert', None, 'tensor'), may hold values from -0.125 to 0.125
- w_down: bfloat16 [64, 1024, 2048], P('expert', 'tensor'), may hold values from -0.75 to 0.75
- expert_ids: int32 [4096, 8], P(('expert', 'tensor')), may hold values from 0 to 63, all different within a row; in each aligned block of 128 rows (0 to 127, 128 to 255, ...) at most 24 rows name the same one
- cotangent: bfloat16 [4096, 2048], P(('expert', 'tensor')), may hold values from -6 to 6
Outputs:
- mixed: bfloat16 [4096, 2048], P(('expert', 'tensor'))
- grad_tokens: float32 [4096, 2048], P(('expert', 'tensor'))
- grad_gain_attn: float32 [2048], replicated
- grad_w_query: float32 [2048, 2048], P(None, 'tensor')
- grad_w_key: float32 [2048, 2048], P(None, 'tensor')
- grad_w_value: float32 [2048, 2048], P(None, 'tensor')
- grad_w_out: float32 [2048, 2048], P('tensor')
- grad_gain_moe: float32 [2048], replicated
- grad_w_router: float32 [2048, 64], replicated
- grad_w_gate: float32 [64, 2048, 1024], P('expert', None, 'tensor')
- grad_w_up: float32 [64, 2048, 1024], P('expert', None, 'tensor')
- grad_w_down: float32 [64, 1024, 2048], P('expert', 'tensor')
The draws below stay inside these ranges and needn't reach their ends.
Inputs may be any that keep to these rules, and one draw needn't show every extreme that they name: `expert_ids`: each row names 8 different experts; among the rows of one device (aligned blocks of 128 rows) no expert is named more than 24 times, and in some blocks one is named exactly 24 times.
All inputs are finite; a program needn't handle non-finite values.
Results may differ from the reference program's by a relative error of at most 0.018.
Values may be sent and summed in bfloat16 or wider, within the bound.
No kernel may reach another device: no remote copies, remote signals or barrier semaphores. Data moves between devices by JAX's collectives and lax.ppermute only.
A program may use at most 448 MiB of HBM per device.

```python
import math
import jax
import jax.numpy as jnp
import numpy as np
from jax import lax

D = 2048
H = 16
KV = 16
HD = 128
FF = 1024
TOPK = 8
TOK = 512
EXPERTS = 64
BLOCK = 128
CAP = 24
TOKENS = 4096
N_EXPERT = 8


def draw_tokens(key, part):
    key = jax.random.fold_in(key, 11)
    row_key, column_key, value_key = jax.random.split(key, 3)
    row_scale = jnp.exp(jax.random.uniform(row_key, (TOKENS, 1), jnp.float32, jnp.log(0.3), jnp.log(3.0)))
    column_scale = jnp.exp(jax.random.uniform(column_key, (1, D), jnp.float32, jnp.log(0.6), jnp.log(1.6)))
    entries = jax.random.truncated_normal(value_key, -3.0, 3.0, (TOKENS, D), jnp.float32)
    return (row_scale * column_scale * entries).astype(jnp.bfloat16)


def steps_of(own_key, dims, pieces, least, high):
    factor_of = 1.0
    for axis_at, shards_of in pieces:
        steps = jax.random.uniform(jax.random.fold_in(jax.random.fold_in(own_key, 6), axis_at), (shards_of,), jnp.float32, least / len(pieces), high / len(pieces))
        factor_of = factor_of * jnp.repeat(jnp.exp(steps), dims[axis_at] // shards_of).reshape((-1,) + (1,) * (len(dims) - 1 - axis_at))
    return factor_of


def shared_out(key, own, number, rows, amount, top, reach, slope):
    sequence = jax.random.permutation(key, amount)
    crowded, usual = load_shares(amount, rows * top, reach, slope, True), load_shares(amount, rows * top, reach, slope, False)
    places = jnp.arange(amount)

    def named(lengths, rotation):
        used = int((lengths > 0).sum())
        fixed = max(1, used // 4)
        shifted = fixed + (places - fixed + rotation * (used - fixed)) % max(1, amount - fixed)
        return jnp.zeros((amount,), jnp.int32).at[sequence[jnp.where(places < fixed, places, shifted)]].set(jnp.asarray(lengths, jnp.int32))

    lengths = jnp.where(number % 4 == 0, named(crowded, number // 4), named(usual, number - number // 4 - 1))
    mixed = jax.random.permutation(jax.random.fold_in(own, 3), amount)
    donor, sink = mixed[0:amount // 2 * 2:2], mixed[1:amount // 2 * 2:2]
    margin = jnp.minimum(lengths[donor] - 1, reach - lengths[sink]) // 2
    margin = jnp.where((donor == sequence[0]) | (sink == sequence[0]) | (lengths[sink] == 0), 0, jnp.maximum(margin, 0))
    shifted = jax.random.randint(jax.random.fold_in(own, 4), (amount // 2,), 0, 1 << 20) % (margin + 1)
    lengths = lengths.at[donor].add(-shifted).at[sink].add(shifted)
    labels = jnp.searchsorted(jnp.cumsum(lengths), jnp.arange(rows * top), side="right").astype(jnp.int32)
    table = labels.reshape(top, rows).T
    table = table[jax.random.permutation(jax.random.fold_in(own, 1), rows)]
    rotation = jax.random.randint(jax.random.fold_in(own, 2), (rows, 1), 0, top)
    return jnp.take_along_axis(table, (jnp.arange(top)[None, :] + rotation) % top, axis=1)


def load_shares(count, total, reach, lean, full):
    portions = [(1 << 20) // math.isqrt(standing ** lean) + 1 for standing in range(1, count + 1)]
    largest = reach if full else min(reach, max(-(-total // count), total * portions[0] // sum(portions)))
    least = 1 if total - largest >= count - 1 else 0
    counts, surplus = [largest] + [least] * (count - 1), total - largest - least * (count - 1)
    while surplus > 0:
        free = [i for i in range(1, count) if counts[i] < largest] or [i for i in range(1, count) if counts[i] < reach]
        whole, remaining = sum([portions[i] for i in free]), surplus
        for i in free:
            more = min(reach - counts[i], max(1, remaining * portions[i] // whole), surplus)
            counts[i] = counts[i] + more
            surplus = surplus - more
    return np.array(counts)


def gaussian(key, extent, scale, reach, cuts=(), held_as=jnp.bfloat16):
    gain = steps_of(key, extent, cuts, -0.22, 0.18) if cuts else 1.0
    values = jax.random.normal(key, extent, jnp.float32) * scale * gain
    return jnp.minimum(jnp.maximum(values, -reach), reach).astype(held_as)


def setup_inputs(seed: int = 0) -> dict:
    splits = jax.random.split(jax.random.key(seed), 14)
    tokens = draw_tokens(jax.random.fold_in(splits[13], 71), 0)
    gain_attn = jnp.clip(1.0 + 0.1 * jax.random.normal(splits[1], (D,), jnp.float32), 0.5, 1.5)
    w_query = gaussian(splits[2], (D, H * HD), D ** -0.5, 0.125, ((1, 4),))
    w_key = gaussian(splits[3], (D, KV * HD), D ** -0.5, 0.125, ((1, 4),))
    w_value = gaussian(splits[4], (D, KV * HD), D ** -0.5, 0.125, ((1, 4),))
    w_out = gaussian(splits[5], (H * HD, D), (H * HD // 256) ** -0.5, 2.0, ((0, 4),))
    gain_moe = jnp.clip(1.0 + 0.1 * jax.random.normal(splits[6], (D,), jnp.float32), 0.5, 1.5)
    w_router = gaussian(splits[7], (D, EXPERTS), (4 * D) ** -0.5, 0.0625)
    w_gate = gaussian(splits[8], (EXPERTS, D, FF), D ** -0.5, 0.125, ((0, 8), (2, 4)))
    w_up = gaussian(splits[9], (EXPERTS, D, FF), D ** -0.5, 0.125, ((0, 8), (2, 4)))
    w_down = gaussian(splits[10], (EXPERTS, FF, D), (FF // 16) ** -0.5, 0.75, ((0, 8), (1, 4)))
    expert_ids_keys = jax.random.split(jax.random.fold_in(splits[11], 1), TOKENS // BLOCK)
    expert_ids_turns = jax.random.permutation(jax.random.fold_in(splits[11], 3), TOKENS // BLOCK)
    expert_ids = jax.vmap(lambda own, number: shared_out(jax.random.fold_in(splits[11], 2), own, number, BLOCK, EXPERTS, TOPK, CAP, 1))(expert_ids_keys, expert_ids_turns).reshape((TOKENS, TOPK))
    cotangent = gaussian(splits[12], (TOKENS, D), 1.0, 6.0, ((0, 32),))
    return {"tokens": tokens, "gain_attn": gain_attn, "w_query": w_query, "w_key": w_key, "w_value": w_value, "w_out": w_out, "gain_moe": gain_moe, "w_router": w_router, "w_gate": w_gate, "w_up": w_up, "w_down": w_down, "expert_ids": expert_ids, "cotangent": cotangent}


eps = 1e-06
theta_base = 10000.0
masked = -1e+30
highest = lax.Precision.HIGHEST

@jax.custom_vjp
def low(v):
    return lax.optimization_barrier(v.astype(jnp.bfloat16)).astype(jnp.float32)

@jax.custom_vjp
def low_back(v):
    return v

def low_keep(v):
    return (low(v), None)

def low_pass(kept, grad):
    return (grad,)

def back_keep(v):
    return (v, None)

def back_low(kept, grad):
    return (low(grad),)
low.defvjp(low_keep, low_pass)
low_back.defvjp(back_keep, back_low)

def product(left_side, right_side):
    return jnp.dot(left_side, right_side, precision=highest, preferred_element_type=jnp.float32)

def rms_norm(source, gain_vec):
    return source * lax.rsqrt(lax.optimization_barrier(jnp.mean(source * source, axis=-1, keepdims=True)) + eps) * gain_vec

def rope_tables(seq_length, head_size):
    half_dim = head_size // 2
    frequency = jnp.exp(-jnp.log(theta_base) * jnp.arange(half_dim, dtype=jnp.float32) * (2.0 / head_size))
    angles = jnp.arange(seq_length, dtype=jnp.float32)[:, None] * frequency[None, :]
    return (jnp.cos(angles)[:, None, :], jnp.sin(angles)[:, None, :])

def rotate(source, cosine_table, sine_table):
    half_dim = source.shape[-1] // 2
    first_half = source[..., :half_dim]
    second = source[..., half_dim:]
    return jnp.concatenate([first_half * cosine_table - second * sine_table, second * cosine_table + first_half * sine_table], axis=-1)

def attend_sequence(packed):
    query_seq, key_seq, value_seq = packed
    grouped = query_seq.reshape(TOK, KV, H // KV, HD)
    scores = low_back(jnp.einsum('qgrd,kgd->grqk', grouped, key_seq, precision=highest) * HD ** (-0.5))
    positions = jnp.arange(TOK, dtype=jnp.int32)
    scores = jnp.where(positions[:, None] >= positions[None, :], scores, masked)
    weights = low(jax.nn.softmax(scores, axis=-1))
    head_rows = jnp.einsum('grqk,kgd->qgrd', weights, value_seq, precision=highest)
    return head_rows.reshape(TOK, H * HD)

def expert_rows(packed):
    rows_in, gate_mat, up_mat, down_mat = packed
    gate_pre = low_back(product(rows_in, gate_mat))
    up_pre = low_back(product(rows_in, up_mat))
    activation = low(jax.nn.silu(gate_pre) * up_pre)
    return low(low_back(product(activation, down_mat)))

def dispatch_places(expert_ids):
    block_total = TOKENS // BLOCK
    matches = (expert_ids[:, :, None] == jnp.arange(EXPERTS, dtype=jnp.int32)[None, None, :]).astype(jnp.int32)
    expert_hits = lax.optimization_barrier(jnp.sum(matches, axis=1)).reshape(block_total, BLOCK, EXPERTS)
    earlier = (jnp.cumsum(expert_hits, axis=1) - expert_hits).reshape(TOKENS, EXPERTS)
    slot_of = lax.optimization_barrier(jnp.sum(matches * earlier[:, None, :], axis=2))
    source_block = (jnp.arange(TOKENS, dtype=jnp.int32) // BLOCK)[:, None]
    return (expert_ids * (block_total * CAP) + source_block * CAP + slot_of).astype(jnp.int32)

def layer(tokens, gain_attn, w_query, w_key, w_value, w_out, gain_moe, w_router, w_gate, w_up, w_down, expert_ids, places):
    block_total = TOKENS // BLOCK
    hidden_one = low(rms_norm(tokens, gain_attn))
    cosine_table, sine_table = rope_tables(TOK, HD)
    queries = low(rotate(low_back(product(hidden_one, w_query)).reshape(N_EXPERT, TOK, H, HD), cosine_table, sine_table))
    key_rows = low(rotate(low_back(product(hidden_one, w_key)).reshape(N_EXPERT, TOK, KV, HD), cosine_table, sine_table))
    value_rows = low(low_back(product(hidden_one, w_value))).reshape(N_EXPERT, TOK, KV, HD)
    head_rows = lax.map(jax.checkpoint(attend_sequence), (queries, key_rows, value_rows))
    head_rows = low(low_back(head_rows.reshape(TOKENS, H * HD)))
    attention = low_back(product(head_rows, w_out))
    middle = tokens + attention
    hidden_two = low(rms_norm(middle, gain_moe))
    logits = low_back(product(hidden_two, w_router))
    chosen = jnp.take_along_axis(logits, expert_ids, axis=1)
    gate_weights = jax.nn.softmax(chosen, axis=-1)
    token_rows = jnp.broadcast_to(hidden_two[:, None, :], (TOKENS, TOPK, D)).reshape(TOKENS * TOPK, D)
    flat_places = places.reshape(-1)
    buffer_rows = jnp.zeros((EXPERTS * block_total * CAP, D), jnp.float32).at[flat_places].set(token_rows)
    buffer_rows = low_back(buffer_rows).reshape(EXPERTS, block_total * CAP, D)
    returned = lax.map(jax.checkpoint(expert_rows), (buffer_rows, w_gate, w_up, w_down)).reshape(EXPERTS * block_total * CAP, D)
    picked = returned[flat_places].reshape(TOKENS, TOPK, D)
    return middle + lax.optimization_barrier(jnp.sum(gate_weights[:, :, None] * picked, axis=1))

def reference(tokens, gain_attn, w_query, w_key, w_value, w_out, gain_moe, w_router, w_gate, w_up, w_down, expert_ids, cotangent):
    floats = (tokens.astype(jnp.float32), gain_attn.astype(jnp.float32), w_query.astype(jnp.float32), w_key.astype(jnp.float32), w_value.astype(jnp.float32), w_out.astype(jnp.float32), gain_moe.astype(jnp.float32), w_router.astype(jnp.float32), w_gate.astype(jnp.float32), w_up.astype(jnp.float32), w_down.astype(jnp.float32))
    places = dispatch_places(expert_ids)

    def forward(*params):
        return layer(*params, expert_ids, places)
    output, pull_back = jax.vjp(forward, *floats)
    grads = pull_back(cotangent.astype(jnp.float32))
    return (output.astype(jnp.bfloat16), grads[0], grads[1], grads[2], grads[3], grads[4], grads[5], grads[6], grads[7], grads[8], grads[9], grads[10])
```

```python
import jax
import jax.numpy as jnp
from jax import lax
from jax.sharding import PartitionSpec as P

HD = 128


eps = 1e-06
theta_base = 10000.0
masked = -1e30

BOTH = ("expert", "tensor")
CORE, ACROSS, ASIDE = 1, 2, 4
PLANES = (0, 8, 16, 24)


def rope_tables(seq_length, head_size):
    half_dim = head_size // 2
    frequency = jnp.exp(
        -jnp.log(theta_base) * jnp.arange(half_dim, dtype=jnp.float32) * (2.0 / head_size)
    )
    angles = jnp.arange(seq_length, dtype=jnp.float32)[:, None] * frequency[None, :]
    return (jnp.cos(angles)[:, None, :], jnp.sin(angles)[:, None, :])


def rotate(source, cosine_table, sine_table):
    half_dim = source.shape[-1] // 2
    first_half = source[..., :half_dim]
    second = source[..., half_dim:]
    return jnp.concatenate(
        [
            first_half * cosine_table - second * sine_table,
            second * cosine_table + first_half * sine_table,
        ],
        axis=-1,
    )


def norm_forward(source, gain_vec):
    inverse = lax.rsqrt(jnp.mean(source * source, axis=-1, keepdims=True) + eps)
    return (inverse, source * inverse * gain_vec)


def norm_backward(source, inverse, gain_vec, grad_in):
    scaled = gain_vec * grad_in
    grad_source = inverse * scaled - source * inverse**3 * jnp.mean(
        scaled * source, axis=-1, keepdims=True
    )
    grad_gain = jnp.sum(grad_in * source * inverse, axis=0)
    return (grad_source, grad_gain)


def block_scores(q_block, key_rows, first_row, score_scale):
    scores = (
        jnp.einsum("qgrd,kgd->grqk", q_block, key_rows, preferred_element_type=jnp.float32)
        * score_scale
    )
    row_ids = first_row + jnp.arange(q_block.shape[0], dtype=jnp.int32)
    allowed = row_ids[:, None] >= jnp.arange(key_rows.shape[0], dtype=jnp.int32)[None, :]
    return jnp.where(allowed, scores, masked)


def routed_layer(
    tokens,
    gain_attn,
    w_query,
    w_key,
    w_value,
    w_out,
    gain_moe,
    w_router,
    w_gate,
    w_up,
    w_down,
    expert_ids,
    cotangent,
):
    seq_length, model_width = tokens.shape
    block_len, top_count = expert_ids.shape
    expert_count = w_router.shape[1]
    local_experts = w_gate.shape[0]
    local_heads = w_query.shape[1] // HD
    local_groups = w_key.shape[1] // HD
    group_size = local_heads // local_groups
    owners = lax.axis_size("expert")
    quarter = lax.axis_index("tensor")
    capacity = 3 * block_len * top_count // (2 * expert_count)
    block_rows = min(512, seq_length)
    block_count = seq_length // block_rows
    score_scale = HD ** (-0.5)
    first_own = quarter * block_len
    inputs = tokens.astype(jnp.float32)
    inverse_one, normed_one = norm_forward(inputs, gain_attn)
    hidden_one = normed_one.astype(jnp.bfloat16)
    cosine_table, sine_table = rope_tables(seq_length, HD)

    def rope_heads(source):
        return rotate(source, cosine_table, sine_table)

    query_raw = jnp.dot(hidden_one, w_query, preferred_element_type=jnp.float32).reshape(
        seq_length, local_heads, HD
    )
    key_raw = jnp.dot(hidden_one, w_key, preferred_element_type=jnp.float32).reshape(
        seq_length, local_groups, HD
    )
    queries = rope_heads(query_raw).astype(jnp.bfloat16)
    key_rows = rope_heads(key_raw).astype(jnp.bfloat16)
    value_rows = (
        jnp.dot(hidden_one, w_value, preferred_element_type=jnp.float32)
        .astype(jnp.bfloat16)
        .reshape(seq_length, local_groups, HD)
    )
    query_blocks = queries.reshape(block_count, block_rows, local_groups, group_size, HD)
    starts = jnp.arange(block_count, dtype=jnp.int32) * block_rows

    def attend_block(packed):
        first_row, q_block = packed
        scores = block_scores(q_block, key_rows, first_row, score_scale)
        row_max = jnp.max(scores, axis=-1, keepdims=True)
        exponent = jnp.exp(scores - row_max)
        row_total = jnp.sum(exponent, axis=-1, keepdims=True)
        weights = (exponent / row_total).astype(jnp.bfloat16)
        head_out = jnp.einsum(
            "grqk,kgd->qgrd", weights, value_rows, preferred_element_type=jnp.float32
        )
        return (head_out.astype(jnp.bfloat16), (row_max + jnp.log(row_total))[..., 0])

    head_blocks, log_totals = lax.map(attend_block, (starts, query_blocks))
    head_rows = head_blocks.reshape(seq_length, local_heads * HD)
    attention = lax.psum_scatter(
        jnp.dot(head_rows, w_out, preferred_element_type=jnp.float32),
        "tensor",
        scatter_dimension=0,
        tiled=True,
    )
    own_inputs = lax.dynamic_slice_in_dim(inputs, first_own, block_len, 0)
    own_inverse = lax.dynamic_slice_in_dim(inverse_one, first_own, block_len, 0)
    middle = own_inputs + attention
    inverse_two, normed_two = norm_forward(middle, gain_moe)
    hidden_two = normed_two.astype(jnp.bfloat16)
    logits = jnp.dot(hidden_two, w_router, preferred_element_type=jnp.float32)
    expert_range = jnp.arange(expert_count, dtype=jnp.int32)
    matches = expert_ids[:, :, None] == expert_range[None, None, :]
    chosen = jnp.sum(jnp.where(matches, logits[:, None, :], 0.0), axis=2)
    gate_weights = jax.nn.softmax(chosen, axis=-1)
    expert_hits = jnp.sum(matches.astype(jnp.int32), axis=1)
    earlier = jnp.cumsum(expert_hits, axis=0) - expert_hits
    slot_of = jnp.sum(jnp.where(matches, earlier[:, None, :], 0), axis=2)
    place = (slot_of * expert_count + expert_ids).reshape(-1)
    token_rows = jnp.broadcast_to(
        hidden_two[:, None, :], (block_len, top_count, model_width)
    ).reshape(block_len * top_count, model_width)
    grad_out = cotangent.astype(jnp.float32)
    gated_grads = (
        (gate_weights[:, :, None] * grad_out[:, None, :])
        .astype(jnp.bfloat16)
        .reshape(block_len * top_count, model_width)
    )
    empty = jnp.zeros((capacity * expert_count, model_width), jnp.bfloat16)
    send_rows = empty.at[place].set(token_rows).reshape(capacity, expert_count, model_width)
    send_grads = empty.at[place].set(gated_grads).reshape(capacity, expert_count, model_width)
    arrived_rows, arrived_grads = (
        lax.all_to_all(send_rows, "expert", split_axis=1, concat_axis=1, tiled=True),
        lax.all_to_all(send_grads, "expert", split_axis=1, concat_axis=1, tiled=True),
    )
    routed = arrived_rows.reshape(capacity, owners, local_experts, model_width)
    grads_in = arrived_grads.reshape(capacity, owners, local_experts, model_width)
    all_rows, all_grads = (
        lax.all_gather(routed, "tensor", axis=0, tiled=True),
        lax.all_gather(grads_in, "tensor", axis=0, tiled=True),
    )
    gate_pre = jnp.einsum("csld,ldf->cslf", all_rows, w_gate, preferred_element_type=jnp.float32)
    up_pre = jnp.einsum("csld,ldf->cslf", all_rows, w_up, preferred_element_type=jnp.float32)
    sigmoid_gate = jax.nn.sigmoid(gate_pre)
    silu_gate = gate_pre * sigmoid_gate
    activation = (silu_gate * up_pre).astype(jnp.bfloat16)
    grad_w_down = jnp.einsum(
        "cslf,csld->lfd", activation, all_grads, preferred_element_type=jnp.float32
    )
    grad_act = jnp.einsum("csld,lfd->cslf", all_grads, w_down, preferred_element_type=jnp.float32)
    grad_gate = (grad_act * up_pre * sigmoid_gate * (1.0 + gate_pre * (1.0 - sigmoid_gate))).astype(
        jnp.bfloat16
    )
    grad_up = (grad_act * silu_gate).astype(jnp.bfloat16)
    grad_w_gate = jnp.einsum(
        "csld,cslf->ldf", all_rows, grad_gate, preferred_element_type=jnp.float32
    )
    grad_w_up = jnp.einsum("csld,cslf->ldf", all_rows, grad_up, preferred_element_type=jnp.float32)
    forward_term = jnp.einsum(
        "cslf,lfd->csld", activation, w_down, preferred_element_type=jnp.float32
    )
    back_term = jnp.einsum("cslf,ldf->csld", grad_gate, w_gate, preferred_element_type=jnp.float32)
    back_term = back_term + jnp.einsum(
        "cslf,ldf->csld", grad_up, w_up, preferred_element_type=jnp.float32
    )
    both_terms = lax.psum_scatter(
        jnp.concatenate([forward_term, back_term], axis=3).astype(jnp.bfloat16),
        "tensor",
        scatter_dimension=0,
        tiled=True,
    )
    returned = both_terms[..., :model_width]
    row_grads = both_terms[..., model_width:]
    returned_home, row_grads_home = (
        lax.all_to_all(
            returned.reshape(capacity, expert_count, model_width),
            "expert",
            split_axis=1,
            concat_axis=1,
            tiled=True,
        ),
        lax.all_to_all(
            row_grads.reshape(capacity, expert_count, model_width),
            "expert",
            split_axis=1,
            concat_axis=1,
            tiled=True,
        ),
    )
    picked = returned_home.reshape(capacity * expert_count, model_width)[place].reshape(
        block_len, top_count, model_width
    )
    mixture = jnp.sum(gate_weights[:, :, None] * picked, axis=1)
    mixed_out = (middle + mixture).astype(jnp.bfloat16)
    grad_gates = jnp.sum(picked * grad_out[:, None, :], axis=2)
    grad_picked = row_grads_home.reshape(capacity * expert_count, model_width)[place].reshape(
        block_len, top_count, model_width
    )
    grad_hidden_disp = jnp.einsum(
        "lk,lkd->ld",
        jnp.ones((block_len, top_count), jnp.bfloat16),
        grad_picked,
        preferred_element_type=jnp.float32,
    )
    grad_chosen = gate_weights * (
        grad_gates - jnp.sum(gate_weights * grad_gates, axis=-1, keepdims=True)
    )
    grad_logits = jnp.sum(jnp.where(matches, grad_chosen[:, :, None], 0.0), axis=1).astype(
        jnp.bfloat16
    )
    grad_router = jnp.einsum(
        "ld,le->de", hidden_two, grad_logits, preferred_element_type=jnp.float32
    )
    grad_hidden_two = grad_hidden_disp + jnp.einsum(
        "le,de->ld", grad_logits, w_router, preferred_element_type=jnp.float32
    )
    grad_normed_two, grad_gain_moe = norm_backward(middle, inverse_two, gain_moe, grad_hidden_two)
    grad_middle = grad_out + grad_normed_two
    grad_attn = grad_middle.astype(jnp.bfloat16)
    grad_attn_all = lax.all_gather(grad_attn, "tensor", axis=0, tiled=True)
    grad_w_out = jnp.einsum(
        "lh,ld->hd", head_rows, grad_attn_all, preferred_element_type=jnp.float32
    )
    grad_heads = jnp.einsum(
        "ld,hd->lh", grad_attn_all, w_out, preferred_element_type=jnp.float32
    ).astype(jnp.bfloat16)
    grad_blocks = grad_heads.reshape(block_count, block_rows, local_groups, group_size, HD)

    def back_block(carried, packed):
        grad_keys, grad_values = carried
        first_row, q_block, g_block, lse_block = packed
        scores = block_scores(q_block, key_rows, first_row, score_scale)
        probability = jnp.exp(scores - lse_block[..., None])
        grad_values = grad_values + jnp.einsum(
            "grqk,qgrd->kgd",
            probability.astype(jnp.bfloat16),
            g_block,
            preferred_element_type=jnp.float32,
        )
        grad_prob = jnp.einsum(
            "qgrd,kgd->grqk", g_block, value_rows, preferred_element_type=jnp.float32
        )
        row_delta = jnp.sum(probability * grad_prob, axis=-1, keepdims=True)
        grad_scores = (probability * (grad_prob - row_delta)).astype(jnp.bfloat16)
        grad_query = (
            jnp.einsum("grqk,kgd->qgrd", grad_scores, key_rows, preferred_element_type=jnp.float32)
            * score_scale
        )
        grad_keys = (
            grad_keys
            + jnp.einsum("grqk,qgrd->kgd", grad_scores, q_block, preferred_element_type=jnp.float32)
            * score_scale
        )
        return ((grad_keys, grad_values), grad_query)

    zero_keys = jnp.zeros((seq_length, local_groups, HD), jnp.float32)
    (grad_keys, grad_values), grad_query_blocks = lax.scan(
        back_block, (zero_keys, zero_keys), (starts, query_blocks, grad_blocks, log_totals)
    )
    grad_query = grad_query_blocks.reshape(seq_length, local_heads, HD)
    grad_query_raw = (
        jax.vjp(rope_heads, query_raw)[1](grad_query)[0]
        .reshape(seq_length, local_heads * HD)
        .astype(jnp.bfloat16)
    )
    grad_key_raw = (
        jax.vjp(rope_heads, key_raw)[1](grad_keys)[0]
        .reshape(seq_length, local_groups * HD)
        .astype(jnp.bfloat16)
    )
    grad_value_raw = grad_values.reshape(seq_length, local_groups * HD).astype(jnp.bfloat16)
    grad_w_query = jnp.einsum(
        "ld,lh->dh", hidden_one, grad_query_raw, preferred_element_type=jnp.float32
    )
    grad_w_key = jnp.einsum(
        "ld,lh->dh", hidden_one, grad_key_raw, preferred_element_type=jnp.float32
    )
    grad_w_value = jnp.einsum(
        "ld,lh->dh", hidden_one, grad_value_raw, preferred_element_type=jnp.float32
    )
    term = jnp.einsum("lh,dh->ld", grad_query_raw, w_query, preferred_element_type=jnp.float32)
    term = term + jnp.einsum("lh,dh->ld", grad_key_raw, w_key, preferred_element_type=jnp.float32)
    grad_hidden_one = lax.psum_scatter(
        (
            term
            + jnp.einsum("lh,dh->ld", grad_value_raw, w_value, preferred_element_type=jnp.float32)
        ).astype(jnp.bfloat16),
        "tensor",
        scatter_dimension=0,
        tiled=True,
    ).astype(jnp.float32)
    grad_normed_one, grad_gain_attn = norm_backward(
        own_inputs, own_inverse, gain_attn, grad_hidden_one
    )
    grad_tokens = grad_middle + grad_normed_one
    attn_sums = lax.psum((grad_w_query, grad_w_key, grad_w_value, grad_w_out), "expert")
    small_sums = lax.psum((grad_gain_attn, grad_gain_moe, grad_router), ("expert", "tensor"))
    return (
        mixed_out,
        grad_tokens,
        small_sums[0],
        attn_sums[0],
        attn_sums[1],
        attn_sums[2],
        attn_sums[3],
        small_sums[1],
        small_sums[2],
        grad_w_gate,
        grad_w_up,
        grad_w_down,
    )


def gathered_layer(
    tokens,
    gain_attn,
    w_query,
    w_key,
    w_value,
    w_out,
    gain_moe,
    w_router,
    w_gate,
    w_up,
    w_down,
    expert_ids,
    cotangent,
):
    seq_length, model_width = tokens.shape
    block_len, top_count = expert_ids.shape
    expert_count = w_router.shape[1]
    local_experts = w_gate.shape[0]
    local_heads = w_query.shape[1] // HD
    quarters = lax.axis_size("tensor")
    device_count = quarters * lax.axis_size("expert")
    quarter = lax.axis_index("tensor")
    device = lax.axis_index(BOTH)
    first_expert = lax.axis_index("expert") * local_experts
    pair_cap = 2 * (3 * block_len * top_count // (2 * expert_count))
    score_scale = HD ** (-0.5)
    narrow = jnp.bfloat16

    def swap(value, even, odd=None):
        odd = even if odd is None else odd
        perm = [(i, i ^ (odd if i & 1 else even)) for i in range(device_count)]
        return lax.ppermute(value, BOTH, perm)

    def gather_plane(own):
        first = swap(own, ACROSS, ASIDE)
        second = swap(own, ASIDE, ACROSS)
        both = swap(first, ASIDE, ACROSS)
        mine = [own, first, second, both]
        return jnp.concatenate(mine + [swap(part, CORE) for part in mine], axis=0)

    def gather_chunks(own):
        return [gather_plane(own if m == 0 else swap(own, m)) for m in PLANES]

    def reduce_plane(parts):
        parts = parts.reshape(8, block_len, model_width)
        mine = parts[:4] + swap(parts[4:], CORE)
        back = swap(mine[3], ASIDE, ACROSS)
        side = swap(mine[2], ASIDE, ACROSS)
        return mine[0] + side + swap(mine[1] + back, ACROSS, ASIDE)

    def reduce_chunks(chunks):
        sums = [reduce_plane(chunk) for chunk in chunks]
        total = sums[0].astype(jnp.float32)
        for mask, part in zip(PLANES[1:], sums[1:]):
            total = total + swap(part, mask).astype(jnp.float32)
        return total

    def slot_sources():
        odd = device & 1
        sources = []
        for mask in PLANES:
            for partner in (0, 1):
                base = device ^ mask ^ partner
                flipped = odd ^ partner
                near = jnp.where(flipped == 0, ACROSS, ASIDE)
                far = jnp.where(flipped == 0, ASIDE, ACROSS)
                sources += [base, base ^ near, base ^ far, base ^ near ^ far]
        return jnp.stack(sources)

    grad_chunks_in = gather_chunks(cotangent)
    ids_all = lax.all_gather(expert_ids, BOTH, axis=0, tiled=False)
    sources = slot_sources()
    ids_by_slot = jnp.take(ids_all, sources, axis=0)

    order = quarter ^ jnp.arange(quarters, dtype=jnp.int32)
    by_block = tokens.reshape(quarters, block_len, model_width)
    inputs = jnp.concatenate(
        [lax.dynamic_slice_in_dim(by_block, order[r], 1, 0)[0] for r in range(quarters)], axis=0
    ).astype(jnp.float32)
    positions = (order[:, None] * block_len + jnp.arange(block_len, dtype=jnp.int32)).reshape(-1)
    inverse_one, normed_one = norm_forward(inputs, gain_attn)
    hidden_one = normed_one.astype(narrow)
    frequency = jnp.exp(
        -jnp.log(theta_base) * jnp.arange(HD // 2, dtype=jnp.float32) * (2.0 / HD)
    )
    angles = positions.astype(jnp.float32)[:, None] * frequency[None, :]
    cosine_table, sine_table = (jnp.cos(angles)[:, None, :], jnp.sin(angles)[:, None, :])

    def project(weights):
        return jnp.dot(hidden_one, weights, preferred_element_type=jnp.float32).reshape(
            seq_length, local_heads, HD
        )

    queries = rotate(project(w_query), cosine_table, sine_table).astype(narrow)
    key_rows = rotate(project(w_key), cosine_table, sine_table).astype(narrow)
    value_rows = project(w_value).astype(narrow)
    allowed = positions[:, None] >= positions[None, :]

    def masked_scores():
        scores = jnp.einsum("qhd,khd->hqk", queries, key_rows, preferred_element_type=jnp.float32)
        return jnp.where(allowed, scores * score_scale, masked)

    scores = masked_scores()
    row_max = jnp.max(scores, axis=-1, keepdims=True)
    exponent = jnp.exp(scores - row_max)
    row_total = jnp.sum(exponent, axis=-1, keepdims=True)
    weights = (exponent / row_total).astype(narrow)
    head_out = jnp.einsum("hqk,khd->qhd", weights, value_rows, preferred_element_type=jnp.float32)
    log_total = row_max + jnp.log(row_total)
    head_rows = head_out.astype(narrow).reshape(seq_length, local_heads * HD)

    def reduce_quarters(full):
        parts = full.reshape(quarters, block_len, model_width)
        sent = swap(jnp.stack([parts[1], parts[3]]).astype(narrow), CORE)
        away = (parts[2] + sent[1].astype(jnp.float32)).astype(narrow)
        return parts[0] + sent[0].astype(jnp.float32) + swap(away, ACROSS).astype(jnp.float32)

    attention = reduce_quarters(jnp.dot(head_rows, w_out, preferred_element_type=jnp.float32))
    own_inputs = inputs[:block_len]
    own_inverse = inverse_one[:block_len]
    middle = own_inputs + attention
    inverse_two, normed_two = norm_forward(middle, gain_moe)
    hidden_two = normed_two.astype(narrow)
    logits = jnp.dot(hidden_two, w_router, preferred_element_type=jnp.float32)
    expert_range = jnp.arange(expert_count, dtype=jnp.int32)
    matches = expert_ids[:, :, None] == expert_range[None, None, :]
    chosen = jnp.sum(jnp.where(matches, logits[:, None, :], 0.0), axis=2)
    gate_weights = jax.nn.softmax(chosen, axis=-1)

    row_chunks_in = gather_chunks(hidden_two)
    local_range = first_expert + jnp.arange(local_experts, dtype=jnp.int32)

    def expert_chunk(rows_in, grads_in, ids):
        pairs = ids.shape[0] // 2
        tokens_in = 2 * block_len
        ids = ids.reshape(pairs, tokens_in, top_count)
        named = jnp.any(ids[..., None] == expert_range, axis=2)
        scored = jnp.dot(rows_in, w_router, preferred_element_type=jnp.float32)
        scored = jnp.where(named, scored.reshape(pairs, tokens_in, expert_count), masked)
        gates = jax.nn.softmax(scored, axis=-1)
        gates = lax.dynamic_slice_in_dim(gates, first_expert, local_experts, 2)
        hits = jnp.any(ids[..., None] == local_range, axis=2)
        counts = hits.astype(jnp.int32)
        slot = jnp.where(hits, jnp.cumsum(counts, axis=1) - counts, -1)
        pick = slot.transpose(0, 2, 1)[:, :, None, :] == jnp.arange(pair_cap)[:, None]
        select = pick.astype(narrow).reshape(pairs, local_experts * pair_cap, tokens_in)
        row_gates = jnp.sum(jnp.where(pick, gates.transpose(0, 2, 1)[:, :, None, :], 0.0), axis=3)
        row_gates = row_gates.transpose(1, 0, 2).reshape(local_experts, pairs * pair_cap, 1)

        def spread(source):
            source = source.reshape(pairs, tokens_in, model_width)
            out = jnp.einsum("prt,ptd->prd", select, source, preferred_element_type=narrow)
            out = out.reshape(pairs, local_experts, pair_cap, model_width)
            return out.transpose(1, 0, 2, 3).reshape(local_experts, pairs * pair_cap, model_width)

        def combine(rows):
            rows = rows.astype(narrow).reshape(local_experts, pairs, pair_cap, model_width)
            rows = rows.transpose(1, 0, 2, 3).reshape(pairs, -1, model_width)
            out = jnp.einsum("prt,prd->ptd", select, rows, preferred_element_type=jnp.float32)
            return out.astype(narrow)

        rows = spread(rows_in)
        row_grads = spread(grads_in)
        gate_pre = jnp.einsum("lrd,ldf->lrf", rows, w_gate, preferred_element_type=jnp.float32)
        up_pre = jnp.einsum("lrd,ldf->lrf", rows, w_up, preferred_element_type=jnp.float32)
        plain = jnp.einsum("lrd,lfd->lrf", row_grads, w_down, preferred_element_type=jnp.float32)
        sigmoid_gate = jax.nn.sigmoid(gate_pre)
        silu_gate = gate_pre * sigmoid_gate
        activation = silu_gate * up_pre
        gate_sums = jnp.sum(activation * plain, axis=2)
        grad_act = row_gates * plain
        gated = (row_gates * activation).astype(narrow)
        grad_gate = grad_act * up_pre * sigmoid_gate * (1.0 + gate_pre * (1.0 - sigmoid_gate))
        grad_gate = grad_gate.astype(narrow)
        grad_up = (grad_act * silu_gate).astype(narrow)
        forward_rows = jnp.einsum("lrf,lfd->lrd", gated, w_down, preferred_element_type=jnp.float32)
        back_rows = jnp.einsum("lrf,ldf->lrd", grad_gate, w_gate, preferred_element_type=jnp.float32)
        back_rows = back_rows + jnp.einsum(
            "lrf,ldf->lrd", grad_up, w_up, preferred_element_type=jnp.float32
        )
        gate_sums = gate_sums.reshape(local_experts, pairs, pair_cap).transpose(1, 0, 2)
        gate_sums = jnp.sum(jnp.where(pick, gate_sums[..., None], 0.0), axis=2)
        gate_sums = gate_sums.reshape(pairs, local_experts, 2, block_len).transpose(0, 2, 1, 3)
        gate_sums = gate_sums.reshape(2 * pairs, local_experts, block_len)
        kept = (rows, row_grads, gated, grad_gate, grad_up)
        return (combine(forward_rows), combine(back_rows), gate_sums, kept)

    mixed_parts, back_parts, sums_parts, kept_parts = [], [], [], []
    for index, (rows_in, grads_in) in enumerate(zip(row_chunks_in, grad_chunks_in)):
        done = expert_chunk(rows_in, grads_in, ids_by_slot[8 * index : 8 * index + 8])
        mixed_parts.append(done[0])
        back_parts.append(done[1])
        sums_parts.append(done[2])
        kept_parts.append(done[3])

    slot_sums = jnp.concatenate(sums_parts, axis=0)
    place = jnp.sum(
        jnp.where(sources[None, :] == jnp.arange(device_count)[:, None], jnp.arange(device_count), 0),
        axis=1,
    )
    wide = jnp.zeros((device_count, expert_count, block_len), jnp.float32)
    wide = lax.dynamic_update_slice_in_dim(
        wide, jnp.take(slot_sums, place, axis=0), first_expert, 1
    )
    own_sums = lax.psum_scatter(wide, BOTH, scatter_dimension=0, tiled=True)[0].T

    grad_out = cotangent.astype(jnp.float32)
    grad_hidden_disp = reduce_chunks(back_parts)
    grad_gates = jnp.sum(jnp.where(matches, own_sums[:, None, :], 0.0), axis=2)
    grad_chosen = gate_weights * (
        grad_gates - jnp.sum(gate_weights * grad_gates, axis=-1, keepdims=True)
    )
    grad_logits = jnp.sum(jnp.where(matches, grad_chosen[:, :, None], 0.0), axis=1).astype(narrow)
    grad_router = jnp.einsum(
        "ld,le->de", hidden_two, grad_logits, preferred_element_type=jnp.float32
    )
    grad_hidden_two = grad_hidden_disp + jnp.einsum(
        "le,de->ld", grad_logits, w_router, preferred_element_type=jnp.float32
    )
    grad_normed_two, grad_gain_moe = norm_backward(middle, inverse_two, gain_moe, grad_hidden_two)
    grad_middle = grad_out + grad_normed_two
    grad_attn = grad_middle.astype(narrow)

    across = swap(grad_attn, ACROSS)
    grad_attn_all = jnp.concatenate(
        [grad_attn, swap(grad_attn, CORE), across, swap(across, CORE)], axis=0
    )
    mixed_parts, grad_attn_all = lax.optimization_barrier((mixed_parts, grad_attn_all))
    mixed_out = (middle + reduce_chunks(mixed_parts)).astype(narrow)

    kept = [jnp.concatenate(parts, axis=1) for parts in zip(*kept_parts)]
    rows_all, row_grads_all, gated_all, grad_gate_all, grad_up_all = kept
    grad_w_down = jnp.einsum(
        "lrf,lrd->lfd", gated_all, row_grads_all, preferred_element_type=jnp.float32
    )
    grad_w_gate = jnp.einsum(
        "lrd,lrf->ldf", rows_all, grad_gate_all, preferred_element_type=jnp.float32
    )
    grad_w_up = jnp.einsum("lrd,lrf->ldf", rows_all, grad_up_all, preferred_element_type=jnp.float32)

    grad_w_out = jnp.einsum(
        "lh,ld->hd", head_rows, grad_attn_all, preferred_element_type=jnp.float32
    )
    grad_heads = (
        jnp.einsum("ld,hd->lh", grad_attn_all, w_out, preferred_element_type=jnp.float32)
        .astype(narrow)
        .reshape(seq_length, local_heads, HD)
    )
    probability = jnp.exp(masked_scores() - log_total)
    grad_values = jnp.einsum(
        "hqk,qhd->khd", probability.astype(narrow), grad_heads, preferred_element_type=jnp.float32
    )
    grad_prob = jnp.einsum(
        "qhd,khd->hqk", grad_heads, value_rows, preferred_element_type=jnp.float32
    )
    row_delta = jnp.sum(probability * grad_prob, axis=-1, keepdims=True)
    grad_scores = (probability * (grad_prob - row_delta)).astype(narrow)
    grad_query = score_scale * jnp.einsum(
        "hqk,khd->qhd", grad_scores, key_rows, preferred_element_type=jnp.float32
    )
    grad_keys = score_scale * jnp.einsum(
        "hqk,qhd->khd", grad_scores, queries, preferred_element_type=jnp.float32
    )

    def flat(source):
        return source.astype(narrow).reshape(seq_length, local_heads * HD)

    grad_query_raw = flat(rotate(grad_query, cosine_table, -sine_table))
    grad_key_raw = flat(rotate(grad_keys, cosine_table, -sine_table))
    grad_value_raw = flat(grad_values)

    def weight_grad(grad_raw):
        return jnp.einsum("ld,lh->dh", hidden_one, grad_raw, preferred_element_type=jnp.float32)

    def back(grad_raw, weights):
        return jnp.einsum("lh,dh->ld", grad_raw, weights, preferred_element_type=jnp.float32)

    grad_hidden_one = reduce_quarters(
        back(grad_query_raw, w_query) + back(grad_key_raw, w_key) + back(grad_value_raw, w_value)
    )
    grad_normed_one, grad_gain_attn = norm_backward(
        own_inputs, own_inverse, gain_attn, grad_hidden_one
    )
    grad_tokens = grad_middle + grad_normed_one
    attn_sums = lax.psum(
        tuple(
            part.astype(narrow)
            for part in (
                weight_grad(grad_query_raw),
                weight_grad(grad_key_raw),
                weight_grad(grad_value_raw),
                grad_w_out,
            )
        ),
        "expert",
    )
    attn_sums = [part.astype(jnp.float32) for part in attn_sums]
    small = jnp.concatenate([grad_router, grad_gain_attn[:, None], grad_gain_moe[:, None]], axis=1)
    small = lax.psum(small, BOTH)
    return (
        mixed_out,
        grad_tokens,
        small[:, expert_count],
        attn_sums[0],
        attn_sums[1],
        attn_sums[2],
        attn_sums[3],
        small[:, expert_count + 1],
        small[:, :expert_count],
        grad_w_gate,
        grad_w_up,
        grad_w_down,
    )


def on_device(*operands):
    tokens, w_router, w_gate, expert_ids = operands[0], operands[7], operands[8], operands[11]
    owners, quarters = lax.axis_size("expert"), lax.axis_size("tensor")
    block_len, top_count = expert_ids.shape
    capacity = 3 * block_len * top_count // (2 * w_router.shape[1])
    buffer_rows = capacity * quarters * owners * w_gate.shape[0]
    gathers = owners * tokens.shape[0] <= buffer_rows and (owners, quarters) == (8, 4)
    return (gathered_layer if gathers else routed_layer)(*operands)


def solution(mesh):
    return jax.shard_map(
        on_device,
        mesh=mesh,
        in_specs=(
            P("expert", None),
            P(),
            P(None, "tensor"),
            P(None, "tensor"),
            P(None, "tensor"),
            P("tensor", None),
            P(),
            P(),
            P("expert", None, "tensor"),
            P("expert", None, "tensor"),
            P("expert", "tensor", None),
            P(("expert", "tensor"), None),
            P(("expert", "tensor"), None),
        ),
        out_specs=(
            P(("expert", "tensor"), None),
            P(("expert", "tensor"), None),
            P(),
            P(None, "tensor"),
            P(None, "tensor"),
            P(None, "tensor"),
            P("tensor", None),
            P(),
            P(),
            P("expert", None, "tensor"),
            P("expert", None, "tensor"),
            P("expert", "tensor", None),
        ),
        check_vma=False,
    )
```

```python
import functools

import jax
import jax.numpy as jnp
from jax import lax
from jax.experimental import pallas as pl
from jax.experimental.pallas import tpu as pltpu
from jax.sharding import PartitionSpec as P

HD = 128


eps = 1e-06
theta_base = 10000.0
masked = -1e30

BOTH = ("expert", "tensor")
CORE, ACROSS, ASIDE, PLANE_NEXT, PLANE_FAR = 1, 2, 4, 8, 16
PLANES = (0, PLANE_NEXT, PLANE_FAR, PLANE_NEXT | PLANE_FAR)
BLOCKS = 8
WEIGHT_SLOTS = 3

(
    G,
    H,
    M,
    R,
    IDS,
    QUERIES,
    KEYS,
    VALUES,
    TOTALS,
    HEADS,
    KEPT,
    SENT,
    RAW,
    HOME,
    SUMS,
    NEAR,
    AWAY,
    OTHER,
    FAR,
    OWN,
    SIDE,
    FULL,
    GOT,
    QUERY,
    KEY,
    VALUE,
    OUT,
    TOKENS,
    SLOTS,
    NAMED,
    ROUTER,
    GATES,
    ATTN,
    RELAY,
    MIXED,
    EXPERTS,
    SMALL,
    GAIN,
) = range(38)


def rope_tables(seq_length, head_size):
    half_dim = head_size // 2
    frequency = jnp.exp(
        -jnp.log(theta_base) * jnp.arange(half_dim, dtype=jnp.float32) * (2.0 / head_size)
    )
    angles = jnp.arange(seq_length, dtype=jnp.float32)[:, None] * frequency[None, :]
    return (jnp.cos(angles)[:, None, :], jnp.sin(angles)[:, None, :])


def rotate(source, cosine_table, sine_table):
    half_dim = source.shape[-1] // 2
    first_half = source[..., :half_dim]
    second = source[..., half_dim:]
    return jnp.concatenate(
        [
            first_half * cosine_table - second * sine_table,
            second * cosine_table + first_half * sine_table,
        ],
        axis=-1,
    )


def norm_forward(source, gain_vec):
    inverse = lax.rsqrt(jnp.mean(source * source, axis=-1, keepdims=True) + eps)
    return (inverse, source * inverse * gain_vec)


def norm_backward(source, inverse, gain_vec, grad_in):
    scaled = gain_vec * grad_in
    grad_source = inverse * scaled - source * inverse**3 * jnp.mean(
        scaled * source, axis=-1, keepdims=True
    )
    grad_gain = jnp.sum(grad_in * source * inverse, axis=0)
    return (grad_source, grad_gain)


def block_scores(q_block, key_rows, first_row, score_scale):
    scores = (
        jnp.einsum("qgrd,kgd->grqk", q_block, key_rows, preferred_element_type=jnp.float32)
        * score_scale
    )
    row_ids = first_row + jnp.arange(q_block.shape[0], dtype=jnp.int32)
    allowed = row_ids[:, None] >= jnp.arange(key_rows.shape[0], dtype=jnp.int32)[None, :]
    return jnp.where(allowed, scores, masked)


def routed_layer(
    tokens,
    gain_attn,
    w_query,
    w_key,
    w_value,
    w_out,
    gain_moe,
    w_router,
    w_gate,
    w_up,
    w_down,
    expert_ids,
    cotangent,
):
    seq_length, model_width = tokens.shape
    block_len, top_count = expert_ids.shape
    expert_count = w_router.shape[1]
    local_experts = w_gate.shape[0]
    local_heads = w_query.shape[1] // HD
    local_groups = w_key.shape[1] // HD
    group_size = local_heads // local_groups
    owners = lax.axis_size("expert")
    quarter = lax.axis_index("tensor")
    capacity = 3 * block_len * top_count // (2 * expert_count)
    block_rows = min(512, seq_length)
    block_count = seq_length // block_rows
    score_scale = HD ** (-0.5)
    first_own = quarter * block_len
    inputs = tokens.astype(jnp.float32)
    inverse_one, normed_one = norm_forward(inputs, gain_attn)
    hidden_one = normed_one.astype(jnp.bfloat16)
    cosine_table, sine_table = rope_tables(seq_length, HD)

    def rope_heads(source):
        return rotate(source, cosine_table, sine_table)

    query_raw = jnp.dot(hidden_one, w_query, preferred_element_type=jnp.float32).reshape(
        seq_length, local_heads, HD
    )
    key_raw = jnp.dot(hidden_one, w_key, preferred_element_type=jnp.float32).reshape(
        seq_length, local_groups, HD
    )
    queries = rope_heads(query_raw).astype(jnp.bfloat16)
    key_rows = rope_heads(key_raw).astype(jnp.bfloat16)
    value_rows = (
        jnp.dot(hidden_one, w_value, preferred_element_type=jnp.float32)
        .astype(jnp.bfloat16)
        .reshape(seq_length, local_groups, HD)
    )
    query_blocks = queries.reshape(block_count, block_rows, local_groups, group_size, HD)
    starts = jnp.arange(block_count, dtype=jnp.int32) * block_rows

    def attend_block(packed):
        first_row, q_block = packed
        scores = block_scores(q_block, key_rows, first_row, score_scale)
        row_max = jnp.max(scores, axis=-1, keepdims=True)
        exponent = jnp.exp(scores - row_max)
        row_total = jnp.sum(exponent, axis=-1, keepdims=True)
        weights = (exponent / row_total).astype(jnp.bfloat16)
        head_out = jnp.einsum(
            "grqk,kgd->qgrd", weights, value_rows, preferred_element_type=jnp.float32
        )
        return (head_out.astype(jnp.bfloat16), (row_max + jnp.log(row_total))[..., 0])

    head_blocks, log_totals = lax.map(attend_block, (starts, query_blocks))
    head_rows = head_blocks.reshape(seq_length, local_heads * HD)
    attention = lax.psum_scatter(
        jnp.dot(head_rows, w_out, preferred_element_type=jnp.float32),
        "tensor",
        scatter_dimension=0,
        tiled=True,
    )
    own_inputs = lax.dynamic_slice_in_dim(inputs, first_own, block_len, 0)
    own_inverse = lax.dynamic_slice_in_dim(inverse_one, first_own, block_len, 0)
    middle = own_inputs + attention
    inverse_two, normed_two = norm_forward(middle, gain_moe)
    hidden_two = normed_two.astype(jnp.bfloat16)
    logits = jnp.dot(hidden_two, w_router, preferred_element_type=jnp.float32)
    expert_range = jnp.arange(expert_count, dtype=jnp.int32)
    matches = expert_ids[:, :, None] == expert_range[None, None, :]
    chosen = jnp.sum(jnp.where(matches, logits[:, None, :], 0.0), axis=2)
    gate_weights = jax.nn.softmax(chosen, axis=-1)
    expert_hits = jnp.sum(matches.astype(jnp.int32), axis=1)
    earlier = jnp.cumsum(expert_hits, axis=0) - expert_hits
    slot_of = jnp.sum(jnp.where(matches, earlier[:, None, :], 0), axis=2)
    place = (slot_of * expert_count + expert_ids).reshape(-1)
    token_rows = jnp.broadcast_to(
        hidden_two[:, None, :], (block_len, top_count, model_width)
    ).reshape(block_len * top_count, model_width)
    grad_out = cotangent.astype(jnp.float32)
    gated_grads = (
        (gate_weights[:, :, None] * grad_out[:, None, :])
        .astype(jnp.bfloat16)
        .reshape(block_len * top_count, model_width)
    )
    empty = jnp.zeros((capacity * expert_count, model_width), jnp.bfloat16)
    send_rows = empty.at[place].set(token_rows).reshape(capacity, expert_count, model_width)
    send_grads = empty.at[place].set(gated_grads).reshape(capacity, expert_count, model_width)
    arrived_rows, arrived_grads = (
        lax.all_to_all(send_rows, "expert", split_axis=1, concat_axis=1, tiled=True),
        lax.all_to_all(send_grads, "expert", split_axis=1, concat_axis=1, tiled=True),
    )
    routed = arrived_rows.reshape(capacity, owners, local_experts, model_width)
    grads_in = arrived_grads.reshape(capacity, owners, local_experts, model_width)
    all_rows, all_grads = (
        lax.all_gather(routed, "tensor", axis=0, tiled=True),
        lax.all_gather(grads_in, "tensor", axis=0, tiled=True),
    )
    gate_pre = jnp.einsum("csld,ldf->cslf", all_rows, w_gate, preferred_element_type=jnp.float32)
    up_pre = jnp.einsum("csld,ldf->cslf", all_rows, w_up, preferred_element_type=jnp.float32)
    sigmoid_gate = jax.nn.sigmoid(gate_pre)
    silu_gate = gate_pre * sigmoid_gate
    activation = (silu_gate * up_pre).astype(jnp.bfloat16)
    grad_w_down = jnp.einsum(
        "cslf,csld->lfd", activation, all_grads, preferred_element_type=jnp.float32
    )
    grad_act = jnp.einsum("csld,lfd->cslf", all_grads, w_down, preferred_element_type=jnp.float32)
    grad_gate = (grad_act * up_pre * sigmoid_gate * (1.0 + gate_pre * (1.0 - sigmoid_gate))).astype(
        jnp.bfloat16
    )
    grad_up = (grad_act * silu_gate).astype(jnp.bfloat16)
    grad_w_gate = jnp.einsum(
        "csld,cslf->ldf", all_rows, grad_gate, preferred_element_type=jnp.float32
    )
    grad_w_up = jnp.einsum("csld,cslf->ldf", all_rows, grad_up, preferred_element_type=jnp.float32)
    forward_term = jnp.einsum(
        "cslf,lfd->csld", activation, w_down, preferred_element_type=jnp.float32
    )
    back_term = jnp.einsum("cslf,ldf->csld", grad_gate, w_gate, preferred_element_type=jnp.float32)
    back_term = back_term + jnp.einsum(
        "cslf,ldf->csld", grad_up, w_up, preferred_element_type=jnp.float32
    )
    both_terms = lax.psum_scatter(
        jnp.concatenate([forward_term, back_term], axis=3).astype(jnp.bfloat16),
        "tensor",
        scatter_dimension=0,
        tiled=True,
    )
    returned = both_terms[..., :model_width]
    row_grads = both_terms[..., model_width:]
    returned_home, row_grads_home = (
        lax.all_to_all(
            returned.reshape(capacity, expert_count, model_width),
            "expert",
            split_axis=1,
            concat_axis=1,
            tiled=True,
        ),
        lax.all_to_all(
            row_grads.reshape(capacity, expert_count, model_width),
            "expert",
            split_axis=1,
            concat_axis=1,
            tiled=True,
        ),
    )
    picked = returned_home.reshape(capacity * expert_count, model_width)[place].reshape(
        block_len, top_count, model_width
    )
    mixture = jnp.sum(gate_weights[:, :, None] * picked, axis=1)
    mixed_out = (middle + mixture).astype(jnp.bfloat16)
    grad_gates = jnp.sum(picked * grad_out[:, None, :], axis=2)
    grad_picked = row_grads_home.reshape(capacity * expert_count, model_width)[place].reshape(
        block_len, top_count, model_width
    )
    grad_hidden_disp = jnp.einsum(
        "lk,lkd->ld",
        jnp.ones((block_len, top_count), jnp.bfloat16),
        grad_picked,
        preferred_element_type=jnp.float32,
    )
    grad_chosen = gate_weights * (
        grad_gates - jnp.sum(gate_weights * grad_gates, axis=-1, keepdims=True)
    )
    grad_logits = jnp.sum(jnp.where(matches, grad_chosen[:, :, None], 0.0), axis=1).astype(
        jnp.bfloat16
    )
    grad_router = jnp.einsum(
        "ld,le->de", hidden_two, grad_logits, preferred_element_type=jnp.float32
    )
    grad_hidden_two = grad_hidden_disp + jnp.einsum(
        "le,de->ld", grad_logits, w_router, preferred_element_type=jnp.float32
    )
    grad_normed_two, grad_gain_moe = norm_backward(middle, inverse_two, gain_moe, grad_hidden_two)
    grad_middle = grad_out + grad_normed_two
    grad_attn = grad_middle.astype(jnp.bfloat16)
    grad_attn_all = lax.all_gather(grad_attn, "tensor", axis=0, tiled=True)
    grad_w_out = jnp.einsum(
        "lh,ld->hd", head_rows, grad_attn_all, preferred_element_type=jnp.float32
    )
    grad_heads = jnp.einsum(
        "ld,hd->lh", grad_attn_all, w_out, preferred_element_type=jnp.float32
    ).astype(jnp.bfloat16)
    grad_blocks = grad_heads.reshape(block_count, block_rows, local_groups, group_size, HD)

    def back_block(carried, packed):
        grad_keys, grad_values = carried
        first_row, q_block, g_block, lse_block = packed
        scores = block_scores(q_block, key_rows, first_row, score_scale)
        probability = jnp.exp(scores - lse_block[..., None])
        grad_values = grad_values + jnp.einsum(
            "grqk,qgrd->kgd",
            probability.astype(jnp.bfloat16),
            g_block,
            preferred_element_type=jnp.float32,
        )
        grad_prob = jnp.einsum(
            "qgrd,kgd->grqk", g_block, value_rows, preferred_element_type=jnp.float32
        )
        row_delta = jnp.sum(probability * grad_prob, axis=-1, keepdims=True)
        grad_scores = (probability * (grad_prob - row_delta)).astype(jnp.bfloat16)
        grad_query = (
            jnp.einsum("grqk,kgd->qgrd", grad_scores, key_rows, preferred_element_type=jnp.float32)
            * score_scale
        )
        grad_keys = (
            grad_keys
            + jnp.einsum("grqk,qgrd->kgd", grad_scores, q_block, preferred_element_type=jnp.float32)
            * score_scale
        )
        return ((grad_keys, grad_values), grad_query)

    zero_keys = jnp.zeros((seq_length, local_groups, HD), jnp.float32)
    (grad_keys, grad_values), grad_query_blocks = lax.scan(
        back_block, (zero_keys, zero_keys), (starts, query_blocks, grad_blocks, log_totals)
    )
    grad_query = grad_query_blocks.reshape(seq_length, local_heads, HD)
    grad_query_raw = (
        jax.vjp(rope_heads, query_raw)[1](grad_query)[0]
        .reshape(seq_length, local_heads * HD)
        .astype(jnp.bfloat16)
    )
    grad_key_raw = (
        jax.vjp(rope_heads, key_raw)[1](grad_keys)[0]
        .reshape(seq_length, local_groups * HD)
        .astype(jnp.bfloat16)
    )
    grad_value_raw = grad_values.reshape(seq_length, local_groups * HD).astype(jnp.bfloat16)
    grad_w_query = jnp.einsum(
        "ld,lh->dh", hidden_one, grad_query_raw, preferred_element_type=jnp.float32
    )
    grad_w_key = jnp.einsum(
        "ld,lh->dh", hidden_one, grad_key_raw, preferred_element_type=jnp.float32
    )
    grad_w_value = jnp.einsum(
        "ld,lh->dh", hidden_one, grad_value_raw, preferred_element_type=jnp.float32
    )
    term = jnp.einsum("lh,dh->ld", grad_query_raw, w_query, preferred_element_type=jnp.float32)
    term = term + jnp.einsum("lh,dh->ld", grad_key_raw, w_key, preferred_element_type=jnp.float32)
    grad_hidden_one = lax.psum_scatter(
        (
            term
            + jnp.einsum("lh,dh->ld", grad_value_raw, w_value, preferred_element_type=jnp.float32)
        ).astype(jnp.bfloat16),
        "tensor",
        scatter_dimension=0,
        tiled=True,
    ).astype(jnp.float32)
    grad_normed_one, grad_gain_attn = norm_backward(
        own_inputs, own_inverse, gain_attn, grad_hidden_one
    )
    grad_tokens = grad_middle + grad_normed_one
    attn_sums = lax.psum((grad_w_query, grad_w_key, grad_w_value, grad_w_out), "expert")
    small_sums = lax.psum((grad_gain_attn, grad_gain_moe, grad_router), ("expert", "tensor"))
    return (
        mixed_out,
        grad_tokens,
        small_sums[0],
        attn_sums[0],
        attn_sums[1],
        attn_sums[2],
        attn_sums[3],
        small_sums[1],
        small_sums[2],
        grad_w_gate,
        grad_w_up,
        grad_w_down,
    )


ROWS_ROWS = (((1,), (1,)), ((), ()))
def dot_nt(left, right):
    return lax.dot_general(left, right, ROWS_ROWS, preferred_element_type=jnp.float32)


def dot_nn(left, right):
    return jnp.dot(left, right, preferred_element_type=jnp.float32)


def expert_kernel(*refs):
    blocks = 2 * BLOCKS
    row_refs, grad_refs = refs[:BLOCKS], refs[BLOCKS:blocks]
    slot_ref, named_ref, router_ref, gate_ref, up_ref, down_ref = refs[blocks : blocks + 6]
    outs = refs[blocks + 6 : blocks + 15]
    mixed_refs, back_refs, sums_ref = outs[:2], outs[2:4], outs[4]
    rows_s, grads_s, x_s, y_s, back_s, out_s, pick_s, place_s = refs[blocks + 15 : blocks + 23]
    gates_s, sums_s, gated_s, side_s, both_s, down_s = refs[blocks + 23 : blocks + 29]
    sems, weight_sems, out_sems, kept_sems = refs[blocks + 29 :]
    pairs, wide, _ = pick_s.shape
    experts = x_s.shape[0]
    hidden = down_s.shape[1]
    cap = wide // experts
    tokens_in = rows_s.shape[1]
    block_len = tokens_in // 2
    narrow = jnp.bfloat16

    def copies(pair):
        out = []
        for half in range(2):
            place = pl.ds(half * block_len, block_len)
            at = 2 * pair + half
            out.append(
                pltpu.make_async_copy(row_refs[at], rows_s.at[pair, place], sems.at[0, at])
            )
            out.append(
                pltpu.make_async_copy(grad_refs[at], grads_s.at[pair, place], sems.at[1, at])
            )
        return out

    def weight_copies(expert, slot):
        sides = [both_s.at[slot, :, pl.ds(k * hidden, hidden)] for k in range(2)]
        return [
            pltpu.make_async_copy(gate_ref.at[expert], sides[0], weight_sems.at[0, slot]),
            pltpu.make_async_copy(up_ref.at[expert], sides[1], weight_sems.at[1, slot]),
            pltpu.make_async_copy(down_ref.at[expert], down_s.at[slot], weight_sems.at[2, slot]),
        ]

    def result_copies(pair):
        half = pairs // 2
        place = pl.ds((pair % half) * tokens_in, tokens_in)
        sides = (rows_s, mixed_refs), (grads_s, back_refs)
        return [
            pltpu.make_async_copy(
                source.at[pair], targets[pair // half].at[place], out_sems.at[k, pair]
            )
            for k, (source, targets) in enumerate(sides)
        ]

    kept_copies = [
        pltpu.make_async_copy(source, target, kept_sems.at[k])
        for k, (source, target) in enumerate(zip((x_s, y_s, gated_s, side_s), outs[5:9]))
    ]

    for pair in range(pairs):
        for copy in copies(pair):
            copy.start()
    for slot in range(WEIGHT_SLOTS):
        for copy in weight_copies(slot, slot):
            copy.start()

    for pair in range(pairs):
        for copy in copies(pair):
            copy.wait()
        rows_in = rows_s[pair]
        logits = dot_nt(router_ref[...], rows_in)
        named = named_ref[pair]
        logits = jnp.where(named > 0.0, logits, masked)
        weights = jnp.exp(logits - jnp.max(logits, axis=0, keepdims=True)) * named
        gates = weights / jnp.sum(weights, axis=0, keepdims=True)
        ranks = lax.broadcasted_iota(jnp.int32, (cap, tokens_in), 0)
        place = pl.ds(pair * cap, cap)
        picks = []
        for expert in range(experts):
            pick = ranks == slot_ref[pair, expert : expert + 1, :]
            row_gates = jnp.sum(
                jnp.where(pick, gates[expert : expert + 1, :], 0.0), axis=1, keepdims=True
            )
            gates_s[expert, place, :] = jnp.broadcast_to(row_gates, (cap, 128))
            picks.append(jnp.where(pick, 1.0, 0.0))
        pick_all = jnp.concatenate(picks, axis=0)
        pick_low = pick_all.astype(narrow)
        pick_s[pair] = pick_low
        place_s[pair] = pick_all.T.astype(narrow)
        for source, target in ((rows_in, x_s), (grads_s[pair], y_s)):
            spread = dot_nn(pick_low, source).astype(narrow)
            for expert in range(experts):
                target[expert, place, :] = spread[expert * cap : (expert + 1) * cap]

    kept_copies[0].start()
    kept_copies[1].start()

    def expert_step(expert, carried):
        slot = lax.rem(expert, WEIGHT_SLOTS)
        for copy in weight_copies(expert, slot):
            copy.wait()
        both = dot_nn(x_s[expert], both_s[slot])
        gate_pre, up_pre = both[:, :hidden], both[:, hidden:]
        plain = dot_nt(y_s[expert], down_s[slot])
        sigmoid_gate = jax.nn.sigmoid(gate_pre)
        silu_gate = gate_pre * sigmoid_gate
        activation = silu_gate * up_pre
        row_gates = gates_s[expert][:, :1]
        sums = jnp.sum(activation * plain, axis=1, keepdims=True)
        sums_s[expert] = jnp.broadcast_to(sums, sums_s.shape[1:])
        grad_act = row_gates * plain
        gated = (row_gates * activation).astype(narrow)
        slope = sigmoid_gate * (1.0 + gate_pre * (1.0 - sigmoid_gate))
        grad_gate = (grad_act * up_pre * slope).astype(narrow)
        grad_up = (grad_act * silu_gate).astype(narrow)
        grad_both = jnp.concatenate([grad_gate, grad_up], axis=1)
        gated_s[expert] = gated
        side_s[expert] = grad_both
        out_s[expert] = dot_nn(gated, down_s[slot]).astype(narrow)
        back_s[expert] = dot_nt(grad_both, both_s[slot]).astype(narrow)

        @pl.when(expert + WEIGHT_SLOTS < experts)
        def _():
            for copy in weight_copies(expert + WEIGHT_SLOTS, slot):
                copy.start()

        return carried

    lax.fori_loop(0, experts, expert_step, 0)
    kept_copies[2].start()
    kept_copies[3].start()

    for pair in range(pairs):
        sides = pl.ds(pair * cap, cap)
        for source, target in ((out_s, rows_s), (back_s, grads_s)):
            stacked = jnp.concatenate(
                [source[expert, sides, :] for expert in range(experts)], axis=0
            )
            target[pair] = dot_nn(place_s[pair], stacked).astype(narrow)
        for copy in result_copies(pair):
            copy.start()
        pick = pick_s[pair].astype(jnp.float32)
        sums = []
        for expert in range(experts):
            column = sums_s[expert, sides, :][:, :1]
            part = pick[expert * cap : (expert + 1) * cap] * column
            sums.append(jnp.sum(part, axis=0, keepdims=True))
        sums_ref[pair] = jnp.concatenate(sums, axis=0)

    for copy in kept_copies:
        copy.wait()
    for pair in range(pairs):
        for copy in result_copies(pair):
            copy.wait()


def expert_chunk(rows_in, grads_in, slots, named, router, w_gate, w_up, w_down, cap):
    pairs, experts, tokens_in = slots.shape
    width, hidden = w_gate.shape[1:]
    rows = pairs * cap
    narrow, wide = jnp.bfloat16, jnp.float32
    shape = jax.ShapeDtypeStruct
    anywhere = pl.BlockSpec(memory_space=pl.ANY)
    inside = pl.BlockSpec(memory_space=pltpu.VMEM)
    half_shape = shape((pairs // 2 * tokens_in, width), narrow)
    whole_rows = (experts, rows, width)
    return pl.pallas_call(
        expert_kernel,
        in_specs=[anywhere] * (2 * BLOCKS) + [inside] * 3 + [anywhere] * 3,
        out_specs=[anywhere] * 4 + [inside] + [anywhere] * 4,
        out_shape=[half_shape] * 4
        + [
            shape((pairs, experts, tokens_in), wide),
            shape(whole_rows, narrow),
            shape(whole_rows, narrow),
            shape((experts, rows, hidden), narrow),
            shape((experts, rows, 2 * hidden), narrow),
        ],
        scratch_shapes=[pltpu.VMEM((pairs, tokens_in, width), narrow)] * 2
        + [pltpu.VMEM(whole_rows, narrow)] * 4
        + [
            pltpu.VMEM((pairs, experts * cap, tokens_in), narrow),
            pltpu.VMEM((pairs, tokens_in, experts * cap), narrow),
            pltpu.VMEM((experts, rows, 128), wide),
            pltpu.VMEM((experts, rows, 128), wide),
            pltpu.VMEM((experts, rows, hidden), narrow),
            pltpu.VMEM((experts, rows, 2 * hidden), narrow),
            pltpu.VMEM((WEIGHT_SLOTS, width, 2 * hidden), narrow),
            pltpu.VMEM((WEIGHT_SLOTS, hidden, width), narrow),
            pltpu.SemaphoreType.DMA((2, BLOCKS)),
            pltpu.SemaphoreType.DMA((3, WEIGHT_SLOTS)),
            pltpu.SemaphoreType.DMA((2, pairs)),
            pltpu.SemaphoreType.DMA((4,)),
        ],
        compiler_params=pltpu.CompilerParams(vmem_limit_bytes=60 << 20),
        cost_estimate=pl.CostEstimate(
            flops=24 * experts * rows * width * hidden,
            bytes_accessed=6 * experts * width * hidden + 4 * experts * rows * width,
            transcendentals=experts * rows * hidden,
        ),
    )(*rows_in, *grads_in, slots, named, router, w_gate, w_up, w_down)


def weight_kernel(parts, given, *refs):
    ins, (gate_ref, up_ref, down_ref) = refs[: 4 * parts], refs[4 * parts + given :]
    rows, grads, gated, both = [
        jnp.concatenate([ref[0] for ref in ins[k * parts : (k + 1) * parts]], axis=0)
        for k in range(4)
    ]
    turn = (((0,), (0,)), ((), ()))
    hidden = gated.shape[1]
    down_ref[0] = lax.dot_general(gated, grads, turn, preferred_element_type=jnp.float32)
    sides = lax.dot_general(rows, both, turn, preferred_element_type=jnp.float32)
    gate_ref[0] = sides[:, :hidden]
    up_ref[0] = sides[:, hidden:]


def weight_grads(kept, begin, count, partial):
    parts = len(kept)
    experts, rows, width = kept[0][0].shape
    hidden = kept[0][2].shape[2]
    operands = [part[k] for k in range(4) for part in kept]
    shape = jax.ShapeDtypeStruct

    def spec(rows, columns):
        return pl.BlockSpec((1, rows, columns), lambda i: (i + begin, 0, 0))

    return pl.pallas_call(
        functools.partial(weight_kernel, parts, len(partial)),
        grid=(count,),
        in_specs=[spec(rows, operand.shape[2]) for operand in operands]
        + [pl.BlockSpec(memory_space=pl.ANY)] * len(partial),
        out_specs=[spec(width, hidden), spec(width, hidden), spec(hidden, width)],
        out_shape=[
            shape((experts, width, hidden), jnp.float32),
            shape((experts, width, hidden), jnp.float32),
            shape((experts, hidden, width), jnp.float32),
        ],
        input_output_aliases={len(operands) + k: k for k in range(len(partial))},
        compiler_params=pltpu.CompilerParams(vmem_limit_bytes=56 << 20),
        cost_estimate=pl.CostEstimate(
            flops=6 * parts * count * rows * width * hidden,
            bytes_accessed=count * (parts * rows * (4 * width + 6 * hidden) + 12 * width * hidden),
            transcendentals=0,
        ),
    )(*operands, *partial)


def gathered_layer(
    tokens,
    gain_attn,
    w_query,
    w_key,
    w_value,
    w_out,
    gain_moe,
    w_router,
    w_gate,
    w_up,
    w_down,
    expert_ids,
    cotangent,
):
    seq_length, model_width = tokens.shape
    block_len, top_count = expert_ids.shape
    expert_count = w_router.shape[1]
    local_experts = w_gate.shape[0]
    local_heads = w_query.shape[1] // HD
    quarters = lax.axis_size("tensor")
    device_count = quarters * lax.axis_size("expert")
    quarter = lax.axis_index("tensor")
    device = lax.axis_index(BOTH)
    first_expert = lax.axis_index("expert") * local_experts
    pair_cap = 2 * (3 * block_len * top_count // (2 * expert_count))
    score_scale = HD ** (-0.5)
    narrow, wide = jnp.bfloat16, jnp.float32

    def swap(value, even, odd=None):
        odd = even if odd is None else odd
        perm = [(i, i ^ (odd if i & 1 else even)) for i in range(device_count)]
        return lax.ppermute(value, BOTH, perm)

    def near(value):
        return swap(value, ACROSS, ASIDE)

    def far(value):
        return swap(value, ASIDE, ACROSS)

    def core(value):
        return swap(value, CORE)

    def add(left, right):
        return (left.astype(wide) + right.astype(wide)).astype(narrow)

    live = {}

    def sync():
        keys = list(live)
        values = lax.optimization_barrier([live[key] for key in keys])
        live.update(zip(keys, values))

    def gather_near(name, plane):
        live[name, plane, 1] = near(live[name, plane, 0])
        live[name, plane, 2] = far(live[name, plane, 0])

    def gather_far(name, plane):
        live[name, plane, 3] = far(live[name, plane, 1])

    def gather_core(name, plane, *slots):
        for slot in slots:
            live[name, plane, 4 + slot] = core(live[name, plane, slot])

    def reduce_core(name, plane):
        live[name, plane, OTHER] = core(live[name, plane, AWAY])

    def reduce_far(name, plane):
        kept = live.pop((name, plane, NEAR)).reshape(4, block_len, model_width)
        got = live.pop((name, plane, OTHER)).reshape(4, block_len, model_width)
        live.pop((name, plane, AWAY))
        sums = [add(kept[i], got[i]) for i in range(4)]
        live[name, plane, SUMS] = sums[:2]
        live[name, plane, FAR] = [far(sums[2]), far(sums[3])]

    def reduce_near(name, plane):
        sums, got = live.pop((name, plane, SUMS)), live.pop((name, plane, FAR))
        live[name, plane, OWN] = add(sums[0], got[0])
        live[name, plane, SIDE] = near(add(sums[1], got[1]))

    def reduced(name, plane):
        return add(live.pop((name, plane, OWN)), live.pop((name, plane, SIDE)))

    def bit(mask):
        return (device // mask) % 2

    odd_core = bit(CORE)
    weight_hops = ((ASIDE, PLANE_NEXT), (PLANE_NEXT, ASIDE), (PLANE_FAR, PLANE_FAR))
    small_hops = tuple((mask, mask) for mask in (CORE, ACROSS, ASIDE, PLANE_NEXT, PLANE_FAR))

    def piece_of(hops):
        piece = 0
        for even, odd in hops:
            piece = 2 * piece + jnp.where(odd_core == 0, bit(even), bit(odd))
        return piece

    pieces_of = {hops: piece_of(hops) for hops in (weight_hops, small_hops)}

    def ordered(pieces, hops):
        own = pieces_of[hops]
        parts = [
            lax.dynamic_slice_in_dim(pieces, own ^ r, 1, 0) for r in range(pieces.shape[0])
        ]
        return jnp.concatenate(parts, axis=0)

    def sum_step(name, step, hops=weight_hops, sent_as=narrow):
        count = len(hops)
        if step == 0:
            full = live.pop((name, FULL))
            pieces = 2**count
            full = full.reshape((pieces, full.shape[0] // pieces) + full.shape[1:])
            kept = ordered(full, hops)
        elif step < count:
            kept = live.pop((name, KEPT)) + live.pop((name, GOT)).astype(wide)
        elif step == count:
            kept = (live.pop((name, KEPT)) + live.pop((name, GOT)).astype(wide)).astype(sent_as)
        else:
            kept = jnp.concatenate([live.pop((name, KEPT)), live.pop((name, GOT))], axis=0)
        if step < count:
            half = kept.shape[0] // 2
            live[name, KEPT] = kept[:half]
            live[name, GOT] = swap(kept[half:].astype(sent_as), *hops[step])
        else:
            live[name, KEPT] = kept
            live[name, GOT] = swap(kept, *hops[2 * count - 1 - step])

    def summed(name, hops=weight_hops):
        pieces = jnp.concatenate([live.pop((name, KEPT)), live.pop((name, GOT))], axis=0)
        pieces = ordered(pieces, hops)
        return pieces.reshape((-1,) + pieces.shape[2:]).astype(wide)

    own, nxt, far_plane, last = PLANES

    live[G, own, 0] = cotangent
    live[G, far_plane, 0] = swap(cotangent, far_plane)
    live[G, nxt, 0] = swap(cotangent, nxt)
    gather_near(G, own)

    order = quarter ^ jnp.arange(quarters, dtype=jnp.int32)
    by_block = tokens.reshape(quarters, block_len, model_width)
    inputs = jnp.concatenate(
        [lax.dynamic_slice_in_dim(by_block, order[r], 1, 0)[0] for r in range(quarters)], axis=0
    ).astype(wide)
    positions = (order[:, None] * block_len + jnp.arange(block_len, dtype=jnp.int32)).reshape(-1)
    inverse_one, normed_one = norm_forward(inputs, gain_attn)
    hidden_one = normed_one.astype(narrow)
    frequency = jnp.exp(
        -jnp.log(theta_base) * jnp.arange(HD // 2, dtype=jnp.float32) * (2.0 / HD)
    )
    angles = positions.astype(wide)[:, None] * frequency[None, :]
    cosine_table, sine_table = (jnp.cos(angles)[:, None, :], jnp.sin(angles)[:, None, :])

    def project(weights):
        return jnp.dot(hidden_one, weights, preferred_element_type=wide).reshape(
            seq_length, local_heads, HD
        )

    live[QUERIES] = rotate(project(w_query), cosine_table, sine_table).astype(narrow)
    live[KEYS] = rotate(project(w_key), cosine_table, sine_table).astype(narrow)
    live[VALUES] = project(w_value).astype(narrow)
    sync()

    live[G, last, 0] = swap(live[G, far_plane, 0], nxt)
    gather_far(G, own)
    gather_near(G, nxt)
    live[IDS] = [expert_ids] + [swap(expert_ids, mask) for mask in PLANES[1:]]
    allowed = positions[:, None] >= positions[None, :]

    def masked_scores():
        scores = jnp.einsum(
            "qhd,khd->hqk", live[QUERIES], live[KEYS], preferred_element_type=wide
        )
        return jnp.where(allowed, scores * score_scale, masked)

    scores = masked_scores()
    row_max = jnp.max(scores, axis=-1, keepdims=True)
    exponent = jnp.exp(scores - row_max)
    row_total = jnp.sum(exponent, axis=-1, keepdims=True)
    weights = (exponent / row_total).astype(narrow)
    head_out = jnp.einsum("hqk,khd->qhd", weights, live[VALUES], preferred_element_type=wide)
    live[TOTALS] = row_max + jnp.log(row_total)
    live[HEADS] = head_out.astype(narrow).reshape(seq_length, local_heads * HD)

    def split_quarters(full):
        parts = full.reshape(quarters, block_len, model_width)
        live[KEPT] = [parts[0], parts[2]]
        live[SENT] = jnp.stack([parts[1], parts[3]]).astype(narrow)

    split_quarters(jnp.dot(live[HEADS], w_out, preferred_element_type=wide))
    sync()

    live[SENT] = core(live[SENT])
    gather_core(G, own, 0, 1, 2, 3)
    ids = jnp.stack(live[IDS])[:, None]
    live[IDS] = [ids, near(ids)]
    sync()

    def cross_quarters():
        kept, sent = live.pop(KEPT), live.pop(SENT).astype(wide)
        live[KEPT] = kept[0] + sent[0]
        live[SENT] = swap((kept[1] + sent[1]).astype(narrow), ACROSS)

    def quarter_sum():
        return live.pop(KEPT) + live.pop(SENT).astype(wide)

    cross_quarters()
    gather_far(G, nxt)
    gather_core(G, nxt, 0, 1, 2)
    ids = jnp.concatenate(live[IDS], axis=1)
    live[IDS] = [ids, far(ids)]
    sync()

    own_inputs = inputs[:block_len]
    own_inverse = inverse_one[:block_len]
    middle = own_inputs + quarter_sum()
    inverse_two, normed_two = norm_forward(middle, gain_moe)
    hidden_two = normed_two.astype(narrow)
    live[H, own, 0] = hidden_two

    gather_near(H, own)
    live[H, far_plane, 0] = swap(hidden_two, far_plane)
    live[H, nxt, 0] = swap(hidden_two, nxt)
    gather_near(G, last)
    gather_core(G, nxt, 3)
    logits = jnp.dot(hidden_two, w_router, preferred_element_type=wide)
    expert_range = jnp.arange(expert_count, dtype=jnp.int32)
    matches = expert_ids[:, :, None] == expert_range[None, None, :]
    chosen = jnp.sum(jnp.where(matches, logits[:, None, :], 0.0), axis=2)
    gate_weights = jax.nn.softmax(chosen, axis=-1)
    ids = jnp.concatenate(live[IDS], axis=1)
    live[IDS] = [ids, core(ids)]
    rolled = (first_expert + expert_range) % expert_count
    live[ROUTER] = jnp.take(w_router.T, rolled, axis=0)
    sync()

    live[H, last, 0] = swap(live[H, far_plane, 0], nxt)
    gather_far(H, own)
    gather_core(H, own, 0, 1, 2)
    gather_far(G, last)
    gather_core(G, last, 0, 1, 2)
    tokens_in = 2 * block_len
    ids = jnp.concatenate(live.pop(IDS), axis=1)
    pairs = ids.shape[1] // 2
    ids = ids.reshape(len(PLANES), pairs, tokens_in, top_count)
    named = jnp.any(ids[:, :, None] == rolled[:, None, None], axis=-1)
    counts = named[:, :, :local_experts].astype(narrow)
    before = jnp.triu(jnp.ones((tokens_in, tokens_in), narrow), 1)
    earlier = jnp.einsum("zplt,tu->zplu", counts, before, preferred_element_type=wide)
    live[SLOTS] = jnp.where(counts > 0, earlier.astype(jnp.int32), -1)
    live[NAMED] = named.astype(wide)
    sync()

    gather_near(H, last)
    gather_core(H, own, 3)
    gather_core(G, last, 3)
    sync()

    def experts(plane):
        index = PLANES.index(plane)
        done = expert_chunk(
            [live.pop((H, plane, slot)) for slot in range(BLOCKS)],
            [live.pop((G, plane, slot)) for slot in range(BLOCKS)],
            live[SLOTS][index],
            live[NAMED][index],
            live[ROUTER],
            w_gate,
            w_up,
            w_down,
            pair_cap,
        )
        live[M, plane, NEAR], live[M, plane, AWAY] = done[:2]
        live[R, plane, NEAR], live[R, plane, AWAY] = done[2:4]
        live[SUMS, plane] = done[4]
        live[KEPT, plane] = done[5:]

    gather_far(H, last)
    gather_core(H, last, 0, 1, 2)
    gather_near(H, far_plane)
    gather_near(G, far_plane)
    experts(own)
    sync()
    gather_core(H, last, 3)
    sync()

    gather_far(H, far_plane)
    gather_far(G, far_plane)
    gather_core(H, far_plane, 0, 1, 2)
    gather_core(G, far_plane, 0, 1, 2)
    gather_near(H, nxt)
    reduce_core(R, own)
    experts(last)
    sync()
    gather_core(H, far_plane, 3)
    gather_core(G, far_plane, 3)
    sync()

    gather_far(H, nxt)
    gather_core(H, nxt, 0, 1, 2)
    reduce_far(R, own)
    reduce_core(R, last)
    experts(far_plane)
    sync()
    gather_core(H, nxt, 3)
    sync()

    reduce_near(R, own)
    reduce_far(R, last)
    reduce_core(R, far_plane)
    experts(nxt)
    sync()

    kept = [live.pop((KEPT, plane)) for plane in PLANES]
    quarter_experts = local_experts // 4

    def some_weight_grads(part):
        live[EXPERTS] = weight_grads(
            kept, part * quarter_experts, quarter_experts, live.get(EXPERTS, [])
        )

    reduce_near(R, last)
    reduce_far(R, far_plane)
    reduce_core(R, nxt)
    sums = jnp.stack([live.pop((SUMS, plane)) for plane in PLANES])
    sums = sums.reshape(len(PLANES), -1, local_experts, 2, block_len).transpose(0, 1, 3, 2, 4)
    sums = sums.reshape(len(PLANES), BLOCKS, local_experts, block_len)
    live[GATES] = [sums[:, :4], core(sums[:, 4:])]
    live[HOME] = reduced(R, own)
    some_weight_grads(0)
    sync()

    live[RELAY] = swap(reduced(R, last), nxt)
    reduce_near(R, far_plane)
    reduce_far(R, nxt)
    sums = live[GATES][0] + live[GATES][1]
    crossed = jnp.stack([sums[:, 0], sums[:, 2], sums[:, 1], sums[:, 3]], axis=1)
    sums = jnp.where(odd_core == 0, sums, crossed)
    live[GATES] = [sums[:, ::2], swap(sums[:, 1::2], ACROSS)]
    some_weight_grads(1)
    sync()

    live[RELAY] = swap(add(reduced(R, far_plane), live[RELAY]), far_plane)
    reduce_near(R, nxt)
    sums = live[GATES][0] + live[GATES][1]
    live[GATES] = [sums[:, 0], swap(sums[:, 1], ASIDE)]
    some_weight_grads(2)
    sync()

    live[HOME] = live[HOME].astype(wide) + live.pop(RELAY).astype(wide)
    live[RELAY] = swap(reduced(R, nxt), nxt)
    sums = jnp.stack(live[GATES], axis=1)
    live[GATES] = [sums[0]] + [swap(sums[i], PLANES[i]) for i in range(1, len(PLANES))]
    some_weight_grads(3)
    sync()

    grad_hidden_disp = live.pop(HOME) + live.pop(RELAY).astype(wide)
    sums = jnp.concatenate(live.pop(GATES), axis=0)
    owner = lax.axis_index("expert")
    sums = [lax.dynamic_slice_in_dim(sums, owner ^ r, 1, 0)[0] for r in range(sums.shape[0])]
    own_sums = jnp.concatenate(sums, axis=0).T
    grad_out = cotangent.astype(wide)
    grad_gates = jnp.sum(jnp.where(matches, own_sums[:, None, :], 0.0), axis=2)
    grad_chosen = gate_weights * (
        grad_gates - jnp.sum(gate_weights * grad_gates, axis=-1, keepdims=True)
    )
    grad_logits = jnp.sum(jnp.where(matches, grad_chosen[:, :, None], 0.0), axis=1).astype(narrow)
    grad_router = jnp.einsum("ld,le->de", hidden_two, grad_logits, preferred_element_type=wide)
    grad_hidden_two = grad_hidden_disp + jnp.einsum(
        "le,de->ld", grad_logits, w_router, preferred_element_type=wide
    )
    grad_normed_two, grad_gain_moe = norm_backward(middle, inverse_two, gain_moe, grad_hidden_two)
    grad_middle = grad_out + grad_normed_two
    grad_attn = grad_middle.astype(narrow)

    small = jnp.concatenate([grad_router.T, grad_gain_moe[None]], axis=0)
    live[SMALL, FULL] = jnp.pad(small, ((0, -small.shape[0] % device_count), (0, 0)))
    small_step = functools.partial(sum_step, SMALL, hops=small_hops, sent_as=wide)

    live[ATTN] = [grad_attn, core(grad_attn), swap(grad_attn, ACROSS)]
    for plane in PLANES:
        reduce_core(M, plane)
    small_step(0)
    sync()
    live[ATTN] = live[ATTN] + [core(live[ATTN][2])]
    reduce_far(M, last)
    small_step(1)
    sync()

    grad_attn_all = jnp.concatenate(live.pop(ATTN), axis=0)
    reduce_near(M, last)
    reduce_far(M, far_plane)
    small_step(2)
    live[OUT, FULL] = jnp.einsum(
        "lh,ld->hd", live[HEADS], grad_attn_all, preferred_element_type=wide
    )
    grad_heads = (
        jnp.einsum("ld,hd->lh", grad_attn_all, w_out, preferred_element_type=wide)
        .astype(narrow)
        .reshape(seq_length, local_heads, HD)
    )
    probability = jnp.exp(masked_scores() - live[TOTALS])
    grad_values = jnp.einsum(
        "hqk,qhd->khd", probability.astype(narrow), grad_heads, preferred_element_type=wide
    )
    grad_prob = jnp.einsum("qhd,khd->hqk", grad_heads, live[VALUES], preferred_element_type=wide)
    row_delta = jnp.sum(probability * grad_prob, axis=-1, keepdims=True)
    grad_scores = (probability * (grad_prob - row_delta)).astype(narrow)
    grad_query = score_scale * jnp.einsum(
        "hqk,khd->qhd", grad_scores, live[KEYS], preferred_element_type=wide
    )
    grad_keys = score_scale * jnp.einsum(
        "hqk,qhd->khd", grad_scores, live[QUERIES], preferred_element_type=wide
    )

    def flat(source):
        return source.astype(narrow).reshape(seq_length, local_heads * HD)

    live[RAW] = [
        flat(rotate(grad_query, cosine_table, -sine_table)),
        flat(rotate(grad_keys, cosine_table, -sine_table)),
        flat(grad_values),
    ]
    sync()

    def back(grad_raw, weights):
        return jnp.einsum("lh,dh->ld", grad_raw, weights, preferred_element_type=wide)

    raw = live.pop(RAW)
    split_quarters(back(raw[0], w_query) + back(raw[1], w_key) + back(raw[2], w_value))
    for name, grad_raw in zip((QUERY, KEY, VALUE), raw):
        live[name, FULL] = jnp.einsum(
            "ld,lh->dh", hidden_one, grad_raw, preferred_element_type=wide
        )
    sum_step(OUT, 0)
    live[MIXED] = swap(reduced(M, last), nxt)
    reduce_near(M, far_plane)
    reduce_far(M, nxt)
    small_step(3)
    sync()

    live[SENT] = core(live[SENT])
    sum_step(OUT, 1)
    sum_step(VALUE, 0)
    live[MIXED] = add(reduced(M, far_plane), live[MIXED])
    small_step(4)
    sync()

    cross_quarters()
    sum_step(OUT, 2)
    sum_step(VALUE, 1)
    sum_step(KEY, 0)
    small_step(5)
    sync()

    grad_normed_one, grad_gain_attn = norm_backward(
        own_inputs, own_inverse, gain_attn, quarter_sum()
    )
    live[TOKENS] = grad_middle + grad_normed_one
    live[GAIN] = [grad_gain_attn[None], jnp.zeros_like(grad_gain_attn)[None]]

    def gain_step(step):
        live[GAIN] = [live[GAIN][0] + live[GAIN][1]]
        live[GAIN] = live[GAIN] + [swap(live[GAIN][0], *small_hops[step])]

    sum_step(OUT, 3)
    sum_step(VALUE, 2)
    sum_step(KEY, 1)
    sum_step(QUERY, 0)
    reduce_far(M, own)
    reduce_near(M, nxt)
    small_step(6)
    gain_step(0)
    sync()

    sum_step(OUT, 4)
    sum_step(VALUE, 3)
    sum_step(KEY, 2)
    sum_step(QUERY, 1)
    reduce_near(M, own)
    small_step(7)
    gain_step(1)
    sync()

    sum_step(OUT, 5)
    sum_step(VALUE, 4)
    sum_step(KEY, 3)
    sum_step(QUERY, 2)
    live[HOME] = reduced(M, own).astype(wide)
    small_step(8)
    gain_step(2)
    sync()

    grad_w_out = summed(OUT)
    sum_step(VALUE, 5)
    sum_step(KEY, 4)
    sum_step(QUERY, 3)
    live[SIDE] = swap(reduced(M, nxt), nxt)
    small_step(9)
    gain_step(3)
    sync()

    grad_w_value = summed(VALUE)
    small = summed(SMALL, small_hops)
    sum_step(KEY, 5)
    sum_step(QUERY, 4)
    live[MIXED] = swap(live[MIXED], far_plane)
    gain_step(4)
    sync()

    grad_w_key = summed(KEY)
    sum_step(QUERY, 5)
    mixed_out = live[HOME] + live[MIXED].astype(wide) + live[SIDE].astype(wide)
    mixed_out = (middle + mixed_out).astype(narrow)
    grad_gain_attn = (live[GAIN][0] + live[GAIN][1])[0]
    sync()
    grad_w_query = summed(QUERY)

    return (
        mixed_out,
        live[TOKENS],
        grad_gain_attn,
        grad_w_query,
        grad_w_key,
        grad_w_value,
        grad_w_out,
        small[expert_count],
        small[:expert_count].T,
        *live[EXPERTS],
    )


def on_device(*operands):
    tokens, w_router, w_gate, expert_ids = operands[0], operands[7], operands[8], operands[11]
    owners, quarters = lax.axis_size("expert"), lax.axis_size("tensor")
    block_len, top_count = expert_ids.shape
    capacity = 3 * block_len * top_count // (2 * w_router.shape[1])
    buffer_rows = capacity * quarters * owners * w_gate.shape[0]
    gathers = owners * tokens.shape[0] <= buffer_rows and (owners, quarters) == (8, 4)
    return (gathered_layer if gathers else routed_layer)(*operands)


def solution(mesh):
    return jax.shard_map(
        on_device,
        mesh=mesh,
        in_specs=(
            P("expert", None),
            P(),
            P(None, "tensor"),
            P(None, "tensor"),
            P(None, "tensor"),
            P("tensor", None),
            P(),
            P(),
            P("expert", None, "tensor"),
            P("expert", None, "tensor"),
            P("expert", "tensor", None),
            P(("expert", "tensor"), None),
            P(("expert", "tensor"), None),
        ),
        out_specs=(
            P(("expert", "tensor"), None),
            P(("expert", "tensor"), None),
            P(),
            P(None, "tensor"),
            P(None, "tensor"),
            P(None, "tensor"),
            P("tensor", None),
            P(),
            P(),
            P("expert", None, "tensor"),
            P("expert", None, "tensor"),
            P("expert", "tensor", None),
        ),
        check_vma=False,
    )
```

```python
import functools

import jax
import jax.numpy as jnp
from jax import lax
from jax.experimental import pallas as pl
from jax.experimental.pallas import tpu as pltpu
from jax.sharding import PartitionSpec as P

HD = 128


eps = 1e-06
theta_base = 10000.0
masked = -1e30

BOTH = ("expert", "tensor")
CORE, ACROSS, ASIDE, PLANE_NEXT, PLANE_FAR = 1, 2, 4, 8, 16
PLANES = (0, PLANE_NEXT, PLANE_FAR, PLANE_NEXT | PLANE_FAR)
BLOCKS = 8
WEIGHT_SLOTS = 3
LANES = 128

(
    G,
    H,
    M,
    R,
    QUERIES,
    KEYS,
    VALUES,
    TOTALS,
    HEADS,
    KEPT,
    SENT,
    RAW,
    HOME,
    SUMS,
    NEAR,
    AWAY,
    OTHER,
    FAR,
    OWN,
    SIDE,
    FULL,
    GOT,
    IN,
    OUT,
    TOKENS,
    NAMED,
    ROUTER,
    GATES,
    ATTN,
    RELAY,
    MIXED,
    EXPERTS,
    SMALL,
    GAIN,
    PAIR,
) = range(35)


def rope_tables(seq_length, head_size):
    half_dim = head_size // 2
    frequency = jnp.exp(
        -jnp.log(theta_base) * jnp.arange(half_dim, dtype=jnp.float32) * (2.0 / head_size)
    )
    angles = jnp.arange(seq_length, dtype=jnp.float32)[:, None] * frequency[None, :]
    return (jnp.cos(angles)[:, None, :], jnp.sin(angles)[:, None, :])


def rotate(source, cosine_table, sine_table):
    half_dim = source.shape[-1] // 2
    first_half = source[..., :half_dim]
    second = source[..., half_dim:]
    return jnp.concatenate(
        [
            first_half * cosine_table - second * sine_table,
            second * cosine_table + first_half * sine_table,
        ],
        axis=-1,
    )


def norm_forward(source, gain_vec):
    inverse = lax.rsqrt(jnp.mean(source * source, axis=-1, keepdims=True) + eps)
    return (inverse, source * inverse * gain_vec)


def norm_backward(source, inverse, gain_vec, grad_in):
    scaled = gain_vec * grad_in
    grad_source = inverse * scaled - source * inverse**3 * jnp.mean(
        scaled * source, axis=-1, keepdims=True
    )
    grad_gain = jnp.sum(grad_in * source * inverse, axis=0)
    return (grad_source, grad_gain)


def block_scores(q_block, key_rows, first_row, score_scale):
    scores = (
        jnp.einsum("qgrd,kgd->grqk", q_block, key_rows, preferred_element_type=jnp.float32)
        * score_scale
    )
    row_ids = first_row + jnp.arange(q_block.shape[0], dtype=jnp.int32)
    allowed = row_ids[:, None] >= jnp.arange(key_rows.shape[0], dtype=jnp.int32)[None, :]
    return jnp.where(allowed, scores, masked)


def routed_layer(
    tokens,
    gain_attn,
    w_query,
    w_key,
    w_value,
    w_out,
    gain_moe,
    w_router,
    w_gate,
    w_up,
    w_down,
    expert_ids,
    cotangent,
):
    seq_length, model_width = tokens.shape
    block_len, top_count = expert_ids.shape
    expert_count = w_router.shape[1]
    local_experts = w_gate.shape[0]
    local_heads = w_query.shape[1] // HD
    local_groups = w_key.shape[1] // HD
    group_size = local_heads // local_groups
    owners = lax.axis_size("expert")
    quarter = lax.axis_index("tensor")
    capacity = 3 * block_len * top_count // (2 * expert_count)
    block_rows = min(512, seq_length)
    block_count = seq_length // block_rows
    score_scale = HD ** (-0.5)
    first_own = quarter * block_len
    inputs = tokens.astype(jnp.float32)
    inverse_one, normed_one = norm_forward(inputs, gain_attn)
    hidden_one = normed_one.astype(jnp.bfloat16)
    cosine_table, sine_table = rope_tables(seq_length, HD)

    def rope_heads(source):
        return rotate(source, cosine_table, sine_table)

    query_raw = jnp.dot(hidden_one, w_query, preferred_element_type=jnp.float32).reshape(
        seq_length, local_heads, HD
    )
    key_raw = jnp.dot(hidden_one, w_key, preferred_element_type=jnp.float32).reshape(
        seq_length, local_groups, HD
    )
    queries = rope_heads(query_raw).astype(jnp.bfloat16)
    key_rows = rope_heads(key_raw).astype(jnp.bfloat16)
    value_rows = (
        jnp.dot(hidden_one, w_value, preferred_element_type=jnp.float32)
        .astype(jnp.bfloat16)
        .reshape(seq_length, local_groups, HD)
    )
    query_blocks = queries.reshape(block_count, block_rows, local_groups, group_size, HD)
    starts = jnp.arange(block_count, dtype=jnp.int32) * block_rows

    def attend_block(packed):
        first_row, q_block = packed
        scores = block_scores(q_block, key_rows, first_row, score_scale)
        row_max = jnp.max(scores, axis=-1, keepdims=True)
        exponent = jnp.exp(scores - row_max)
        row_total = jnp.sum(exponent, axis=-1, keepdims=True)
        weights = (exponent / row_total).astype(jnp.bfloat16)
        head_out = jnp.einsum(
            "grqk,kgd->qgrd", weights, value_rows, preferred_element_type=jnp.float32
        )
        return (head_out.astype(jnp.bfloat16), (row_max + jnp.log(row_total))[..., 0])

    head_blocks, log_totals = lax.map(attend_block, (starts, query_blocks))
    head_rows = head_blocks.reshape(seq_length, local_heads * HD)
    attention = lax.psum_scatter(
        jnp.dot(head_rows, w_out, preferred_element_type=jnp.float32),
        "tensor",
        scatter_dimension=0,
        tiled=True,
    )
    own_inputs = lax.dynamic_slice_in_dim(inputs, first_own, block_len, 0)
    own_inverse = lax.dynamic_slice_in_dim(inverse_one, first_own, block_len, 0)
    middle = own_inputs + attention
    inverse_two, normed_two = norm_forward(middle, gain_moe)
    hidden_two = normed_two.astype(jnp.bfloat16)
    logits = jnp.dot(hidden_two, w_router, preferred_element_type=jnp.float32)
    expert_range = jnp.arange(expert_count, dtype=jnp.int32)
    matches = expert_ids[:, :, None] == expert_range[None, None, :]
    chosen = jnp.sum(jnp.where(matches, logits[:, None, :], 0.0), axis=2)
    gate_weights = jax.nn.softmax(chosen, axis=-1)
    expert_hits = jnp.sum(matches.astype(jnp.int32), axis=1)
    earlier = jnp.cumsum(expert_hits, axis=0) - expert_hits
    slot_of = jnp.sum(jnp.where(matches, earlier[:, None, :], 0), axis=2)
    place = (slot_of * expert_count + expert_ids).reshape(-1)
    token_rows = jnp.broadcast_to(
        hidden_two[:, None, :], (block_len, top_count, model_width)
    ).reshape(block_len * top_count, model_width)
    grad_out = cotangent.astype(jnp.float32)
    gated_grads = (
        (gate_weights[:, :, None] * grad_out[:, None, :])
        .astype(jnp.bfloat16)
        .reshape(block_len * top_count, model_width)
    )
    empty = jnp.zeros((capacity * expert_count, model_width), jnp.bfloat16)
    send_rows = empty.at[place].set(token_rows).reshape(capacity, expert_count, model_width)
    send_grads = empty.at[place].set(gated_grads).reshape(capacity, expert_count, model_width)
    arrived_rows, arrived_grads = (
        lax.all_to_all(send_rows, "expert", split_axis=1, concat_axis=1, tiled=True),
        lax.all_to_all(send_grads, "expert", split_axis=1, concat_axis=1, tiled=True),
    )
    routed = arrived_rows.reshape(capacity, owners, local_experts, model_width)
    grads_in = arrived_grads.reshape(capacity, owners, local_experts, model_width)
    all_rows, all_grads = (
        lax.all_gather(routed, "tensor", axis=0, tiled=True),
        lax.all_gather(grads_in, "tensor", axis=0, tiled=True),
    )
    gate_pre = jnp.einsum("csld,ldf->cslf", all_rows, w_gate, preferred_element_type=jnp.float32)
    up_pre = jnp.einsum("csld,ldf->cslf", all_rows, w_up, preferred_element_type=jnp.float32)
    sigmoid_gate = jax.nn.sigmoid(gate_pre)
    silu_gate = gate_pre * sigmoid_gate
    activation = (silu_gate * up_pre).astype(jnp.bfloat16)
    grad_w_down = jnp.einsum(
        "cslf,csld->lfd", activation, all_grads, preferred_element_type=jnp.float32
    )
    grad_act = jnp.einsum("csld,lfd->cslf", all_grads, w_down, preferred_element_type=jnp.float32)
    grad_gate = (grad_act * up_pre * sigmoid_gate * (1.0 + gate_pre * (1.0 - sigmoid_gate))).astype(
        jnp.bfloat16
    )
    grad_up = (grad_act * silu_gate).astype(jnp.bfloat16)
    grad_w_gate = jnp.einsum(
        "csld,cslf->ldf", all_rows, grad_gate, preferred_element_type=jnp.float32
    )
    grad_w_up = jnp.einsum("csld,cslf->ldf", all_rows, grad_up, preferred_element_type=jnp.float32)
    forward_term = jnp.einsum(
        "cslf,lfd->csld", activation, w_down, preferred_element_type=jnp.float32
    )
    back_term = jnp.einsum("cslf,ldf->csld", grad_gate, w_gate, preferred_element_type=jnp.float32)
    back_term = back_term + jnp.einsum(
        "cslf,ldf->csld", grad_up, w_up, preferred_element_type=jnp.float32
    )
    both_terms = lax.psum_scatter(
        jnp.concatenate([forward_term, back_term], axis=3).astype(jnp.bfloat16),
        "tensor",
        scatter_dimension=0,
        tiled=True,
    )
    returned = both_terms[..., :model_width]
    row_grads = both_terms[..., model_width:]
    returned_home, row_grads_home = (
        lax.all_to_all(
            returned.reshape(capacity, expert_count, model_width),
            "expert",
            split_axis=1,
            concat_axis=1,
            tiled=True,
        ),
        lax.all_to_all(
            row_grads.reshape(capacity, expert_count, model_width),
            "expert",
            split_axis=1,
            concat_axis=1,
            tiled=True,
        ),
    )
    picked = returned_home.reshape(capacity * expert_count, model_width)[place].reshape(
        block_len, top_count, model_width
    )
    mixture = jnp.sum(gate_weights[:, :, None] * picked, axis=1)
    mixed_out = (middle + mixture).astype(jnp.bfloat16)
    grad_gates = jnp.sum(picked * grad_out[:, None, :], axis=2)
    grad_picked = row_grads_home.reshape(capacity * expert_count, model_width)[place].reshape(
        block_len, top_count, model_width
    )
    grad_hidden_disp = jnp.einsum(
        "lk,lkd->ld",
        jnp.ones((block_len, top_count), jnp.bfloat16),
        grad_picked,
        preferred_element_type=jnp.float32,
    )
    grad_chosen = gate_weights * (
        grad_gates - jnp.sum(gate_weights * grad_gates, axis=-1, keepdims=True)
    )
    grad_logits = jnp.sum(jnp.where(matches, grad_chosen[:, :, None], 0.0), axis=1).astype(
        jnp.bfloat16
    )
    grad_router = jnp.einsum(
        "ld,le->de", hidden_two, grad_logits, preferred_element_type=jnp.float32
    )
    grad_hidden_two = grad_hidden_disp + jnp.einsum(
        "le,de->ld", grad_logits, w_router, preferred_element_type=jnp.float32
    )
    grad_normed_two, grad_gain_moe = norm_backward(middle, inverse_two, gain_moe, grad_hidden_two)
    grad_middle = grad_out + grad_normed_two
    grad_attn = grad_middle.astype(jnp.bfloat16)
    grad_attn_all = lax.all_gather(grad_attn, "tensor", axis=0, tiled=True)
    grad_w_out = jnp.einsum(
        "lh,ld->hd", head_rows, grad_attn_all, preferred_element_type=jnp.float32
    )
    grad_heads = jnp.einsum(
        "ld,hd->lh", grad_attn_all, w_out, preferred_element_type=jnp.float32
    ).astype(jnp.bfloat16)
    grad_blocks = grad_heads.reshape(block_count, block_rows, local_groups, group_size, HD)

    def back_block(carried, packed):
        grad_keys, grad_values = carried
        first_row, q_block, g_block, lse_block = packed
        scores = block_scores(q_block, key_rows, first_row, score_scale)
        probability = jnp.exp(scores - lse_block[..., None])
        grad_values = grad_values + jnp.einsum(
            "grqk,qgrd->kgd",
            probability.astype(jnp.bfloat16),
            g_block,
            preferred_element_type=jnp.float32,
        )
        grad_prob = jnp.einsum(
            "qgrd,kgd->grqk", g_block, value_rows, preferred_element_type=jnp.float32
        )
        row_delta = jnp.sum(probability * grad_prob, axis=-1, keepdims=True)
        grad_scores = (probability * (grad_prob - row_delta)).astype(jnp.bfloat16)
        grad_query = (
            jnp.einsum("grqk,kgd->qgrd", grad_scores, key_rows, preferred_element_type=jnp.float32)
            * score_scale
        )
        grad_keys = (
            grad_keys
            + jnp.einsum("grqk,qgrd->kgd", grad_scores, q_block, preferred_element_type=jnp.float32)
            * score_scale
        )
        return ((grad_keys, grad_values), grad_query)

    zero_keys = jnp.zeros((seq_length, local_groups, HD), jnp.float32)
    (grad_keys, grad_values), grad_query_blocks = lax.scan(
        back_block, (zero_keys, zero_keys), (starts, query_blocks, grad_blocks, log_totals)
    )
    grad_query = grad_query_blocks.reshape(seq_length, local_heads, HD)
    grad_query_raw = (
        jax.vjp(rope_heads, query_raw)[1](grad_query)[0]
        .reshape(seq_length, local_heads * HD)
        .astype(jnp.bfloat16)
    )
    grad_key_raw = (
        jax.vjp(rope_heads, key_raw)[1](grad_keys)[0]
        .reshape(seq_length, local_groups * HD)
        .astype(jnp.bfloat16)
    )
    grad_value_raw = grad_values.reshape(seq_length, local_groups * HD).astype(jnp.bfloat16)
    grad_w_query = jnp.einsum(
        "ld,lh->dh", hidden_one, grad_query_raw, preferred_element_type=jnp.float32
    )
    grad_w_key = jnp.einsum(
        "ld,lh->dh", hidden_one, grad_key_raw, preferred_element_type=jnp.float32
    )
    grad_w_value = jnp.einsum(
        "ld,lh->dh", hidden_one, grad_value_raw, preferred_element_type=jnp.float32
    )
    term = jnp.einsum("lh,dh->ld", grad_query_raw, w_query, preferred_element_type=jnp.float32)
    term = term + jnp.einsum("lh,dh->ld", grad_key_raw, w_key, preferred_element_type=jnp.float32)
    grad_hidden_one = lax.psum_scatter(
        (
            term
            + jnp.einsum("lh,dh->ld", grad_value_raw, w_value, preferred_element_type=jnp.float32)
        ).astype(jnp.bfloat16),
        "tensor",
        scatter_dimension=0,
        tiled=True,
    ).astype(jnp.float32)
    grad_normed_one, grad_gain_attn = norm_backward(
        own_inputs, own_inverse, gain_attn, grad_hidden_one
    )
    grad_tokens = grad_middle + grad_normed_one
    attn_sums = lax.psum((grad_w_query, grad_w_key, grad_w_value, grad_w_out), "expert")
    small_sums = lax.psum((grad_gain_attn, grad_gain_moe, grad_router), ("expert", "tensor"))
    return (
        mixed_out,
        grad_tokens,
        small_sums[0],
        attn_sums[0],
        attn_sums[1],
        attn_sums[2],
        attn_sums[3],
        small_sums[1],
        small_sums[2],
        grad_w_gate,
        grad_w_up,
        grad_w_down,
    )


ROWS_ROWS = (((1,), (1,)), ((), ()))
def dot_nt(left, right):
    return lax.dot_general(left, right, ROWS_ROWS, preferred_element_type=jnp.float32)


def dot_nn(left, right):
    return jnp.dot(left, right, preferred_element_type=jnp.float32)


def expert_kernel(places, top_count, *refs):
    row_places, grad_places = places
    given = 1 + max(place[0] for place in row_places + grad_places)
    numbers_ref, router_ref, gate_ref, up_ref, down_ref = refs[given : given + 5]
    outs = refs[given + 5 : given + 14]
    mixed_refs, back_refs, sums_ref = outs[:2], outs[2:4], outs[4]
    rows_s, grads_s, ids_s, x_s, y_s, back_s, out_s = refs[given + 14 : given + 21]
    pick_s, place_s, gates_s, sums_s, gated_s, side_s = refs[given + 21 : given + 27]
    both_s, down_s, sems, weight_sems, out_sems, kept_sems = refs[given + 27 :]
    pairs, wide, _ = pick_s.shape
    experts = x_s.shape[0]
    hidden = down_s.shape[1]
    cap = wide // experts
    tokens_in, width = rows_s.shape[1:]
    block_len = tokens_in // 2
    narrow = jnp.bfloat16

    def copies(pair):
        out = []
        for half in range(2):
            target = pl.ds(half * block_len, block_len)
            at = 2 * pair + half
            array, row, column = row_places[at]
            rows = refs[array].at[pl.ds(row, block_len), pl.ds(column, width)]
            array, row, column = grad_places[at]
            block = refs[array].at[pl.ds(row, block_len)]
            grads = block.at[:, pl.ds(column, width)]
            ids = block.at[:, pl.ds(column + width, LANES)]
            for k, (source, scratch) in enumerate(
                ((rows, rows_s), (grads, grads_s), (ids, ids_s))
            ):
                out.append(
                    pltpu.make_async_copy(source, scratch.at[pair, target], sems.at[k, at])
                )
        return out

    def weight_copies(expert, slot):
        sides = [both_s.at[slot, :, pl.ds(k * hidden, hidden)] for k in range(2)]
        return [
            pltpu.make_async_copy(gate_ref.at[expert], sides[0], weight_sems.at[0, slot]),
            pltpu.make_async_copy(up_ref.at[expert], sides[1], weight_sems.at[1, slot]),
            pltpu.make_async_copy(down_ref.at[expert], down_s.at[slot], weight_sems.at[2, slot]),
        ]

    def result_copies(pair):
        half = pairs // 2
        place = pl.ds((pair % half) * tokens_in, tokens_in)
        sides = (rows_s, mixed_refs), (grads_s, back_refs)
        return [
            pltpu.make_async_copy(
                source.at[pair], targets[pair // half].at[place], out_sems.at[k, pair]
            )
            for k, (source, targets) in enumerate(sides)
        ]

    kept_copies = [
        pltpu.make_async_copy(source, target, kept_sems.at[k])
        for k, (source, target) in enumerate(zip((x_s, y_s, gated_s, side_s), outs[5:9]))
    ]

    for pair in range(pairs):
        for copy in copies(pair):
            copy.start()
    for slot in range(WEIGHT_SLOTS):
        for copy in weight_copies(slot, slot):
            copy.start()

    earlier = lax.broadcasted_iota(jnp.int32, (tokens_in, tokens_in), 0)
    later = lax.broadcasted_iota(jnp.int32, (tokens_in, tokens_in), 1)
    before = jnp.where(earlier < later, 1.0, 0.0).astype(narrow)

    for pair in range(pairs):
        for copy in copies(pair):
            copy.wait()
        rows_in = rows_s[pair]
        logits = dot_nt(router_ref[...], rows_in)
        ids = ids_s[pair].astype(jnp.float32).T
        named = jnp.zeros(logits.shape, jnp.float32)
        for k in range(top_count):
            named = jnp.where(ids[k : k + 1, :] == numbers_ref[:, :1], 1.0, named)
        hits = named[:experts]
        slots = jnp.where(hits > 0.0, dot_nn(hits.astype(narrow), before), -1.0)
        slots = slots.astype(jnp.int32)
        logits = jnp.where(named > 0.0, logits, masked)
        weights = jnp.exp(logits - jnp.max(logits, axis=0, keepdims=True)) * named
        gates = weights / jnp.sum(weights, axis=0, keepdims=True)
        ranks = lax.broadcasted_iota(jnp.int32, (cap, tokens_in), 0)
        place = pl.ds(pair * cap, cap)
        picks = []
        for expert in range(experts):
            pick = ranks == slots[expert : expert + 1, :]
            row_gates = jnp.sum(
                jnp.where(pick, gates[expert : expert + 1, :], 0.0), axis=1, keepdims=True
            )
            gates_s[expert, place, :] = jnp.broadcast_to(row_gates, (cap, LANES))
            picks.append(jnp.where(pick, 1.0, 0.0))
        pick_all = jnp.concatenate(picks, axis=0)
        pick_low = pick_all.astype(narrow)
        pick_s[pair] = pick_low
        place_s[pair] = pick_all.T.astype(narrow)
        for source, target in ((rows_in, x_s), (grads_s[pair], y_s)):
            spread = dot_nn(pick_low, source).astype(narrow)
            for expert in range(experts):
                target[expert, place, :] = spread[expert * cap : (expert + 1) * cap]

    kept_copies[0].start()
    kept_copies[1].start()

    def expert_step(expert, carried):
        slot = lax.rem(expert, WEIGHT_SLOTS)
        for copy in weight_copies(expert, slot):
            copy.wait()
        both = dot_nn(x_s[expert], both_s[slot])
        gate_pre, up_pre = both[:, :hidden], both[:, hidden:]
        plain = dot_nt(y_s[expert], down_s[slot])
        sigmoid_gate = jax.nn.sigmoid(gate_pre)
        silu_gate = gate_pre * sigmoid_gate
        activation = silu_gate * up_pre
        row_gates = gates_s[expert][:, :1]
        sums = jnp.sum(activation * plain, axis=1, keepdims=True)
        sums_s[expert] = jnp.broadcast_to(sums, sums_s.shape[1:])
        grad_act = row_gates * plain
        gated = (row_gates * activation).astype(narrow)
        slope = sigmoid_gate * (1.0 + gate_pre * (1.0 - sigmoid_gate))
        grad_gate = (grad_act * up_pre * slope).astype(narrow)
        grad_up = (grad_act * silu_gate).astype(narrow)
        grad_both = jnp.concatenate([grad_gate, grad_up], axis=1)
        gated_s[expert] = gated
        side_s[expert] = grad_both
        out_s[expert] = dot_nn(gated, down_s[slot]).astype(narrow)
        back_s[expert] = dot_nt(grad_both, both_s[slot]).astype(narrow)

        @pl.when(expert + WEIGHT_SLOTS < experts)
        def _():
            for copy in weight_copies(expert + WEIGHT_SLOTS, slot):
                copy.start()

        return carried

    lax.fori_loop(0, experts, expert_step, 0)
    kept_copies[2].start()
    kept_copies[3].start()

    for pair in range(pairs):
        sides = pl.ds(pair * cap, cap)
        for source, target in ((out_s, rows_s), (back_s, grads_s)):
            stacked = jnp.concatenate(
                [source[expert, sides, :] for expert in range(experts)], axis=0
            )
            target[pair] = dot_nn(place_s[pair], stacked).astype(narrow)
        for copy in result_copies(pair):
            copy.start()
        pick = pick_s[pair].astype(jnp.float32)
        sums = []
        for expert in range(experts):
            column = sums_s[expert, sides, :][:, :1]
            part = pick[expert * cap : (expert + 1) * cap] * column
            sums.append(jnp.sum(part, axis=0, keepdims=True))
        sums_ref[pair] = jnp.concatenate(sums, axis=0)

    for copy in kept_copies:
        copy.wait()
    for pair in range(pairs):
        for copy in result_copies(pair):
            copy.wait()


def expert_chunk(arrays, places, numbers, router, w_gate, w_up, w_down, tokens_in, top_count, cap):
    experts, width, hidden = w_gate.shape
    pairs = BLOCKS // 2
    rows = pairs * cap
    narrow, wide = jnp.bfloat16, jnp.float32
    shape = jax.ShapeDtypeStruct
    anywhere = pl.BlockSpec(memory_space=pl.ANY)
    inside = pl.BlockSpec(memory_space=pltpu.VMEM)
    half_shape = shape((pairs // 2 * tokens_in, width), narrow)
    whole_rows = (experts, rows, width)
    return pl.pallas_call(
        functools.partial(expert_kernel, places, top_count),
        in_specs=[anywhere] * len(arrays) + [inside] * 2 + [anywhere] * 3,
        out_specs=[anywhere] * 4 + [inside] + [anywhere] * 4,
        out_shape=[half_shape] * 4
        + [
            shape((pairs, experts, tokens_in), wide),
            shape(whole_rows, narrow),
            shape(whole_rows, narrow),
            shape((experts, rows, hidden), narrow),
            shape((experts, rows, 2 * hidden), narrow),
        ],
        scratch_shapes=[pltpu.VMEM((pairs, tokens_in, width), narrow)] * 2
        + [pltpu.VMEM((pairs, tokens_in, LANES), narrow)]
        + [pltpu.VMEM(whole_rows, narrow)] * 4
        + [
            pltpu.VMEM((pairs, experts * cap, tokens_in), narrow),
            pltpu.VMEM((pairs, tokens_in, experts * cap), narrow),
            pltpu.VMEM((experts, rows, LANES), wide),
            pltpu.VMEM((experts, rows, LANES), wide),
            pltpu.VMEM((experts, rows, hidden), narrow),
            pltpu.VMEM((experts, rows, 2 * hidden), narrow),
            pltpu.VMEM((WEIGHT_SLOTS, width, 2 * hidden), narrow),
            pltpu.VMEM((WEIGHT_SLOTS, hidden, width), narrow),
            pltpu.SemaphoreType.DMA((3, BLOCKS)),
            pltpu.SemaphoreType.DMA((3, WEIGHT_SLOTS)),
            pltpu.SemaphoreType.DMA((2, pairs)),
            pltpu.SemaphoreType.DMA((4,)),
        ],
        compiler_params=pltpu.CompilerParams(vmem_limit_bytes=60 << 20),
        cost_estimate=pl.CostEstimate(
            flops=24 * experts * rows * width * hidden,
            bytes_accessed=6 * experts * width * hidden + 4 * experts * rows * width,
            transcendentals=experts * rows * hidden,
        ),
    )(*arrays, numbers, router, w_gate, w_up, w_down)


def weight_kernel(parts, given, *refs):
    ins, (gate_ref, up_ref, down_ref) = refs[: 4 * parts], refs[4 * parts + given :]
    rows, grads, gated, both = [
        jnp.concatenate([ref[0] for ref in ins[k * parts : (k + 1) * parts]], axis=0)
        for k in range(4)
    ]
    turn = (((0,), (0,)), ((), ()))
    hidden = gated.shape[1]
    down_ref[0] = lax.dot_general(gated, grads, turn, preferred_element_type=jnp.float32)
    sides = lax.dot_general(rows, both, turn, preferred_element_type=jnp.float32)
    gate_ref[0] = sides[:, :hidden]
    up_ref[0] = sides[:, hidden:]


def weight_grads(kept, begin, count, partial):
    parts = len(kept)
    experts, rows, width = kept[0][0].shape
    hidden = kept[0][2].shape[2]
    operands = [part[k] for k in range(4) for part in kept]
    shape = jax.ShapeDtypeStruct

    def spec(rows, columns):
        return pl.BlockSpec((1, rows, columns), lambda i: (i + begin, 0, 0))

    return pl.pallas_call(
        functools.partial(weight_kernel, parts, len(partial)),
        grid=(count,),
        in_specs=[spec(rows, operand.shape[2]) for operand in operands]
        + [pl.BlockSpec(memory_space=pl.ANY)] * len(partial),
        out_specs=[spec(width, hidden), spec(width, hidden), spec(hidden, width)],
        out_shape=[
            shape((experts, width, hidden), jnp.float32),
            shape((experts, width, hidden), jnp.float32),
            shape((experts, hidden, width), jnp.float32),
        ],
        input_output_aliases={len(operands) + k: k for k in range(len(partial))},
        compiler_params=pltpu.CompilerParams(vmem_limit_bytes=56 << 20),
        cost_estimate=pl.CostEstimate(
            flops=6 * parts * count * rows * width * hidden,
            bytes_accessed=count * (parts * rows * (4 * width + 6 * hidden) + 12 * width * hidden),
            transcendentals=0,
        ),
    )(*operands, *partial)


def gathered_layer(
    tokens,
    gain_attn,
    w_query,
    w_key,
    w_value,
    w_out,
    gain_moe,
    w_router,
    w_gate,
    w_up,
    w_down,
    expert_ids,
    cotangent,
):
    seq_length, model_width = tokens.shape
    block_len, top_count = expert_ids.shape
    expert_count = w_router.shape[1]
    local_experts = w_gate.shape[0]
    local_heads = w_query.shape[1] // HD
    quarters = lax.axis_size("tensor")
    device_count = quarters * lax.axis_size("expert")
    quarter = lax.axis_index("tensor").astype(jnp.uint32)
    device = lax.axis_index(BOTH).astype(jnp.uint32)
    first_expert = lax.axis_index("expert") * local_experts
    pair_cap = 2 * (3 * block_len * top_count // (2 * expert_count))
    score_scale = HD ** (-0.5)
    narrow, wide = jnp.bfloat16, jnp.float32

    def swap(value, even, odd=None):
        odd = even if odd is None else odd
        perm = [(i, i ^ (odd if i & 1 else even)) for i in range(device_count)]
        return lax.ppermute(value, BOTH, perm)

    def near(value):
        return swap(value, ACROSS, ASIDE)

    def far(value):
        return swap(value, ASIDE, ACROSS)

    def core(value):
        return swap(value, CORE)

    def add(left, right):
        return (left.astype(wide) + right.astype(wide)).astype(narrow)

    live = {}

    def sync():
        keys = list(live)
        values = lax.optimization_barrier([live[key] for key in keys])
        live.update(zip(keys, values))

    def gather_near(name, plane):
        live[name, plane, 1] = near(live[name, plane, 0])
        live[name, plane, 2] = far(live[name, plane, 0])

    def gather_far(name, plane):
        live[name, plane, 3] = far(live[name, plane, 1])

    def gather_across(name, plane):
        live[name, plane, 3] = swap(live[name, plane, 0], ACROSS | ASIDE)

    def gather_core(name, plane, *slots):
        blocks = [live[name, plane, slot] for slot in slots]
        live[name, plane, (OTHER,) + slots] = core(jnp.concatenate(blocks, axis=0))

    def blocks_of(name, plane):
        found = {}
        for key in list(live):
            if isinstance(key, tuple) and key[:2] == (name, plane):
                slots = key[2]
                array = live.pop(key)
                if isinstance(slots, tuple):
                    for i, slot in enumerate(slots[1:]):
                        found[4 + slot] = (array, i * block_len)
                else:
                    found[slots] = (array, 0)
        return [found[slot] for slot in range(BLOCKS)]

    def reduce_core(name, plane):
        live[name, plane, OTHER] = core(live.pop((name, plane, AWAY)))

    def reduce_far(name, plane):
        kept = live.pop((name, plane, NEAR)).reshape(4, block_len, model_width)
        got = live.pop((name, plane, OTHER)).reshape(4, block_len, model_width)
        live[name, plane, SUMS] = add(kept[:2], got[:2])
        live[name, plane, FAR] = far(add(kept[2:], got[2:]))

    def reduce_near(name, plane):
        sums, got = live.pop((name, plane, SUMS)), live.pop((name, plane, FAR))
        live[name, plane, OWN] = add(sums[0], got[0])
        live[name, plane, SIDE] = near(add(sums[1], got[1]))

    def reduced(name, plane):
        return add(live.pop((name, plane, OWN)), live.pop((name, plane, SIDE)))

    def bit(mask):
        return (device // mask) % 2

    odd_core = bit(CORE)
    weight_hops = ((ASIDE, PLANE_NEXT), (PLANE_NEXT, ASIDE), (PLANE_FAR, PLANE_FAR))
    small_hops = tuple((mask, mask) for mask in (CORE, ACROSS, ASIDE, PLANE_NEXT, PLANE_FAR))

    def joined(own, got, side):
        count = own.shape[0]
        both = jnp.zeros((2 * count,) + own.shape[1:], own.dtype)
        both = lax.dynamic_update_slice_in_dim(both, own, side * count, 0)
        return lax.dynamic_update_slice_in_dim(both, got, (1 - side) * count, 0)

    def sum_step(name, step, hops=weight_hops, sent_as=narrow):
        count = len(hops)
        sides = [jnp.where(odd_core == 0, bit(even), bit(odd)) for even, odd in hops]
        if step == 0:
            kept = live.pop((name, FULL))
        elif step <= count:
            kept = live.pop((name, KEPT)) + live.pop((name, GOT)).astype(wide)
        else:
            kept = joined(live.pop((name, KEPT)), live.pop((name, GOT)), sides[2 * count - step])
        if step < count:
            half = kept.shape[0] // 2
            side = sides[step]
            live[name, KEPT] = lax.dynamic_slice_in_dim(kept, side * half, half, 0)
            sent = lax.dynamic_slice_in_dim(kept, (1 - side) * half, half, 0)
            live[name, GOT] = swap(sent.astype(sent_as), *hops[step])
        else:
            kept = kept.astype(sent_as)
            live[name, KEPT] = kept
            live[name, GOT] = swap(kept, *hops[2 * count - 1 - step])

    def summed(name, hops=weight_hops):
        even, odd = hops[0]
        side = jnp.where(odd_core == 0, bit(even), bit(odd))
        return joined(live.pop((name, KEPT)), live.pop((name, GOT)), side).astype(wide)

    own, nxt, far_plane, last = PLANES

    named_ids = jnp.pad(expert_ids.astype(narrow), ((0, 0), (0, LANES - top_count)))
    live[G, own, 0] = jnp.concatenate([cotangent, named_ids], axis=1)
    live[G, nxt, 0] = swap(live[G, own, 0], nxt)
    live[G, last, 0] = swap(live[G, own, 0], last)
    gather_near(G, own)

    by_block = tokens.reshape(quarters, block_len, model_width)
    inputs = jnp.concatenate(
        [lax.dynamic_slice_in_dim(by_block, quarter ^ r, 1, 0)[0] for r in range(quarters)], axis=0
    )
    inputs = lax.optimization_barrier(inputs).astype(wide)
    order = quarter.astype(jnp.int32) ^ jnp.arange(quarters, dtype=jnp.int32)
    positions = (order[:, None] * block_len + jnp.arange(block_len, dtype=jnp.int32)).reshape(-1)
    inverse_one, normed_one = norm_forward(inputs, gain_attn)
    hidden_one = normed_one.astype(narrow)
    frequency = jnp.exp(
        -jnp.log(theta_base) * jnp.arange(HD // 2, dtype=jnp.float32) * (2.0 / HD)
    )
    angles = positions.astype(wide)[:, None] * frequency[None, :]
    cosine_table, sine_table = (jnp.cos(angles)[:, None, :], jnp.sin(angles)[:, None, :])

    def project(weights):
        return jnp.dot(hidden_one, weights, preferred_element_type=wide).reshape(
            seq_length, local_heads, HD
        )

    live[QUERIES] = rotate(project(w_query), cosine_table, sine_table).astype(narrow)
    live[KEYS] = rotate(project(w_key), cosine_table, sine_table).astype(narrow)
    live[VALUES] = project(w_value).astype(narrow)
    sync()

    gather_far(G, own)
    gather_near(G, nxt)
    live[G, far_plane, 0] = swap(live[G, own, 0], far_plane)
    allowed = positions[:, None] >= positions[None, :]

    def masked_scores():
        scores = jnp.einsum(
            "qhd,khd->hqk", live[QUERIES], live[KEYS], preferred_element_type=wide
        )
        return jnp.where(allowed, scores * score_scale, masked)

    scores = masked_scores()
    row_max = jnp.max(scores, axis=-1, keepdims=True)
    exponent = jnp.exp(scores - row_max)
    row_total = jnp.sum(exponent, axis=-1, keepdims=True)
    weights = (exponent / row_total).astype(narrow)
    head_out = jnp.einsum("hqk,khd->qhd", weights, live[VALUES], preferred_element_type=wide)
    live[TOTALS] = row_max + jnp.log(row_total)
    live[HEADS] = head_out.astype(narrow).reshape(seq_length, local_heads * HD)

    def split_quarters(full):
        parts = full.reshape(quarters, block_len, model_width)
        live[KEPT] = [parts[0], parts[2]]
        live[SENT] = jnp.stack([parts[1], parts[3]]).astype(narrow)

    split_quarters(jnp.dot(live[HEADS], w_out, preferred_element_type=wide))
    sync()

    live[SENT] = core(live[SENT])
    gather_far(G, nxt)
    gather_core(G, own, 0, 1, 2, 3)
    sync()

    def cross_quarters():
        kept, sent = live.pop(KEPT), live.pop(SENT).astype(wide)
        live[KEPT] = kept[0] + sent[0]
        live[SENT] = swap((kept[1] + sent[1]).astype(narrow), ACROSS)

    def quarter_sum():
        return live.pop(KEPT) + live.pop(SENT).astype(wide)

    cross_quarters()
    gather_core(G, nxt, 0, 1, 2, 3)
    sync()

    own_inputs = inputs[:block_len]
    own_inverse = inverse_one[:block_len]
    middle = own_inputs + quarter_sum()
    inverse_two, normed_two = norm_forward(middle, gain_moe)
    hidden_two = normed_two.astype(narrow)
    live[H, own, 0] = hidden_two

    gather_near(H, own)
    live[H, nxt, 0] = swap(hidden_two, nxt)
    logits = jnp.dot(hidden_two, w_router, preferred_element_type=wide)
    expert_range = jnp.arange(expert_count, dtype=jnp.int32)
    matches = expert_ids[:, :, None] == expert_range[None, None, :]
    chosen = jnp.sum(jnp.where(matches, logits[:, None, :], 0.0), axis=2)
    gate_weights = jax.nn.softmax(chosen, axis=-1)
    rolled = (first_expert + expert_range) % expert_count
    live[ROUTER] = jnp.take(w_router.T, rolled, axis=0)
    live[NAMED] = jnp.broadcast_to(rolled.astype(wide)[:, None], (expert_count, LANES))
    sync()

    gather_far(H, own)
    gather_near(H, nxt)
    live[H, last, 0] = swap(live[H, own, 0], last)
    sync()

    gather_far(H, nxt)
    gather_core(H, own, 0, 1, 2, 3)
    live[PAIR, last, 0] = jnp.concatenate([live.pop((H, last, 0)), live.pop((G, last, 0))], axis=1)
    sync()

    def experts(plane):
        if (PAIR, plane, 0) in live:
            rows = blocks_of(PAIR, plane)
            grads, column = rows, model_width
        else:
            rows, grads, column = blocks_of(H, plane), blocks_of(G, plane), 0
        arrays = []
        for array, _ in rows + grads:
            if not any(array is other for other in arrays):
                arrays.append(array)

        def placed(blocks, column):
            indices = [[array is other for other in arrays].index(True) for array, _ in blocks]
            return [(index, row, column) for index, (_, row) in zip(indices, blocks)]

        done = expert_chunk(
            arrays,
            (placed(rows, 0), placed(grads, column)),
            live[NAMED],
            live[ROUTER],
            w_gate,
            w_up,
            w_down,
            2 * block_len,
            top_count,
            pair_cap,
        )
        live[M, plane, NEAR], live[M, plane, AWAY] = done[:2]
        live[R, plane, NEAR], live[R, plane, AWAY] = done[2:4]
        live[SUMS, plane] = done[4]
        live[KEPT, plane] = done[5:]

    hidden_two_sent = live[H, own, 0]
    gather_core(H, nxt, 0, 1, 2, 3)
    gather_near(PAIR, last)
    live[H, far_plane, 0] = swap(hidden_two_sent, far_plane)
    experts(own)
    sync()

    gather_far(PAIR, last)
    gather_core(PAIR, last, 0, 1, 2)
    live[PAIR, far_plane, 0] = jnp.concatenate(
        [live.pop((H, far_plane, 0)), live.pop((G, far_plane, 0))], axis=1
    )
    gather_near(PAIR, far_plane)
    reduce_core(R, own)
    experts(nxt)
    sync()
    gather_core(PAIR, last, 3)
    sync()

    gather_far(PAIR, far_plane)
    gather_core(PAIR, far_plane, 0, 1, 2)
    reduce_far(R, own)
    reduce_core(R, nxt)
    reduce_core(M, own)
    experts(last)
    sync()
    gather_core(PAIR, far_plane, 3)
    reduce_core(R, last)
    sync()

    reduce_near(R, own)
    reduce_far(R, nxt)
    reduce_far(R, last)
    reduce_core(M, nxt)
    experts(far_plane)
    sync()

    part_experts = local_experts // 4

    def some_weight_grads(part):
        kept = [live[KEPT, plane] for plane in PLANES]
        live[EXPERTS] = weight_grads(kept, part * part_experts, part_experts, live.get(EXPERTS, []))

    reduce_core(R, far_plane)
    sums = jnp.stack([live.pop((SUMS, plane)) for plane in PLANES])
    sums = sums.reshape(len(PLANES), -1, local_experts, 2, block_len).transpose(0, 1, 3, 2, 4)
    sums = sums.reshape(len(PLANES), BLOCKS, local_experts, block_len)
    live[GATES] = [sums[:, :4], core(sums[:, 4:])]
    reduce_core(M, last)
    sync()

    reduce_near(R, last)
    reduce_near(R, nxt)
    reduce_far(R, far_plane)
    sums = live[GATES][0] + live[GATES][1]
    crossed = jnp.stack([sums[:, 0], sums[:, 2], sums[:, 1], sums[:, 3]], axis=1)
    sums = jnp.where(odd_core == 0, sums, crossed)
    live[GATES] = [sums[:, ::2], swap(sums[:, 1::2], ACROSS)]
    live[HOME] = reduced(R, own)
    some_weight_grads(0)
    some_weight_grads(1)
    sync()

    live[RELAY] = swap(reduced(R, last), nxt)
    reduce_near(R, far_plane)
    sums = live[GATES][0] + live[GATES][1]
    live[GATES] = [sums[:, 0], swap(sums[:, 1], ASIDE)]
    reduce_core(M, far_plane)
    reduce_far(M, last)
    some_weight_grads(2)
    sync()

    live[RELAY] = swap(add(reduced(R, far_plane), live[RELAY]), far_plane)
    live[SIDE] = swap(reduced(R, nxt), nxt)
    sums = jnp.stack(live[GATES], axis=1)
    live[GATES] = [sums[0]] + [swap(sums[i], PLANES[i]) for i in range(1, len(PLANES))]
    reduce_near(M, last)
    reduce_far(M, far_plane)
    some_weight_grads(3)
    sync()
    for plane in PLANES:
        live.pop((KEPT, plane))

    grad_hidden_disp = live.pop(HOME).astype(wide) + live.pop(RELAY).astype(wide)
    grad_hidden_disp = grad_hidden_disp + live.pop(SIDE).astype(wide)
    sums = jnp.concatenate(live.pop(GATES), axis=0)
    owner = lax.axis_index("expert").astype(jnp.uint32)
    sums = [lax.dynamic_slice_in_dim(sums, owner ^ r, 1, 0)[0] for r in range(sums.shape[0])]
    own_sums = jnp.concatenate(sums, axis=0).T
    grad_out = cotangent.astype(wide)
    grad_gates = jnp.sum(jnp.where(matches, own_sums[:, None, :], 0.0), axis=2)
    grad_chosen = gate_weights * (
        grad_gates - jnp.sum(gate_weights * grad_gates, axis=-1, keepdims=True)
    )
    grad_logits = jnp.sum(jnp.where(matches, grad_chosen[:, :, None], 0.0), axis=1).astype(narrow)
    grad_router = jnp.einsum("ld,le->de", hidden_two, grad_logits, preferred_element_type=wide)
    grad_hidden_two = grad_hidden_disp + jnp.einsum(
        "le,de->ld", grad_logits, w_router, preferred_element_type=wide
    )
    grad_normed_two, grad_gain_moe = norm_backward(middle, inverse_two, gain_moe, grad_hidden_two)
    grad_middle = grad_out + grad_normed_two
    grad_attn = grad_middle.astype(narrow)

    small = jnp.concatenate([grad_router, grad_gain_moe[:, None]], axis=1)
    live[SMALL, FULL] = small.reshape(device_count, -1, small.shape[1])
    small_step = functools.partial(sum_step, SMALL, hops=small_hops, sent_as=wide)

    live[ATTN] = [grad_attn, core(grad_attn), swap(grad_attn, ACROSS)]
    sync()
    live[ATTN] = live[ATTN] + [core(live[ATTN][2])]
    small_step(0)
    sync()

    grad_attn_all = jnp.concatenate(live.pop(ATTN), axis=0)
    live[MIXED] = swap(reduced(M, last), nxt)
    reduce_near(M, far_plane)
    reduce_far(M, nxt)
    reduce_far(M, own)
    small_step(1)
    live[OUT, FULL] = jnp.einsum(
        "lh,ld->hd", live[HEADS], grad_attn_all, preferred_element_type=wide
    )
    grad_heads = (
        jnp.einsum("ld,hd->lh", grad_attn_all, w_out, preferred_element_type=wide)
        .astype(narrow)
        .reshape(seq_length, local_heads, HD)
    )
    probability = jnp.exp(masked_scores() - live[TOTALS])
    grad_values = jnp.einsum(
        "hqk,qhd->khd", probability.astype(narrow), grad_heads, preferred_element_type=wide
    )
    grad_prob = jnp.einsum("qhd,khd->hqk", grad_heads, live[VALUES], preferred_element_type=wide)
    row_delta = jnp.sum(probability * grad_prob, axis=-1, keepdims=True)
    grad_scores = (probability * (grad_prob - row_delta)).astype(narrow)
    grad_query = score_scale * jnp.einsum(
        "hqk,khd->qhd", grad_scores, live[KEYS], preferred_element_type=wide
    )
    grad_keys = score_scale * jnp.einsum(
        "hqk,qhd->khd", grad_scores, live[QUERIES], preferred_element_type=wide
    )

    def flat(source):
        return source.astype(narrow).reshape(seq_length, local_heads * HD)

    live[RAW] = [
        flat(rotate(grad_query, cosine_table, -sine_table)),
        flat(rotate(grad_keys, cosine_table, -sine_table)),
        flat(grad_values),
    ]
    sync()

    def back(grad_raw, weights):
        return jnp.einsum("lh,dh->ld", grad_raw, weights, preferred_element_type=wide)

    raw = live.pop(RAW)
    split_quarters(back(raw[0], w_query) + back(raw[1], w_key) + back(raw[2], w_value))
    live[IN, FULL] = jnp.einsum(
        "ld,lh->dh", hidden_one, jnp.concatenate(raw, axis=1), preferred_element_type=wide
    )
    sum_step(OUT, 0)
    live[MIXED] = swap(add(reduced(M, far_plane), live[MIXED]), far_plane)
    reduce_near(M, nxt)
    reduce_near(M, own)
    small_step(2)
    sync()

    live[SENT] = core(live[SENT])
    sum_step(IN, 0)
    sum_step(OUT, 1)
    small_step(3)
    live[SIDE] = reduced(M, nxt)
    live[HOME] = reduced(M, own)
    sync()

    cross_quarters()
    sum_step(IN, 1)
    sum_step(OUT, 2)
    small_step(4)
    sync()

    grad_normed_one, grad_gain_attn = norm_backward(
        own_inputs, own_inverse, gain_attn, quarter_sum()
    )
    live[TOKENS] = grad_middle + grad_normed_one
    live[GAIN] = [grad_gain_attn[None], jnp.zeros_like(grad_gain_attn)[None]]

    def gain_step(step):
        live[GAIN] = [live[GAIN][0] + live[GAIN][1]]
        live[GAIN] = live[GAIN] + [swap(live[GAIN][0], *small_hops[step])]

    sum_step(IN, 2)
    sum_step(OUT, 3)
    live[SIDE] = swap(live[SIDE], nxt)
    small_step(5)
    gain_step(0)
    sync()

    sum_step(IN, 3)
    sum_step(OUT, 4)
    small_step(6)
    small_step(7)
    gain_step(1)
    sync()

    sum_step(IN, 4)
    sum_step(OUT, 5)
    small_step(8)
    gain_step(2)
    gain_step(3)
    sync()

    grad_w_out = summed(OUT)
    sum_step(IN, 5)
    mixed_out = live[HOME].astype(wide) + live[MIXED].astype(wide) + live[SIDE].astype(wide)
    mixed_out = (middle + mixed_out).astype(narrow)
    small_step(9)
    gain_step(4)
    sync()
    grad_gain_attn = (live[GAIN][0] + live[GAIN][1])[0]
    small = summed(SMALL, small_hops).reshape(model_width, -1)
    grad_w_in = summed(IN)
    columns = local_heads * HD

    return (
        mixed_out,
        live[TOKENS],
        grad_gain_attn,
        grad_w_in[:, :columns],
        grad_w_in[:, columns : 2 * columns],
        grad_w_in[:, 2 * columns :],
        grad_w_out,
        small[:, expert_count],
        small[:, :expert_count],
        *live[EXPERTS],
    )


def on_device(*operands):
    tokens, w_router, w_gate, expert_ids = operands[0], operands[7], operands[8], operands[11]
    owners, quarters = lax.axis_size("expert"), lax.axis_size("tensor")
    block_len, top_count = expert_ids.shape
    capacity = 3 * block_len * top_count // (2 * w_router.shape[1])
    buffer_rows = capacity * quarters * owners * w_gate.shape[0]
    gathers = owners * tokens.shape[0] <= buffer_rows and (owners, quarters) == (8, 4)
    return (gathered_layer if gathers else routed_layer)(*operands)


def solution(mesh):
    return jax.shard_map(
        on_device,
        mesh=mesh,
        in_specs=(
            P("expert", None),
            P(),
            P(None, "tensor"),
            P(None, "tensor"),
            P(None, "tensor"),
            P("tensor", None),
            P(),
            P(),
            P("expert", None, "tensor"),
            P("expert", None, "tensor"),
            P("expert", "tensor", None),
            P(("expert", "tensor"), None),
            P(("expert", "tensor"), None),
        ),
        out_specs=(
            P(("expert", "tensor"), None),
            P(("expert", "tensor"), None),
            P(),
            P(None, "tensor"),
            P(None, "tensor"),
            P(None, "tensor"),
            P("tensor", None),
            P(),
            P(),
            P("expert", None, "tensor"),
            P("expert", None, "tensor"),
            P("expert", "tensor", None),
        ),
        check_vma=False,
    )
```

```python
import functools

import jax
import jax.numpy as jnp
from jax import lax
from jax.experimental import pallas as pl
from jax.experimental.pallas import tpu as pltpu
from jax.sharding import PartitionSpec as P

HD = 128


eps = 1e-06
theta_base = 10000.0
masked = -1e30

BOTH = ("expert", "tensor")
CORE, ACROSS, ASIDE, PLANE_NEXT, PLANE_FAR = 1, 2, 4, 8, 16
PLANES = (0, PLANE_NEXT, PLANE_FAR, PLANE_NEXT | PLANE_FAR)
BLOCKS = 8
WEIGHT_SLOTS = 3
LANES = 128

(
    G,
    H,
    M,
    R,
    QUERIES,
    KEYS,
    VALUES,
    TOTALS,
    HEADS,
    KEPT,
    SENT,
    RAW,
    HOME,
    SUMS,
    NEAR,
    AWAY,
    OTHER,
    FAR,
    OWN,
    SIDE,
    FULL,
    GOT,
    IN,
    OUT,
    TOKENS,
    NAMED,
    ROUTER,
    GATES,
    ATTN,
    RELAY,
    MIXED,
    EXPERTS,
    SMALL,
    GAIN,
    PAIR,
) = range(35)


def rope_tables(seq_length, head_size):
    half_dim = head_size // 2
    frequency = jnp.exp(
        -jnp.log(theta_base) * jnp.arange(half_dim, dtype=jnp.float32) * (2.0 / head_size)
    )
    angles = jnp.arange(seq_length, dtype=jnp.float32)[:, None] * frequency[None, :]
    return (jnp.cos(angles)[:, None, :], jnp.sin(angles)[:, None, :])


def rotate(source, cosine_table, sine_table):
    half_dim = source.shape[-1] // 2
    first_half = source[..., :half_dim]
    second = source[..., half_dim:]
    return jnp.concatenate(
        [
            first_half * cosine_table - second * sine_table,
            second * cosine_table + first_half * sine_table,
        ],
        axis=-1,
    )


def norm_forward(source, gain_vec):
    inverse = lax.rsqrt(jnp.mean(source * source, axis=-1, keepdims=True) + eps)
    return (inverse, source * inverse * gain_vec)


def norm_backward(source, inverse, gain_vec, grad_in):
    scaled = gain_vec * grad_in
    grad_source = inverse * scaled - source * inverse**3 * jnp.mean(
        scaled * source, axis=-1, keepdims=True
    )
    grad_gain = jnp.sum(grad_in * source * inverse, axis=0)
    return (grad_source, grad_gain)


def block_scores(q_block, key_rows, first_row, score_scale):
    scores = (
        jnp.einsum("qgrd,kgd->grqk", q_block, key_rows, preferred_element_type=jnp.float32)
        * score_scale
    )
    row_ids = first_row + jnp.arange(q_block.shape[0], dtype=jnp.int32)
    allowed = row_ids[:, None] >= jnp.arange(key_rows.shape[0], dtype=jnp.int32)[None, :]
    return jnp.where(allowed, scores, masked)


def routed_layer(
    tokens,
    gain_attn,
    w_query,
    w_key,
    w_value,
    w_out,
    gain_moe,
    w_router,
    w_gate,
    w_up,
    w_down,
    expert_ids,
    cotangent,
):
    seq_length, model_width = tokens.shape
    block_len, top_count = expert_ids.shape
    expert_count = w_router.shape[1]
    local_experts = w_gate.shape[0]
    local_heads = w_query.shape[1] // HD
    local_groups = w_key.shape[1] // HD
    group_size = local_heads // local_groups
    owners = lax.axis_size("expert")
    quarter = lax.axis_index("tensor")
    capacity = 3 * block_len * top_count // (2 * expert_count)
    block_rows = min(512, seq_length)
    block_count = seq_length // block_rows
    score_scale = HD ** (-0.5)
    first_own = quarter * block_len
    inputs = tokens.astype(jnp.float32)
    inverse_one, normed_one = norm_forward(inputs, gain_attn)
    hidden_one = normed_one.astype(jnp.bfloat16)
    cosine_table, sine_table = rope_tables(seq_length, HD)

    def rope_heads(source):
        return rotate(source, cosine_table, sine_table)

    query_raw = jnp.dot(hidden_one, w_query, preferred_element_type=jnp.float32).reshape(
        seq_length, local_heads, HD
    )
    key_raw = jnp.dot(hidden_one, w_key, preferred_element_type=jnp.float32).reshape(
        seq_length, local_groups, HD
    )
    queries = rope_heads(query_raw).astype(jnp.bfloat16)
    key_rows = rope_heads(key_raw).astype(jnp.bfloat16)
    value_rows = (
        jnp.dot(hidden_one, w_value, preferred_element_type=jnp.float32)
        .astype(jnp.bfloat16)
        .reshape(seq_length, local_groups, HD)
    )
    query_blocks = queries.reshape(block_count, block_rows, local_groups, group_size, HD)
    starts = jnp.arange(block_count, dtype=jnp.int32) * block_rows

    def attend_block(packed):
        first_row, q_block = packed
        scores = block_scores(q_block, key_rows, first_row, score_scale)
        row_max = jnp.max(scores, axis=-1, keepdims=True)
        exponent = jnp.exp(scores - row_max)
        row_total = jnp.sum(exponent, axis=-1, keepdims=True)
        weights = (exponent / row_total).astype(jnp.bfloat16)
        head_out = jnp.einsum(
            "grqk,kgd->qgrd", weights, value_rows, preferred_element_type=jnp.float32
        )
        return (head_out.astype(jnp.bfloat16), (row_max + jnp.log(row_total))[..., 0])

    head_blocks, log_totals = lax.map(attend_block, (starts, query_blocks))
    head_rows = head_blocks.reshape(seq_length, local_heads * HD)
    attention = lax.psum_scatter(
        jnp.dot(head_rows, w_out, preferred_element_type=jnp.float32),
        "tensor",
        scatter_dimension=0,
        tiled=True,
    )
    own_inputs = lax.dynamic_slice_in_dim(inputs, first_own, block_len, 0)
    own_inverse = lax.dynamic_slice_in_dim(inverse_one, first_own, block_len, 0)
    middle = own_inputs + attention
    inverse_two, normed_two = norm_forward(middle, gain_moe)
    hidden_two = normed_two.astype(jnp.bfloat16)
    logits = jnp.dot(hidden_two, w_router, preferred_element_type=jnp.float32)
    expert_range = jnp.arange(expert_count, dtype=jnp.int32)
    matches = expert_ids[:, :, None] == expert_range[None, None, :]
    chosen = jnp.sum(jnp.where(matches, logits[:, None, :], 0.0), axis=2)
    gate_weights = jax.nn.softmax(chosen, axis=-1)
    expert_hits = jnp.sum(matches.astype(jnp.int32), axis=1)
    earlier = jnp.cumsum(expert_hits, axis=0) - expert_hits
    slot_of = jnp.sum(jnp.where(matches, earlier[:, None, :], 0), axis=2)
    place = (slot_of * expert_count + expert_ids).reshape(-1)
    token_rows = jnp.broadcast_to(
        hidden_two[:, None, :], (block_len, top_count, model_width)
    ).reshape(block_len * top_count, model_width)
    grad_out = cotangent.astype(jnp.float32)
    gated_grads = (
        (gate_weights[:, :, None] * grad_out[:, None, :])
        .astype(jnp.bfloat16)
        .reshape(block_len * top_count, model_width)
    )
    empty = jnp.zeros((capacity * expert_count, model_width), jnp.bfloat16)
    send_rows = empty.at[place].set(token_rows).reshape(capacity, expert_count, model_width)
    send_grads = empty.at[place].set(gated_grads).reshape(capacity, expert_count, model_width)
    arrived_rows, arrived_grads = (
        lax.all_to_all(send_rows, "expert", split_axis=1, concat_axis=1, tiled=True),
        lax.all_to_all(send_grads, "expert", split_axis=1, concat_axis=1, tiled=True),
    )
    routed = arrived_rows.reshape(capacity, owners, local_experts, model_width)
    grads_in = arrived_grads.reshape(capacity, owners, local_experts, model_width)
    all_rows, all_grads = (
        lax.all_gather(routed, "tensor", axis=0, tiled=True),
        lax.all_gather(grads_in, "tensor", axis=0, tiled=True),
    )
    gate_pre = jnp.einsum("csld,ldf->cslf", all_rows, w_gate, preferred_element_type=jnp.float32)
    up_pre = jnp.einsum("csld,ldf->cslf", all_rows, w_up, preferred_element_type=jnp.float32)
    sigmoid_gate = jax.nn.sigmoid(gate_pre)
    silu_gate = gate_pre * sigmoid_gate
    activation = (silu_gate * up_pre).astype(jnp.bfloat16)
    grad_w_down = jnp.einsum(
        "cslf,csld->lfd", activation, all_grads, preferred_element_type=jnp.float32
    )
    grad_act = jnp.einsum("csld,lfd->cslf", all_grads, w_down, preferred_element_type=jnp.float32)
    grad_gate = (grad_act * up_pre * sigmoid_gate * (1.0 + gate_pre * (1.0 - sigmoid_gate))).astype(
        jnp.bfloat16
    )
    grad_up = (grad_act * silu_gate).astype(jnp.bfloat16)
    grad_w_gate = jnp.einsum(
        "csld,cslf->ldf", all_rows, grad_gate, preferred_element_type=jnp.float32
    )
    grad_w_up = jnp.einsum("csld,cslf->ldf", all_rows, grad_up, preferred_element_type=jnp.float32)
    forward_term = jnp.einsum(
        "cslf,lfd->csld", activation, w_down, preferred_element_type=jnp.float32
    )
    back_term = jnp.einsum("cslf,ldf->csld", grad_gate, w_gate, preferred_element_type=jnp.float32)
    back_term = back_term + jnp.einsum(
        "cslf,ldf->csld", grad_up, w_up, preferred_element_type=jnp.float32
    )
    both_terms = lax.psum_scatter(
        jnp.concatenate([forward_term, back_term], axis=3).astype(jnp.bfloat16),
        "tensor",
        scatter_dimension=0,
        tiled=True,
    )
    returned = both_terms[..., :model_width]
    row_grads = both_terms[..., model_width:]
    returned_home, row_grads_home = (
        lax.all_to_all(
            returned.reshape(capacity, expert_count, model_width),
            "expert",
            split_axis=1,
            concat_axis=1,
            tiled=True,
        ),
        lax.all_to_all(
            row_grads.reshape(capacity, expert_count, model_width),
            "expert",
            split_axis=1,
            concat_axis=1,
            tiled=True,
        ),
    )
    picked = returned_home.reshape(capacity * expert_count, model_width)[place].reshape(
        block_len, top_count, model_width
    )
    mixture = jnp.sum(gate_weights[:, :, None] * picked, axis=1)
    mixed_out = (middle + mixture).astype(jnp.bfloat16)
    grad_gates = jnp.sum(picked * grad_out[:, None, :], axis=2)
    grad_picked = row_grads_home.reshape(capacity * expert_count, model_width)[place].reshape(
        block_len, top_count, model_width
    )
    grad_hidden_disp = jnp.einsum(
        "lk,lkd->ld",
        jnp.ones((block_len, top_count), jnp.bfloat16),
        grad_picked,
        preferred_element_type=jnp.float32,
    )
    grad_chosen = gate_weights * (
        grad_gates - jnp.sum(gate_weights * grad_gates, axis=-1, keepdims=True)
    )
    grad_logits = jnp.sum(jnp.where(matches, grad_chosen[:, :, None], 0.0), axis=1).astype(
        jnp.bfloat16
    )
    grad_router = jnp.einsum(
        "ld,le->de", hidden_two, grad_logits, preferred_element_type=jnp.float32
    )
    grad_hidden_two = grad_hidden_disp + jnp.einsum(
        "le,de->ld", grad_logits, w_router, preferred_element_type=jnp.float32
    )
    grad_normed_two, grad_gain_moe = norm_backward(middle, inverse_two, gain_moe, grad_hidden_two)
    grad_middle = grad_out + grad_normed_two
    grad_attn = grad_middle.astype(jnp.bfloat16)
    grad_attn_all = lax.all_gather(grad_attn, "tensor", axis=0, tiled=True)
    grad_w_out = jnp.einsum(
        "lh,ld->hd", head_rows, grad_attn_all, preferred_element_type=jnp.float32
    )
    grad_heads = jnp.einsum(
        "ld,hd->lh", grad_attn_all, w_out, preferred_element_type=jnp.float32
    ).astype(jnp.bfloat16)
    grad_blocks = grad_heads.reshape(block_count, block_rows, local_groups, group_size, HD)

    def back_block(carried, packed):
        grad_keys, grad_values = carried
        first_row, q_block, g_block, lse_block = packed
        scores = block_scores(q_block, key_rows, first_row, score_scale)
        probability = jnp.exp(scores - lse_block[..., None])
        grad_values = grad_values + jnp.einsum(
            "grqk,qgrd->kgd",
            probability.astype(jnp.bfloat16),
            g_block,
            preferred_element_type=jnp.float32,
        )
        grad_prob = jnp.einsum(
            "qgrd,kgd->grqk", g_block, value_rows, preferred_element_type=jnp.float32
        )
        row_delta = jnp.sum(probability * grad_prob, axis=-1, keepdims=True)
        grad_scores = (probability * (grad_prob - row_delta)).astype(jnp.bfloat16)
        grad_query = (
            jnp.einsum("grqk,kgd->qgrd", grad_scores, key_rows, preferred_element_type=jnp.float32)
            * score_scale
        )
        grad_keys = (
            grad_keys
            + jnp.einsum("grqk,qgrd->kgd", grad_scores, q_block, preferred_element_type=jnp.float32)
            * score_scale
        )
        return ((grad_keys, grad_values), grad_query)

    zero_keys = jnp.zeros((seq_length, local_groups, HD), jnp.float32)
    (grad_keys, grad_values), grad_query_blocks = lax.scan(
        back_block, (zero_keys, zero_keys), (starts, query_blocks, grad_blocks, log_totals)
    )
    grad_query = grad_query_blocks.reshape(seq_length, local_heads, HD)
    grad_query_raw = (
        jax.vjp(rope_heads, query_raw)[1](grad_query)[0]
        .reshape(seq_length, local_heads * HD)
        .astype(jnp.bfloat16)
    )
    grad_key_raw = (
        jax.vjp(rope_heads, key_raw)[1](grad_keys)[0]
        .reshape(seq_length, local_groups * HD)
        .astype(jnp.bfloat16)
    )
    grad_value_raw = grad_values.reshape(seq_length, local_groups * HD).astype(jnp.bfloat16)
    grad_w_query = jnp.einsum(
        "ld,lh->dh", hidden_one, grad_query_raw, preferred_element_type=jnp.float32
    )
    grad_w_key = jnp.einsum(
        "ld,lh->dh", hidden_one, grad_key_raw, preferred_element_type=jnp.float32
    )
    grad_w_value = jnp.einsum(
        "ld,lh->dh", hidden_one, grad_value_raw, preferred_element_type=jnp.float32
    )
    term = jnp.einsum("lh,dh->ld", grad_query_raw, w_query, preferred_element_type=jnp.float32)
    term = term + jnp.einsum("lh,dh->ld", grad_key_raw, w_key, preferred_element_type=jnp.float32)
    grad_hidden_one = lax.psum_scatter(
        (
            term
            + jnp.einsum("lh,dh->ld", grad_value_raw, w_value, preferred_element_type=jnp.float32)
        ).astype(jnp.bfloat16),
        "tensor",
        scatter_dimension=0,
        tiled=True,
    ).astype(jnp.float32)
    grad_normed_one, grad_gain_attn = norm_backward(
        own_inputs, own_inverse, gain_attn, grad_hidden_one
    )
    grad_tokens = grad_middle + grad_normed_one
    attn_sums = lax.psum((grad_w_query, grad_w_key, grad_w_value, grad_w_out), "expert")
    small_sums = lax.psum((grad_gain_attn, grad_gain_moe, grad_router), ("expert", "tensor"))
    return (
        mixed_out,
        grad_tokens,
        small_sums[0],
        attn_sums[0],
        attn_sums[1],
        attn_sums[2],
        attn_sums[3],
        small_sums[1],
        small_sums[2],
        grad_w_gate,
        grad_w_up,
        grad_w_down,
    )


ROWS_ROWS = (((1,), (1,)), ((), ()))
def dot_nt(left, right):
    return lax.dot_general(left, right, ROWS_ROWS, preferred_element_type=jnp.float32)


def dot_nn(left, right):
    return jnp.dot(left, right, preferred_element_type=jnp.float32)


def expert_kernel(places, top_count, *refs):
    row_places, grad_places = places
    given = 1 + max(place[0] for place in row_places + grad_places)
    numbers_ref, router_ref, gate_ref, up_ref, down_ref = refs[given : given + 5]
    outs = refs[given + 5 : given + 14]
    mixed_refs, back_refs, sums_ref = outs[:2], outs[2:4], outs[4]
    rows_s, grads_s, ids_s, x_s, y_s, back_s, out_s = refs[given + 14 : given + 21]
    pick_s, place_s, gates_s, sums_s, gated_s, side_s = refs[given + 21 : given + 27]
    both_s, down_s, sems, weight_sems, out_sems, kept_sems = refs[given + 27 :]
    pairs, wide, _ = pick_s.shape
    experts = x_s.shape[0]
    hidden = down_s.shape[1]
    cap = wide // experts
    tokens_in, width = rows_s.shape[1:]
    block_len = tokens_in // 2
    narrow = jnp.bfloat16

    def copies(pair):
        out = []
        for half in range(2):
            target = pl.ds(half * block_len, block_len)
            at = 2 * pair + half
            array, row, column = row_places[at]
            rows = refs[array].at[pl.ds(row, block_len), pl.ds(column, width)]
            array, row, column = grad_places[at]
            block = refs[array].at[pl.ds(row, block_len)]
            grads = block.at[:, pl.ds(column, width)]
            ids = block.at[:, pl.ds(column + width, LANES)]
            for k, (source, scratch) in enumerate(
                ((rows, rows_s), (grads, grads_s), (ids, ids_s))
            ):
                out.append(
                    pltpu.make_async_copy(source, scratch.at[pair, target], sems.at[k, at])
                )
        return out

    def weight_copies(expert, slot):
        sides = [both_s.at[slot, :, pl.ds(k * hidden, hidden)] for k in range(2)]
        return [
            pltpu.make_async_copy(gate_ref.at[expert], sides[0], weight_sems.at[0, slot]),
            pltpu.make_async_copy(up_ref.at[expert], sides[1], weight_sems.at[1, slot]),
            pltpu.make_async_copy(down_ref.at[expert], down_s.at[slot], weight_sems.at[2, slot]),
        ]

    def result_copies(pair):
        half = pairs // 2
        place = pl.ds((pair % half) * tokens_in, tokens_in)
        sides = (rows_s, mixed_refs), (grads_s, back_refs)
        return [
            pltpu.make_async_copy(
                source.at[pair], targets[pair // half].at[place], out_sems.at[k, pair]
            )
            for k, (source, targets) in enumerate(sides)
        ]

    kept_copies = [
        pltpu.make_async_copy(source, target, kept_sems.at[k])
        for k, (source, target) in enumerate(zip((x_s, y_s, gated_s, side_s), outs[5:9]))
    ]

    for pair in range(pairs):
        for copy in copies(pair):
            copy.start()
    for slot in range(WEIGHT_SLOTS):
        for copy in weight_copies(slot, slot):
            copy.start()

    earlier = lax.broadcasted_iota(jnp.int32, (tokens_in, tokens_in), 0)
    later = lax.broadcasted_iota(jnp.int32, (tokens_in, tokens_in), 1)
    before = jnp.where(earlier < later, 1.0, 0.0).astype(narrow)

    for pair in range(pairs):
        for copy in copies(pair):
            copy.wait()
        rows_in = rows_s[pair]
        logits = dot_nt(router_ref[...], rows_in)
        ids = ids_s[pair].astype(jnp.float32).T
        named = jnp.zeros(logits.shape, jnp.float32)
        for k in range(top_count):
            named = jnp.where(ids[k : k + 1, :] == numbers_ref[:, :1], 1.0, named)
        hits = named[:experts]
        slots = jnp.where(hits > 0.0, dot_nn(hits.astype(narrow), before), -1.0)
        slots = slots.astype(jnp.int32)
        logits = jnp.where(named > 0.0, logits, masked)
        weights = jnp.exp(logits - jnp.max(logits, axis=0, keepdims=True)) * named
        gates = weights / jnp.sum(weights, axis=0, keepdims=True)
        ranks = lax.broadcasted_iota(jnp.int32, (cap, tokens_in), 0)
        place = pl.ds(pair * cap, cap)
        picks = []
        for expert in range(experts):
            pick = ranks == slots[expert : expert + 1, :]
            row_gates = jnp.sum(
                jnp.where(pick, gates[expert : expert + 1, :], 0.0), axis=1, keepdims=True
            )
            gates_s[expert, place, :] = jnp.broadcast_to(row_gates, (cap, LANES))
            picks.append(jnp.where(pick, 1.0, 0.0))
        pick_all = jnp.concatenate(picks, axis=0)
        pick_low = pick_all.astype(narrow)
        pick_s[pair] = pick_low
        place_s[pair] = pick_all.T.astype(narrow)
        for source, target in ((rows_in, x_s), (grads_s[pair], y_s)):
            spread = dot_nn(pick_low, source).astype(narrow)
            for expert in range(experts):
                target[expert, place, :] = spread[expert * cap : (expert + 1) * cap]

    kept_copies[0].start()
    kept_copies[1].start()

    def expert_step(expert, carried):
        slot = lax.rem(expert, WEIGHT_SLOTS)
        for copy in weight_copies(expert, slot):
            copy.wait()
        both = dot_nn(x_s[expert], both_s[slot])
        gate_pre, up_pre = both[:, :hidden], both[:, hidden:]
        plain = dot_nt(y_s[expert], down_s[slot])
        sigmoid_gate = jax.nn.sigmoid(gate_pre)
        silu_gate = gate_pre * sigmoid_gate
        activation = silu_gate * up_pre
        row_gates = gates_s[expert][:, :1]
        sums = jnp.sum(activation * plain, axis=1, keepdims=True)
        sums_s[expert] = jnp.broadcast_to(sums, sums_s.shape[1:])
        grad_act = row_gates * plain
        gated = (row_gates * activation).astype(narrow)
        slope = sigmoid_gate * (1.0 + gate_pre * (1.0 - sigmoid_gate))
        grad_gate = (grad_act * up_pre * slope).astype(narrow)
        grad_up = (grad_act * silu_gate).astype(narrow)
        grad_both = jnp.concatenate([grad_gate, grad_up], axis=1)
        gated_s[expert] = gated
        side_s[expert] = grad_both
        out_s[expert] = dot_nn(gated, down_s[slot]).astype(narrow)
        back_s[expert] = dot_nt(grad_both, both_s[slot]).astype(narrow)

        @pl.when(expert + WEIGHT_SLOTS < experts)
        def _():
            for copy in weight_copies(expert + WEIGHT_SLOTS, slot):
                copy.start()

        return carried

    lax.fori_loop(0, experts, expert_step, 0)
    kept_copies[2].start()
    kept_copies[3].start()

    for pair in range(pairs):
        sides = pl.ds(pair * cap, cap)
        for source, target in ((out_s, rows_s), (back_s, grads_s)):
            stacked = jnp.concatenate(
                [source[expert, sides, :] for expert in range(experts)], axis=0
            )
            target[pair] = dot_nn(place_s[pair], stacked).astype(narrow)
        for copy in result_copies(pair):
            copy.start()
        pick = pick_s[pair].astype(jnp.float32)
        sums = []
        for expert in range(experts):
            column = sums_s[expert, sides, :][:, :1]
            part = pick[expert * cap : (expert + 1) * cap] * column
            sums.append(jnp.sum(part, axis=0, keepdims=True))
        sums_ref[pair] = jnp.concatenate(sums, axis=0)

    for copy in kept_copies:
        copy.wait()
    for pair in range(pairs):
        for copy in result_copies(pair):
            copy.wait()


def expert_chunk(arrays, places, numbers, router, w_gate, w_up, w_down, tokens_in, top_count, cap):
    experts, width, hidden = w_gate.shape
    pairs = BLOCKS // 2
    rows = pairs * cap
    narrow, wide = jnp.bfloat16, jnp.float32
    shape = jax.ShapeDtypeStruct
    anywhere = pl.BlockSpec(memory_space=pl.ANY)
    inside = pl.BlockSpec(memory_space=pltpu.VMEM)
    half_shape = shape((pairs // 2 * tokens_in, width), narrow)
    whole_rows = (experts, rows, width)
    return pl.pallas_call(
        functools.partial(expert_kernel, places, top_count),
        in_specs=[anywhere] * len(arrays) + [inside] * 2 + [anywhere] * 3,
        out_specs=[anywhere] * 4 + [inside] + [anywhere] * 4,
        out_shape=[half_shape] * 4
        + [
            shape((pairs, experts, tokens_in), wide),
            shape(whole_rows, narrow),
            shape(whole_rows, narrow),
            shape((experts, rows, hidden), narrow),
            shape((experts, rows, 2 * hidden), narrow),
        ],
        scratch_shapes=[pltpu.VMEM((pairs, tokens_in, width), narrow)] * 2
        + [pltpu.VMEM((pairs, tokens_in, LANES), narrow)]
        + [pltpu.VMEM(whole_rows, narrow)] * 4
        + [
            pltpu.VMEM((pairs, experts * cap, tokens_in), narrow),
            pltpu.VMEM((pairs, tokens_in, experts * cap), narrow),
            pltpu.VMEM((experts, rows, LANES), wide),
            pltpu.VMEM((experts, rows, LANES), wide),
            pltpu.VMEM((experts, rows, hidden), narrow),
            pltpu.VMEM((experts, rows, 2 * hidden), narrow),
            pltpu.VMEM((WEIGHT_SLOTS, width, 2 * hidden), narrow),
            pltpu.VMEM((WEIGHT_SLOTS, hidden, width), narrow),
            pltpu.SemaphoreType.DMA((3, BLOCKS)),
            pltpu.SemaphoreType.DMA((3, WEIGHT_SLOTS)),
            pltpu.SemaphoreType.DMA((2, pairs)),
            pltpu.SemaphoreType.DMA((4,)),
        ],
        compiler_params=pltpu.CompilerParams(vmem_limit_bytes=60 << 20),
        cost_estimate=pl.CostEstimate(
            flops=24 * experts * rows * width * hidden,
            bytes_accessed=6 * experts * width * hidden + 4 * experts * rows * width,
            transcendentals=experts * rows * hidden,
        ),
    )(*arrays, numbers, router, w_gate, w_up, w_down)


def weight_kernel(parts, given, *refs):
    ins, (gate_ref, up_ref, down_ref) = refs[: 4 * parts], refs[4 * parts + given :]
    rows, grads, gated, both = [
        jnp.concatenate([ref[0] for ref in ins[k * parts : (k + 1) * parts]], axis=0)
        for k in range(4)
    ]
    turn = (((0,), (0,)), ((), ()))
    hidden = gated.shape[1]
    down_ref[0] = lax.dot_general(gated, grads, turn, preferred_element_type=jnp.float32)
    sides = lax.dot_general(rows, both, turn, preferred_element_type=jnp.float32)
    gate_ref[0] = sides[:, :hidden]
    up_ref[0] = sides[:, hidden:]


def weight_grads(kept, begin, count, partial):
    parts = len(kept)
    experts, rows, width = kept[0][0].shape
    hidden = kept[0][2].shape[2]
    operands = [part[k] for k in range(4) for part in kept]
    shape = jax.ShapeDtypeStruct

    def spec(rows, columns):
        return pl.BlockSpec((1, rows, columns), lambda i: (i + begin, 0, 0))

    return pl.pallas_call(
        functools.partial(weight_kernel, parts, len(partial)),
        grid=(count,),
        in_specs=[spec(rows, operand.shape[2]) for operand in operands]
        + [pl.BlockSpec(memory_space=pl.ANY)] * len(partial),
        out_specs=[spec(width, hidden), spec(width, hidden), spec(hidden, width)],
        out_shape=[
            shape((experts, width, hidden), jnp.float32),
            shape((experts, width, hidden), jnp.float32),
            shape((experts, hidden, width), jnp.float32),
        ],
        input_output_aliases={len(operands) + k: k for k in range(len(partial))},
        compiler_params=pltpu.CompilerParams(vmem_limit_bytes=56 << 20),
        cost_estimate=pl.CostEstimate(
            flops=6 * parts * count * rows * width * hidden,
            bytes_accessed=count * (parts * rows * (4 * width + 6 * hidden) + 12 * width * hidden),
            transcendentals=0,
        ),
    )(*operands, *partial)


def gathered_layer(
    tokens,
    gain_attn,
    w_query,
    w_key,
    w_value,
    w_out,
    gain_moe,
    w_router,
    w_gate,
    w_up,
    w_down,
    expert_ids,
    cotangent,
):
    seq_length, model_width = tokens.shape
    block_len, top_count = expert_ids.shape
    expert_count = w_router.shape[1]
    local_experts = w_gate.shape[0]
    local_heads = w_query.shape[1] // HD
    quarters = lax.axis_size("tensor")
    device_count = quarters * lax.axis_size("expert")
    quarter = lax.axis_index("tensor").astype(jnp.uint32)
    device = lax.axis_index(BOTH).astype(jnp.uint32)
    first_expert = lax.axis_index("expert") * local_experts
    pair_cap = 2 * (3 * block_len * top_count // (2 * expert_count))
    score_scale = HD ** (-0.5)
    narrow, wide = jnp.bfloat16, jnp.float32

    def swap(value, even, odd=None):
        odd = even if odd is None else odd
        perm = [(i, i ^ (odd if i & 1 else even)) for i in range(device_count)]
        return lax.ppermute(value, BOTH, perm)

    def near(value):
        return swap(value, ACROSS, ASIDE)

    def far(value):
        return swap(value, ASIDE, ACROSS)

    def core(value):
        return swap(value, CORE)

    def add(left, right):
        return (left.astype(wide) + right.astype(wide)).astype(narrow)

    live = {}

    def sync():
        keys = list(live)
        values = lax.optimization_barrier([live[key] for key in keys])
        live.update(zip(keys, values))

    def gather_near(name, plane):
        live[name, plane, 1] = near(live[name, plane, 0])
        live[name, plane, 2] = far(live[name, plane, 0])

    def gather_far(name, plane):
        live[name, plane, 3] = far(live[name, plane, 1])

    def gather_across(name, plane):
        live[name, plane, 3] = swap(live[name, plane, 0], ACROSS | ASIDE)

    def gather_core(name, plane, *slots):
        blocks = [live[name, plane, slot] for slot in slots]
        live[name, plane, (OTHER,) + slots] = core(jnp.concatenate(blocks, axis=0))

    def blocks_of(name, plane):
        found = {}
        for key in list(live):
            if isinstance(key, tuple) and key[:2] == (name, plane):
                slots = key[2]
                array = live.pop(key)
                if isinstance(slots, tuple):
                    for i, slot in enumerate(slots[1:]):
                        found[4 + slot] = (array, i * block_len)
                else:
                    found[slots] = (array, 0)
        return [found[slot] for slot in range(BLOCKS)]

    def reduce_core(name, plane):
        live[name, plane, OTHER] = core(live.pop((name, plane, AWAY)))

    def reduce_far(name, plane):
        kept = live[name, plane, NEAR].reshape(4, block_len, model_width)
        got = live[name, plane, OTHER].reshape(4, block_len, model_width)
        live[name, plane, FAR] = far(add(kept[2:], got[2:]))

    def reduce_near(name, plane):
        kept = live.pop((name, plane, NEAR)).reshape(4, block_len, model_width)
        got = live.pop((name, plane, OTHER)).reshape(4, block_len, model_width)
        back = live.pop((name, plane, FAR))
        sums = [
            kept[i].astype(wide) + got[i].astype(wide) + back[i].astype(wide) for i in range(2)
        ]
        live[name, plane, OWN] = sums[0].astype(narrow)
        live[name, plane, SIDE] = near(sums[1].astype(narrow))

    def reduced(name, plane):
        return add(live.pop((name, plane, OWN)), live.pop((name, plane, SIDE)))

    def bit(mask):
        return (device // mask) % 2

    odd_core = bit(CORE)
    weight_hops = ((ASIDE, PLANE_NEXT), (PLANE_NEXT, ASIDE), (PLANE_FAR, PLANE_FAR))
    small_hops = tuple((mask, mask) for mask in (CORE, ACROSS, ASIDE, PLANE_NEXT, PLANE_FAR))

    def joined(own, got, side):
        count = own.shape[0]
        both = jnp.zeros((2 * count,) + own.shape[1:], own.dtype)
        both = lax.dynamic_update_slice_in_dim(both, own, side * count, 0)
        return lax.dynamic_update_slice_in_dim(both, got, (1 - side) * count, 0)

    def sum_step(name, step, hops=weight_hops, sent_as=narrow):
        count = len(hops)
        sides = [jnp.where(odd_core == 0, bit(even), bit(odd)) for even, odd in hops]
        if step == 0:
            kept = live.pop((name, FULL))
        elif step <= count:
            kept = live.pop((name, KEPT)) + live.pop((name, GOT)).astype(wide)
        else:
            kept = joined(live.pop((name, KEPT)), live.pop((name, GOT)), sides[2 * count - step])
        if step < count:
            half = kept.shape[0] // 2
            side = sides[step]
            live[name, KEPT] = lax.dynamic_slice_in_dim(kept, side * half, half, 0)
            sent = lax.dynamic_slice_in_dim(kept, (1 - side) * half, half, 0)
            live[name, GOT] = swap(sent.astype(sent_as), *hops[step])
        else:
            kept = kept.astype(sent_as)
            live[name, KEPT] = kept
            live[name, GOT] = swap(kept, *hops[2 * count - 1 - step])

    def summed(name, hops=weight_hops):
        even, odd = hops[0]
        side = jnp.where(odd_core == 0, bit(even), bit(odd))
        return joined(live.pop((name, KEPT)), live.pop((name, GOT)), side).astype(wide)

    own, nxt, far_plane, last = PLANES

    named_ids = jnp.pad(expert_ids.astype(narrow), ((0, 0), (0, LANES - top_count)))
    live[G, own, 0] = jnp.concatenate([cotangent, named_ids], axis=1)
    half_block = block_len // 2
    live[G, nxt, 0] = swap(live[G, own, 0], nxt)
    live[G, far_plane, 0] = [swap(live[G, own, 0][:half_block], far_plane)]
    gather_near(G, own)

    by_block = tokens.reshape(quarters, block_len, model_width)
    inputs = jnp.concatenate(
        [lax.dynamic_slice_in_dim(by_block, quarter ^ r, 1, 0)[0] for r in range(quarters)], axis=0
    )
    inputs = lax.optimization_barrier(inputs)
    order = quarter.astype(jnp.int32) ^ jnp.arange(quarters, dtype=jnp.int32)
    positions = (order[:, None] * block_len + jnp.arange(block_len, dtype=jnp.int32)).reshape(-1)
    inverse_one, normed_one = norm_forward(inputs.astype(wide), gain_attn)
    hidden_one = normed_one.astype(narrow)
    frequency = jnp.exp(
        -jnp.log(theta_base) * jnp.arange(HD // 2, dtype=jnp.float32) * (2.0 / HD)
    )
    angles = positions.astype(wide)[:, None] * frequency[None, :]
    cosine_table, sine_table = (jnp.cos(angles)[:, None, :], jnp.sin(angles)[:, None, :])

    def project(weights):
        return jnp.dot(hidden_one, weights, preferred_element_type=wide).reshape(
            seq_length, local_heads, HD
        )

    live[QUERIES] = rotate(project(w_query), cosine_table, sine_table).astype(narrow)
    live[KEYS] = rotate(project(w_key), cosine_table, sine_table).astype(narrow)
    live[VALUES] = project(w_value).astype(narrow)
    sync()

    gather_far(G, own)
    gather_near(G, nxt)
    live[G, far_plane, 0] = live[G, far_plane, 0] + [
        swap(live[G, own, 0][half_block:], far_plane)
    ]
    allowed = positions[:, None] >= positions[None, :]

    def masked_scores():
        scores = jnp.einsum(
            "qhd,khd->hqk", live[QUERIES], live[KEYS], preferred_element_type=wide
        )
        return jnp.where(allowed, scores * score_scale, masked)

    scores = masked_scores()
    row_max = jnp.max(scores, axis=-1, keepdims=True)
    exponent = jnp.exp(scores - row_max)
    row_total = jnp.sum(exponent, axis=-1, keepdims=True)
    weights = (exponent / row_total).astype(narrow)
    head_out = jnp.einsum("hqk,khd->qhd", weights, live[VALUES], preferred_element_type=wide)
    live[TOTALS] = row_max + jnp.log(row_total)
    live[HEADS] = head_out.astype(narrow).reshape(seq_length, local_heads * HD)

    def split_quarters(full):
        parts = full.reshape(quarters, block_len, model_width)
        live[KEPT] = [parts[0], parts[2]]
        live[SENT] = jnp.stack([parts[1], parts[3]]).astype(narrow)

    split_quarters(jnp.dot(live[HEADS], w_out, preferred_element_type=wide))
    sync()

    live[SENT] = core(live[SENT])
    gather_far(G, nxt)
    live[G, far_plane, 0] = jnp.concatenate(live[G, far_plane, 0], axis=0)
    sync()

    def cross_quarters():
        kept, sent = live.pop(KEPT), live.pop(SENT).astype(wide)
        live[KEPT] = kept[0] + sent[0]
        live[SENT] = swap((kept[1] + sent[1]).astype(narrow), ACROSS)

    def quarter_sum():
        return live.pop(KEPT) + live.pop(SENT).astype(wide)

    cross_quarters()
    live[G, last, 0] = swap(live[G, far_plane, 0], nxt)
    sync()

    own_inputs = inputs[:block_len].astype(wide)
    own_inverse = inverse_one[:block_len]
    middle = own_inputs + quarter_sum()
    inverse_two, normed_two = norm_forward(middle, gain_moe)
    hidden_two = normed_two.astype(narrow)
    live[H, own, 0] = hidden_two

    gather_near(H, own)
    live[H, nxt, 0] = swap(hidden_two, nxt)
    gather_core(G, own, 0, 1, 2, 3)
    logits = jnp.dot(hidden_two, w_router, preferred_element_type=wide)
    expert_range = jnp.arange(expert_count, dtype=jnp.int32)
    matches = expert_ids[:, :, None] == expert_range[None, None, :]
    chosen = jnp.sum(jnp.where(matches, logits[:, None, :], 0.0), axis=2)
    gate_weights = jax.nn.softmax(chosen, axis=-1)
    rolled = (first_expert + expert_range) % expert_count
    live[ROUTER] = jnp.take(w_router.T, rolled, axis=0)
    live[NAMED] = jnp.broadcast_to(rolled.astype(wide)[:, None], (expert_count, LANES))
    sync()

    gather_far(H, own)
    gather_near(H, nxt)
    hidden_two = live[H, own, 0]
    gather_core(G, nxt, 0, 1, 2, 3)
    live[H, last, 0] = [swap(hidden_two[:half_block], last)]
    sync()

    gather_far(H, nxt)
    gather_core(H, own, 0, 1, 2, 3)
    hidden_two = live[H, own, 0]
    live[H, last, 0] = live[H, last, 0] + [swap(hidden_two[half_block:], last)]
    sync()

    def join_pair(plane):
        rows, grads = [live.pop((name, plane, 0)) for name in (H, G)]
        if isinstance(rows, list):
            rows = jnp.concatenate(rows, axis=0)
        live[PAIR, plane, 0] = jnp.concatenate([rows, grads], axis=1)

    def experts(plane):
        if (PAIR, plane, 0) in live:
            rows = blocks_of(PAIR, plane)
            grads, column = rows, model_width
        else:
            rows, grads, column = blocks_of(H, plane), blocks_of(G, plane), 0
        arrays = []
        for array, _ in rows + grads:
            if not any(array is other for other in arrays):
                arrays.append(array)

        def placed(blocks, column):
            indices = [[array is other for other in arrays].index(True) for array, _ in blocks]
            return [(index, row, column) for index, (_, row) in zip(indices, blocks)]

        done = expert_chunk(
            arrays,
            (placed(rows, 0), placed(grads, column)),
            live[NAMED],
            live[ROUTER],
            w_gate,
            w_up,
            w_down,
            2 * block_len,
            top_count,
            pair_cap,
        )
        live[M, plane, NEAR], live[M, plane, AWAY] = done[:2]
        live[R, plane, NEAR], live[R, plane, AWAY] = done[2:4]
        live[SUMS, plane] = done[4]
        live[KEPT, plane] = done[5:]

    gather_core(H, nxt, 0, 1, 2, 3)
    join_pair(last)
    gather_near(PAIR, last)
    live[H, far_plane, 0] = swap(live[H, own, 0], far_plane)
    experts(own)
    sync()

    gather_far(PAIR, last)
    gather_core(PAIR, last, 0, 1, 2)
    join_pair(far_plane)
    gather_near(PAIR, far_plane)
    reduce_core(R, own)
    experts(nxt)
    sync()
    gather_core(PAIR, last, 3)
    sync()

    gather_far(PAIR, far_plane)
    gather_core(PAIR, far_plane, 0, 1, 2)
    reduce_far(R, own)
    reduce_core(R, nxt)
    reduce_core(M, own)
    experts(last)
    sync()
    gather_core(PAIR, far_plane, 3)
    reduce_core(R, last)
    sync()

    reduce_near(R, own)
    reduce_far(R, nxt)
    reduce_far(R, last)
    reduce_core(M, nxt)
    experts(far_plane)
    sync()

    part_experts = local_experts // 4

    def some_weight_grads(part):
        kept = [live[KEPT, plane] for plane in PLANES]
        live[EXPERTS] = weight_grads(kept, part * part_experts, part_experts, live.get(EXPERTS, []))

    reduce_core(R, far_plane)
    sums = jnp.stack([live.pop((SUMS, plane)) for plane in PLANES])
    sums = sums.reshape(len(PLANES), -1, local_experts, 2, block_len).transpose(0, 1, 3, 2, 4)
    sums = sums.reshape(len(PLANES), BLOCKS, local_experts, block_len)
    live[GATES] = [sums[:, :4], core(sums[:, 4:])]
    reduce_core(M, last)
    sync()

    reduce_far(R, far_plane)
    reduce_near(R, last)
    reduce_near(R, nxt)
    sums = live[GATES][0] + live[GATES][1]
    crossed = jnp.stack([sums[:, 0], sums[:, 2], sums[:, 1], sums[:, 3]], axis=1)
    sums = jnp.where(odd_core == 0, sums, crossed)
    live[GATES] = [sums[:, ::2], swap(sums[:, 1::2], ACROSS)]
    sync()

    live[RELAY] = swap(reduced(R, last), nxt)
    reduce_near(R, far_plane)
    sums = live[GATES][0] + live[GATES][1]
    sums = jnp.stack([sums[:, 0], swap(sums[:, 1], ASIDE)], axis=1)
    live[GATES] = [sums[::2], swap(sums[1::2], nxt)]
    reduce_core(M, far_plane)
    live[HOME] = reduced(R, own)
    live[SIDE] = reduced(R, nxt)
    sync()

    live[RELAY] = swap(add(reduced(R, far_plane), live[RELAY]), far_plane)
    live[SIDE] = swap(live[SIDE], nxt)
    sums = jnp.stack(live[GATES], axis=1)
    live[GATES] = [sums[0], swap(sums[1], far_plane)]
    reduce_far(M, last)
    reduce_far(M, far_plane)
    sync()

    grad_hidden_disp = live.pop(HOME).astype(wide) + live.pop(RELAY).astype(wide)
    grad_hidden_disp = grad_hidden_disp + live.pop(SIDE).astype(wide)
    sums = jnp.concatenate(live.pop(GATES), axis=0).reshape(-1, local_experts, block_len)
    owner = lax.axis_index("expert").astype(jnp.uint32)
    sums = [lax.dynamic_slice_in_dim(sums, owner ^ r, 1, 0)[0] for r in range(sums.shape[0])]
    own_sums = jnp.concatenate(sums, axis=0).T
    grad_out = cotangent.astype(wide)
    grad_gates = jnp.sum(jnp.where(matches, own_sums[:, None, :], 0.0), axis=2)
    grad_chosen = gate_weights * (
        grad_gates - jnp.sum(gate_weights * grad_gates, axis=-1, keepdims=True)
    )
    grad_logits = jnp.sum(jnp.where(matches, grad_chosen[:, :, None], 0.0), axis=1).astype(narrow)
    grad_router = jnp.einsum("ld,le->de", hidden_two, grad_logits, preferred_element_type=wide)
    grad_hidden_two = grad_hidden_disp + jnp.einsum(
        "le,de->ld", grad_logits, w_router, preferred_element_type=wide
    )
    grad_normed_two, grad_gain_moe = norm_backward(middle, inverse_two, gain_moe, grad_hidden_two)
    grad_middle = grad_out + grad_normed_two
    grad_attn = grad_middle.astype(narrow)

    small = jnp.concatenate([grad_router, grad_gain_moe[:, None]], axis=1)
    live[SMALL, FULL] = small.reshape(device_count, -1, small.shape[1])
    small_step = functools.partial(sum_step, SMALL, hops=small_hops, sent_as=wide)

    live[ATTN] = [grad_attn, core(grad_attn), swap(grad_attn, ACROSS)]
    small_step(0)
    sync()
    live[ATTN] = live[ATTN] + [core(live[ATTN][2])]
    small_step(1)
    sync()

    grad_attn_all = jnp.concatenate(live.pop(ATTN), axis=0)
    reduce_near(M, last)
    reduce_near(M, far_plane)
    small_step(2)
    live[OUT, FULL] = jnp.einsum(
        "lh,ld->hd", live[HEADS], grad_attn_all, preferred_element_type=wide
    )
    grad_heads = (
        jnp.einsum("ld,hd->lh", grad_attn_all, w_out, preferred_element_type=wide)
        .astype(narrow)
        .reshape(seq_length, local_heads, HD)
    )
    live[RAW] = grad_heads
    sync()

    grad_heads = live.pop(RAW)
    live[MIXED] = swap(reduced(M, last), nxt)
    reduce_far(M, nxt)
    probability = jnp.exp(masked_scores() - live[TOTALS])
    grad_values = jnp.einsum(
        "hqk,qhd->khd", probability.astype(narrow), grad_heads, preferred_element_type=wide
    )
    grad_prob = jnp.einsum("qhd,khd->hqk", grad_heads, live[VALUES], preferred_element_type=wide)
    row_delta = jnp.sum(probability * grad_prob, axis=-1, keepdims=True)
    grad_scores = (probability * (grad_prob - row_delta)).astype(narrow)
    grad_query = score_scale * jnp.einsum(
        "hqk,khd->qhd", grad_scores, live[KEYS], preferred_element_type=wide
    )
    grad_keys = score_scale * jnp.einsum(
        "hqk,qhd->khd", grad_scores, live[QUERIES], preferred_element_type=wide
    )

    def flat(source):
        return source.astype(narrow).reshape(seq_length, local_heads * HD)

    live[RAW] = [
        flat(rotate(grad_query, cosine_table, -sine_table)),
        flat(rotate(grad_keys, cosine_table, -sine_table)),
        flat(grad_values),
    ]
    sync()

    def back(grad_raw, weights):
        return jnp.einsum("lh,dh->ld", grad_raw, weights, preferred_element_type=wide)

    raw = live.pop(RAW)
    split_quarters(back(raw[0], w_query) + back(raw[1], w_key) + back(raw[2], w_value))
    live[IN, FULL] = jnp.einsum(
        "ld,lh->dh", hidden_one, jnp.concatenate(raw, axis=1), preferred_element_type=wide
    )
    sum_step(OUT, 0)
    sum_step(OUT, 1)
    live[MIXED] = swap(add(reduced(M, far_plane), live[MIXED]), far_plane)
    reduce_near(M, nxt)
    small_step(3)
    sync()

    live[SENT] = core(live[SENT])
    sum_step(IN, 0)
    sum_step(OUT, 2)
    small_step(4)
    some_weight_grads(0)
    sync()

    cross_quarters()
    sum_step(IN, 1)
    sum_step(OUT, 3)
    small_step(5)
    some_weight_grads(1)
    sync()

    grad_normed_one, grad_gain_attn = norm_backward(
        own_inputs, own_inverse, gain_attn, quarter_sum()
    )
    live[TOKENS] = grad_middle + grad_normed_one
    live[GAIN] = [grad_gain_attn[None], jnp.zeros_like(grad_gain_attn)[None]]

    def gain_step(step):
        live[GAIN] = [live[GAIN][0] + live[GAIN][1]]
        live[GAIN] = live[GAIN] + [swap(live[GAIN][0], *small_hops[step])]

    sum_step(IN, 2)
    sum_step(OUT, 4)
    reduce_far(M, own)
    live[SIDE] = swap(reduced(M, nxt), nxt)
    small_step(6)
    gain_step(0)
    some_weight_grads(2)
    sync()

    sum_step(IN, 3)
    sum_step(OUT, 5)
    reduce_near(M, own)
    small_step(7)
    gain_step(1)
    some_weight_grads(3)
    sync()
    for plane in PLANES:
        live.pop((KEPT, plane))

    mixed_out = middle + reduced(M, own).astype(wide) + live.pop(MIXED).astype(wide)
    live[MIXED] = (mixed_out + live.pop(SIDE).astype(wide)).astype(narrow)
    live[OUT] = summed(OUT)
    sum_step(IN, 4)
    small_step(8)
    gain_step(2)
    gain_step(3)
    sync()

    columns = local_heads * HD
    small_step(9)
    gain_step(4)
    sum_step(IN, 5)
    even, odd = weight_hops[0]
    side = jnp.where(odd_core == 0, bit(even), bit(odd))
    half = live[IN, KEPT].shape[0]

    def put(whole, part, index, at):
        part = part[:, index * columns : (index + 1) * columns].astype(wide)
        return lax.dynamic_update_slice_in_dim(whole, part, at * half, 0)

    empty = jnp.zeros((2 * half, columns), wide)
    live[RAW] = [put(empty, live[IN, KEPT], index, side) for index in range(3)]
    sync()
    grads_in = [put(whole, live[IN, GOT], i, 1 - side) for i, whole in enumerate(live[RAW])]
    grad_gain_attn = (live[GAIN][0] + live[GAIN][1])[0]
    small = summed(SMALL, small_hops).reshape(model_width, -1)

    return (
        live[MIXED],
        live[TOKENS],
        grad_gain_attn,
        *grads_in,
        live[OUT],
        small[:, expert_count],
        small[:, :expert_count],
        *live[EXPERTS],
    )


def on_device(*operands):
    tokens, w_router, w_gate, expert_ids = operands[0], operands[7], operands[8], operands[11]
    owners, quarters = lax.axis_size("expert"), lax.axis_size("tensor")
    block_len, top_count = expert_ids.shape
    capacity = 3 * block_len * top_count // (2 * w_router.shape[1])
    buffer_rows = capacity * quarters * owners * w_gate.shape[0]
    gathers = owners * tokens.shape[0] <= buffer_rows and (owners, quarters) == (8, 4)
    return (gathered_layer if gathers else routed_layer)(*operands)


def solution(mesh):
    return jax.shard_map(
        on_device,
        mesh=mesh,
        in_specs=(
            P("expert", None),
            P(),
            P(None, "tensor"),
            P(None, "tensor"),
            P(None, "tensor"),
            P("tensor", None),
            P(),
            P(),
            P("expert", None, "tensor"),
            P("expert", None, "tensor"),
            P("expert", "tensor", None),
            P(("expert", "tensor"), None),
            P(("expert", "tensor"), None),
        ),
        out_specs=(
            P(("expert", "tensor"), None),
            P(("expert", "tensor"), None),
            P(),
            P(None, "tensor"),
            P(None, "tensor"),
            P(None, "tensor"),
            P("tensor", None),
            P(),
            P(),
            P("expert", None, "tensor"),
            P("expert", None, "tensor"),
            P("expert", "tensor", None),
        ),
        check_vma=False,
    )
```

```python
import functools

import jax
import jax.numpy as jnp
from jax import lax
from jax.experimental import pallas as pl
from jax.experimental.pallas import tpu as pltpu
from jax.sharding import PartitionSpec as P

HD = 128


eps = 1e-06
theta_base = 10000.0
masked = -1e30

BOTH = ("expert", "tensor")
CORE, ACROSS, ASIDE, PLANE_NEXT, PLANE_FAR = 1, 2, 4, 8, 16
PLANES = (0, PLANE_NEXT, PLANE_FAR, PLANE_NEXT | PLANE_FAR)
BLOCKS = 8
WEIGHT_SLOTS = 3
LANES = 128

(
    G,
    H,
    M,
    R,
    QUERIES,
    KEYS,
    VALUES,
    TOTALS,
    HEADS,
    KEPT,
    SENT,
    RAW,
    HOME,
    SUMS,
    NEAR,
    AWAY,
    OTHER,
    FAR,
    OWN,
    SIDE,
    FULL,
    GOT,
    IN,
    OUT,
    TOKENS,
    NAMED,
    ROUTER,
    GATES,
    ATTN,
    RELAY,
    MIXED,
    EXPERTS,
    SMALL,
    GAIN,
    PAIR,
) = range(35)


def rope_tables(seq_length, head_size):
    half_dim = head_size // 2
    frequency = jnp.exp(
        -jnp.log(theta_base) * jnp.arange(half_dim, dtype=jnp.float32) * (2.0 / head_size)
    )
    angles = jnp.arange(seq_length, dtype=jnp.float32)[:, None] * frequency[None, :]
    return (jnp.cos(angles)[:, None, :], jnp.sin(angles)[:, None, :])


def rotate(source, cosine_table, sine_table):
    half_dim = source.shape[-1] // 2
    first_half = source[..., :half_dim]
    second = source[..., half_dim:]
    return jnp.concatenate(
        [
            first_half * cosine_table - second * sine_table,
            second * cosine_table + first_half * sine_table,
        ],
        axis=-1,
    )


def norm_forward(source, gain_vec):
    inverse = lax.rsqrt(jnp.mean(source * source, axis=-1, keepdims=True) + eps)
    return (inverse, source * inverse * gain_vec)


def norm_backward(source, inverse, gain_vec, grad_in):
    scaled = gain_vec * grad_in
    grad_source = inverse * scaled - source * inverse**3 * jnp.mean(
        scaled * source, axis=-1, keepdims=True
    )
    grad_gain = jnp.sum(grad_in * source * inverse, axis=0)
    return (grad_source, grad_gain)


def block_scores(q_block, key_rows, first_row, score_scale):
    scores = (
        jnp.einsum("qgrd,kgd->grqk", q_block, key_rows, preferred_element_type=jnp.float32)
        * score_scale
    )
    row_ids = first_row + jnp.arange(q_block.shape[0], dtype=jnp.int32)
    allowed = row_ids[:, None] >= jnp.arange(key_rows.shape[0], dtype=jnp.int32)[None, :]
    return jnp.where(allowed, scores, masked)


def routed_layer(
    tokens,
    gain_attn,
    w_query,
    w_key,
    w_value,
    w_out,
    gain_moe,
    w_router,
    w_gate,
    w_up,
    w_down,
    expert_ids,
    cotangent,
):
    seq_length, model_width = tokens.shape
    block_len, top_count = expert_ids.shape
    expert_count = w_router.shape[1]
    local_experts = w_gate.shape[0]
    local_heads = w_query.shape[1] // HD
    local_groups = w_key.shape[1] // HD
    group_size = local_heads // local_groups
    owners = lax.axis_size("expert")
    quarter = lax.axis_index("tensor")
    capacity = 3 * block_len * top_count // (2 * expert_count)
    block_rows = min(512, seq_length)
    block_count = seq_length // block_rows
    score_scale = HD ** (-0.5)
    first_own = quarter * block_len
    inputs = tokens.astype(jnp.float32)
    inverse_one, normed_one = norm_forward(inputs, gain_attn)
    hidden_one = normed_one.astype(jnp.bfloat16)
    cosine_table, sine_table = rope_tables(seq_length, HD)

    def rope_heads(source):
        return rotate(source, cosine_table, sine_table)

    query_raw = jnp.dot(hidden_one, w_query, preferred_element_type=jnp.float32).reshape(
        seq_length, local_heads, HD
    )
    key_raw = jnp.dot(hidden_one, w_key, preferred_element_type=jnp.float32).reshape(
        seq_length, local_groups, HD
    )
    queries = rope_heads(query_raw).astype(jnp.bfloat16)
    key_rows = rope_heads(key_raw).astype(jnp.bfloat16)
    value_rows = (
        jnp.dot(hidden_one, w_value, preferred_element_type=jnp.float32)
        .astype(jnp.bfloat16)
        .reshape(seq_length, local_groups, HD)
    )
    query_blocks = queries.reshape(block_count, block_rows, local_groups, group_size, HD)
    starts = jnp.arange(block_count, dtype=jnp.int32) * block_rows

    def attend_block(packed):
        first_row, q_block = packed
        scores = block_scores(q_block, key_rows, first_row, score_scale)
        row_max = jnp.max(scores, axis=-1, keepdims=True)
        exponent = jnp.exp(scores - row_max)
        row_total = jnp.sum(exponent, axis=-1, keepdims=True)
        weights = (exponent / row_total).astype(jnp.bfloat16)
        head_out = jnp.einsum(
            "grqk,kgd->qgrd", weights, value_rows, preferred_element_type=jnp.float32
        )
        return (head_out.astype(jnp.bfloat16), (row_max + jnp.log(row_total))[..., 0])

    head_blocks, log_totals = lax.map(attend_block, (starts, query_blocks))
    head_rows = head_blocks.reshape(seq_length, local_heads * HD)
    attention = lax.psum_scatter(
        jnp.dot(head_rows, w_out, preferred_element_type=jnp.float32),
        "tensor",
        scatter_dimension=0,
        tiled=True,
    )
    own_inputs = lax.dynamic_slice_in_dim(inputs, first_own, block_len, 0)
    own_inverse = lax.dynamic_slice_in_dim(inverse_one, first_own, block_len, 0)
    middle = own_inputs + attention
    inverse_two, normed_two = norm_forward(middle, gain_moe)
    hidden_two = normed_two.astype(jnp.bfloat16)
    logits = jnp.dot(hidden_two, w_router, preferred_element_type=jnp.float32)
    expert_range = jnp.arange(expert_count, dtype=jnp.int32)
    matches = expert_ids[:, :, None] == expert_range[None, None, :]
    chosen = jnp.sum(jnp.where(matches, logits[:, None, :], 0.0), axis=2)
    gate_weights = jax.nn.softmax(chosen, axis=-1)
    expert_hits = jnp.sum(matches.astype(jnp.int32), axis=1)
    earlier = jnp.cumsum(expert_hits, axis=0) - expert_hits
    slot_of = jnp.sum(jnp.where(matches, earlier[:, None, :], 0), axis=2)
    place = (slot_of * expert_count + expert_ids).reshape(-1)
    token_rows = jnp.broadcast_to(
        hidden_two[:, None, :], (block_len, top_count, model_width)
    ).reshape(block_len * top_count, model_width)
    grad_out = cotangent.astype(jnp.float32)
    gated_grads = (
        (gate_weights[:, :, None] * grad_out[:, None, :])
        .astype(jnp.bfloat16)
        .reshape(block_len * top_count, model_width)
    )
    empty = jnp.zeros((capacity * expert_count, model_width), jnp.bfloat16)
    send_rows = empty.at[place].set(token_rows).reshape(capacity, expert_count, model_width)
    send_grads = empty.at[place].set(gated_grads).reshape(capacity, expert_count, model_width)
    arrived_rows, arrived_grads = (
        lax.all_to_all(send_rows, "expert", split_axis=1, concat_axis=1, tiled=True),
        lax.all_to_all(send_grads, "expert", split_axis=1, concat_axis=1, tiled=True),
    )
    routed = arrived_rows.reshape(capacity, owners, local_experts, model_width)
    grads_in = arrived_grads.reshape(capacity, owners, local_experts, model_width)
    all_rows, all_grads = (
        lax.all_gather(routed, "tensor", axis=0, tiled=True),
        lax.all_gather(grads_in, "tensor", axis=0, tiled=True),
    )
    gate_pre = jnp.einsum("csld,ldf->cslf", all_rows, w_gate, preferred_element_type=jnp.float32)
    up_pre = jnp.einsum("csld,ldf->cslf", all_rows, w_up, preferred_element_type=jnp.float32)
    sigmoid_gate = jax.nn.sigmoid(gate_pre)
    silu_gate = gate_pre * sigmoid_gate
    activation = (silu_gate * up_pre).astype(jnp.bfloat16)
    grad_w_down = jnp.einsum(
        "cslf,csld->lfd", activation, all_grads, preferred_element_type=jnp.float32
    )
    grad_act = jnp.einsum("csld,lfd->cslf", all_grads, w_down, preferred_element_type=jnp.float32)
    grad_gate = (grad_act * up_pre * sigmoid_gate * (1.0 + gate_pre * (1.0 - sigmoid_gate))).astype(
        jnp.bfloat16
    )
    grad_up = (grad_act * silu_gate).astype(jnp.bfloat16)
    grad_w_gate = jnp.einsum(
        "csld,cslf->ldf", all_rows, grad_gate, preferred_element_type=jnp.float32
    )
    grad_w_up = jnp.einsum("csld,cslf->ldf", all_rows, grad_up, preferred_element_type=jnp.float32)
    forward_term = jnp.einsum(
        "cslf,lfd->csld", activation, w_down, preferred_element_type=jnp.float32
    )
    back_term = jnp.einsum("cslf,ldf->csld", grad_gate, w_gate, preferred_element_type=jnp.float32)
    back_term = back_term + jnp.einsum(
        "cslf,ldf->csld", grad_up, w_up, preferred_element_type=jnp.float32
    )
    both_terms = lax.psum_scatter(
        jnp.concatenate([forward_term, back_term], axis=3).astype(jnp.bfloat16),
        "tensor",
        scatter_dimension=0,
        tiled=True,
    )
    returned = both_terms[..., :model_width]
    row_grads = both_terms[..., model_width:]
    returned_home, row_grads_home = (
        lax.all_to_all(
            returned.reshape(capacity, expert_count, model_width),
            "expert",
            split_axis=1,
            concat_axis=1,
            tiled=True,
        ),
        lax.all_to_all(
            row_grads.reshape(capacity, expert_count, model_width),
            "expert",
            split_axis=1,
            concat_axis=1,
            tiled=True,
        ),
    )
    picked = returned_home.reshape(capacity * expert_count, model_width)[place].reshape(
        block_len, top_count, model_width
    )
    mixture = jnp.sum(gate_weights[:, :, None] * picked, axis=1)
    mixed_out = (middle + mixture).astype(jnp.bfloat16)
    grad_gates = jnp.sum(picked * grad_out[:, None, :], axis=2)
    grad_picked = row_grads_home.reshape(capacity * expert_count, model_width)[place].reshape(
        block_len, top_count, model_width
    )
    grad_hidden_disp = jnp.einsum(
        "lk,lkd->ld",
        jnp.ones((block_len, top_count), jnp.bfloat16),
        grad_picked,
        preferred_element_type=jnp.float32,
    )
    grad_chosen = gate_weights * (
        grad_gates - jnp.sum(gate_weights * grad_gates, axis=-1, keepdims=True)
    )
    grad_logits = jnp.sum(jnp.where(matches, grad_chosen[:, :, None], 0.0), axis=1).astype(
        jnp.bfloat16
    )
    grad_router = jnp.einsum(
        "ld,le->de", hidden_two, grad_logits, preferred_element_type=jnp.float32
    )
    grad_hidden_two = grad_hidden_disp + jnp.einsum(
        "le,de->ld", grad_logits, w_router, preferred_element_type=jnp.float32
    )
    grad_normed_two, grad_gain_moe = norm_backward(middle, inverse_two, gain_moe, grad_hidden_two)
    grad_middle = grad_out + grad_normed_two
    grad_attn = grad_middle.astype(jnp.bfloat16)
    grad_attn_all = lax.all_gather(grad_attn, "tensor", axis=0, tiled=True)
    grad_w_out = jnp.einsum(
        "lh,ld->hd", head_rows, grad_attn_all, preferred_element_type=jnp.float32
    )
    grad_heads = jnp.einsum(
        "ld,hd->lh", grad_attn_all, w_out, preferred_element_type=jnp.float32
    ).astype(jnp.bfloat16)
    grad_blocks = grad_heads.reshape(block_count, block_rows, local_groups, group_size, HD)

    def back_block(carried, packed):
        grad_keys, grad_values = carried
        first_row, q_block, g_block, lse_block = packed
        scores = block_scores(q_block, key_rows, first_row, score_scale)
        probability = jnp.exp(scores - lse_block[..., None])
        grad_values = grad_values + jnp.einsum(
            "grqk,qgrd->kgd",
            probability.astype(jnp.bfloat16),
            g_block,
            preferred_element_type=jnp.float32,
        )
        grad_prob = jnp.einsum(
            "qgrd,kgd->grqk", g_block, value_rows, preferred_element_type=jnp.float32
        )
        row_delta = jnp.sum(probability * grad_prob, axis=-1, keepdims=True)
        grad_scores = (probability * (grad_prob - row_delta)).astype(jnp.bfloat16)
        grad_query = (
            jnp.einsum("grqk,kgd->qgrd", grad_scores, key_rows, preferred_element_type=jnp.float32)
            * score_scale
        )
        grad_keys = (
            grad_keys
            + jnp.einsum("grqk,qgrd->kgd", grad_scores, q_block, preferred_element_type=jnp.float32)
            * score_scale
        )
        return ((grad_keys, grad_values), grad_query)

    zero_keys = jnp.zeros((seq_length, local_groups, HD), jnp.float32)
    (grad_keys, grad_values), grad_query_blocks = lax.scan(
        back_block, (zero_keys, zero_keys), (starts, query_blocks, grad_blocks, log_totals)
    )
    grad_query = grad_query_blocks.reshape(seq_length, local_heads, HD)
    grad_query_raw = (
        jax.vjp(rope_heads, query_raw)[1](grad_query)[0]
        .reshape(seq_length, local_heads * HD)
        .astype(jnp.bfloat16)
    )
    grad_key_raw = (
        jax.vjp(rope_heads, key_raw)[1](grad_keys)[0]
        .reshape(seq_length, local_groups * HD)
        .astype(jnp.bfloat16)
    )
    grad_value_raw = grad_values.reshape(seq_length, local_groups * HD).astype(jnp.bfloat16)
    grad_w_query = jnp.einsum(
        "ld,lh->dh", hidden_one, grad_query_raw, preferred_element_type=jnp.float32
    )
    grad_w_key = jnp.einsum(
        "ld,lh->dh", hidden_one, grad_key_raw, preferred_element_type=jnp.float32
    )
    grad_w_value = jnp.einsum(
        "ld,lh->dh", hidden_one, grad_value_raw, preferred_element_type=jnp.float32
    )
    term = jnp.einsum("lh,dh->ld", grad_query_raw, w_query, preferred_element_type=jnp.float32)
    term = term + jnp.einsum("lh,dh->ld", grad_key_raw, w_key, preferred_element_type=jnp.float32)
    grad_hidden_one = lax.psum_scatter(
        (
            term
            + jnp.einsum("lh,dh->ld", grad_value_raw, w_value, preferred_element_type=jnp.float32)
        ).astype(jnp.bfloat16),
        "tensor",
        scatter_dimension=0,
        tiled=True,
    ).astype(jnp.float32)
    grad_normed_one, grad_gain_attn = norm_backward(
        own_inputs, own_inverse, gain_attn, grad_hidden_one
    )
    grad_tokens = grad_middle + grad_normed_one
    attn_sums = lax.psum((grad_w_query, grad_w_key, grad_w_value, grad_w_out), "expert")
    small_sums = lax.psum((grad_gain_attn, grad_gain_moe, grad_router), ("expert", "tensor"))
    return (
        mixed_out,
        grad_tokens,
        small_sums[0],
        attn_sums[0],
        attn_sums[1],
        attn_sums[2],
        attn_sums[3],
        small_sums[1],
        small_sums[2],
        grad_w_gate,
        grad_w_up,
        grad_w_down,
    )


ROWS_ROWS = (((1,), (1,)), ((), ()))
def dot_nt(left, right):
    return lax.dot_general(left, right, ROWS_ROWS, preferred_element_type=jnp.float32)


def dot_nn(left, right):
    return jnp.dot(left, right, preferred_element_type=jnp.float32)


def expert_kernel(places, top_count, *refs):
    row_places, grad_places = places
    given = 1 + max(place[0] for place in row_places + grad_places)
    numbers_ref, router_ref, gate_ref, up_ref, down_ref = refs[given : given + 5]
    outs = refs[given + 5 : given + 14]
    mixed_refs, back_refs, sums_ref = outs[:2], outs[2:4], outs[4]
    rows_s, grads_s, ids_s, x_s, y_s, back_s, out_s = refs[given + 14 : given + 21]
    pick_s, place_s, gates_s, sums_s, gated_s, side_s = refs[given + 21 : given + 27]
    both_s, down_s, sems, weight_sems, out_sems, kept_sems = refs[given + 27 :]
    pairs, wide, _ = pick_s.shape
    experts = x_s.shape[0]
    hidden = down_s.shape[1]
    cap = wide // experts
    tokens_in, width = rows_s.shape[1:]
    block_len = tokens_in // 2
    narrow = jnp.bfloat16

    def copies(pair):
        out = []
        for half in range(2):
            target = pl.ds(half * block_len, block_len)
            at = 2 * pair + half
            array, row, column = row_places[at]
            rows = refs[array].at[pl.ds(row, block_len), pl.ds(column, width)]
            array, row, column = grad_places[at]
            block = refs[array].at[pl.ds(row, block_len)]
            grads = block.at[:, pl.ds(column, width)]
            ids = block.at[:, pl.ds(column + width, LANES)]
            for k, (source, scratch) in enumerate(
                ((rows, rows_s), (grads, grads_s), (ids, ids_s))
            ):
                out.append(
                    pltpu.make_async_copy(source, scratch.at[pair, target], sems.at[k, at])
                )
        return out

    def weight_copies(expert, slot):
        sides = [both_s.at[slot, :, pl.ds(k * hidden, hidden)] for k in range(2)]
        return [
            pltpu.make_async_copy(gate_ref.at[expert], sides[0], weight_sems.at[0, slot]),
            pltpu.make_async_copy(up_ref.at[expert], sides[1], weight_sems.at[1, slot]),
            pltpu.make_async_copy(down_ref.at[expert], down_s.at[slot], weight_sems.at[2, slot]),
        ]

    def result_copies(pair):
        half = pairs // 2
        place = pl.ds((pair % half) * tokens_in, tokens_in)
        sides = (rows_s, mixed_refs), (grads_s, back_refs)
        return [
            pltpu.make_async_copy(
                source.at[pair], targets[pair // half].at[place], out_sems.at[k, pair]
            )
            for k, (source, targets) in enumerate(sides)
        ]

    kept_copies = [
        pltpu.make_async_copy(source, target, kept_sems.at[k])
        for k, (source, target) in enumerate(zip((x_s, y_s, gated_s, side_s), outs[5:9]))
    ]

    for pair in range(pairs):
        for copy in copies(pair):
            copy.start()
    for slot in range(WEIGHT_SLOTS):
        for copy in weight_copies(slot, slot):
            copy.start()

    earlier = lax.broadcasted_iota(jnp.int32, (tokens_in, tokens_in), 0)
    later = lax.broadcasted_iota(jnp.int32, (tokens_in, tokens_in), 1)
    before = jnp.where(earlier < later, 1.0, 0.0).astype(narrow)

    for pair in range(pairs):
        for copy in copies(pair):
            copy.wait()
        rows_in = rows_s[pair]
        logits = dot_nt(router_ref[...], rows_in)
        ids = ids_s[pair].astype(jnp.float32).T
        named = jnp.zeros(logits.shape, jnp.float32)
        for k in range(top_count):
            named = jnp.where(ids[k : k + 1, :] == numbers_ref[:, :1], 1.0, named)
        hits = named[:experts]
        slots = jnp.where(hits > 0.0, dot_nn(hits.astype(narrow), before), -1.0)
        slots = slots.astype(jnp.int32)
        logits = jnp.where(named > 0.0, logits, masked)
        weights = jnp.exp(logits - jnp.max(logits, axis=0, keepdims=True)) * named
        gates = weights / jnp.sum(weights, axis=0, keepdims=True)
        ranks = lax.broadcasted_iota(jnp.int32, (cap, tokens_in), 0)
        place = pl.ds(pair * cap, cap)
        picks = []
        for expert in range(experts):
            pick = ranks == slots[expert : expert + 1, :]
            row_gates = jnp.sum(
                jnp.where(pick, gates[expert : expert + 1, :], 0.0), axis=1, keepdims=True
            )
            gates_s[expert, place, :] = jnp.broadcast_to(row_gates, (cap, LANES))
            picks.append(jnp.where(pick, 1.0, 0.0))
        pick_all = jnp.concatenate(picks, axis=0)
        pick_low = pick_all.astype(narrow)
        pick_s[pair] = pick_low
        place_s[pair] = pick_all.T.astype(narrow)
        for source, target in ((rows_in, x_s), (grads_s[pair], y_s)):
            spread = dot_nn(pick_low, source).astype(narrow)
            for expert in range(experts):
                target[expert, place, :] = spread[expert * cap : (expert + 1) * cap]

    kept_copies[0].start()
    kept_copies[1].start()

    def expert_step(expert, carried):
        slot = lax.rem(expert, WEIGHT_SLOTS)
        for copy in weight_copies(expert, slot):
            copy.wait()
        both = dot_nn(x_s[expert], both_s[slot])
        gate_pre, up_pre = both[:, :hidden], both[:, hidden:]
        plain = dot_nt(y_s[expert], down_s[slot])
        sigmoid_gate = jax.nn.sigmoid(gate_pre)
        silu_gate = gate_pre * sigmoid_gate
        activation = silu_gate * up_pre
        row_gates = gates_s[expert][:, :1]
        sums = jnp.sum(activation * plain, axis=1, keepdims=True)
        sums_s[expert] = jnp.broadcast_to(sums, sums_s.shape[1:])
        grad_act = row_gates * plain
        gated = (row_gates * activation).astype(narrow)
        slope = sigmoid_gate * (1.0 + gate_pre * (1.0 - sigmoid_gate))
        grad_gate = (grad_act * up_pre * slope).astype(narrow)
        grad_up = (grad_act * silu_gate).astype(narrow)
        grad_both = jnp.concatenate([grad_gate, grad_up], axis=1)
        gated_s[expert] = gated
        side_s[expert] = grad_both
        out_s[expert] = dot_nn(gated, down_s[slot]).astype(narrow)
        back_s[expert] = dot_nt(grad_both, both_s[slot]).astype(narrow)

        @pl.when(expert + WEIGHT_SLOTS < experts)
        def _():
            for copy in weight_copies(expert + WEIGHT_SLOTS, slot):
                copy.start()

        return carried

    lax.fori_loop(0, experts, expert_step, 0)
    kept_copies[2].start()
    kept_copies[3].start()

    for pair in range(pairs):
        sides = pl.ds(pair * cap, cap)
        for source, target in ((out_s, rows_s), (back_s, grads_s)):
            stacked = jnp.concatenate(
                [source[expert, sides, :] for expert in range(experts)], axis=0
            )
            target[pair] = dot_nn(place_s[pair], stacked).astype(narrow)
        for copy in result_copies(pair):
            copy.start()
        pick = pick_s[pair].astype(jnp.float32)
        sums = []
        for expert in range(experts):
            column = sums_s[expert, sides, :][:, :1]
            part = pick[expert * cap : (expert + 1) * cap] * column
            sums.append(jnp.sum(part, axis=0, keepdims=True))
        sums_ref[pair] = jnp.concatenate(sums, axis=0)

    for copy in kept_copies:
        copy.wait()
    for pair in range(pairs):
        for copy in result_copies(pair):
            copy.wait()


def expert_chunk(arrays, places, numbers, router, w_gate, w_up, w_down, tokens_in, top_count, cap):
    experts, width, hidden = w_gate.shape
    pairs = BLOCKS // 2
    rows = pairs * cap
    narrow, wide = jnp.bfloat16, jnp.float32
    shape = jax.ShapeDtypeStruct
    anywhere = pl.BlockSpec(memory_space=pl.ANY)
    inside = pl.BlockSpec(memory_space=pltpu.VMEM)
    half_shape = shape((pairs // 2 * tokens_in, width), narrow)
    whole_rows = (experts, rows, width)
    return pl.pallas_call(
        functools.partial(expert_kernel, places, top_count),
        in_specs=[anywhere] * len(arrays) + [inside] * 2 + [anywhere] * 3,
        out_specs=[anywhere] * 4 + [inside] + [anywhere] * 4,
        out_shape=[half_shape] * 4
        + [
            shape((pairs, experts, tokens_in), wide),
            shape(whole_rows, narrow),
            shape(whole_rows, narrow),
            shape((experts, rows, hidden), narrow),
            shape((experts, rows, 2 * hidden), narrow),
        ],
        scratch_shapes=[pltpu.VMEM((pairs, tokens_in, width), narrow)] * 2
        + [pltpu.VMEM((pairs, tokens_in, LANES), narrow)]
        + [pltpu.VMEM(whole_rows, narrow)] * 4
        + [
            pltpu.VMEM((pairs, experts * cap, tokens_in), narrow),
            pltpu.VMEM((pairs, tokens_in, experts * cap), narrow),
            pltpu.VMEM((experts, rows, LANES), wide),
            pltpu.VMEM((experts, rows, LANES), wide),
            pltpu.VMEM((experts, rows, hidden), narrow),
            pltpu.VMEM((experts, rows, 2 * hidden), narrow),
            pltpu.VMEM((WEIGHT_SLOTS, width, 2 * hidden), narrow),
            pltpu.VMEM((WEIGHT_SLOTS, hidden, width), narrow),
            pltpu.SemaphoreType.DMA((3, BLOCKS)),
            pltpu.SemaphoreType.DMA((3, WEIGHT_SLOTS)),
            pltpu.SemaphoreType.DMA((2, pairs)),
            pltpu.SemaphoreType.DMA((4,)),
        ],
        compiler_params=pltpu.CompilerParams(vmem_limit_bytes=60 << 20),
        cost_estimate=pl.CostEstimate(
            flops=24 * experts * rows * width * hidden,
            bytes_accessed=6 * experts * width * hidden + 4 * experts * rows * width,
            transcendentals=experts * rows * hidden,
        ),
    )(*arrays, numbers, router, w_gate, w_up, w_down)


def weight_kernel(parts, given, *refs):
    ins, (gate_ref, up_ref, down_ref) = refs[: 4 * parts], refs[4 * parts + given :]
    rows, grads, gated, both = [
        jnp.concatenate([ref[0] for ref in ins[k * parts : (k + 1) * parts]], axis=0)
        for k in range(4)
    ]
    turn = (((0,), (0,)), ((), ()))
    hidden = gated.shape[1]
    down_ref[0] = lax.dot_general(gated, grads, turn, preferred_element_type=jnp.float32)
    sides = lax.dot_general(rows, both, turn, preferred_element_type=jnp.float32)
    gate_ref[0] = sides[:, :hidden]
    up_ref[0] = sides[:, hidden:]


def weight_grads(kept, begin, count, partial):
    parts = len(kept)
    experts, rows, width = kept[0][0].shape
    hidden = kept[0][2].shape[2]
    operands = [part[k] for k in range(4) for part in kept]
    shape = jax.ShapeDtypeStruct

    def spec(rows, columns):
        return pl.BlockSpec((1, rows, columns), lambda i: (i + begin, 0, 0))

    return pl.pallas_call(
        functools.partial(weight_kernel, parts, len(partial)),
        grid=(count,),
        in_specs=[spec(rows, operand.shape[2]) for operand in operands]
        + [pl.BlockSpec(memory_space=pl.ANY)] * len(partial),
        out_specs=[spec(width, hidden), spec(width, hidden), spec(hidden, width)],
        out_shape=[
            shape((experts, width, hidden), jnp.float32),
            shape((experts, width, hidden), jnp.float32),
            shape((experts, hidden, width), jnp.float32),
        ],
        input_output_aliases={len(operands) + k: k for k in range(len(partial))},
        compiler_params=pltpu.CompilerParams(vmem_limit_bytes=56 << 20),
        cost_estimate=pl.CostEstimate(
            flops=6 * parts * count * rows * width * hidden,
            bytes_accessed=count * (parts * rows * (4 * width + 6 * hidden) + 12 * width * hidden),
            transcendentals=0,
        ),
    )(*operands, *partial)


def gathered_layer(
    tokens,
    gain_attn,
    w_query,
    w_key,
    w_value,
    w_out,
    gain_moe,
    w_router,
    w_gate,
    w_up,
    w_down,
    expert_ids,
    cotangent,
):
    seq_length, model_width = tokens.shape
    block_len, top_count = expert_ids.shape
    expert_count = w_router.shape[1]
    local_experts = w_gate.shape[0]
    local_heads = w_query.shape[1] // HD
    quarters = lax.axis_size("tensor")
    device_count = quarters * lax.axis_size("expert")
    quarter = lax.axis_index("tensor").astype(jnp.uint32)
    device = lax.axis_index(BOTH).astype(jnp.uint32)
    first_expert = lax.axis_index("expert") * local_experts
    pair_cap = 2 * (3 * block_len * top_count // (2 * expert_count))
    score_scale = HD ** (-0.5)
    narrow, wide = jnp.bfloat16, jnp.float32

    def swap(value, even, odd=None):
        odd = even if odd is None else odd
        perm = [(i, i ^ (odd if i & 1 else even)) for i in range(device_count)]
        return lax.ppermute(value, BOTH, perm)

    def near(value):
        return swap(value, ACROSS, ASIDE)

    def far(value):
        return swap(value, ASIDE, ACROSS)

    def core(value):
        return swap(value, CORE)

    def add(left, right):
        return (left.astype(wide) + right.astype(wide)).astype(narrow)

    live = {}

    def sync():
        keys = list(live)
        values = lax.optimization_barrier([live[key] for key in keys])
        live.update(zip(keys, values))

    def gather_near(name, plane):
        live[name, plane, 1] = near(live[name, plane, 0])
        live[name, plane, 2] = far(live[name, plane, 0])

    def gather_far(name, plane):
        live[name, plane, 3] = far(live[name, plane, 1])

    def gather_across(name, plane):
        live[name, plane, 3] = swap(live[name, plane, 0], ACROSS | ASIDE)

    def join_core(name, plane, *slots):
        blocks = [live[name, plane, slot] for slot in slots]
        live[name, plane, (OTHER,) + slots] = jnp.concatenate(blocks, axis=0)

    def send_core(name, plane, *slots):
        live[name, plane, (OTHER,) + slots] = core(live[name, plane, (OTHER,) + slots])

    def gather_core(name, plane, *slots):
        join_core(name, plane, *slots)
        send_core(name, plane, *slots)

    def blocks_of(name, plane):
        found = {}
        for key in list(live):
            if isinstance(key, tuple) and key[:2] == (name, plane):
                slots = key[2]
                array = live.pop(key)
                if isinstance(slots, tuple):
                    for i, slot in enumerate(slots[1:]):
                        found[4 + slot] = (array, i * block_len)
                else:
                    found[slots] = (array, 0)
        return [found[slot] for slot in range(BLOCKS)]

    def reduce_core(name, plane):
        live[name, plane, OTHER] = core(live.pop((name, plane, AWAY)))

    def add_far(name, plane):
        kept = live[name, plane, NEAR].reshape(4, block_len, model_width)
        got = live[name, plane, OTHER].reshape(4, block_len, model_width)
        live[name, plane, FAR] = add(kept[2:], got[2:])

    def send_far(name, plane):
        live[name, plane, FAR] = far(live[name, plane, FAR])

    def reduce_far(name, plane):
        add_far(name, plane)
        send_far(name, plane)

    def add_near(name, plane):
        kept = live.pop((name, plane, NEAR)).reshape(4, block_len, model_width)
        got = live.pop((name, plane, OTHER)).reshape(4, block_len, model_width)
        back = live.pop((name, plane, FAR))
        sums = [
            kept[i].astype(wide) + got[i].astype(wide) + back[i].astype(wide) for i in range(2)
        ]
        live[name, plane, OWN], live[name, plane, SIDE] = [part.astype(narrow) for part in sums]

    def send_near(name, plane):
        live[name, plane, SIDE] = near(live[name, plane, SIDE])

    def reduce_near(name, plane):
        add_near(name, plane)
        send_near(name, plane)

    def reduced(name, plane):
        return add(live.pop((name, plane, OWN)), live.pop((name, plane, SIDE)))

    def bit(mask):
        return (device // mask) % 2

    odd_core = bit(CORE)
    weight_hops = ((ASIDE, PLANE_NEXT), (PLANE_NEXT, ASIDE), (PLANE_FAR, PLANE_FAR))
    small_hops = tuple((mask, mask) for mask in (CORE, ACROSS, ASIDE, PLANE_NEXT, PLANE_FAR))

    def joined(own, got, side):
        count = own.shape[0]
        both = jnp.zeros((2 * count,) + own.shape[1:], own.dtype)
        both = lax.dynamic_update_slice_in_dim(both, own, side * count, 0)
        return lax.dynamic_update_slice_in_dim(both, got, (1 - side) * count, 0)

    def sum_step(name, step, hops=weight_hops, sent_as=narrow):
        count = len(hops)
        sides = [jnp.where(odd_core == 0, bit(even), bit(odd)) for even, odd in hops]
        if step == 0:
            kept = live.pop((name, FULL))
        elif step <= count:
            kept = live.pop((name, KEPT)) + live.pop((name, GOT)).astype(wide)
        else:
            kept = joined(live.pop((name, KEPT)), live.pop((name, GOT)), sides[2 * count - step])
        if step < count:
            half = kept.shape[0] // 2
            side = sides[step]
            live[name, KEPT] = lax.dynamic_slice_in_dim(kept, side * half, half, 0)
            sent = lax.dynamic_slice_in_dim(kept, (1 - side) * half, half, 0)
            live[name, GOT] = swap(sent.astype(sent_as), *hops[step])
        else:
            kept = kept.astype(sent_as)
            live[name, KEPT] = kept
            live[name, GOT] = swap(kept, *hops[2 * count - 1 - step])

    def summed(name, hops=weight_hops):
        even, odd = hops[0]
        side = jnp.where(odd_core == 0, bit(even), bit(odd))
        return joined(live.pop((name, KEPT)), live.pop((name, GOT)), side).astype(wide)

    own, nxt, far_plane, last = PLANES

    named_ids = jnp.pad(expert_ids.astype(narrow), ((0, 0), (0, LANES - top_count)))
    live[G, own, 0] = jnp.concatenate([cotangent, named_ids], axis=1)
    half_block = block_len // 2
    live[G, nxt, 0] = swap(live[G, own, 0], nxt)
    live[G, far_plane, 0] = [swap(live[G, own, 0][:half_block], far_plane)]
    gather_near(G, own)

    by_block = tokens.reshape(quarters, block_len, model_width)
    inputs = jnp.concatenate(
        [lax.dynamic_slice_in_dim(by_block, quarter ^ r, 1, 0)[0] for r in range(quarters)], axis=0
    )
    inputs = lax.optimization_barrier(inputs)
    order = quarter.astype(jnp.int32) ^ jnp.arange(quarters, dtype=jnp.int32)
    positions = (order[:, None] * block_len + jnp.arange(block_len, dtype=jnp.int32)).reshape(-1)
    inverse_one, normed_one = norm_forward(inputs.astype(wide), gain_attn)
    hidden_one = normed_one.astype(narrow)
    frequency = jnp.exp(
        -jnp.log(theta_base) * jnp.arange(HD // 2, dtype=jnp.float32) * (2.0 / HD)
    )
    angles = positions.astype(wide)[:, None] * frequency[None, :]
    cosine_table, sine_table = (jnp.cos(angles)[:, None, :], jnp.sin(angles)[:, None, :])

    def project(weights):
        return jnp.dot(hidden_one, weights, preferred_element_type=wide).reshape(
            seq_length, local_heads, HD
        )

    live[QUERIES] = rotate(project(w_query), cosine_table, sine_table).astype(narrow)
    live[KEYS] = rotate(project(w_key), cosine_table, sine_table).astype(narrow)
    live[VALUES] = project(w_value).astype(narrow)
    sync()

    gather_far(G, own)
    gather_near(G, nxt)
    live[G, far_plane, 0] = live[G, far_plane, 0] + [
        swap(live[G, own, 0][half_block:], far_plane)
    ]
    allowed = positions[:, None] >= positions[None, :]

    def masked_scores():
        scores = jnp.einsum(
            "qhd,khd->hqk", live[QUERIES], live[KEYS], preferred_element_type=wide
        )
        return jnp.where(allowed, scores * score_scale, masked)

    scores = masked_scores()
    row_max = jnp.max(scores, axis=-1, keepdims=True)
    exponent = jnp.exp(scores - row_max)
    row_total = jnp.sum(exponent, axis=-1, keepdims=True)
    weights = (exponent / row_total).astype(narrow)
    head_out = jnp.einsum("hqk,khd->qhd", weights, live[VALUES], preferred_element_type=wide)
    live[TOTALS] = row_max + jnp.log(row_total)
    live[HEADS] = head_out.astype(narrow).reshape(seq_length, local_heads * HD)

    def split_quarters(full):
        parts = full.reshape(quarters, block_len, model_width)
        live[KEPT] = [parts[0], parts[2]]
        live[SENT] = jnp.stack([parts[1], parts[3]]).astype(narrow)

    split_quarters(jnp.dot(live[HEADS], w_out, preferred_element_type=wide))
    sync()

    expert_range = jnp.arange(expert_count, dtype=jnp.int32)
    rolled = (first_expert + expert_range) % expert_count
    live[ROUTER] = jnp.take(w_router.T, rolled, axis=0)
    live[NAMED] = jnp.broadcast_to(rolled.astype(wide)[:, None], (expert_count, LANES))
    live[SENT] = core(live[SENT])
    gather_far(G, nxt)
    live[G, far_plane, 0] = jnp.concatenate(live[G, far_plane, 0], axis=0)
    sync()

    def cross_quarters():
        kept, sent = live.pop(KEPT), live.pop(SENT).astype(wide)
        live[KEPT] = kept[0] + sent[0]
        live[SENT] = swap((kept[1] + sent[1]).astype(narrow), ACROSS)

    def quarter_sum():
        return live.pop(KEPT) + live.pop(SENT).astype(wide)

    cross_quarters()
    live[G, last, 0] = swap(live[G, far_plane, 0], nxt)
    sync()

    own_inputs = inputs[:block_len].astype(wide)
    own_inverse = inverse_one[:block_len]
    middle = own_inputs + quarter_sum()
    inverse_two, normed_two = norm_forward(middle, gain_moe)
    hidden_two = normed_two.astype(narrow)
    live[H, own, 0] = hidden_two

    gather_near(H, own)
    live[H, nxt, 0] = swap(hidden_two, nxt)
    logits = jnp.dot(hidden_two, w_router, preferred_element_type=wide)
    expert_range = jnp.arange(expert_count, dtype=jnp.int32)
    matches = expert_ids[:, :, None] == expert_range[None, None, :]
    chosen = jnp.sum(jnp.where(matches, logits[:, None, :], 0.0), axis=2)
    gate_weights = jax.nn.softmax(chosen, axis=-1)
    sync()

    gather_far(H, own)
    gather_near(H, nxt)
    hidden_two = live[H, own, 0]
    gather_core(G, own, 0, 1, 2, 3)
    live[H, last, 0] = [swap(hidden_two[:half_block], last)]
    sync()

    gather_far(H, nxt)
    gather_core(H, own, 0, 1, 2, 3)
    gather_core(G, nxt, 0, 1, 2, 3)
    hidden_two = live[H, own, 0]
    live[H, last, 0] = live[H, last, 0] + [swap(hidden_two[half_block:], last)]
    sync()

    def join_pair(plane):
        rows, grads = [live.pop((name, plane, 0)) for name in (H, G)]
        if isinstance(rows, list):
            rows = jnp.concatenate(rows, axis=0)
        live[PAIR, plane, 0] = jnp.concatenate([rows, grads], axis=1)

    def experts(plane):
        if (PAIR, plane, 0) in live:
            rows = blocks_of(PAIR, plane)
            grads, column = rows, model_width
        else:
            rows, grads, column = blocks_of(H, plane), blocks_of(G, plane), 0
        arrays = []
        for array, _ in rows + grads:
            if not any(array is other for other in arrays):
                arrays.append(array)

        def placed(blocks, column):
            indices = [[array is other for other in arrays].index(True) for array, _ in blocks]
            return [(index, row, column) for index, (_, row) in zip(indices, blocks)]

        done = expert_chunk(
            arrays,
            (placed(rows, 0), placed(grads, column)),
            live[NAMED],
            live[ROUTER],
            w_gate,
            w_up,
            w_down,
            2 * block_len,
            top_count,
            pair_cap,
        )
        live[M, plane, NEAR], live[M, plane, AWAY] = done[:2]
        live[R, plane, NEAR], live[R, plane, AWAY] = done[2:4]
        live[SUMS, plane] = done[4]
        live[KEPT, plane] = done[5:]

    gather_core(H, nxt, 0, 1, 2, 3)
    join_pair(last)
    gather_near(PAIR, last)
    gather_core(PAIR, last, 0)
    live[H, far_plane, 0] = swap(live[H, own, 0], far_plane)
    experts(own)
    sync()

    gather_far(PAIR, last)
    gather_core(PAIR, last, 1, 2)
    join_pair(far_plane)
    gather_near(PAIR, far_plane)
    reduce_core(R, own)
    experts(nxt)
    sync()
    gather_core(PAIR, last, 3)
    join_core(PAIR, far_plane, 0, 1, 2)
    add_far(R, own)
    sync()

    gather_far(PAIR, far_plane)
    send_core(PAIR, far_plane, 0, 1, 2)
    send_far(R, own)
    reduce_core(R, nxt)
    reduce_core(M, own)
    experts(last)
    sync()
    gather_core(PAIR, far_plane, 3)
    reduce_core(R, last)
    add_near(R, own)
    add_far(R, nxt)
    sync()

    send_near(R, own)
    send_far(R, nxt)
    reduce_far(R, last)
    reduce_core(M, nxt)
    experts(far_plane)
    sync()

    part_experts = local_experts // 4

    def some_weight_grads(part):
        kept = [live[KEPT, plane] for plane in PLANES]
        live[EXPERTS] = weight_grads(kept, part * part_experts, part_experts, live.get(EXPERTS, []))

    reduce_core(R, far_plane)
    sums = jnp.stack([live.pop((SUMS, plane)) for plane in PLANES])
    sums = sums.reshape(len(PLANES), -1, local_experts, 2, block_len).transpose(0, 1, 3, 2, 4)
    sums = sums.reshape(len(PLANES), BLOCKS, local_experts, block_len)
    live[GATES] = [sums[:, :4], core(sums[:, 4:])]
    reduce_core(M, last)
    add_near(R, last)
    sync()

    reduce_far(R, far_plane)
    send_near(R, last)
    add_near(R, nxt)
    live[HOME] = reduced(R, own)
    sums = live[GATES][0] + live[GATES][1]
    crossed = jnp.stack([sums[:, 0], sums[:, 2], sums[:, 1], sums[:, 3]], axis=1)
    sums = jnp.where(odd_core == 0, sums, crossed)
    sums = sums[:, ::2] + swap(sums[:, 1::2], ACROSS)
    live[GATES] = [sums[:, 0], swap(sums[:, 1], ASIDE)]
    sync()

    live[RELAY] = swap(reduced(R, last), nxt)
    reduce_near(R, far_plane)
    sums = jnp.stack(live[GATES], axis=1)
    live[GATES] = [sums[::2], swap(sums[1::2], nxt)]
    send_near(R, nxt)
    add_far(M, nxt)
    add_far(M, last)
    sync()

    live[RELAY] = swap(add(reduced(R, far_plane), live[RELAY]), far_plane)
    live[SIDE] = swap(reduced(R, nxt), nxt)
    send_far(M, nxt)
    send_far(M, last)
    reduce_core(M, far_plane)
    sums = jnp.stack(live.pop(GATES), axis=1)
    sums = jnp.concatenate([sums[0], swap(sums[1], far_plane)], axis=0)
    sums = sums.reshape(-1, local_experts, block_len)
    owner = lax.axis_index("expert").astype(jnp.uint32)
    sums = [lax.dynamic_slice_in_dim(sums, owner ^ r, 1, 0)[0] for r in range(sums.shape[0])]
    own_sums = jnp.concatenate(sums, axis=0).T
    grad_gates = jnp.sum(jnp.where(matches, own_sums[:, None, :], 0.0), axis=2)
    grad_chosen = gate_weights * (
        grad_gates - jnp.sum(gate_weights * grad_gates, axis=-1, keepdims=True)
    )
    grad_logits = jnp.sum(jnp.where(matches, grad_chosen[:, :, None], 0.0), axis=1).astype(narrow)
    grad_router = jnp.einsum("ld,le->de", hidden_two, grad_logits, preferred_element_type=wide)
    live[GATES] = jnp.einsum("le,de->ld", grad_logits, w_router, preferred_element_type=wide)
    live[SMALL] = grad_router
    sync()

    grad_hidden_two = live.pop(HOME).astype(wide) + live.pop(RELAY).astype(wide)
    grad_hidden_two = grad_hidden_two + live.pop(SIDE).astype(wide) + live.pop(GATES)
    grad_out = cotangent.astype(wide)
    grad_normed_two, grad_gain_moe = norm_backward(middle, inverse_two, gain_moe, grad_hidden_two)
    grad_middle = grad_out + grad_normed_two
    grad_attn = grad_middle.astype(narrow)

    small = jnp.concatenate([live.pop(SMALL), grad_gain_moe[:, None]], axis=1)
    live[SMALL, FULL] = small.reshape(device_count, -1, small.shape[1])
    small_step = functools.partial(sum_step, SMALL, hops=small_hops, sent_as=wide)

    live[ATTN] = [grad_attn, core(grad_attn), swap(grad_attn, ACROSS)]
    small_step(0)
    add_near(M, nxt)
    add_near(M, last)
    sync()
    live[ATTN] = live[ATTN] + [core(live[ATTN][2])]
    sync()

    grad_attn_all = jnp.concatenate(live.pop(ATTN), axis=0)
    live[OUT, FULL] = jnp.einsum(
        "lh,ld->hd", live[HEADS], grad_attn_all, preferred_element_type=wide
    )
    grad_heads = (
        jnp.einsum("ld,hd->lh", grad_attn_all, w_out, preferred_element_type=wide)
        .astype(narrow)
        .reshape(seq_length, local_heads, HD)
    )
    live[RAW] = grad_heads
    sync()

    grad_heads = live.pop(RAW)
    sum_step(OUT, 0)
    small_step(1)
    send_near(M, nxt)
    probability = jnp.exp(masked_scores() - live[TOTALS])
    grad_values = jnp.einsum(
        "hqk,qhd->khd", probability.astype(narrow), grad_heads, preferred_element_type=wide
    )
    grad_prob = jnp.einsum("qhd,khd->hqk", grad_heads, live[VALUES], preferred_element_type=wide)
    row_delta = jnp.sum(probability * grad_prob, axis=-1, keepdims=True)
    grad_scores = (probability * (grad_prob - row_delta)).astype(narrow)
    grad_query = score_scale * jnp.einsum(
        "hqk,khd->qhd", grad_scores, live[KEYS], preferred_element_type=wide
    )
    grad_keys = score_scale * jnp.einsum(
        "hqk,qhd->khd", grad_scores, live[QUERIES], preferred_element_type=wide
    )

    def flat(source):
        return source.astype(narrow).reshape(seq_length, local_heads * HD)

    live[RAW] = [
        flat(rotate(grad_query, cosine_table, -sine_table)),
        flat(rotate(grad_keys, cosine_table, -sine_table)),
        flat(grad_values),
    ]
    flying = live.pop((OUT, GOT))
    sync()
    live[OUT, GOT] = flying

    def back(grad_raw, weights):
        return jnp.einsum("lh,dh->ld", grad_raw, weights, preferred_element_type=wide)

    raw = live.pop(RAW)
    partial = back(raw[0], w_query) + back(raw[1], w_key) + back(raw[2], w_value)
    split_quarters(partial)
    live[GAIN] = partial
    live[IN, FULL] = jnp.einsum(
        "ld,lh->dh", hidden_one, jnp.concatenate(raw, axis=1), preferred_element_type=wide
    )
    sum_step(OUT, 1)
    small_step(2)
    live[MIXED] = swap(reduced(M, nxt), nxt)
    sync()

    live[SENT] = core(live[SENT])
    sum_step(IN, 0)
    sum_step(OUT, 2)
    some_weight_grads(0)
    gain = jnp.sum(live.pop(GAIN) * inputs.astype(wide) * inverse_one, axis=0)
    live[GAIN] = [gain[None], jnp.zeros_like(gain)[None]]

    def gain_step(step):
        live[GAIN] = [live[GAIN][0] + live[GAIN][1]]
        live[GAIN] = live[GAIN] + [swap(live[GAIN][0], *small_hops[step])]

    small_step(3)
    gain_step(0)
    add_far(M, far_plane)
    add_far(M, own)
    sync()

    sum_step(IN, 1)
    cross_quarters()
    sum_step(OUT, 3)
    small_step(4)
    gain_step(1)
    some_weight_grads(1)
    sync()

    sum_step(IN, 2)
    own_grad = quarter_sum()
    grad_normed_one = norm_backward(own_inputs, own_inverse, gain_attn, own_grad)[0]
    live[TOKENS] = grad_middle + grad_normed_one
    sum_step(OUT, 4)
    small_step(5)
    send_near(M, last)
    send_far(M, far_plane)
    some_weight_grads(2)
    sync()

    sum_step(IN, 3)
    sum_step(OUT, 5)
    small_step(6)
    live[RELAY] = swap(reduced(M, last), nxt)
    reduce_near(M, far_plane)
    some_weight_grads(3)
    sync()
    for plane in PLANES:
        live.pop((KEPT, plane))

    sum_step(IN, 4)
    live[OUT] = summed(OUT)
    live[RELAY] = swap(add(reduced(M, far_plane), live[RELAY]), far_plane)
    send_far(M, own)
    small_step(7)
    small_step(8)
    gain_step(2)
    sync()

    columns = local_heads * HD
    sum_step(IN, 5)
    small_step(9)
    gain_step(3)
    gain_step(4)
    reduce_near(M, own)
    live[MIXED] = middle + live.pop(MIXED).astype(wide) + live.pop(RELAY).astype(wide)
    even, odd = weight_hops[0]
    side = jnp.where(odd_core == 0, bit(even), bit(odd))
    half = live[IN, KEPT].shape[0]

    def put(whole, part, index, at):
        part = part[:, index * columns : (index + 1) * columns].astype(wide)
        return lax.dynamic_update_slice_in_dim(whole, part, at * half, 0)

    empty = jnp.zeros((2 * half, columns), wide)
    live[RAW] = [put(empty, live[IN, KEPT], index, side) for index in range(3)]
    sync()
    mixed_out = (live.pop(MIXED) + reduced(M, own).astype(wide)).astype(narrow)
    grads_in = [put(whole, live[IN, GOT], i, 1 - side) for i, whole in enumerate(live[RAW])]
    small = summed(SMALL, small_hops).reshape(model_width, -1)

    return (
        mixed_out,
        live[TOKENS],
        (live[GAIN][0] + live[GAIN][1])[0],
        *grads_in,
        live[OUT],
        small[:, expert_count],
        small[:, :expert_count],
        *live[EXPERTS],
    )


def on_device(*operands):
    tokens, w_router, w_gate, expert_ids = operands[0], operands[7], operands[8], operands[11]
    owners, quarters = lax.axis_size("expert"), lax.axis_size("tensor")
    block_len, top_count = expert_ids.shape
    capacity = 3 * block_len * top_count // (2 * w_router.shape[1])
    buffer_rows = capacity * quarters * owners * w_gate.shape[0]
    gathers = owners * tokens.shape[0] <= buffer_rows and (owners, quarters) == (8, 4)
    return (gathered_layer if gathers else routed_layer)(*operands)


def solution(mesh):
    return jax.shard_map(
        on_device,
        mesh=mesh,
        in_specs=(
            P("expert", None),
            P(),
            P(None, "tensor"),
            P(None, "tensor"),
            P(None, "tensor"),
            P("tensor", None),
            P(),
            P(),
            P("expert", None, "tensor"),
            P("expert", None, "tensor"),
            P("expert", "tensor", None),
            P(("expert", "tensor"), None),
            P(("expert", "tensor"), None),
        ),
        out_specs=(
            P(("expert", "tensor"), None),
            P(("expert", "tensor"), None),
            P(),
            P(None, "tensor"),
            P(None, "tensor"),
            P(None, "tensor"),
            P("tensor", None),
            P(),
            P(),
            P("expert", None, "tensor"),
            P("expert", None, "tensor"),
            P("expert", "tensor", None),
        ),
        check_vma=False,
    )
```

```python
import functools

import jax
import jax.numpy as jnp
from jax import lax
from jax.experimental import pallas as pl
from jax.experimental.pallas import tpu as pltpu
from jax.sharding import PartitionSpec as P

HD = 128


eps = 1e-06
theta_base = 10000.0
masked = -1e30

BOTH = ("expert", "tensor")
CORE, ACROSS, ASIDE, PLANE_NEXT, PLANE_FAR = 1, 2, 4, 8, 16
PLANES = (0, PLANE_NEXT, PLANE_FAR, PLANE_NEXT | PLANE_FAR)
BLOCKS = 8
WEIGHT_SLOTS = 3
LANES = 128

(
    G,
    H,
    M,
    R,
    QUERIES,
    KEYS,
    VALUES,
    TOTALS,
    HEADS,
    KEPT,
    SENT,
    RAW,
    HOME,
    SUMS,
    NEAR,
    AWAY,
    OTHER,
    FAR,
    OWN,
    SIDE,
    FULL,
    GOT,
    IN,
    OUT,
    TOKENS,
    NAMED,
    ROUTER,
    GATES,
    ATTN,
    RELAY,
    MIXED,
    EXPERTS,
    SMALL,
    GAIN,
    PAIR,
) = range(35)


def rope_tables(seq_length, head_size):
    half_dim = head_size // 2
    frequency = jnp.exp(
        -jnp.log(theta_base) * jnp.arange(half_dim, dtype=jnp.float32) * (2.0 / head_size)
    )
    angles = jnp.arange(seq_length, dtype=jnp.float32)[:, None] * frequency[None, :]
    return (jnp.cos(angles)[:, None, :], jnp.sin(angles)[:, None, :])


def rotate(source, cosine_table, sine_table):
    half_dim = source.shape[-1] // 2
    first_half = source[..., :half_dim]
    second = source[..., half_dim:]
    return jnp.concatenate(
        [
            first_half * cosine_table - second * sine_table,
            second * cosine_table + first_half * sine_table,
        ],
        axis=-1,
    )


def norm_forward(source, gain_vec):
    inverse = lax.rsqrt(jnp.mean(source * source, axis=-1, keepdims=True) + eps)
    return (inverse, source * inverse * gain_vec)


def norm_backward(source, inverse, gain_vec, grad_in):
    scaled = gain_vec * grad_in
    grad_source = inverse * scaled - source * inverse**3 * jnp.mean(
        scaled * source, axis=-1, keepdims=True
    )
    grad_gain = jnp.sum(grad_in * source * inverse, axis=0)
    return (grad_source, grad_gain)


def block_scores(q_block, key_rows, first_row, score_scale):
    scores = (
        jnp.einsum("qgrd,kgd->grqk", q_block, key_rows, preferred_element_type=jnp.float32)
        * score_scale
    )
    row_ids = first_row + jnp.arange(q_block.shape[0], dtype=jnp.int32)
    allowed = row_ids[:, None] >= jnp.arange(key_rows.shape[0], dtype=jnp.int32)[None, :]
    return jnp.where(allowed, scores, masked)


def routed_layer(
    tokens,
    gain_attn,
    w_query,
    w_key,
    w_value,
    w_out,
    gain_moe,
    w_router,
    w_gate,
    w_up,
    w_down,
    expert_ids,
    cotangent,
):
    seq_length, model_width = tokens.shape
    block_len, top_count = expert_ids.shape
    expert_count = w_router.shape[1]
    local_experts = w_gate.shape[0]
    local_heads = w_query.shape[1] // HD
    local_groups = w_key.shape[1] // HD
    group_size = local_heads // local_groups
    owners = lax.axis_size("expert")
    quarter = lax.axis_index("tensor")
    capacity = 3 * block_len * top_count // (2 * expert_count)
    block_rows = min(512, seq_length)
    block_count = seq_length // block_rows
    score_scale = HD ** (-0.5)
    first_own = quarter * block_len
    inputs = tokens.astype(jnp.float32)
    inverse_one, normed_one = norm_forward(inputs, gain_attn)
    hidden_one = normed_one.astype(jnp.bfloat16)
    cosine_table, sine_table = rope_tables(seq_length, HD)

    def rope_heads(source):
        return rotate(source, cosine_table, sine_table)

    query_raw = jnp.dot(hidden_one, w_query, preferred_element_type=jnp.float32).reshape(
        seq_length, local_heads, HD
    )
    key_raw = jnp.dot(hidden_one, w_key, preferred_element_type=jnp.float32).reshape(
        seq_length, local_groups, HD
    )
    queries = rope_heads(query_raw).astype(jnp.bfloat16)
    key_rows = rope_heads(key_raw).astype(jnp.bfloat16)
    value_rows = (
        jnp.dot(hidden_one, w_value, preferred_element_type=jnp.float32)
        .astype(jnp.bfloat16)
        .reshape(seq_length, local_groups, HD)
    )
    query_blocks = queries.reshape(block_count, block_rows, local_groups, group_size, HD)
    starts = jnp.arange(block_count, dtype=jnp.int32) * block_rows

    def attend_block(packed):
        first_row, q_block = packed
        scores = block_scores(q_block, key_rows, first_row, score_scale)
        row_max = jnp.max(scores, axis=-1, keepdims=True)
        exponent = jnp.exp(scores - row_max)
        row_total = jnp.sum(exponent, axis=-1, keepdims=True)
        weights = (exponent / row_total).astype(jnp.bfloat16)
        head_out = jnp.einsum(
            "grqk,kgd->qgrd", weights, value_rows, preferred_element_type=jnp.float32
        )
        return (head_out.astype(jnp.bfloat16), (row_max + jnp.log(row_total))[..., 0])

    head_blocks, log_totals = lax.map(attend_block, (starts, query_blocks))
    head_rows = head_blocks.reshape(seq_length, local_heads * HD)
    attention = lax.psum_scatter(
        jnp.dot(head_rows, w_out, preferred_element_type=jnp.float32),
        "tensor",
        scatter_dimension=0,
        tiled=True,
    )
    own_inputs = lax.dynamic_slice_in_dim(inputs, first_own, block_len, 0)
    own_inverse = lax.dynamic_slice_in_dim(inverse_one, first_own, block_len, 0)
    middle = own_inputs + attention
    inverse_two, normed_two = norm_forward(middle, gain_moe)
    hidden_two = normed_two.astype(jnp.bfloat16)
    logits = jnp.dot(hidden_two, w_router, preferred_element_type=jnp.float32)
    expert_range = jnp.arange(expert_count, dtype=jnp.int32)
    matches = expert_ids[:, :, None] == expert_range[None, None, :]
    chosen = jnp.sum(jnp.where(matches, logits[:, None, :], 0.0), axis=2)
    gate_weights = jax.nn.softmax(chosen, axis=-1)
    expert_hits = jnp.sum(matches.astype(jnp.int32), axis=1)
    earlier = jnp.cumsum(expert_hits, axis=0) - expert_hits
    slot_of = jnp.sum(jnp.where(matches, earlier[:, None, :], 0), axis=2)
    place = (slot_of * expert_count + expert_ids).reshape(-1)
    token_rows = jnp.broadcast_to(
        hidden_two[:, None, :], (block_len, top_count, model_width)
    ).reshape(block_len * top_count, model_width)
    grad_out = cotangent.astype(jnp.float32)
    gated_grads = (
        (gate_weights[:, :, None] * grad_out[:, None, :])
        .astype(jnp.bfloat16)
        .reshape(block_len * top_count, model_width)
    )
    empty = jnp.zeros((capacity * expert_count, model_width), jnp.bfloat16)
    send_rows = empty.at[place].set(token_rows).reshape(capacity, expert_count, model_width)
    send_grads = empty.at[place].set(gated_grads).reshape(capacity, expert_count, model_width)
    arrived_rows, arrived_grads = (
        lax.all_to_all(send_rows, "expert", split_axis=1, concat_axis=1, tiled=True),
        lax.all_to_all(send_grads, "expert", split_axis=1, concat_axis=1, tiled=True),
    )
    routed = arrived_rows.reshape(capacity, owners, local_experts, model_width)
    grads_in = arrived_grads.reshape(capacity, owners, local_experts, model_width)
    all_rows, all_grads = (
        lax.all_gather(routed, "tensor", axis=0, tiled=True),
        lax.all_gather(grads_in, "tensor", axis=0, tiled=True),
    )
    gate_pre = jnp.einsum("csld,ldf->cslf", all_rows, w_gate, preferred_element_type=jnp.float32)
    up_pre = jnp.einsum("csld,ldf->cslf", all_rows, w_up, preferred_element_type=jnp.float32)
    sigmoid_gate = jax.nn.sigmoid(gate_pre)
    silu_gate = gate_pre * sigmoid_gate
    activation = (silu_gate * up_pre).astype(jnp.bfloat16)
    grad_w_down = jnp.einsum(
        "cslf,csld->lfd", activation, all_grads, preferred_element_type=jnp.float32
    )
    grad_act = jnp.einsum("csld,lfd->cslf", all_grads, w_down, preferred_element_type=jnp.float32)
    grad_gate = (grad_act * up_pre * sigmoid_gate * (1.0 + gate_pre * (1.0 - sigmoid_gate))).astype(
        jnp.bfloat16
    )
    grad_up = (grad_act * silu_gate).astype(jnp.bfloat16)
    grad_w_gate = jnp.einsum(
        "csld,cslf->ldf", all_rows, grad_gate, preferred_element_type=jnp.float32
    )
    grad_w_up = jnp.einsum("csld,cslf->ldf", all_rows, grad_up, preferred_element_type=jnp.float32)
    forward_term = jnp.einsum(
        "cslf,lfd->csld", activation, w_down, preferred_element_type=jnp.float32
    )
    back_term = jnp.einsum("cslf,ldf->csld", grad_gate, w_gate, preferred_element_type=jnp.float32)
    back_term = back_term + jnp.einsum(
        "cslf,ldf->csld", grad_up, w_up, preferred_element_type=jnp.float32
    )
    both_terms = lax.psum_scatter(
        jnp.concatenate([forward_term, back_term], axis=3).astype(jnp.bfloat16),
        "tensor",
        scatter_dimension=0,
        tiled=True,
    )
    returned = both_terms[..., :model_width]
    row_grads = both_terms[..., model_width:]
    returned_home, row_grads_home = (
        lax.all_to_all(
            returned.reshape(capacity, expert_count, model_width),
            "expert",
            split_axis=1,
            concat_axis=1,
            tiled=True,
        ),
        lax.all_to_all(
            row_grads.reshape(capacity, expert_count, model_width),
            "expert",
            split_axis=1,
            concat_axis=1,
            tiled=True,
        ),
    )
    picked = returned_home.reshape(capacity * expert_count, model_width)[place].reshape(
        block_len, top_count, model_width
    )
    mixture = jnp.sum(gate_weights[:, :, None] * picked, axis=1)
    mixed_out = (middle + mixture).astype(jnp.bfloat16)
    grad_gates = jnp.sum(picked * grad_out[:, None, :], axis=2)
    grad_picked = row_grads_home.reshape(capacity * expert_count, model_width)[place].reshape(
        block_len, top_count, model_width
    )
    grad_hidden_disp = jnp.einsum(
        "lk,lkd->ld",
        jnp.ones((block_len, top_count), jnp.bfloat16),
        grad_picked,
        preferred_element_type=jnp.float32,
    )
    grad_chosen = gate_weights * (
        grad_gates - jnp.sum(gate_weights * grad_gates, axis=-1, keepdims=True)
    )
    grad_logits = jnp.sum(jnp.where(matches, grad_chosen[:, :, None], 0.0), axis=1).astype(
        jnp.bfloat16
    )
    grad_router = jnp.einsum(
        "ld,le->de", hidden_two, grad_logits, preferred_element_type=jnp.float32
    )
    grad_hidden_two = grad_hidden_disp + jnp.einsum(
        "le,de->ld", grad_logits, w_router, preferred_element_type=jnp.float32
    )
    grad_normed_two, grad_gain_moe = norm_backward(middle, inverse_two, gain_moe, grad_hidden_two)
    grad_middle = grad_out + grad_normed_two
    grad_attn = grad_middle.astype(jnp.bfloat16)
    grad_attn_all = lax.all_gather(grad_attn, "tensor", axis=0, tiled=True)
    grad_w_out = jnp.einsum(
        "lh,ld->hd", head_rows, grad_attn_all, preferred_element_type=jnp.float32
    )
    grad_heads = jnp.einsum(
        "ld,hd->lh", grad_attn_all, w_out, preferred_element_type=jnp.float32
    ).astype(jnp.bfloat16)
    grad_blocks = grad_heads.reshape(block_count, block_rows, local_groups, group_size, HD)

    def back_block(carried, packed):
        grad_keys, grad_values = carried
        first_row, q_block, g_block, lse_block = packed
        scores = block_scores(q_block, key_rows, first_row, score_scale)
        probability = jnp.exp(scores - lse_block[..., None])
        grad_values = grad_values + jnp.einsum(
            "grqk,qgrd->kgd",
            probability.astype(jnp.bfloat16),
            g_block,
            preferred_element_type=jnp.float32,
        )
        grad_prob = jnp.einsum(
            "qgrd,kgd->grqk", g_block, value_rows, preferred_element_type=jnp.float32
        )
        row_delta = jnp.sum(probability * grad_prob, axis=-1, keepdims=True)
        grad_scores = (probability * (grad_prob - row_delta)).astype(jnp.bfloat16)
        grad_query = (
            jnp.einsum("grqk,kgd->qgrd", grad_scores, key_rows, preferred_element_type=jnp.float32)
            * score_scale
        )
        grad_keys = (
            grad_keys
            + jnp.einsum("grqk,qgrd->kgd", grad_scores, q_block, preferred_element_type=jnp.float32)
            * score_scale
        )
        return ((grad_keys, grad_values), grad_query)

    zero_keys = jnp.zeros((seq_length, local_groups, HD), jnp.float32)
    (grad_keys, grad_values), grad_query_blocks = lax.scan(
        back_block, (zero_keys, zero_keys), (starts, query_blocks, grad_blocks, log_totals)
    )
    grad_query = grad_query_blocks.reshape(seq_length, local_heads, HD)
    grad_query_raw = (
        jax.vjp(rope_heads, query_raw)[1](grad_query)[0]
        .reshape(seq_length, local_heads * HD)
        .astype(jnp.bfloat16)
    )
    grad_key_raw = (
        jax.vjp(rope_heads, key_raw)[1](grad_keys)[0]
        .reshape(seq_length, local_groups * HD)
        .astype(jnp.bfloat16)
    )
    grad_value_raw = grad_values.reshape(seq_length, local_groups * HD).astype(jnp.bfloat16)
    grad_w_query = jnp.einsum(
        "ld,lh->dh", hidden_one, grad_query_raw, preferred_element_type=jnp.float32
    )
    grad_w_key = jnp.einsum(
        "ld,lh->dh", hidden_one, grad_key_raw, preferred_element_type=jnp.float32
    )
    grad_w_value = jnp.einsum(
        "ld,lh->dh", hidden_one, grad_value_raw, preferred_element_type=jnp.float32
    )
    term = jnp.einsum("lh,dh->ld", grad_query_raw, w_query, preferred_element_type=jnp.float32)
    term = term + jnp.einsum("lh,dh->ld", grad_key_raw, w_key, preferred_element_type=jnp.float32)
    grad_hidden_one = lax.psum_scatter(
        (
            term
            + jnp.einsum("lh,dh->ld", grad_value_raw, w_value, preferred_element_type=jnp.float32)
        ).astype(jnp.bfloat16),
        "tensor",
        scatter_dimension=0,
        tiled=True,
    ).astype(jnp.float32)
    grad_normed_one, grad_gain_attn = norm_backward(
        own_inputs, own_inverse, gain_attn, grad_hidden_one
    )
    grad_tokens = grad_middle + grad_normed_one
    attn_sums = lax.psum((grad_w_query, grad_w_key, grad_w_value, grad_w_out), "expert")
    small_sums = lax.psum((grad_gain_attn, grad_gain_moe, grad_router), ("expert", "tensor"))
    return (
        mixed_out,
        grad_tokens,
        small_sums[0],
        attn_sums[0],
        attn_sums[1],
        attn_sums[2],
        attn_sums[3],
        small_sums[1],
        small_sums[2],
        grad_w_gate,
        grad_w_up,
        grad_w_down,
    )


ROWS_ROWS = (((1,), (1,)), ((), ()))
def dot_nt(left, right):
    return lax.dot_general(left, right, ROWS_ROWS, preferred_element_type=jnp.float32)


def dot_nn(left, right):
    return jnp.dot(left, right, preferred_element_type=jnp.float32)


def expert_kernel(places, top_count, *refs):
    row_places, grad_places = places
    given = 1 + max(place[0] for place in row_places + grad_places)
    numbers_ref, router_ref, gate_ref, up_ref, down_ref = refs[given : given + 5]
    outs = refs[given + 5 : given + 14]
    mixed_refs, back_refs, sums_ref = outs[:2], outs[2:4], outs[4]
    rows_s, grads_s, ids_s, x_s, y_s, back_s, out_s = refs[given + 14 : given + 21]
    pick_s, place_s, gates_s, sums_s, gated_s, side_s = refs[given + 21 : given + 27]
    both_s, down_s, sems, weight_sems, out_sems, kept_sems = refs[given + 27 :]
    pairs, wide, _ = pick_s.shape
    experts = x_s.shape[0]
    hidden = down_s.shape[1]
    cap = wide // experts
    tokens_in, width = rows_s.shape[1:]
    block_len = tokens_in // 2
    narrow = jnp.bfloat16

    def copies(pair):
        out = []
        for half in range(2):
            target = pl.ds(half * block_len, block_len)
            at = 2 * pair + half
            array, row, column = row_places[at]
            rows = refs[array].at[pl.ds(row, block_len), pl.ds(column, width)]
            array, row, column = grad_places[at]
            block = refs[array].at[pl.ds(row, block_len)]
            grads = block.at[:, pl.ds(column, width)]
            ids = block.at[:, pl.ds(column + width, LANES)]
            for k, (source, scratch) in enumerate(
                ((rows, rows_s), (grads, grads_s), (ids, ids_s))
            ):
                out.append(
                    pltpu.make_async_copy(source, scratch.at[pair, target], sems.at[k, at])
                )
        return out

    def weight_copies(expert, slot):
        sides = [both_s.at[slot, :, pl.ds(k * hidden, hidden)] for k in range(2)]
        return [
            pltpu.make_async_copy(gate_ref.at[expert], sides[0], weight_sems.at[0, slot]),
            pltpu.make_async_copy(up_ref.at[expert], sides[1], weight_sems.at[1, slot]),
            pltpu.make_async_copy(down_ref.at[expert], down_s.at[slot], weight_sems.at[2, slot]),
        ]

    def result_copies(pair):
        half = pairs // 2
        place = pl.ds((pair % half) * tokens_in, tokens_in)
        sides = (rows_s, mixed_refs), (grads_s, back_refs)
        return [
            pltpu.make_async_copy(
                source.at[pair], targets[pair // half].at[place], out_sems.at[k, pair]
            )
            for k, (source, targets) in enumerate(sides)
        ]

    kept_copies = [
        pltpu.make_async_copy(source, target, kept_sems.at[k])
        for k, (source, target) in enumerate(zip((x_s, y_s, gated_s, side_s), outs[5:9]))
    ]

    for pair in range(pairs):
        for copy in copies(pair):
            copy.start()
    for slot in range(WEIGHT_SLOTS):
        for copy in weight_copies(slot, slot):
            copy.start()

    earlier = lax.broadcasted_iota(jnp.int32, (tokens_in, tokens_in), 0)
    later = lax.broadcasted_iota(jnp.int32, (tokens_in, tokens_in), 1)
    before = jnp.where(earlier < later, 1.0, 0.0).astype(narrow)

    for pair in range(pairs):
        for copy in copies(pair):
            copy.wait()
        rows_in = rows_s[pair]
        logits = dot_nt(router_ref[...], rows_in)
        ids = ids_s[pair].astype(jnp.float32).T
        named = jnp.zeros(logits.shape, jnp.float32)
        for k in range(top_count):
            named = jnp.where(ids[k : k + 1, :] == numbers_ref[:, :1], 1.0, named)
        hits = named[:experts]
        slots = jnp.where(hits > 0.0, dot_nn(hits.astype(narrow), before), -1.0)
        slots = slots.astype(jnp.int32)
        logits = jnp.where(named > 0.0, logits, masked)
        weights = jnp.exp(logits - jnp.max(logits, axis=0, keepdims=True)) * named
        gates = weights / jnp.sum(weights, axis=0, keepdims=True)
        ranks = lax.broadcasted_iota(jnp.int32, (cap, tokens_in), 0)
        place = pl.ds(pair * cap, cap)
        picks = []
        for expert in range(experts):
            pick = ranks == slots[expert : expert + 1, :]
            row_gates = jnp.sum(
                jnp.where(pick, gates[expert : expert + 1, :], 0.0), axis=1, keepdims=True
            )
            gates_s[expert, place, :] = jnp.broadcast_to(row_gates, (cap, LANES))
            picks.append(jnp.where(pick, 1.0, 0.0))
        pick_all = jnp.concatenate(picks, axis=0)
        pick_low = pick_all.astype(narrow)
        pick_s[pair] = pick_low
        place_s[pair] = pick_all.T.astype(narrow)
        for source, target in ((rows_in, x_s), (grads_s[pair], y_s)):
            spread = dot_nn(pick_low, source).astype(narrow)
            for expert in range(experts):
                target[expert, place, :] = spread[expert * cap : (expert + 1) * cap]

    kept_copies[0].start()
    kept_copies[1].start()

    def expert_step(expert, carried):
        slot = lax.rem(expert, WEIGHT_SLOTS)
        for copy in weight_copies(expert, slot):
            copy.wait()
        both = dot_nn(x_s[expert], both_s[slot])
        gate_pre, up_pre = both[:, :hidden], both[:, hidden:]
        plain = dot_nt(y_s[expert], down_s[slot])
        sigmoid_gate = jax.nn.sigmoid(gate_pre)
        silu_gate = gate_pre * sigmoid_gate
        activation = silu_gate * up_pre
        row_gates = gates_s[expert][:, :1]
        sums = jnp.sum(activation * plain, axis=1, keepdims=True)
        sums_s[expert] = jnp.broadcast_to(sums, sums_s.shape[1:])
        grad_act = row_gates * plain
        gated = (row_gates * activation).astype(narrow)
        slope = sigmoid_gate * (1.0 + gate_pre * (1.0 - sigmoid_gate))
        grad_gate = (grad_act * up_pre * slope).astype(narrow)
        grad_up = (grad_act * silu_gate).astype(narrow)
        grad_both = jnp.concatenate([grad_gate, grad_up], axis=1)
        gated_s[expert] = gated
        side_s[expert] = grad_both
        out_s[expert] = dot_nn(gated, down_s[slot]).astype(narrow)
        back_s[expert] = dot_nt(grad_both, both_s[slot]).astype(narrow)

        @pl.when(expert + WEIGHT_SLOTS < experts)
        def _():
            for copy in weight_copies(expert + WEIGHT_SLOTS, slot):
                copy.start()

        return carried

    lax.fori_loop(0, experts, expert_step, 0)
    kept_copies[2].start()
    kept_copies[3].start()

    for pair in range(pairs):
        sides = pl.ds(pair * cap, cap)
        for source, target in ((out_s, rows_s), (back_s, grads_s)):
            stacked = jnp.concatenate(
                [source[expert, sides, :] for expert in range(experts)], axis=0
            )
            target[pair] = dot_nn(place_s[pair], stacked).astype(narrow)
        for copy in result_copies(pair):
            copy.start()
        pick = pick_s[pair].astype(jnp.float32)
        sums = []
        for expert in range(experts):
            column = sums_s[expert, sides, :][:, :1]
            part = pick[expert * cap : (expert + 1) * cap] * column
            sums.append(jnp.sum(part, axis=0, keepdims=True))
        sums_ref[pair] = jnp.concatenate(sums, axis=0)

    for copy in kept_copies:
        copy.wait()
    for pair in range(pairs):
        for copy in result_copies(pair):
            copy.wait()


def expert_chunk(arrays, places, numbers, router, w_gate, w_up, w_down, tokens_in, top_count, cap):
    experts, width, hidden = w_gate.shape
    pairs = BLOCKS // 2
    rows = pairs * cap
    narrow, wide = jnp.bfloat16, jnp.float32
    shape = jax.ShapeDtypeStruct
    anywhere = pl.BlockSpec(memory_space=pl.ANY)
    inside = pl.BlockSpec(memory_space=pltpu.VMEM)
    half_shape = shape((pairs // 2 * tokens_in, width), narrow)
    whole_rows = (experts, rows, width)
    return pl.pallas_call(
        functools.partial(expert_kernel, places, top_count),
        in_specs=[anywhere] * len(arrays) + [inside] * 2 + [anywhere] * 3,
        out_specs=[anywhere] * 4 + [inside] + [anywhere] * 4,
        out_shape=[half_shape] * 4
        + [
            shape((pairs, experts, tokens_in), wide),
            shape(whole_rows, narrow),
            shape(whole_rows, narrow),
            shape((experts, rows, hidden), narrow),
            shape((experts, rows, 2 * hidden), narrow),
        ],
        scratch_shapes=[pltpu.VMEM((pairs, tokens_in, width), narrow)] * 2
        + [pltpu.VMEM((pairs, tokens_in, LANES), narrow)]
        + [pltpu.VMEM(whole_rows, narrow)] * 4
        + [
            pltpu.VMEM((pairs, experts * cap, tokens_in), narrow),
            pltpu.VMEM((pairs, tokens_in, experts * cap), narrow),
            pltpu.VMEM((experts, rows, LANES), wide),
            pltpu.VMEM((experts, rows, LANES), wide),
            pltpu.VMEM((experts, rows, hidden), narrow),
            pltpu.VMEM((experts, rows, 2 * hidden), narrow),
            pltpu.VMEM((WEIGHT_SLOTS, width, 2 * hidden), narrow),
            pltpu.VMEM((WEIGHT_SLOTS, hidden, width), narrow),
            pltpu.SemaphoreType.DMA((3, BLOCKS)),
            pltpu.SemaphoreType.DMA((3, WEIGHT_SLOTS)),
            pltpu.SemaphoreType.DMA((2, pairs)),
            pltpu.SemaphoreType.DMA((4,)),
        ],
        compiler_params=pltpu.CompilerParams(vmem_limit_bytes=60 << 20),
        cost_estimate=pl.CostEstimate(
            flops=24 * experts * rows * width * hidden,
            bytes_accessed=6 * experts * width * hidden + 4 * experts * rows * width,
            transcendentals=experts * rows * hidden,
        ),
    )(*arrays, numbers, router, w_gate, w_up, w_down)


def weight_kernel(parts, given, *refs):
    ins, (gate_ref, up_ref, down_ref) = refs[: 4 * parts], refs[4 * parts + given :]
    rows, grads, gated, both = [
        jnp.concatenate([ref[0] for ref in ins[k * parts : (k + 1) * parts]], axis=0)
        for k in range(4)
    ]
    turn = (((0,), (0,)), ((), ()))
    hidden = gated.shape[1]
    down_ref[0] = lax.dot_general(gated, grads, turn, preferred_element_type=jnp.float32)
    sides = lax.dot_general(rows, both, turn, preferred_element_type=jnp.float32)
    gate_ref[0] = sides[:, :hidden]
    up_ref[0] = sides[:, hidden:]


def weight_grads(kept, begin, count, partial):
    parts = len(kept)
    experts, rows, width = kept[0][0].shape
    hidden = kept[0][2].shape[2]
    operands = [part[k] for k in range(4) for part in kept]
    shape = jax.ShapeDtypeStruct

    def spec(rows, columns):
        return pl.BlockSpec((1, rows, columns), lambda i: (i + begin, 0, 0))

    return pl.pallas_call(
        functools.partial(weight_kernel, parts, len(partial)),
        grid=(count,),
        in_specs=[spec(rows, operand.shape[2]) for operand in operands]
        + [pl.BlockSpec(memory_space=pl.ANY)] * len(partial),
        out_specs=[spec(width, hidden), spec(width, hidden), spec(hidden, width)],
        out_shape=[
            shape((experts, width, hidden), jnp.float32),
            shape((experts, width, hidden), jnp.float32),
            shape((experts, hidden, width), jnp.float32),
        ],
        input_output_aliases={len(operands) + k: k for k in range(len(partial))},
        compiler_params=pltpu.CompilerParams(vmem_limit_bytes=56 << 20),
        cost_estimate=pl.CostEstimate(
            flops=6 * parts * count * rows * width * hidden,
            bytes_accessed=count * (parts * rows * (4 * width + 6 * hidden) + 12 * width * hidden),
            transcendentals=0,
        ),
    )(*operands, *partial)


def gathered_layer(
    tokens,
    gain_attn,
    w_query,
    w_key,
    w_value,
    w_out,
    gain_moe,
    w_router,
    w_gate,
    w_up,
    w_down,
    expert_ids,
    cotangent,
):
    seq_length, model_width = tokens.shape
    block_len, top_count = expert_ids.shape
    expert_count = w_router.shape[1]
    local_experts = w_gate.shape[0]
    local_heads = w_query.shape[1] // HD
    quarters = lax.axis_size("tensor")
    device_count = quarters * lax.axis_size("expert")
    quarter = lax.axis_index("tensor").astype(jnp.uint32)
    device = lax.axis_index(BOTH).astype(jnp.uint32)
    first_expert = lax.axis_index("expert") * local_experts
    pair_cap = 2 * (3 * block_len * top_count // (2 * expert_count))
    score_scale = HD ** (-0.5)
    narrow, wide = jnp.bfloat16, jnp.float32

    def swap(value, even, odd=None):
        odd = even if odd is None else odd
        perm = [(i, i ^ (odd if i & 1 else even)) for i in range(device_count)]
        return lax.ppermute(value, BOTH, perm)

    def near(value):
        return swap(value, ACROSS, ASIDE)

    def far(value):
        return swap(value, ASIDE, ACROSS)

    def core(value):
        return swap(value, CORE)

    def add(left, right):
        return (left.astype(wide) + right.astype(wide)).astype(narrow)

    live = {}

    def sync():
        keys = list(live)
        values = lax.optimization_barrier([live[key] for key in keys])
        live.update(zip(keys, values))

    def gather_near(name, plane):
        live[name, plane, 1] = near(live[name, plane, 0])
        live[name, plane, 2] = far(live[name, plane, 0])

    def gather_far(name, plane):
        live[name, plane, 3] = far(live[name, plane, 1])

    def gather_across(name, plane):
        live[name, plane, 3] = swap(live[name, plane, 0], ACROSS | ASIDE)

    def join_core(name, plane, *slots):
        blocks = [live[name, plane, slot] for slot in slots]
        live[name, plane, (OTHER,) + slots] = jnp.concatenate(blocks, axis=0)

    def send_core(name, plane, *slots):
        live[name, plane, (OTHER,) + slots] = core(live[name, plane, (OTHER,) + slots])

    def gather_core(name, plane, *slots):
        join_core(name, plane, *slots)
        send_core(name, plane, *slots)

    def blocks_of(name, plane):
        found = {}
        for key in list(live):
            if isinstance(key, tuple) and key[:2] == (name, plane):
                slots = key[2]
                array = live.pop(key)
                if isinstance(slots, tuple):
                    for i, slot in enumerate(slots[1:]):
                        found[4 + slot] = (array, i * block_len)
                else:
                    found[slots] = (array, 0)
        return [found[slot] for slot in range(BLOCKS)]

    def reduce_core(name, plane):
        live[name, plane, OTHER] = core(live.pop((name, plane, AWAY)))

    def add_far(name, plane):
        kept = live[name, plane, NEAR].reshape(4, block_len, model_width)
        got = live[name, plane, OTHER].reshape(4, block_len, model_width)
        live[name, plane, FAR] = add(kept[2:], got[2:])

    def send_far(name, plane):
        live[name, plane, FAR] = far(live[name, plane, FAR])

    def reduce_far(name, plane):
        add_far(name, plane)
        send_far(name, plane)

    def add_near(name, plane):
        kept = live.pop((name, plane, NEAR)).reshape(4, block_len, model_width)
        got = live.pop((name, plane, OTHER)).reshape(4, block_len, model_width)
        back = live.pop((name, plane, FAR))
        sums = [
            kept[i].astype(wide) + got[i].astype(wide) + back[i].astype(wide) for i in range(2)
        ]
        live[name, plane, OWN], live[name, plane, SIDE] = [part.astype(narrow) for part in sums]

    def send_near(name, plane):
        live[name, plane, SIDE] = near(live[name, plane, SIDE])

    def reduce_near(name, plane):
        add_near(name, plane)
        send_near(name, plane)

    def reduced(name, plane):
        return add(live.pop((name, plane, OWN)), live.pop((name, plane, SIDE)))

    def bit(mask):
        return (device // mask) % 2

    odd_core = bit(CORE)
    weight_hops = ((ASIDE, PLANE_NEXT), (PLANE_NEXT, ASIDE), (PLANE_FAR, PLANE_FAR))
    small_hops = tuple((mask, mask) for mask in (CORE, ACROSS, ASIDE, PLANE_NEXT, PLANE_FAR))

    def joined(own, got, side):
        count = own.shape[0]
        both = jnp.zeros((2 * count,) + own.shape[1:], own.dtype)
        both = lax.dynamic_update_slice_in_dim(both, own, side * count, 0)
        return lax.dynamic_update_slice_in_dim(both, got, (1 - side) * count, 0)

    def sum_step(name, step, hops=weight_hops, sent_as=narrow):
        count = len(hops)
        sides = [jnp.where(odd_core == 0, bit(even), bit(odd)) for even, odd in hops]
        if step == 0:
            kept = live.pop((name, FULL))
        elif step <= count:
            kept = live.pop((name, KEPT)) + live.pop((name, GOT)).astype(wide)
        else:
            kept = joined(live.pop((name, KEPT)), live.pop((name, GOT)), sides[2 * count - step])
        if step < count:
            half = kept.shape[0] // 2
            side = sides[step]
            live[name, KEPT] = lax.dynamic_slice_in_dim(kept, side * half, half, 0)
            sent = lax.dynamic_slice_in_dim(kept, (1 - side) * half, half, 0)
            live[name, GOT] = swap(sent.astype(sent_as), *hops[step])
        else:
            kept = kept.astype(sent_as)
            live[name, KEPT] = kept
            live[name, GOT] = swap(kept, *hops[2 * count - 1 - step])

    def summed(name, hops=weight_hops):
        even, odd = hops[0]
        side = jnp.where(odd_core == 0, bit(even), bit(odd))
        return joined(live.pop((name, KEPT)), live.pop((name, GOT)), side).astype(wide)

    own, nxt, far_plane, last = PLANES

    named_ids = jnp.pad(expert_ids.astype(narrow), ((0, 0), (0, LANES - top_count)))
    live[G, own, 0] = jnp.concatenate([cotangent, named_ids], axis=1)
    half_block = block_len // 2
    live[G, nxt, 0] = swap(live[G, own, 0], nxt)
    live[G, far_plane, 0] = [swap(live[G, own, 0][:half_block], far_plane)]
    gather_near(G, own)

    by_block = tokens.reshape(quarters, block_len, model_width)
    inputs = jnp.concatenate(
        [lax.dynamic_slice_in_dim(by_block, quarter ^ r, 1, 0)[0] for r in range(quarters)], axis=0
    )
    inputs = lax.optimization_barrier(inputs)
    order = quarter.astype(jnp.int32) ^ jnp.arange(quarters, dtype=jnp.int32)
    positions = (order[:, None] * block_len + jnp.arange(block_len, dtype=jnp.int32)).reshape(-1)
    inverse_one, normed_one = norm_forward(inputs.astype(wide), gain_attn)
    hidden_one = normed_one.astype(narrow)
    frequency = jnp.exp(
        -jnp.log(theta_base) * jnp.arange(HD // 2, dtype=jnp.float32) * (2.0 / HD)
    )
    angles = positions.astype(wide)[:, None] * frequency[None, :]
    cosine_table, sine_table = (jnp.cos(angles)[:, None, :], jnp.sin(angles)[:, None, :])

    def project(weights):
        return jnp.dot(hidden_one, weights, preferred_element_type=wide).reshape(
            seq_length, local_heads, HD
        )

    live[QUERIES] = rotate(project(w_query), cosine_table, sine_table).astype(narrow)
    live[KEYS] = rotate(project(w_key), cosine_table, sine_table).astype(narrow)
    live[VALUES] = project(w_value).astype(narrow)
    sync()

    gather_far(G, own)
    gather_near(G, nxt)
    live[G, far_plane, 0] = live[G, far_plane, 0] + [
        swap(live[G, own, 0][half_block:], far_plane)
    ]
    allowed = positions[:, None] >= positions[None, :]

    def masked_scores():
        scores = jnp.einsum(
            "qhd,khd->hqk", live[QUERIES], live[KEYS], preferred_element_type=wide
        )
        return jnp.where(allowed, scores * score_scale, masked)

    scores = masked_scores()
    row_max = jnp.max(scores, axis=-1, keepdims=True)
    exponent = jnp.exp(scores - row_max)
    row_total = jnp.sum(exponent, axis=-1, keepdims=True)
    weights = (exponent / row_total).astype(narrow)
    head_out = jnp.einsum("hqk,khd->qhd", weights, live[VALUES], preferred_element_type=wide)
    live[TOTALS] = row_max + jnp.log(row_total)
    live[HEADS] = head_out.astype(narrow).reshape(seq_length, local_heads * HD)

    def split_quarters(full):
        parts = full.reshape(quarters, block_len, model_width)
        live[KEPT] = [parts[0], parts[2]]
        live[SENT] = jnp.stack([parts[1], parts[3]]).astype(narrow)

    split_quarters(jnp.dot(live[HEADS], w_out, preferred_element_type=wide))
    sync()

    expert_range = jnp.arange(expert_count, dtype=jnp.int32)
    rolled = (first_expert + expert_range) % expert_count
    live[ROUTER] = jnp.take(w_router.T, rolled, axis=0)
    live[NAMED] = jnp.broadcast_to(rolled.astype(wide)[:, None], (expert_count, LANES))
    live[SENT] = core(live[SENT])
    gather_far(G, nxt)
    live[G, far_plane, 0] = jnp.concatenate(live[G, far_plane, 0], axis=0)
    sync()

    def cross_quarters():
        kept, sent = live.pop(KEPT), live.pop(SENT).astype(wide)
        live[KEPT] = kept[0] + sent[0]
        live[SENT] = swap((kept[1] + sent[1]).astype(narrow), ACROSS)

    def quarter_sum():
        return live.pop(KEPT) + live.pop(SENT).astype(wide)

    cross_quarters()
    live[G, last, 0] = swap(live[G, far_plane, 0], nxt)
    sync()

    own_inputs = inputs[:block_len].astype(wide)
    own_inverse = inverse_one[:block_len]
    middle = own_inputs + quarter_sum()
    inverse_two, normed_two = norm_forward(middle, gain_moe)
    hidden_two = normed_two.astype(narrow)
    live[H, own, 0] = hidden_two

    gather_near(H, own)
    live[H, nxt, 0] = swap(hidden_two, nxt)
    logits = jnp.dot(hidden_two, w_router, preferred_element_type=wide)
    expert_range = jnp.arange(expert_count, dtype=jnp.int32)
    matches = expert_ids[:, :, None] == expert_range[None, None, :]
    chosen = jnp.sum(jnp.where(matches, logits[:, None, :], 0.0), axis=2)
    gate_weights = jax.nn.softmax(chosen, axis=-1)
    sync()

    gather_far(H, own)
    gather_near(H, nxt)
    hidden_two = live[H, own, 0]
    gather_core(G, own, 0, 1, 2, 3)
    live[H, last, 0] = [swap(hidden_two[:half_block], last)]
    sync()

    gather_far(H, nxt)
    gather_core(H, own, 0, 1, 2, 3)
    gather_core(G, nxt, 0, 1, 2, 3)
    hidden_two = live[H, own, 0]
    live[H, last, 0] = live[H, last, 0] + [swap(hidden_two[half_block:], last)]
    sync()

    def join_pair(plane):
        rows, grads = [live.pop((name, plane, 0)) for name in (H, G)]
        if isinstance(rows, list):
            rows = jnp.concatenate(rows, axis=0)
        live[PAIR, plane, 0] = jnp.concatenate([rows, grads], axis=1)

    def experts(plane):
        if (PAIR, plane, 0) in live:
            rows = blocks_of(PAIR, plane)
            grads, column = rows, model_width
        else:
            rows, grads, column = blocks_of(H, plane), blocks_of(G, plane), 0
        arrays = []
        for array, _ in rows + grads:
            if not any(array is other for other in arrays):
                arrays.append(array)

        def placed(blocks, column):
            indices = [[array is other for other in arrays].index(True) for array, _ in blocks]
            return [(index, row, column) for index, (_, row) in zip(indices, blocks)]

        done = expert_chunk(
            arrays,
            (placed(rows, 0), placed(grads, column)),
            live[NAMED],
            live[ROUTER],
            w_gate,
            w_up,
            w_down,
            2 * block_len,
            top_count,
            pair_cap,
        )
        live[M, plane, NEAR], live[M, plane, AWAY] = done[:2]
        live[R, plane, NEAR], live[R, plane, AWAY] = done[2:4]
        live[SUMS, plane] = done[4]
        live[KEPT, plane] = done[5:]

    gather_core(H, nxt, 0, 1, 2, 3)
    join_pair(last)
    gather_near(PAIR, last)
    gather_core(PAIR, last, 0)
    live[H, far_plane, 0] = swap(live[H, own, 0], far_plane)
    experts(own)
    sync()

    gather_far(PAIR, last)
    gather_core(PAIR, last, 1, 2)
    join_pair(far_plane)
    gather_near(PAIR, far_plane)
    reduce_core(R, own)
    experts(nxt)
    sync()
    gather_core(PAIR, last, 3)
    join_core(PAIR, far_plane, 0, 1, 2)
    add_far(R, own)
    sync()

    gather_far(PAIR, far_plane)
    send_core(PAIR, far_plane, 0, 1, 2)
    send_far(R, own)
    reduce_core(R, nxt)
    reduce_core(M, own)
    experts(last)
    sync()
    gather_core(PAIR, far_plane, 3)
    reduce_core(R, last)
    add_near(R, own)
    add_far(R, nxt)
    sync()

    send_near(R, own)
    send_far(R, nxt)
    reduce_far(R, last)
    reduce_core(M, nxt)
    experts(far_plane)
    sync()

    part_experts = local_experts // 4

    def some_weight_grads(part):
        kept = [live[KEPT, plane] for plane in PLANES]
        live[EXPERTS] = weight_grads(kept, part * part_experts, part_experts, live.get(EXPERTS, []))

    reduce_core(R, far_plane)
    sums = jnp.stack([live.pop((SUMS, plane)) for plane in PLANES])
    sums = sums.reshape(len(PLANES), -1, local_experts, 2, block_len).transpose(0, 1, 3, 2, 4)
    sums = sums.reshape(len(PLANES), BLOCKS, local_experts, block_len)
    live[GATES] = [sums[:, :4], core(sums[:, 4:])]
    reduce_core(M, last)
    add_near(R, last)
    sync()

    reduce_far(R, far_plane)
    send_near(R, last)
    add_near(R, nxt)
    live[HOME] = reduced(R, own)
    sums = live[GATES][0] + live[GATES][1]
    crossed = jnp.stack([sums[:, 0], sums[:, 2], sums[:, 1], sums[:, 3]], axis=1)
    sums = jnp.where(odd_core == 0, sums, crossed)
    sums = sums[:, ::2] + swap(sums[:, 1::2], ACROSS)
    live[GATES] = [sums[:, 0], swap(sums[:, 1], ASIDE)]
    sync()

    live[RELAY] = swap(reduced(R, last), nxt)
    reduce_near(R, far_plane)
    sums = jnp.stack(live[GATES], axis=1)
    live[GATES] = [sums[::2], swap(sums[1::2], nxt)]
    send_near(R, nxt)
    add_far(M, nxt)
    add_far(M, last)
    sync()

    live[RELAY] = swap(add(reduced(R, far_plane), live[RELAY]), far_plane)
    live[SIDE] = swap(reduced(R, nxt), nxt)
    send_far(M, nxt)
    send_far(M, last)
    reduce_core(M, far_plane)
    sums = jnp.stack(live.pop(GATES), axis=1)
    sums = jnp.concatenate([sums[0], swap(sums[1], far_plane)], axis=0)
    sums = sums.reshape(-1, local_experts, block_len)
    owner = lax.axis_index("expert").astype(jnp.uint32)
    sums = [lax.dynamic_slice_in_dim(sums, owner ^ r, 1, 0)[0] for r in range(sums.shape[0])]
    own_sums = jnp.concatenate(sums, axis=0).T
    grad_gates = jnp.sum(jnp.where(matches, own_sums[:, None, :], 0.0), axis=2)
    grad_chosen = gate_weights * (
        grad_gates - jnp.sum(gate_weights * grad_gates, axis=-1, keepdims=True)
    )
    grad_logits = jnp.sum(jnp.where(matches, grad_chosen[:, :, None], 0.0), axis=1).astype(narrow)
    grad_router = jnp.einsum("ld,le->de", hidden_two, grad_logits, preferred_element_type=wide)
    live[GATES] = jnp.einsum("le,de->ld", grad_logits, w_router, preferred_element_type=wide)
    live[SMALL] = grad_router
    sync()

    grad_hidden_two = live.pop(HOME).astype(wide) + live.pop(RELAY).astype(wide)
    grad_hidden_two = grad_hidden_two + live.pop(SIDE).astype(wide) + live.pop(GATES)
    grad_out = cotangent.astype(wide)
    grad_normed_two, grad_gain_moe = norm_backward(middle, inverse_two, gain_moe, grad_hidden_two)
    grad_middle = grad_out + grad_normed_two
    grad_attn = grad_middle.astype(narrow)

    small = jnp.concatenate([live.pop(SMALL), grad_gain_moe[:, None]], axis=1)
    live[SMALL, FULL] = small.reshape(device_count, -1, small.shape[1])
    small_step = functools.partial(sum_step, SMALL, hops=small_hops, sent_as=wide)

    live[ATTN] = [grad_attn, core(grad_attn), swap(grad_attn, ACROSS)]
    small_step(0)
    add_near(M, nxt)
    add_near(M, last)
    sync()
    live[ATTN] = live[ATTN] + [core(live[ATTN][2])]
    sync()

    grad_attn_all = jnp.concatenate(live.pop(ATTN), axis=0)
    live[OUT, FULL] = jnp.einsum(
        "lh,ld->hd", live[HEADS], grad_attn_all, preferred_element_type=wide
    )
    grad_heads = (
        jnp.einsum("ld,hd->lh", grad_attn_all, w_out, preferred_element_type=wide)
        .astype(narrow)
        .reshape(seq_length, local_heads, HD)
    )
    live[RAW] = grad_heads
    sync()

    grad_heads = live.pop(RAW)
    sum_step(OUT, 0)
    send_near(M, nxt)
    probability = jnp.exp(masked_scores() - live[TOTALS])
    grad_values = jnp.einsum(
        "hqk,qhd->khd", probability.astype(narrow), grad_heads, preferred_element_type=wide
    )
    grad_prob = jnp.einsum("qhd,khd->hqk", grad_heads, live[VALUES], preferred_element_type=wide)
    row_delta = jnp.sum(probability * grad_prob, axis=-1, keepdims=True)
    grad_scores = (probability * (grad_prob - row_delta)).astype(narrow)
    grad_query = score_scale * jnp.einsum(
        "hqk,khd->qhd", grad_scores, live[KEYS], preferred_element_type=wide
    )
    grad_keys = score_scale * jnp.einsum(
        "hqk,qhd->khd", grad_scores, live[QUERIES], preferred_element_type=wide
    )

    def flat(source):
        return source.astype(narrow).reshape(seq_length, local_heads * HD)

    live[RAW] = [
        flat(rotate(grad_query, cosine_table, -sine_table)),
        flat(rotate(grad_keys, cosine_table, -sine_table)),
        flat(grad_values),
    ]
    flying = live.pop((OUT, GOT))
    sync()
    live[OUT, GOT] = flying

    def back(grad_raw, weights):
        return jnp.einsum("lh,dh->ld", grad_raw, weights, preferred_element_type=wide)

    raw = live.pop(RAW)
    partial = back(raw[0], w_query) + back(raw[1], w_key) + back(raw[2], w_value)
    split_quarters(partial)
    live[GAIN] = partial
    live[IN, FULL] = jnp.einsum(
        "ld,lh->dh", hidden_one, jnp.concatenate(raw, axis=1), preferred_element_type=wide
    )
    sum_step(OUT, 1)
    small_step(1)
    small_step(2)
    live[MIXED] = swap(reduced(M, nxt), nxt)
    sync()

    live[SENT] = core(live[SENT])
    sum_step(IN, 0)
    sum_step(OUT, 2)
    some_weight_grads(0)
    gain = jnp.sum(live.pop(GAIN) * inputs.astype(wide) * inverse_one, axis=0)
    live[GAIN] = [gain[None], jnp.zeros_like(gain)[None]]

    def gain_step(step):
        live[GAIN] = [live[GAIN][0] + live[GAIN][1]]
        live[GAIN] = live[GAIN] + [swap(live[GAIN][0], *small_hops[step])]

    small_step(3)
    gain_step(0)
    add_far(M, far_plane)
    add_far(M, own)
    sync()

    sum_step(IN, 1)
    cross_quarters()
    sum_step(OUT, 3)
    small_step(4)
    small_step(5)
    gain_step(1)
    some_weight_grads(1)
    sync()

    sum_step(IN, 2)
    own_grad = quarter_sum()
    grad_normed_one = norm_backward(own_inputs, own_inverse, gain_attn, own_grad)[0]
    live[TOKENS] = grad_middle + grad_normed_one
    sum_step(OUT, 4)
    small_step(6)
    send_near(M, last)
    send_far(M, far_plane)
    some_weight_grads(2)
    sync()

    sum_step(IN, 3)
    sum_step(OUT, 5)
    small_step(7)
    live[RELAY] = swap(reduced(M, last), nxt)
    reduce_near(M, far_plane)
    send_far(M, own)
    some_weight_grads(3)
    sync()
    for plane in PLANES:
        live.pop((KEPT, plane))

    sum_step(IN, 4)
    live[OUT] = summed(OUT)
    live[RELAY] = swap(add(reduced(M, far_plane), live[RELAY]), far_plane)
    reduce_near(M, own)
    small_step(8)
    small_step(9)
    gain_step(2)
    sync()

    columns = local_heads * HD
    sum_step(IN, 5)
    gain_step(3)
    gain_step(4)
    small = summed(SMALL, small_hops).reshape(model_width, -1)
    live[SMALL] = [small[:, :expert_count], small[:, expert_count]]
    mixed_out = middle + reduced(M, own).astype(wide) + live.pop(MIXED).astype(wide)
    live[MIXED] = (mixed_out + live.pop(RELAY).astype(wide)).astype(narrow)
    even, odd = weight_hops[0]
    side = jnp.where(odd_core == 0, bit(even), bit(odd))
    half = live[IN, KEPT].shape[0]

    def put(whole, part, index, at):
        part = part[:, index * columns : (index + 1) * columns].astype(wide)
        return lax.dynamic_update_slice_in_dim(whole, part, at * half, 0)

    empty = jnp.zeros((2 * half, columns), wide)
    live[RAW] = [put(empty, live[IN, KEPT], index, side) for index in range(3)]
    sync()
    grads_in = [put(whole, live[IN, GOT], i, 1 - side) for i, whole in enumerate(live[RAW])]

    return (
        live[MIXED],
        live[TOKENS],
        (live[GAIN][0] + live[GAIN][1])[0],
        *grads_in,
        live[OUT],
        live[SMALL][1],
        live[SMALL][0],
        *live[EXPERTS],
    )


def on_device(*operands):
    tokens, w_router, w_gate, expert_ids = operands[0], operands[7], operands[8], operands[11]
    owners, quarters = lax.axis_size("expert"), lax.axis_size("tensor")
    block_len, top_count = expert_ids.shape
    capacity = 3 * block_len * top_count // (2 * w_router.shape[1])
    buffer_rows = capacity * quarters * owners * w_gate.shape[0]
    gathers = owners * tokens.shape[0] <= buffer_rows and (owners, quarters) == (8, 4)
    return (gathered_layer if gathers else routed_layer)(*operands)


def solution(mesh):
    return jax.shard_map(
        on_device,
        mesh=mesh,
        in_specs=(
            P("expert", None),
            P(),
            P(None, "tensor"),
            P(None, "tensor"),
            P(None, "tensor"),
            P("tensor", None),
            P(),
            P(),
            P("expert", None, "tensor"),
            P("expert", None, "tensor"),
            P("expert", "tensor", None),
            P(("expert", "tensor"), None),
            P(("expert", "tensor"), None),
        ),
        out_specs=(
            P(("expert", "tensor"), None),
            P(("expert", "tensor"), None),
            P(),
            P(None, "tensor"),
            P(None, "tensor"),
            P(None, "tensor"),
            P("tensor", None),
            P(),
            P(),
            P("expert", None, "tensor"),
            P("expert", None, "tensor"),
            P("expert", "tensor", None),
        ),
        check_vma=False,
    )
```

```python
import functools

import jax
import jax.numpy as jnp
from jax import lax
from jax.experimental import pallas as pl
from jax.experimental.pallas import tpu as pltpu
from jax.sharding import PartitionSpec as P

HD = 128


eps = 1e-06
theta_base = 10000.0
masked = -1e30

BOTH = ("expert", "tensor")
CORE, ACROSS, ASIDE, PLANE_NEXT, PLANE_FAR = 1, 2, 4, 8, 16
PLANES = (0, PLANE_NEXT, PLANE_FAR, PLANE_NEXT | PLANE_FAR)
BLOCKS = 8
WEIGHT_SLOTS = 3
LANES = 128

(
    G,
    H,
    M,
    R,
    QUERIES,
    KEYS,
    VALUES,
    TOTALS,
    HEADS,
    KEPT,
    SENT,
    RAW,
    HOME,
    SUMS,
    NEAR,
    AWAY,
    OTHER,
    FAR,
    OWN,
    SIDE,
    FULL,
    GOT,
    IN,
    OUT,
    TOKENS,
    NAMED,
    ROUTER,
    GATES,
    ATTN,
    RELAY,
    MIXED,
    EXPERTS,
    SMALL,
    GAIN,
    PAIR,
) = range(35)


def rope_tables(seq_length, head_size):
    half_dim = head_size // 2
    frequency = jnp.exp(
        -jnp.log(theta_base) * jnp.arange(half_dim, dtype=jnp.float32) * (2.0 / head_size)
    )
    angles = jnp.arange(seq_length, dtype=jnp.float32)[:, None] * frequency[None, :]
    return (jnp.cos(angles)[:, None, :], jnp.sin(angles)[:, None, :])


def rotate(source, cosine_table, sine_table):
    half_dim = source.shape[-1] // 2
    first_half = source[..., :half_dim]
    second = source[..., half_dim:]
    return jnp.concatenate(
        [
            first_half * cosine_table - second * sine_table,
            second * cosine_table + first_half * sine_table,
        ],
        axis=-1,
    )


def norm_forward(source, gain_vec):
    inverse = lax.rsqrt(jnp.mean(source * source, axis=-1, keepdims=True) + eps)
    return (inverse, source * inverse * gain_vec)


def norm_backward(source, inverse, gain_vec, grad_in):
    scaled = gain_vec * grad_in
    grad_source = inverse * scaled - source * inverse**3 * jnp.mean(
        scaled * source, axis=-1, keepdims=True
    )
    grad_gain = jnp.sum(grad_in * source * inverse, axis=0)
    return (grad_source, grad_gain)


def block_scores(q_block, key_rows, first_row, score_scale):
    scores = (
        jnp.einsum("qgrd,kgd->grqk", q_block, key_rows, preferred_element_type=jnp.float32)
        * score_scale
    )
    row_ids = first_row + jnp.arange(q_block.shape[0], dtype=jnp.int32)
    allowed = row_ids[:, None] >= jnp.arange(key_rows.shape[0], dtype=jnp.int32)[None, :]
    return jnp.where(allowed, scores, masked)


def routed_layer(
    tokens,
    gain_attn,
    w_query,
    w_key,
    w_value,
    w_out,
    gain_moe,
    w_router,
    w_gate,
    w_up,
    w_down,
    expert_ids,
    cotangent,
):
    seq_length, model_width = tokens.shape
    block_len, top_count = expert_ids.shape
    expert_count = w_router.shape[1]
    local_experts = w_gate.shape[0]
    local_heads = w_query.shape[1] // HD
    local_groups = w_key.shape[1] // HD
    group_size = local_heads // local_groups
    owners = lax.axis_size("expert")
    quarter = lax.axis_index("tensor")
    capacity = 3 * block_len * top_count // (2 * expert_count)
    block_rows = min(512, seq_length)
    block_count = seq_length // block_rows
    score_scale = HD ** (-0.5)
    first_own = quarter * block_len
    inputs = tokens.astype(jnp.float32)
    inverse_one, normed_one = norm_forward(inputs, gain_attn)
    hidden_one = normed_one.astype(jnp.bfloat16)
    cosine_table, sine_table = rope_tables(seq_length, HD)

    def rope_heads(source):
        return rotate(source, cosine_table, sine_table)

    query_raw = jnp.dot(hidden_one, w_query, preferred_element_type=jnp.float32).reshape(
        seq_length, local_heads, HD
    )
    key_raw = jnp.dot(hidden_one, w_key, preferred_element_type=jnp.float32).reshape(
        seq_length, local_groups, HD
    )
    queries = rope_heads(query_raw).astype(jnp.bfloat16)
    key_rows = rope_heads(key_raw).astype(jnp.bfloat16)
    value_rows = (
        jnp.dot(hidden_one, w_value, preferred_element_type=jnp.float32)
        .astype(jnp.bfloat16)
        .reshape(seq_length, local_groups, HD)
    )
    query_blocks = queries.reshape(block_count, block_rows, local_groups, group_size, HD)
    starts = jnp.arange(block_count, dtype=jnp.int32) * block_rows

    def attend_block(packed):
        first_row, q_block = packed
        scores = block_scores(q_block, key_rows, first_row, score_scale)
        row_max = jnp.max(scores, axis=-1, keepdims=True)
        exponent = jnp.exp(scores - row_max)
        row_total = jnp.sum(exponent, axis=-1, keepdims=True)
        weights = (exponent / row_total).astype(jnp.bfloat16)
        head_out = jnp.einsum(
            "grqk,kgd->qgrd", weights, value_rows, preferred_element_type=jnp.float32
        )
        return (head_out.astype(jnp.bfloat16), (row_max + jnp.log(row_total))[..., 0])

    head_blocks, log_totals = lax.map(attend_block, (starts, query_blocks))
    head_rows = head_blocks.reshape(seq_length, local_heads * HD)
    attention = lax.psum_scatter(
        jnp.dot(head_rows, w_out, preferred_element_type=jnp.float32),
        "tensor",
        scatter_dimension=0,
        tiled=True,
    )
    own_inputs = lax.dynamic_slice_in_dim(inputs, first_own, block_len, 0)
    own_inverse = lax.dynamic_slice_in_dim(inverse_one, first_own, block_len, 0)
    middle = own_inputs + attention
    inverse_two, normed_two = norm_forward(middle, gain_moe)
    hidden_two = normed_two.astype(jnp.bfloat16)
    logits = jnp.dot(hidden_two, w_router, preferred_element_type=jnp.float32)
    expert_range = jnp.arange(expert_count, dtype=jnp.int32)
    matches = expert_ids[:, :, None] == expert_range[None, None, :]
    chosen = jnp.sum(jnp.where(matches, logits[:, None, :], 0.0), axis=2)
    gate_weights = jax.nn.softmax(chosen, axis=-1)
    expert_hits = jnp.sum(matches.astype(jnp.int32), axis=1)
    earlier = jnp.cumsum(expert_hits, axis=0) - expert_hits
    slot_of = jnp.sum(jnp.where(matches, earlier[:, None, :], 0), axis=2)
    place = (slot_of * expert_count + expert_ids).reshape(-1)
    token_rows = jnp.broadcast_to(
        hidden_two[:, None, :], (block_len, top_count, model_width)
    ).reshape(block_len * top_count, model_width)
    grad_out = cotangent.astype(jnp.float32)
    gated_grads = (
        (gate_weights[:, :, None] * grad_out[:, None, :])
        .astype(jnp.bfloat16)
        .reshape(block_len * top_count, model_width)
    )
    empty = jnp.zeros((capacity * expert_count, model_width), jnp.bfloat16)
    send_rows = empty.at[place].set(token_rows).reshape(capacity, expert_count, model_width)
    send_grads = empty.at[place].set(gated_grads).reshape(capacity, expert_count, model_width)
    arrived_rows, arrived_grads = (
        lax.all_to_all(send_rows, "expert", split_axis=1, concat_axis=1, tiled=True),
        lax.all_to_all(send_grads, "expert", split_axis=1, concat_axis=1, tiled=True),
    )
    routed = arrived_rows.reshape(capacity, owners, local_experts, model_width)
    grads_in = arrived_grads.reshape(capacity, owners, local_experts, model_width)
    all_rows, all_grads = (
        lax.all_gather(routed, "tensor", axis=0, tiled=True),
        lax.all_gather(grads_in, "tensor", axis=0, tiled=True),
    )
    gate_pre = jnp.einsum("csld,ldf->cslf", all_rows, w_gate, preferred_element_type=jnp.float32)
    up_pre = jnp.einsum("csld,ldf->cslf", all_rows, w_up, preferred_element_type=jnp.float32)
    sigmoid_gate = jax.nn.sigmoid(gate_pre)
    silu_gate = gate_pre * sigmoid_gate
    activation = (silu_gate * up_pre).astype(jnp.bfloat16)
    grad_w_down = jnp.einsum(
        "cslf,csld->lfd", activation, all_grads, preferred_element_type=jnp.float32
    )
    grad_act = jnp.einsum("csld,lfd->cslf", all_grads, w_down, preferred_element_type=jnp.float32)
    grad_gate = (grad_act * up_pre * sigmoid_gate * (1.0 + gate_pre * (1.0 - sigmoid_gate))).astype(
        jnp.bfloat16
    )
    grad_up = (grad_act * silu_gate).astype(jnp.bfloat16)
    grad_w_gate = jnp.einsum(
        "csld,cslf->ldf", all_rows, grad_gate, preferred_element_type=jnp.float32
    )
    grad_w_up = jnp.einsum("csld,cslf->ldf", all_rows, grad_up, preferred_element_type=jnp.float32)
    forward_term = jnp.einsum(
        "cslf,lfd->csld", activation, w_down, preferred_element_type=jnp.float32
    )
    back_term = jnp.einsum("cslf,ldf->csld", grad_gate, w_gate, preferred_element_type=jnp.float32)
    back_term = back_term + jnp.einsum(
        "cslf,ldf->csld", grad_up, w_up, preferred_element_type=jnp.float32
    )
    both_terms = lax.psum_scatter(
        jnp.concatenate([forward_term, back_term], axis=3).astype(jnp.bfloat16),
        "tensor",
        scatter_dimension=0,
        tiled=True,
    )
    returned = both_terms[..., :model_width]
    row_grads = both_terms[..., model_width:]
    returned_home, row_grads_home = (
        lax.all_to_all(
            returned.reshape(capacity, expert_count, model_width),
            "expert",
            split_axis=1,
            concat_axis=1,
            tiled=True,
        ),
        lax.all_to_all(
            row_grads.reshape(capacity, expert_count, model_width),
            "expert",
            split_axis=1,
            concat_axis=1,
            tiled=True,
        ),
    )
    picked = returned_home.reshape(capacity * expert_count, model_width)[place].reshape(
        block_len, top_count, model_width
    )
    mixture = jnp.sum(gate_weights[:, :, None] * picked, axis=1)
    mixed_out = (middle + mixture).astype(jnp.bfloat16)
    grad_gates = jnp.sum(picked * grad_out[:, None, :], axis=2)
    grad_picked = row_grads_home.reshape(capacity * expert_count, model_width)[place].reshape(
        block_len, top_count, model_width
    )
    grad_hidden_disp = jnp.einsum(
        "lk,lkd->ld",
        jnp.ones((block_len, top_count), jnp.bfloat16),
        grad_picked,
        preferred_element_type=jnp.float32,
    )
    grad_chosen = gate_weights * (
        grad_gates - jnp.sum(gate_weights * grad_gates, axis=-1, keepdims=True)
    )
    grad_logits = jnp.sum(jnp.where(matches, grad_chosen[:, :, None], 0.0), axis=1).astype(
        jnp.bfloat16
    )
    grad_router = jnp.einsum(
        "ld,le->de", hidden_two, grad_logits, preferred_element_type=jnp.float32
    )
    grad_hidden_two = grad_hidden_disp + jnp.einsum(
        "le,de->ld", grad_logits, w_router, preferred_element_type=jnp.float32
    )
    grad_normed_two, grad_gain_moe = norm_backward(middle, inverse_two, gain_moe, grad_hidden_two)
    grad_middle = grad_out + grad_normed_two
    grad_attn = grad_middle.astype(jnp.bfloat16)
    grad_attn_all = lax.all_gather(grad_attn, "tensor", axis=0, tiled=True)
    grad_w_out = jnp.einsum(
        "lh,ld->hd", head_rows, grad_attn_all, preferred_element_type=jnp.float32
    )
    grad_heads = jnp.einsum(
        "ld,hd->lh", grad_attn_all, w_out, preferred_element_type=jnp.float32
    ).astype(jnp.bfloat16)
    grad_blocks = grad_heads.reshape(block_count, block_rows, local_groups, group_size, HD)

    def back_block(carried, packed):
        grad_keys, grad_values = carried
        first_row, q_block, g_block, lse_block = packed
        scores = block_scores(q_block, key_rows, first_row, score_scale)
        probability = jnp.exp(scores - lse_block[..., None])
        grad_values = grad_values + jnp.einsum(
            "grqk,qgrd->kgd",
            probability.astype(jnp.bfloat16),
            g_block,
            preferred_element_type=jnp.float32,
        )
        grad_prob = jnp.einsum(
            "qgrd,kgd->grqk", g_block, value_rows, preferred_element_type=jnp.float32
        )
        row_delta = jnp.sum(probability * grad_prob, axis=-1, keepdims=True)
        grad_scores = (probability * (grad_prob - row_delta)).astype(jnp.bfloat16)
        grad_query = (
            jnp.einsum("grqk,kgd->qgrd", grad_scores, key_rows, preferred_element_type=jnp.float32)
            * score_scale
        )
        grad_keys = (
            grad_keys
            + jnp.einsum("grqk,qgrd->kgd", grad_scores, q_block, preferred_element_type=jnp.float32)
            * score_scale
        )
        return ((grad_keys, grad_values), grad_query)

    zero_keys = jnp.zeros((seq_length, local_groups, HD), jnp.float32)
    (grad_keys, grad_values), grad_query_blocks = lax.scan(
        back_block, (zero_keys, zero_keys), (starts, query_blocks, grad_blocks, log_totals)
    )
    grad_query = grad_query_blocks.reshape(seq_length, local_heads, HD)
    grad_query_raw = (
        jax.vjp(rope_heads, query_raw)[1](grad_query)[0]
        .reshape(seq_length, local_heads * HD)
        .astype(jnp.bfloat16)
    )
    grad_key_raw = (
        jax.vjp(rope_heads, key_raw)[1](grad_keys)[0]
        .reshape(seq_length, local_groups * HD)
        .astype(jnp.bfloat16)
    )
    grad_value_raw = grad_values.reshape(seq_length, local_groups * HD).astype(jnp.bfloat16)
    grad_w_query = jnp.einsum(
        "ld,lh->dh", hidden_one, grad_query_raw, preferred_element_type=jnp.float32
    )
    grad_w_key = jnp.einsum(
        "ld,lh->dh", hidden_one, grad_key_raw, preferred_element_type=jnp.float32
    )
    grad_w_value = jnp.einsum(
        "ld,lh->dh", hidden_one, grad_value_raw, preferred_element_type=jnp.float32
    )
    term = jnp.einsum("lh,dh->ld", grad_query_raw, w_query, preferred_element_type=jnp.float32)
    term = term + jnp.einsum("lh,dh->ld", grad_key_raw, w_key, preferred_element_type=jnp.float32)
    grad_hidden_one = lax.psum_scatter(
        (
            term
            + jnp.einsum("lh,dh->ld", grad_value_raw, w_value, preferred_element_type=jnp.float32)
        ).astype(jnp.bfloat16),
        "tensor",
        scatter_dimension=0,
        tiled=True,
    ).astype(jnp.float32)
    grad_normed_one, grad_gain_attn = norm_backward(
        own_inputs, own_inverse, gain_attn, grad_hidden_one
    )
    grad_tokens = grad_middle + grad_normed_one
    attn_sums = lax.psum((grad_w_query, grad_w_key, grad_w_value, grad_w_out), "expert")
    small_sums = lax.psum((grad_gain_attn, grad_gain_moe, grad_router), ("expert", "tensor"))
    return (
        mixed_out,
        grad_tokens,
        small_sums[0],
        attn_sums[0],
        attn_sums[1],
        attn_sums[2],
        attn_sums[3],
        small_sums[1],
        small_sums[2],
        grad_w_gate,
        grad_w_up,
        grad_w_down,
    )


ROWS_ROWS = (((1,), (1,)), ((), ()))
def dot_nt(left, right):
    return lax.dot_general(left, right, ROWS_ROWS, preferred_element_type=jnp.float32)


def dot_nn(left, right):
    return jnp.dot(left, right, preferred_element_type=jnp.float32)


def expert_kernel(places, top_count, *refs):
    row_places, grad_places = places
    given = 1 + max(place[0] for place in row_places + grad_places)
    numbers_ref, router_ref, gate_ref, up_ref, down_ref = refs[given : given + 5]
    outs = refs[given + 5 : given + 14]
    mixed_refs, back_refs, sums_ref = outs[:2], outs[2:4], outs[4]
    rows_s, grads_s, ids_s, x_s, y_s, back_s, out_s = refs[given + 14 : given + 21]
    pick_s, place_s, gates_s, sums_s, gated_s, side_s = refs[given + 21 : given + 27]
    both_s, down_s, sems, weight_sems, out_sems, kept_sems = refs[given + 27 :]
    pairs, wide, _ = pick_s.shape
    experts = x_s.shape[0]
    hidden = down_s.shape[1]
    cap = wide // experts
    tokens_in, width = rows_s.shape[1:]
    block_len = tokens_in // 2
    narrow = jnp.bfloat16

    def copies(pair):
        out = []
        for half in range(2):
            target = pl.ds(half * block_len, block_len)
            at = 2 * pair + half
            array, row, column = row_places[at]
            rows = refs[array].at[pl.ds(row, block_len), pl.ds(column, width)]
            array, row, column = grad_places[at]
            block = refs[array].at[pl.ds(row, block_len)]
            grads = block.at[:, pl.ds(column, width)]
            ids = block.at[:, pl.ds(column + width, LANES)]
            for k, (source, scratch) in enumerate(
                ((rows, rows_s), (grads, grads_s), (ids, ids_s))
            ):
                out.append(
                    pltpu.make_async_copy(source, scratch.at[pair, target], sems.at[k, at])
                )
        return out

    def weight_copies(expert, slot):
        sides = [both_s.at[slot, :, pl.ds(k * hidden, hidden)] for k in range(2)]
        return [
            pltpu.make_async_copy(gate_ref.at[expert], sides[0], weight_sems.at[0, slot]),
            pltpu.make_async_copy(up_ref.at[expert], sides[1], weight_sems.at[1, slot]),
            pltpu.make_async_copy(down_ref.at[expert], down_s.at[slot], weight_sems.at[2, slot]),
        ]

    def result_copies(pair):
        half = pairs // 2
        place = pl.ds((pair % half) * tokens_in, tokens_in)
        sides = (rows_s, mixed_refs), (grads_s, back_refs)
        return [
            pltpu.make_async_copy(
                source.at[pair], targets[pair // half].at[place], out_sems.at[k, pair]
            )
            for k, (source, targets) in enumerate(sides)
        ]

    kept_copies = [
        pltpu.make_async_copy(source, target, kept_sems.at[k])
        for k, (source, target) in enumerate(zip((x_s, y_s, gated_s, side_s), outs[5:9]))
    ]

    for pair in range(pairs):
        for copy in copies(pair):
            copy.start()
    for slot in range(WEIGHT_SLOTS):
        for copy in weight_copies(slot, slot):
            copy.start()

    earlier = lax.broadcasted_iota(jnp.int32, (tokens_in, tokens_in), 0)
    later = lax.broadcasted_iota(jnp.int32, (tokens_in, tokens_in), 1)
    before = jnp.where(earlier < later, 1.0, 0.0).astype(narrow)

    for pair in range(pairs):
        for copy in copies(pair):
            copy.wait()
        rows_in = rows_s[pair]
        logits = dot_nt(router_ref[...], rows_in)
        ids = ids_s[pair].astype(jnp.float32).T
        named = jnp.zeros(logits.shape, jnp.float32)
        for k in range(top_count):
            named = jnp.where(ids[k : k + 1, :] == numbers_ref[:, :1], 1.0, named)
        hits = named[:experts]
        slots = jnp.where(hits > 0.0, dot_nn(hits.astype(narrow), before), -1.0)
        slots = slots.astype(jnp.int32)
        logits = jnp.where(named > 0.0, logits, masked)
        weights = jnp.exp(logits - jnp.max(logits, axis=0, keepdims=True)) * named
        gates = weights / jnp.sum(weights, axis=0, keepdims=True)
        ranks = lax.broadcasted_iota(jnp.int32, (cap, tokens_in), 0)
        place = pl.ds(pair * cap, cap)
        picks = []
        for expert in range(experts):
            pick = ranks == slots[expert : expert + 1, :]
            row_gates = jnp.sum(
                jnp.where(pick, gates[expert : expert + 1, :], 0.0), axis=1, keepdims=True
            )
            gates_s[expert, place, :] = jnp.broadcast_to(row_gates, (cap, LANES))
            picks.append(jnp.where(pick, 1.0, 0.0))
        pick_all = jnp.concatenate(picks, axis=0)
        pick_low = pick_all.astype(narrow)
        pick_s[pair] = pick_low
        place_s[pair] = pick_all.T.astype(narrow)
        for source, target in ((rows_in, x_s), (grads_s[pair], y_s)):
            spread = dot_nn(pick_low, source).astype(narrow)
            for expert in range(experts):
                target[expert, place, :] = spread[expert * cap : (expert + 1) * cap]

    kept_copies[0].start()
    kept_copies[1].start()

    def expert_step(expert, carried):
        slot = lax.rem(expert, WEIGHT_SLOTS)
        for copy in weight_copies(expert, slot):
            copy.wait()
        both = dot_nn(x_s[expert], both_s[slot])
        gate_pre, up_pre = both[:, :hidden], both[:, hidden:]
        plain = dot_nt(y_s[expert], down_s[slot])
        sigmoid_gate = jax.nn.sigmoid(gate_pre)
        silu_gate = gate_pre * sigmoid_gate
        activation = silu_gate * up_pre
        row_gates = gates_s[expert][:, :1]
        sums = jnp.sum(activation * plain, axis=1, keepdims=True)
        sums_s[expert] = jnp.broadcast_to(sums, sums_s.shape[1:])
        grad_act = row_gates * plain
        gated = (row_gates * activation).astype(narrow)
        slope = sigmoid_gate * (1.0 + gate_pre * (1.0 - sigmoid_gate))
        grad_gate = (grad_act * up_pre * slope).astype(narrow)
        grad_up = (grad_act * silu_gate).astype(narrow)
        grad_both = jnp.concatenate([grad_gate, grad_up], axis=1)
        gated_s[expert] = gated
        side_s[expert] = grad_both
        out_s[expert] = dot_nn(gated, down_s[slot]).astype(narrow)
        back_s[expert] = dot_nt(grad_both, both_s[slot]).astype(narrow)

        @pl.when(expert + WEIGHT_SLOTS < experts)
        def _():
            for copy in weight_copies(expert + WEIGHT_SLOTS, slot):
                copy.start()

        return carried

    lax.fori_loop(0, experts, expert_step, 0)
    kept_copies[2].start()
    kept_copies[3].start()

    for pair in range(pairs):
        sides = pl.ds(pair * cap, cap)
        for source, target in ((out_s, rows_s), (back_s, grads_s)):
            stacked = jnp.concatenate(
                [source[expert, sides, :] for expert in range(experts)], axis=0
            )
            target[pair] = dot_nn(place_s[pair], stacked).astype(narrow)
        for copy in result_copies(pair):
            copy.start()
        pick = pick_s[pair].astype(jnp.float32)
        sums = []
        for expert in range(experts):
            column = sums_s[expert, sides, :][:, :1]
            part = pick[expert * cap : (expert + 1) * cap] * column
            sums.append(jnp.sum(part, axis=0, keepdims=True))
        sums_ref[pair] = jnp.concatenate(sums, axis=0)

    for copy in kept_copies:
        copy.wait()
    for pair in range(pairs):
        for copy in result_copies(pair):
            copy.wait()


def expert_chunk(arrays, places, numbers, router, w_gate, w_up, w_down, tokens_in, top_count, cap):
    experts, width, hidden = w_gate.shape
    pairs = BLOCKS // 2
    rows = pairs * cap
    narrow, wide = jnp.bfloat16, jnp.float32
    shape = jax.ShapeDtypeStruct
    anywhere = pl.BlockSpec(memory_space=pl.ANY)
    inside = pl.BlockSpec(memory_space=pltpu.VMEM)
    half_shape = shape((pairs // 2 * tokens_in, width), narrow)
    whole_rows = (experts, rows, width)
    return pl.pallas_call(
        functools.partial(expert_kernel, places, top_count),
        in_specs=[anywhere] * len(arrays) + [inside] * 2 + [anywhere] * 3,
        out_specs=[anywhere] * 4 + [inside] + [anywhere] * 4,
        out_shape=[half_shape] * 4
        + [
            shape((pairs, experts, tokens_in), wide),
            shape(whole_rows, narrow),
            shape(whole_rows, narrow),
            shape((experts, rows, hidden), narrow),
            shape((experts, rows, 2 * hidden), narrow),
        ],
        scratch_shapes=[pltpu.VMEM((pairs, tokens_in, width), narrow)] * 2
        + [pltpu.VMEM((pairs, tokens_in, LANES), narrow)]
        + [pltpu.VMEM(whole_rows, narrow)] * 4
        + [
            pltpu.VMEM((pairs, experts * cap, tokens_in), narrow),
            pltpu.VMEM((pairs, tokens_in, experts * cap), narrow),
            pltpu.VMEM((experts, rows, LANES), wide),
            pltpu.VMEM((experts, rows, LANES), wide),
            pltpu.VMEM((experts, rows, hidden), narrow),
            pltpu.VMEM((experts, rows, 2 * hidden), narrow),
            pltpu.VMEM((WEIGHT_SLOTS, width, 2 * hidden), narrow),
            pltpu.VMEM((WEIGHT_SLOTS, hidden, width), narrow),
            pltpu.SemaphoreType.DMA((3, BLOCKS)),
            pltpu.SemaphoreType.DMA((3, WEIGHT_SLOTS)),
            pltpu.SemaphoreType.DMA((2, pairs)),
            pltpu.SemaphoreType.DMA((4,)),
        ],
        compiler_params=pltpu.CompilerParams(vmem_limit_bytes=60 << 20),
        cost_estimate=pl.CostEstimate(
            flops=24 * experts * rows * width * hidden,
            bytes_accessed=6 * experts * width * hidden + 4 * experts * rows * width,
            transcendentals=experts * rows * hidden,
        ),
    )(*arrays, numbers, router, w_gate, w_up, w_down)


def weight_kernel(parts, given, *refs):
    ins, (gate_ref, up_ref, down_ref) = refs[: 4 * parts], refs[4 * parts + given :]
    rows, grads, gated, both = [
        jnp.concatenate([ref[0] for ref in ins[k * parts : (k + 1) * parts]], axis=0)
        for k in range(4)
    ]
    turn = (((0,), (0,)), ((), ()))
    hidden = gated.shape[1]
    down_ref[0] = lax.dot_general(gated, grads, turn, preferred_element_type=jnp.float32)
    sides = lax.dot_general(rows, both, turn, preferred_element_type=jnp.float32)
    gate_ref[0] = sides[:, :hidden]
    up_ref[0] = sides[:, hidden:]


def weight_grads(kept, begin, count, partial):
    parts = len(kept)
    experts, rows, width = kept[0][0].shape
    hidden = kept[0][2].shape[2]
    operands = [part[k] for k in range(4) for part in kept]
    shape = jax.ShapeDtypeStruct

    def spec(rows, columns):
        return pl.BlockSpec((1, rows, columns), lambda i: (i + begin, 0, 0))

    return pl.pallas_call(
        functools.partial(weight_kernel, parts, len(partial)),
        grid=(count,),
        in_specs=[spec(rows, operand.shape[2]) for operand in operands]
        + [pl.BlockSpec(memory_space=pl.ANY)] * len(partial),
        out_specs=[spec(width, hidden), spec(width, hidden), spec(hidden, width)],
        out_shape=[
            shape((experts, width, hidden), jnp.float32),
            shape((experts, width, hidden), jnp.float32),
            shape((experts, hidden, width), jnp.float32),
        ],
        input_output_aliases={len(operands) + k: k for k in range(len(partial))},
        compiler_params=pltpu.CompilerParams(vmem_limit_bytes=56 << 20),
        cost_estimate=pl.CostEstimate(
            flops=6 * parts * count * rows * width * hidden,
            bytes_accessed=count * (parts * rows * (4 * width + 6 * hidden) + 12 * width * hidden),
            transcendentals=0,
        ),
    )(*operands, *partial)


def gathered_layer(
    tokens,
    gain_attn,
    w_query,
    w_key,
    w_value,
    w_out,
    gain_moe,
    w_router,
    w_gate,
    w_up,
    w_down,
    expert_ids,
    cotangent,
):
    seq_length, model_width = tokens.shape
    block_len, top_count = expert_ids.shape
    expert_count = w_router.shape[1]
    local_experts = w_gate.shape[0]
    local_heads = w_query.shape[1] // HD
    quarters = lax.axis_size("tensor")
    device_count = quarters * lax.axis_size("expert")
    quarter = lax.axis_index("tensor").astype(jnp.uint32)
    device = lax.axis_index(BOTH).astype(jnp.uint32)
    first_expert = lax.axis_index("expert") * local_experts
    pair_cap = 2 * (3 * block_len * top_count // (2 * expert_count))
    score_scale = HD ** (-0.5)
    narrow, wide = jnp.bfloat16, jnp.float32

    def swap(value, even, odd=None):
        odd = even if odd is None else odd
        perm = [(i, i ^ (odd if i & 1 else even)) for i in range(device_count)]
        return lax.ppermute(value, BOTH, perm)

    def near(value):
        return swap(value, ACROSS, ASIDE)

    def far(value):
        return swap(value, ASIDE, ACROSS)

    def core(value):
        return swap(value, CORE)

    def add(left, right):
        return (left.astype(wide) + right.astype(wide)).astype(narrow)

    live = {}

    def sync():
        keys = list(live)
        values = lax.optimization_barrier([live[key] for key in keys])
        live.update(zip(keys, values))

    def gather_near(name, plane):
        live[name, plane, 1] = near(live[name, plane, 0])
        live[name, plane, 2] = far(live[name, plane, 0])

    def gather_far(name, plane):
        live[name, plane, 3] = far(live[name, plane, 1])

    def gather_across(name, plane):
        live[name, plane, 3] = swap(live[name, plane, 0], ACROSS | ASIDE)

    def join_core(name, plane, *slots):
        blocks = [live[name, plane, slot] for slot in slots]
        live[name, plane, (OTHER,) + slots] = jnp.concatenate(blocks, axis=0)

    def send_core(name, plane, *slots):
        live[name, plane, (OTHER,) + slots] = core(live[name, plane, (OTHER,) + slots])

    def gather_core(name, plane, *slots):
        join_core(name, plane, *slots)
        send_core(name, plane, *slots)

    def blocks_of(name, plane):
        found = {}
        for key in list(live):
            if isinstance(key, tuple) and key[:2] == (name, plane):
                slots = key[2]
                array = live.pop(key)
                if isinstance(slots, tuple):
                    for i, slot in enumerate(slots[1:]):
                        found[4 + slot] = (array, i * block_len)
                else:
                    found[slots] = (array, 0)
        return [found[slot] for slot in range(BLOCKS)]

    def reduce_core(name, plane):
        live[name, plane, OTHER] = core(live.pop((name, plane, AWAY)))

    def add_far(name, plane):
        kept = live[name, plane, NEAR].reshape(4, block_len, model_width)
        got = live[name, plane, OTHER].reshape(4, block_len, model_width)
        live[name, plane, FAR] = add(kept[2:], got[2:])

    def send_far(name, plane):
        live[name, plane, FAR] = far(live[name, plane, FAR])

    def reduce_far(name, plane):
        add_far(name, plane)
        send_far(name, plane)

    def add_near(name, plane):
        kept = live.pop((name, plane, NEAR)).reshape(4, block_len, model_width)
        got = live.pop((name, plane, OTHER)).reshape(4, block_len, model_width)
        back = live.pop((name, plane, FAR))
        sums = [
            kept[i].astype(wide) + got[i].astype(wide) + back[i].astype(wide) for i in range(2)
        ]
        live[name, plane, OWN], live[name, plane, SIDE] = [part.astype(narrow) for part in sums]

    def send_near(name, plane):
        live[name, plane, SIDE] = near(live[name, plane, SIDE])

    def reduce_near(name, plane):
        add_near(name, plane)
        send_near(name, plane)

    def reduced(name, plane):
        return add(live.pop((name, plane, OWN)), live.pop((name, plane, SIDE)))

    def bit(mask):
        return (device // mask) % 2

    odd_core = bit(CORE)
    weight_hops = ((ASIDE, PLANE_NEXT), (PLANE_NEXT, ASIDE), (PLANE_FAR, PLANE_FAR))
    small_hops = tuple((mask, mask) for mask in (CORE, ACROSS, ASIDE, PLANE_NEXT, PLANE_FAR))

    def joined(own, got, side):
        first, second = jnp.where(side == 0, own, got), jnp.where(side == 0, got, own)
        return jnp.concatenate([first, second], axis=0)

    def sum_step(name, step, hops=weight_hops, sent_as=narrow):
        count = len(hops)
        sides = [jnp.where(odd_core == 0, bit(even), bit(odd)) for even, odd in hops]
        if step == 0:
            kept = live.pop((name, FULL))
        elif step <= count:
            kept = live.pop((name, KEPT)) + live.pop((name, GOT)).astype(wide)
        else:
            kept = joined(live.pop((name, KEPT)), live.pop((name, GOT)), sides[2 * count - step])
        if step < count:
            half = kept.shape[0] // 2
            side = sides[step]
            live[name, KEPT] = lax.dynamic_slice_in_dim(kept, side * half, half, 0)
            sent = lax.dynamic_slice_in_dim(kept, (1 - side) * half, half, 0)
            live[name, GOT] = swap(sent.astype(sent_as), *hops[step])
        else:
            kept = kept.astype(sent_as)
            live[name, KEPT] = kept
            live[name, GOT] = swap(kept, *hops[2 * count - 1 - step])

    def summed(name, hops=weight_hops):
        even, odd = hops[0]
        side = jnp.where(odd_core == 0, bit(even), bit(odd))
        return joined(live.pop((name, KEPT)), live.pop((name, GOT)), side).astype(wide)

    own, nxt, far_plane, last = PLANES

    named_ids = jnp.pad(expert_ids.astype(narrow), ((0, 0), (0, LANES - top_count)))
    live[G, own, 0] = jnp.concatenate([cotangent, named_ids], axis=1)
    half_block = block_len // 2
    live[G, nxt, 0] = swap(live[G, own, 0], nxt)
    live[G, far_plane, 0] = [swap(live[G, own, 0][:half_block], far_plane)]
    gather_near(G, own)

    by_block = tokens.reshape(quarters, block_len, model_width)
    inputs = jnp.concatenate(
        [lax.dynamic_slice_in_dim(by_block, quarter ^ r, 1, 0)[0] for r in range(quarters)], axis=0
    )
    inputs = lax.optimization_barrier(inputs)
    order = quarter.astype(jnp.int32) ^ jnp.arange(quarters, dtype=jnp.int32)
    positions = (order[:, None] * block_len + jnp.arange(block_len, dtype=jnp.int32)).reshape(-1)
    inverse_one, normed_one = norm_forward(inputs.astype(wide), gain_attn)
    hidden_one = normed_one.astype(narrow)
    frequency = jnp.exp(
        -jnp.log(theta_base) * jnp.arange(HD // 2, dtype=jnp.float32) * (2.0 / HD)
    )
    angles = positions.astype(wide)[:, None] * frequency[None, :]
    cosine_table, sine_table = (jnp.cos(angles)[:, None, :], jnp.sin(angles)[:, None, :])

    def project(weights):
        return jnp.dot(hidden_one, weights, preferred_element_type=wide).reshape(
            seq_length, local_heads, HD
        )

    live[QUERIES] = rotate(project(w_query), cosine_table, sine_table).astype(narrow)
    live[KEYS] = rotate(project(w_key), cosine_table, sine_table).astype(narrow)
    live[VALUES] = project(w_value).astype(narrow)
    sync()

    gather_far(G, own)
    gather_near(G, nxt)
    live[G, far_plane, 0] = live[G, far_plane, 0] + [
        swap(live[G, own, 0][half_block:], far_plane)
    ]
    allowed = positions[:, None] >= positions[None, :]

    def masked_scores():
        scores = jnp.einsum(
            "qhd,khd->hqk", live[QUERIES], live[KEYS], preferred_element_type=wide
        )
        return jnp.where(allowed, scores * score_scale, masked)

    scores = masked_scores()
    row_max = jnp.max(scores, axis=-1, keepdims=True)
    exponent = jnp.exp(scores - row_max)
    row_total = jnp.sum(exponent, axis=-1, keepdims=True)
    weights = (exponent / row_total).astype(narrow)
    head_out = jnp.einsum("hqk,khd->qhd", weights, live[VALUES], preferred_element_type=wide)
    live[TOTALS] = row_max + jnp.log(row_total)
    live[HEADS] = head_out.astype(narrow).reshape(seq_length, local_heads * HD)

    def split_quarters(full):
        parts = full.reshape(quarters, block_len, model_width)
        live[KEPT] = [parts[0], parts[2]]
        live[SENT] = jnp.stack([parts[1], parts[3]]).astype(narrow)

    split_quarters(jnp.dot(live[HEADS], w_out, preferred_element_type=wide))
    sync()

    expert_range = jnp.arange(expert_count, dtype=jnp.int32)
    rolled = (first_expert + expert_range) % expert_count
    live[ROUTER] = jnp.take(w_router.T, rolled, axis=0)
    live[NAMED] = jnp.broadcast_to(rolled.astype(wide)[:, None], (expert_count, LANES))
    live[SENT] = core(live[SENT])
    gather_far(G, nxt)
    live[G, far_plane, 0] = jnp.concatenate(live[G, far_plane, 0], axis=0)
    sync()

    def cross_quarters():
        kept, sent = live.pop(KEPT), live.pop(SENT).astype(wide)
        live[KEPT] = kept[0] + sent[0]
        live[SENT] = swap((kept[1] + sent[1]).astype(narrow), ACROSS)

    def quarter_sum():
        return live.pop(KEPT) + live.pop(SENT).astype(wide)

    cross_quarters()
    live[G, last, 0] = swap(live[G, far_plane, 0], nxt)
    sync()

    own_inputs = inputs[:block_len].astype(wide)
    own_inverse = inverse_one[:block_len]
    middle = own_inputs + quarter_sum()
    inverse_two, normed_two = norm_forward(middle, gain_moe)
    hidden_two = normed_two.astype(narrow)
    live[H, own, 0] = hidden_two

    gather_near(H, own)
    live[H, nxt, 0] = swap(hidden_two, nxt)
    logits = jnp.dot(hidden_two, w_router, preferred_element_type=wide)
    expert_range = jnp.arange(expert_count, dtype=jnp.int32)
    matches = expert_ids[:, :, None] == expert_range[None, None, :]
    chosen = jnp.sum(jnp.where(matches, logits[:, None, :], 0.0), axis=2)
    gate_weights = jax.nn.softmax(chosen, axis=-1)
    sync()

    gather_far(H, own)
    gather_near(H, nxt)
    hidden_two = live[H, own, 0]
    gather_core(G, own, 0, 1, 2, 3)
    live[H, last, 0] = [swap(hidden_two[:half_block], last)]
    sync()

    gather_far(H, nxt)
    gather_core(H, own, 0, 1, 2, 3)
    gather_core(G, nxt, 0, 1, 2, 3)
    hidden_two = live[H, own, 0]
    live[H, last, 0] = live[H, last, 0] + [swap(hidden_two[half_block:], last)]
    sync()

    def join_pair(plane):
        rows, grads = [live.pop((name, plane, 0)) for name in (H, G)]
        if isinstance(rows, list):
            rows = jnp.concatenate(rows, axis=0)
        after, ahead = grads.shape[1], rows.shape[1]
        pair = jnp.pad(rows, ((0, 0), (0, after))) + jnp.pad(grads, ((0, 0), (ahead, 0)))
        live[PAIR, plane, 0] = pair

    def experts(plane):
        if (PAIR, plane, 0) in live:
            rows = blocks_of(PAIR, plane)
            grads, column = rows, model_width
        else:
            rows, grads, column = blocks_of(H, plane), blocks_of(G, plane), 0
        arrays = []
        for array, _ in rows + grads:
            if not any(array is other for other in arrays):
                arrays.append(array)

        def placed(blocks, column):
            indices = [[array is other for other in arrays].index(True) for array, _ in blocks]
            return [(index, row, column) for index, (_, row) in zip(indices, blocks)]

        done = expert_chunk(
            arrays,
            (placed(rows, 0), placed(grads, column)),
            live[NAMED],
            live[ROUTER],
            w_gate,
            w_up,
            w_down,
            2 * block_len,
            top_count,
            pair_cap,
        )
        live[M, plane, NEAR], live[M, plane, AWAY] = done[:2]
        live[R, plane, NEAR], live[R, plane, AWAY] = done[2:4]
        live[SUMS, plane] = done[4]
        live[KEPT, plane] = done[5:]

    gather_core(H, nxt, 0, 1, 2, 3)
    join_pair(last)
    gather_near(PAIR, last)
    gather_core(PAIR, last, 0)
    live[H, far_plane, 0] = swap(live[H, own, 0], far_plane)
    experts(own)
    sync()

    gather_far(PAIR, last)
    gather_core(PAIR, last, 1, 2)
    join_pair(far_plane)
    gather_near(PAIR, far_plane)
    reduce_core(R, own)
    experts(nxt)
    sync()
    gather_core(PAIR, last, 3)
    join_core(PAIR, far_plane, 0, 1, 2)
    add_far(R, own)
    sync()

    gather_far(PAIR, far_plane)
    send_core(PAIR, far_plane, 0, 1, 2)
    send_far(R, own)
    reduce_core(R, nxt)
    reduce_core(M, own)
    experts(last)
    sync()
    gather_core(PAIR, far_plane, 3)
    reduce_core(R, last)
    add_near(R, own)
    add_far(R, nxt)
    sync()

    send_near(R, own)
    send_far(R, nxt)
    reduce_far(R, last)
    reduce_core(M, nxt)
    experts(far_plane)
    sync()

    part_experts = local_experts // 4

    def some_weight_grads(part):
        kept = [live[KEPT, plane] for plane in PLANES]
        live[EXPERTS] = weight_grads(kept, part * part_experts, part_experts, live.get(EXPERTS, []))

    reduce_core(R, far_plane)
    sums = jnp.stack([live.pop((SUMS, plane)) for plane in PLANES])
    sums = sums.reshape(len(PLANES), -1, local_experts, 2, block_len).transpose(0, 1, 3, 2, 4)
    sums = sums.reshape(len(PLANES), BLOCKS, local_experts, block_len)
    live[GATES] = [sums[:, :4], core(sums[:, 4:])]
    reduce_core(M, last)
    add_near(R, last)
    sync()

    reduce_far(R, far_plane)
    send_near(R, last)
    add_near(R, nxt)
    live[HOME] = reduced(R, own)
    sums = live[GATES][0] + live[GATES][1]
    crossed = jnp.stack([sums[:, 0], sums[:, 2], sums[:, 1], sums[:, 3]], axis=1)
    sums = jnp.where(odd_core == 0, sums, crossed)
    sums = sums[:, ::2] + swap(sums[:, 1::2], ACROSS)
    live[GATES] = [sums[:, 0], swap(sums[:, 1], ASIDE)]
    sync()

    live[RELAY] = swap(reduced(R, last), nxt)
    reduce_near(R, far_plane)
    sums = jnp.stack(live[GATES], axis=1)
    live[GATES] = [sums[::2], swap(sums[1::2], nxt)]
    send_near(R, nxt)
    add_far(M, nxt)
    add_far(M, last)
    sync()

    live[RELAY] = swap(add(reduced(R, far_plane), live[RELAY]), far_plane)
    live[SIDE] = swap(reduced(R, nxt), nxt)
    send_far(M, nxt)
    send_far(M, last)
    reduce_core(M, far_plane)
    sums = jnp.stack(live.pop(GATES), axis=1)
    sums = jnp.concatenate([sums[0], swap(sums[1], far_plane)], axis=0)
    sums = sums.reshape(-1, local_experts, block_len)
    owner = lax.axis_index("expert").astype(jnp.uint32)
    sums = [lax.dynamic_slice_in_dim(sums, owner ^ r, 1, 0)[0] for r in range(sums.shape[0])]
    own_sums = jnp.concatenate(sums, axis=0).T
    grad_gates = jnp.sum(jnp.where(matches, own_sums[:, None, :], 0.0), axis=2)
    grad_chosen = gate_weights * (
        grad_gates - jnp.sum(gate_weights * grad_gates, axis=-1, keepdims=True)
    )
    grad_logits = jnp.sum(jnp.where(matches, grad_chosen[:, :, None], 0.0), axis=1).astype(narrow)
    grad_router = jnp.einsum("ld,le->de", hidden_two, grad_logits, preferred_element_type=wide)
    live[GATES] = jnp.einsum("le,de->ld", grad_logits, w_router, preferred_element_type=wide)
    live[SMALL] = grad_router
    sync()

    grad_hidden_two = live.pop(HOME).astype(wide) + live.pop(RELAY).astype(wide)
    grad_hidden_two = grad_hidden_two + live.pop(SIDE).astype(wide) + live.pop(GATES)
    grad_out = cotangent.astype(wide)
    grad_normed_two, grad_gain_moe = norm_backward(middle, inverse_two, gain_moe, grad_hidden_two)
    grad_middle = grad_out + grad_normed_two
    grad_attn = grad_middle.astype(narrow)

    small = jnp.concatenate([live.pop(SMALL), grad_gain_moe[:, None]], axis=1)
    live[SMALL, FULL] = small.reshape(device_count, -1, small.shape[1])
    small_step = functools.partial(sum_step, SMALL, hops=small_hops, sent_as=wide)

    live[ATTN] = [grad_attn, core(grad_attn), swap(grad_attn, ACROSS)]
    small_step(0)
    add_near(M, nxt)
    add_near(M, last)
    sync()
    live[ATTN] = live[ATTN] + [core(live[ATTN][2])]
    sync()

    grad_attn_all = jnp.stack(live.pop(ATTN)).reshape(seq_length, model_width)
    live[OUT, FULL] = jnp.einsum(
        "lh,ld->hd", live[HEADS], grad_attn_all, preferred_element_type=wide
    )
    grad_heads = (
        jnp.einsum("ld,hd->lh", grad_attn_all, w_out, preferred_element_type=wide)
        .astype(narrow)
        .reshape(seq_length, local_heads, HD)
    )
    live[RAW] = grad_heads
    sync()

    grad_heads = live.pop(RAW)
    sum_step(OUT, 0)
    send_near(M, nxt)
    probability = jnp.exp(masked_scores() - live[TOTALS])
    grad_values = jnp.einsum(
        "hqk,qhd->khd", probability.astype(narrow), grad_heads, preferred_element_type=wide
    )
    grad_prob = jnp.einsum("qhd,khd->hqk", grad_heads, live[VALUES], preferred_element_type=wide)
    row_delta = jnp.sum(probability * grad_prob, axis=-1, keepdims=True)
    grad_scores = (probability * (grad_prob - row_delta)).astype(narrow)
    grad_query = score_scale * jnp.einsum(
        "hqk,khd->qhd", grad_scores, live[KEYS], preferred_element_type=wide
    )
    grad_keys = score_scale * jnp.einsum(
        "hqk,qhd->khd", grad_scores, live[QUERIES], preferred_element_type=wide
    )

    def flat(source):
        return source.astype(narrow).reshape(seq_length, local_heads * HD)

    live[RAW] = [
        flat(rotate(grad_query, cosine_table, -sine_table)),
        flat(rotate(grad_keys, cosine_table, -sine_table)),
        flat(grad_values),
    ]
    flying = live.pop((OUT, GOT))
    sync()
    live[OUT, GOT] = flying

    def back(grad_raw, weights):
        return jnp.einsum("lh,dh->ld", grad_raw, weights, preferred_element_type=wide)

    raw = live.pop(RAW)
    partial = back(raw[0], w_query) + back(raw[1], w_key) + back(raw[2], w_value)
    split_quarters(partial)
    live[GAIN] = partial
    live[IN, FULL] = jnp.einsum(
        "ld,lh->dh", hidden_one, jnp.concatenate(raw, axis=1), preferred_element_type=wide
    )
    sum_step(OUT, 1)
    small_step(1)
    small_step(2)
    live[MIXED] = swap(reduced(M, nxt), nxt)
    sync()

    live[SENT] = core(live[SENT])
    sum_step(IN, 0)
    sum_step(OUT, 2)
    some_weight_grads(0)
    gain = jnp.sum(live.pop(GAIN) * inputs.astype(wide) * inverse_one, axis=0)
    live[GAIN] = [gain[None], jnp.zeros_like(gain)[None]]

    def gain_step(step):
        live[GAIN] = [live[GAIN][0] + live[GAIN][1]]
        live[GAIN] = live[GAIN] + [swap(live[GAIN][0], *small_hops[step])]

    small_step(3)
    gain_step(0)
    add_far(M, far_plane)
    add_far(M, own)
    sync()

    sum_step(IN, 1)
    cross_quarters()
    sum_step(OUT, 3)
    small_step(4)
    small_step(5)
    gain_step(1)
    some_weight_grads(1)
    sync()

    sum_step(IN, 2)
    own_grad = quarter_sum()
    grad_normed_one = norm_backward(own_inputs, own_inverse, gain_attn, own_grad)[0]
    live[TOKENS] = grad_middle + grad_normed_one
    sum_step(OUT, 4)
    small_step(6)
    send_near(M, last)
    send_far(M, far_plane)
    some_weight_grads(2)
    sync()

    sum_step(IN, 3)
    sum_step(OUT, 5)
    small_step(7)
    live[RELAY] = swap(reduced(M, last), nxt)
    reduce_near(M, far_plane)
    send_far(M, own)
    some_weight_grads(3)
    sync()
    for plane in PLANES:
        live.pop((KEPT, plane))

    sum_step(IN, 4)
    live[OUT] = summed(OUT)
    live[RELAY] = swap(add(reduced(M, far_plane), live[RELAY]), far_plane)
    reduce_near(M, own)
    small_step(8)
    small_step(9)
    gain_step(2)
    sync()

    columns = local_heads * HD
    sum_step(IN, 5)
    gain_step(3)
    gain_step(4)
    small = summed(SMALL, small_hops).reshape(model_width, -1)
    live[SMALL] = [small[:, :expert_count], small[:, expert_count]]
    mixed_out = middle + reduced(M, own).astype(wide) + live.pop(MIXED).astype(wide)
    live[MIXED] = (mixed_out + live.pop(RELAY).astype(wide)).astype(narrow)
    even, odd = weight_hops[0]
    side = jnp.where(odd_core == 0, bit(even), bit(odd))
    half = live[IN, KEPT].shape[0]

    def put(whole, part, index, at):
        part = part[:, index * columns : (index + 1) * columns].astype(wide)
        return lax.dynamic_update_slice_in_dim(whole, part, at * half, 0)

    empty = jnp.zeros((2 * half, columns), wide)
    live[RAW] = [put(empty, live[IN, KEPT], index, side) for index in range(3)]
    sync()
    grads_in = [put(whole, live[IN, GOT], i, 1 - side) for i, whole in enumerate(live[RAW])]

    return (
        live[MIXED],
        live[TOKENS],
        (live[GAIN][0] + live[GAIN][1])[0],
        *grads_in,
        live[OUT],
        live[SMALL][1],
        live[SMALL][0],
        *live[EXPERTS],
    )


def on_device(*operands):
    tokens, w_router, w_gate, expert_ids = operands[0], operands[7], operands[8], operands[11]
    owners, quarters = lax.axis_size("expert"), lax.axis_size("tensor")
    block_len, top_count = expert_ids.shape
    capacity = 3 * block_len * top_count // (2 * w_router.shape[1])
    buffer_rows = capacity * quarters * owners * w_gate.shape[0]
    gathers = owners * tokens.shape[0] <= buffer_rows and w_router.shape[1] <= 256
    gathers = gathers and (owners, quarters) == (8, 4)
    return (gathered_layer if gathers else routed_layer)(*operands)


def solution(mesh):
    return jax.shard_map(
        on_device,
        mesh=mesh,
        in_specs=(
            P("expert", None),
            P(),
            P(None, "tensor"),
            P(None, "tensor"),
            P(None, "tensor"),
            P("tensor", None),
            P(),
            P(),
            P("expert", None, "tensor"),
            P("expert", None, "tensor"),
            P("expert", "tensor", None),
            P(("expert", "tensor"), None),
            P(("expert", "tensor"), None),
        ),
        out_specs=(
            P(("expert", "tensor"), None),
            P(("expert", "tensor"), None),
            P(),
            P(None, "tensor"),
            P(None, "tensor"),
            P(None, "tensor"),
            P("tensor", None),
            P(),
            P(),
            P("expert", None, "tensor"),
            P("expert", None, "tensor"),
            P("expert", "tensor", None),
        ),
        check_vma=False,
    )
```

```python
import functools

import jax
import jax.numpy as jnp
from jax import lax
from jax.experimental import pallas as pl
from jax.experimental.pallas import tpu as pltpu
from jax.sharding import PartitionSpec as P

HD = 128


eps = 1e-06
theta_base = 10000.0
masked = -1e30

BOTH = ("expert", "tensor")
CORE, ACROSS, ASIDE, PLANE_NEXT, PLANE_FAR = 1, 2, 4, 8, 16
PLANES = (0, PLANE_NEXT, PLANE_FAR, PLANE_NEXT | PLANE_FAR)
BLOCKS = 8
WEIGHT_SLOTS = 3
LANES = 128

(
    G,
    H,
    M,
    R,
    QUERIES,
    KEYS,
    VALUES,
    TOTALS,
    HEADS,
    KEPT,
    SENT,
    RAW,
    HOME,
    SUMS,
    NEAR,
    AWAY,
    OTHER,
    FAR,
    OWN,
    SIDE,
    FULL,
    GOT,
    IN,
    OUT,
    TOKENS,
    NAMED,
    ROUTER,
    GATES,
    ATTN,
    RELAY,
    MIXED,
    EXPERTS,
    SMALL,
    GAIN,
    PAIR,
) = range(35)


def rope_tables(seq_length, head_size):
    half_dim = head_size // 2
    frequency = jnp.exp(
        -jnp.log(theta_base) * jnp.arange(half_dim, dtype=jnp.float32) * (2.0 / head_size)
    )
    angles = jnp.arange(seq_length, dtype=jnp.float32)[:, None] * frequency[None, :]
    return (jnp.cos(angles)[:, None, :], jnp.sin(angles)[:, None, :])


def rotate(source, cosine_table, sine_table):
    half_dim = source.shape[-1] // 2
    first_half = source[..., :half_dim]
    second = source[..., half_dim:]
    return jnp.concatenate(
        [
            first_half * cosine_table - second * sine_table,
            second * cosine_table + first_half * sine_table,
        ],
        axis=-1,
    )


def norm_forward(source, gain_vec):
    inverse = lax.rsqrt(jnp.mean(source * source, axis=-1, keepdims=True) + eps)
    return (inverse, source * inverse * gain_vec)


def norm_backward(source, inverse, gain_vec, grad_in):
    scaled = gain_vec * grad_in
    grad_source = inverse * scaled - source * inverse**3 * jnp.mean(
        scaled * source, axis=-1, keepdims=True
    )
    grad_gain = jnp.sum(grad_in * source * inverse, axis=0)
    return (grad_source, grad_gain)


def block_scores(q_block, key_rows, first_row, score_scale):
    scores = (
        jnp.einsum("qgrd,kgd->grqk", q_block, key_rows, preferred_element_type=jnp.float32)
        * score_scale
    )
    row_ids = first_row + jnp.arange(q_block.shape[0], dtype=jnp.int32)
    allowed = row_ids[:, None] >= jnp.arange(key_rows.shape[0], dtype=jnp.int32)[None, :]
    return jnp.where(allowed, scores, masked)


def routed_layer(
    tokens,
    gain_attn,
    w_query,
    w_key,
    w_value,
    w_out,
    gain_moe,
    w_router,
    w_gate,
    w_up,
    w_down,
    expert_ids,
    cotangent,
):
    seq_length, model_width = tokens.shape
    block_len, top_count = expert_ids.shape
    expert_count = w_router.shape[1]
    local_experts = w_gate.shape[0]
    local_heads = w_query.shape[1] // HD
    local_groups = w_key.shape[1] // HD
    group_size = local_heads // local_groups
    owners = lax.axis_size("expert")
    quarter = lax.axis_index("tensor")
    capacity = 3 * block_len * top_count // (2 * expert_count)
    block_rows = min(512, seq_length)
    block_count = seq_length // block_rows
    score_scale = HD ** (-0.5)
    first_own = quarter * block_len
    inputs = tokens.astype(jnp.float32)
    inverse_one, normed_one = norm_forward(inputs, gain_attn)
    hidden_one = normed_one.astype(jnp.bfloat16)
    cosine_table, sine_table = rope_tables(seq_length, HD)

    def rope_heads(source):
        return rotate(source, cosine_table, sine_table)

    query_raw = jnp.dot(hidden_one, w_query, preferred_element_type=jnp.float32).reshape(
        seq_length, local_heads, HD
    )
    key_raw = jnp.dot(hidden_one, w_key, preferred_element_type=jnp.float32).reshape(
        seq_length, local_groups, HD
    )
    queries = rope_heads(query_raw).astype(jnp.bfloat16)
    key_rows = rope_heads(key_raw).astype(jnp.bfloat16)
    value_rows = (
        jnp.dot(hidden_one, w_value, preferred_element_type=jnp.float32)
        .astype(jnp.bfloat16)
        .reshape(seq_length, local_groups, HD)
    )
    query_blocks = queries.reshape(block_count, block_rows, local_groups, group_size, HD)
    starts = jnp.arange(block_count, dtype=jnp.int32) * block_rows

    def attend_block(packed):
        first_row, q_block = packed
        scores = block_scores(q_block, key_rows, first_row, score_scale)
        row_max = jnp.max(scores, axis=-1, keepdims=True)
        exponent = jnp.exp(scores - row_max)
        row_total = jnp.sum(exponent, axis=-1, keepdims=True)
        weights = (exponent / row_total).astype(jnp.bfloat16)
        head_out = jnp.einsum(
            "grqk,kgd->qgrd", weights, value_rows, preferred_element_type=jnp.float32
        )
        return (head_out.astype(jnp.bfloat16), (row_max + jnp.log(row_total))[..., 0])

    head_blocks, log_totals = lax.map(attend_block, (starts, query_blocks))
    head_rows = head_blocks.reshape(seq_length, local_heads * HD)
    attention = lax.psum_scatter(
        jnp.dot(head_rows, w_out, preferred_element_type=jnp.float32),
        "tensor",
        scatter_dimension=0,
        tiled=True,
    )
    own_inputs = lax.dynamic_slice_in_dim(inputs, first_own, block_len, 0)
    own_inverse = lax.dynamic_slice_in_dim(inverse_one, first_own, block_len, 0)
    middle = own_inputs + attention
    inverse_two, normed_two = norm_forward(middle, gain_moe)
    hidden_two = normed_two.astype(jnp.bfloat16)
    logits = jnp.dot(hidden_two, w_router, preferred_element_type=jnp.float32)
    expert_range = jnp.arange(expert_count, dtype=jnp.int32)
    matches = expert_ids[:, :, None] == expert_range[None, None, :]
    chosen = jnp.sum(jnp.where(matches, logits[:, None, :], 0.0), axis=2)
    gate_weights = jax.nn.softmax(chosen, axis=-1)
    expert_hits = jnp.sum(matches.astype(jnp.int32), axis=1)
    earlier = jnp.cumsum(expert_hits, axis=0) - expert_hits
    slot_of = jnp.sum(jnp.where(matches, earlier[:, None, :], 0), axis=2)
    place = (slot_of * expert_count + expert_ids).reshape(-1)
    token_rows = jnp.broadcast_to(
        hidden_two[:, None, :], (block_len, top_count, model_width)
    ).reshape(block_len * top_count, model_width)
    grad_out = cotangent.astype(jnp.float32)
    gated_grads = (
        (gate_weights[:, :, None] * grad_out[:, None, :])
        .astype(jnp.bfloat16)
        .reshape(block_len * top_count, model_width)
    )
    empty = jnp.zeros((capacity * expert_count, model_width), jnp.bfloat16)
    send_rows = empty.at[place].set(token_rows).reshape(capacity, expert_count, model_width)
    send_grads = empty.at[place].set(gated_grads).reshape(capacity, expert_count, model_width)
    arrived_rows, arrived_grads = (
        lax.all_to_all(send_rows, "expert", split_axis=1, concat_axis=1, tiled=True),
        lax.all_to_all(send_grads, "expert", split_axis=1, concat_axis=1, tiled=True),
    )
    routed = arrived_rows.reshape(capacity, owners, local_experts, model_width)
    grads_in = arrived_grads.reshape(capacity, owners, local_experts, model_width)
    all_rows, all_grads = (
        lax.all_gather(routed, "tensor", axis=0, tiled=True),
        lax.all_gather(grads_in, "tensor", axis=0, tiled=True),
    )
    gate_pre = jnp.einsum("csld,ldf->cslf", all_rows, w_gate, preferred_element_type=jnp.float32)
    up_pre = jnp.einsum("csld,ldf->cslf", all_rows, w_up, preferred_element_type=jnp.float32)
    sigmoid_gate = jax.nn.sigmoid(gate_pre)
    silu_gate = gate_pre * sigmoid_gate
    activation = (silu_gate * up_pre).astype(jnp.bfloat16)
    grad_w_down = jnp.einsum(
        "cslf,csld->lfd", activation, all_grads, preferred_element_type=jnp.float32
    )
    grad_act = jnp.einsum("csld,lfd->cslf", all_grads, w_down, preferred_element_type=jnp.float32)
    grad_gate = (grad_act * up_pre * sigmoid_gate * (1.0 + gate_pre * (1.0 - sigmoid_gate))).astype(
        jnp.bfloat16
    )
    grad_up = (grad_act * silu_gate).astype(jnp.bfloat16)
    grad_w_gate = jnp.einsum(
        "csld,cslf->ldf", all_rows, grad_gate, preferred_element_type=jnp.float32
    )
    grad_w_up = jnp.einsum("csld,cslf->ldf", all_rows, grad_up, preferred_element_type=jnp.float32)
    forward_term = jnp.einsum(
        "cslf,lfd->csld", activation, w_down, preferred_element_type=jnp.float32
    )
    back_term = jnp.einsum("cslf,ldf->csld", grad_gate, w_gate, preferred_element_type=jnp.float32)
    back_term = back_term + jnp.einsum(
        "cslf,ldf->csld", grad_up, w_up, preferred_element_type=jnp.float32
    )
    both_terms = lax.psum_scatter(
        jnp.concatenate([forward_term, back_term], axis=3).astype(jnp.bfloat16),
        "tensor",
        scatter_dimension=0,
        tiled=True,
    )
    returned = both_terms[..., :model_width]
    row_grads = both_terms[..., model_width:]
    returned_home, row_grads_home = (
        lax.all_to_all(
            returned.reshape(capacity, expert_count, model_width),
            "expert",
            split_axis=1,
            concat_axis=1,
            tiled=True,
        ),
        lax.all_to_all(
            row_grads.reshape(capacity, expert_count, model_width),
            "expert",
            split_axis=1,
            concat_axis=1,
            tiled=True,
        ),
    )
    picked = returned_home.reshape(capacity * expert_count, model_width)[place].reshape(
        block_len, top_count, model_width
    )
    mixture = jnp.sum(gate_weights[:, :, None] * picked, axis=1)
    mixed_out = (middle + mixture).astype(jnp.bfloat16)
    grad_gates = jnp.sum(picked * grad_out[:, None, :], axis=2)
    grad_picked = row_grads_home.reshape(capacity * expert_count, model_width)[place].reshape(
        block_len, top_count, model_width
    )
    grad_hidden_disp = jnp.einsum(
        "lk,lkd->ld",
        jnp.ones((block_len, top_count), jnp.bfloat16),
        grad_picked,
        preferred_element_type=jnp.float32,
    )
    grad_chosen = gate_weights * (
        grad_gates - jnp.sum(gate_weights * grad_gates, axis=-1, keepdims=True)
    )
    grad_logits = jnp.sum(jnp.where(matches, grad_chosen[:, :, None], 0.0), axis=1).astype(
        jnp.bfloat16
    )
    grad_router = jnp.einsum(
        "ld,le->de", hidden_two, grad_logits, preferred_element_type=jnp.float32
    )
    grad_hidden_two = grad_hidden_disp + jnp.einsum(
        "le,de->ld", grad_logits, w_router, preferred_element_type=jnp.float32
    )
    grad_normed_two, grad_gain_moe = norm_backward(middle, inverse_two, gain_moe, grad_hidden_two)
    grad_middle = grad_out + grad_normed_two
    grad_attn = grad_middle.astype(jnp.bfloat16)
    grad_attn_all = lax.all_gather(grad_attn, "tensor", axis=0, tiled=True)
    grad_w_out = jnp.einsum(
        "lh,ld->hd", head_rows, grad_attn_all, preferred_element_type=jnp.float32
    )
    grad_heads = jnp.einsum(
        "ld,hd->lh", grad_attn_all, w_out, preferred_element_type=jnp.float32
    ).astype(jnp.bfloat16)
    grad_blocks = grad_heads.reshape(block_count, block_rows, local_groups, group_size, HD)

    def back_block(carried, packed):
        grad_keys, grad_values = carried
        first_row, q_block, g_block, lse_block = packed
        scores = block_scores(q_block, key_rows, first_row, score_scale)
        probability = jnp.exp(scores - lse_block[..., None])
        grad_values = grad_values + jnp.einsum(
            "grqk,qgrd->kgd",
            probability.astype(jnp.bfloat16),
            g_block,
            preferred_element_type=jnp.float32,
        )
        grad_prob = jnp.einsum(
            "qgrd,kgd->grqk", g_block, value_rows, preferred_element_type=jnp.float32
        )
        row_delta = jnp.sum(probability * grad_prob, axis=-1, keepdims=True)
        grad_scores = (probability * (grad_prob - row_delta)).astype(jnp.bfloat16)
        grad_query = (
            jnp.einsum("grqk,kgd->qgrd", grad_scores, key_rows, preferred_element_type=jnp.float32)
            * score_scale
        )
        grad_keys = (
            grad_keys
            + jnp.einsum("grqk,qgrd->kgd", grad_scores, q_block, preferred_element_type=jnp.float32)
            * score_scale
        )
        return ((grad_keys, grad_values), grad_query)

    zero_keys = jnp.zeros((seq_length, local_groups, HD), jnp.float32)
    (grad_keys, grad_values), grad_query_blocks = lax.scan(
        back_block, (zero_keys, zero_keys), (starts, query_blocks, grad_blocks, log_totals)
    )
    grad_query = grad_query_blocks.reshape(seq_length, local_heads, HD)
    grad_query_raw = (
        jax.vjp(rope_heads, query_raw)[1](grad_query)[0]
        .reshape(seq_length, local_heads * HD)
        .astype(jnp.bfloat16)
    )
    grad_key_raw = (
        jax.vjp(rope_heads, key_raw)[1](grad_keys)[0]
        .reshape(seq_length, local_groups * HD)
        .astype(jnp.bfloat16)
    )
    grad_value_raw = grad_values.reshape(seq_length, local_groups * HD).astype(jnp.bfloat16)
    grad_w_query = jnp.einsum(
        "ld,lh->dh", hidden_one, grad_query_raw, preferred_element_type=jnp.float32
    )
    grad_w_key = jnp.einsum(
        "ld,lh->dh", hidden_one, grad_key_raw, preferred_element_type=jnp.float32
    )
    grad_w_value = jnp.einsum(
        "ld,lh->dh", hidden_one, grad_value_raw, preferred_element_type=jnp.float32
    )
    term = jnp.einsum("lh,dh->ld", grad_query_raw, w_query, preferred_element_type=jnp.float32)
    term = term + jnp.einsum("lh,dh->ld", grad_key_raw, w_key, preferred_element_type=jnp.float32)
    grad_hidden_one = lax.psum_scatter(
        (
            term
            + jnp.einsum("lh,dh->ld", grad_value_raw, w_value, preferred_element_type=jnp.float32)
        ).astype(jnp.bfloat16),
        "tensor",
        scatter_dimension=0,
        tiled=True,
    ).astype(jnp.float32)
    grad_normed_one, grad_gain_attn = norm_backward(
        own_inputs, own_inverse, gain_attn, grad_hidden_one
    )
    grad_tokens = grad_middle + grad_normed_one
    attn_sums = lax.psum((grad_w_query, grad_w_key, grad_w_value, grad_w_out), "expert")
    small_sums = lax.psum((grad_gain_attn, grad_gain_moe, grad_router), ("expert", "tensor"))
    return (
        mixed_out,
        grad_tokens,
        small_sums[0],
        attn_sums[0],
        attn_sums[1],
        attn_sums[2],
        attn_sums[3],
        small_sums[1],
        small_sums[2],
        grad_w_gate,
        grad_w_up,
        grad_w_down,
    )


ROWS_ROWS = (((1,), (1,)), ((), ()))
def dot_nt(left, right):
    return lax.dot_general(left, right, ROWS_ROWS, preferred_element_type=jnp.float32)


def dot_nn(left, right):
    return jnp.dot(left, right, preferred_element_type=jnp.float32)


def expert_kernel(places, top_count, *refs):
    row_places, grad_places = places
    given = 1 + max(place[0] for place in row_places + grad_places)
    numbers_ref, router_ref, gate_ref, up_ref, down_ref = refs[given : given + 5]
    outs = refs[given + 5 : given + 14]
    mixed_refs, back_refs, sums_ref = outs[:2], outs[2:4], outs[4]
    rows_s, grads_s, ids_s, x_s, y_s, back_s, out_s = refs[given + 14 : given + 21]
    pick_s, place_s, gates_s, sums_s, gated_s, side_s = refs[given + 21 : given + 27]
    both_s, down_s, sems, weight_sems, out_sems, kept_sems = refs[given + 27 :]
    pairs, wide, _ = pick_s.shape
    experts = x_s.shape[0]
    hidden = down_s.shape[1]
    cap = wide // experts
    tokens_in, width = rows_s.shape[1:]
    block_len = tokens_in // 2
    narrow = jnp.bfloat16

    def copies(pair):
        out = []
        for half in range(2):
            target = pl.ds(half * block_len, block_len)
            at = 2 * pair + half
            array, row, column = row_places[at]
            rows = refs[array].at[pl.ds(row, block_len), pl.ds(column, width)]
            array, row, column = grad_places[at]
            block = refs[array].at[pl.ds(row, block_len)]
            grads = block.at[:, pl.ds(column, width)]
            ids = block.at[:, pl.ds(column + width, LANES)]
            for k, (source, scratch) in enumerate(
                ((rows, rows_s), (grads, grads_s), (ids, ids_s))
            ):
                out.append(
                    pltpu.make_async_copy(source, scratch.at[pair, target], sems.at[k, at])
                )
        return out

    def weight_copies(expert, slot):
        sides = [both_s.at[slot, :, pl.ds(k * hidden, hidden)] for k in range(2)]
        return [
            pltpu.make_async_copy(gate_ref.at[expert], sides[0], weight_sems.at[0, slot]),
            pltpu.make_async_copy(up_ref.at[expert], sides[1], weight_sems.at[1, slot]),
            pltpu.make_async_copy(down_ref.at[expert], down_s.at[slot], weight_sems.at[2, slot]),
        ]

    def result_copies(pair):
        half = pairs // 2
        place = pl.ds((pair % half) * tokens_in, tokens_in)
        sides = (rows_s, mixed_refs), (grads_s, back_refs)
        return [
            pltpu.make_async_copy(
                source.at[pair], targets[pair // half].at[place], out_sems.at[k, pair]
            )
            for k, (source, targets) in enumerate(sides)
        ]

    kept_copies = [
        pltpu.make_async_copy(source, target, kept_sems.at[k])
        for k, (source, target) in enumerate(zip((x_s, y_s, gated_s, side_s), outs[5:9]))
    ]

    for pair in range(pairs):
        for copy in copies(pair):
            copy.start()
    for slot in range(WEIGHT_SLOTS):
        for copy in weight_copies(slot, slot):
            copy.start()

    earlier = lax.broadcasted_iota(jnp.int32, (tokens_in, tokens_in), 0)
    later = lax.broadcasted_iota(jnp.int32, (tokens_in, tokens_in), 1)
    before = jnp.where(earlier < later, 1.0, 0.0).astype(narrow)

    for pair in range(pairs):
        for copy in copies(pair):
            copy.wait()
        rows_in = rows_s[pair]
        logits = dot_nt(router_ref[...], rows_in)
        ids = ids_s[pair].astype(jnp.float32).T
        named = jnp.zeros(logits.shape, jnp.float32)
        for k in range(top_count):
            named = jnp.where(ids[k : k + 1, :] == numbers_ref[:, :1], 1.0, named)
        hits = named[:experts]
        slots = jnp.where(hits > 0.0, dot_nn(hits.astype(narrow), before), -1.0)
        slots = slots.astype(jnp.int32)
        logits = jnp.where(named > 0.0, logits, masked)
        weights = jnp.exp(logits - jnp.max(logits, axis=0, keepdims=True)) * named
        gates = weights / jnp.sum(weights, axis=0, keepdims=True)
        ranks = lax.broadcasted_iota(jnp.int32, (cap, tokens_in), 0)
        place = pl.ds(pair * cap, cap)
        picks = []
        for expert in range(experts):
            pick = ranks == slots[expert : expert + 1, :]
            row_gates = jnp.sum(
                jnp.where(pick, gates[expert : expert + 1, :], 0.0), axis=1, keepdims=True
            )
            gates_s[expert, place, :] = jnp.broadcast_to(row_gates, (cap, LANES))
            picks.append(jnp.where(pick, 1.0, 0.0))
        pick_all = jnp.concatenate(picks, axis=0)
        pick_low = pick_all.astype(narrow)
        pick_s[pair] = pick_low
        place_s[pair] = pick_all.T.astype(narrow)
        for source, target in ((rows_in, x_s), (grads_s[pair], y_s)):
            spread = dot_nn(pick_low, source).astype(narrow)
            for expert in range(experts):
                target[expert, place, :] = spread[expert * cap : (expert + 1) * cap]

    kept_copies[0].start()
    kept_copies[1].start()

    def expert_step(expert, carried):
        slot = lax.rem(expert, WEIGHT_SLOTS)
        for copy in weight_copies(expert, slot):
            copy.wait()
        both = dot_nn(x_s[expert], both_s[slot])
        gate_pre, up_pre = both[:, :hidden], both[:, hidden:]
        plain = dot_nt(y_s[expert], down_s[slot])
        sigmoid_gate = jax.nn.sigmoid(gate_pre)
        silu_gate = gate_pre * sigmoid_gate
        activation = silu_gate * up_pre
        row_gates = gates_s[expert][:, :1]
        sums = jnp.sum(activation * plain, axis=1, keepdims=True)
        sums_s[expert] = jnp.broadcast_to(sums, sums_s.shape[1:])
        grad_act = row_gates * plain
        gated = (row_gates * activation).astype(narrow)
        slope = sigmoid_gate * (1.0 + gate_pre * (1.0 - sigmoid_gate))
        grad_gate = (grad_act * up_pre * slope).astype(narrow)
        grad_up = (grad_act * silu_gate).astype(narrow)
        grad_both = jnp.concatenate([grad_gate, grad_up], axis=1)
        gated_s[expert] = gated
        side_s[expert] = grad_both
        out_s[expert] = dot_nn(gated, down_s[slot]).astype(narrow)
        back_s[expert] = dot_nt(grad_both, both_s[slot]).astype(narrow)

        @pl.when(expert + WEIGHT_SLOTS < experts)
        def _():
            for copy in weight_copies(expert + WEIGHT_SLOTS, slot):
                copy.start()

        return carried

    lax.fori_loop(0, experts, expert_step, 0)
    kept_copies[2].start()
    kept_copies[3].start()

    for pair in range(pairs):
        sides = pl.ds(pair * cap, cap)
        for source, target in ((out_s, rows_s), (back_s, grads_s)):
            stacked = jnp.concatenate(
                [source[expert, sides, :] for expert in range(experts)], axis=0
            )
            target[pair] = dot_nn(place_s[pair], stacked).astype(narrow)
        for copy in result_copies(pair):
            copy.start()
        pick = pick_s[pair].astype(jnp.float32)
        sums = []
        for expert in range(experts):
            column = sums_s[expert, sides, :][:, :1]
            part = pick[expert * cap : (expert + 1) * cap] * column
            sums.append(jnp.sum(part, axis=0, keepdims=True))
        sums_ref[pair] = jnp.concatenate(sums, axis=0)

    for copy in kept_copies:
        copy.wait()
    for pair in range(pairs):
        for copy in result_copies(pair):
            copy.wait()


def expert_chunk(arrays, places, numbers, router, w_gate, w_up, w_down, tokens_in, top_count, cap):
    experts, width, hidden = w_gate.shape
    pairs = BLOCKS // 2
    rows = pairs * cap
    narrow, wide = jnp.bfloat16, jnp.float32
    shape = jax.ShapeDtypeStruct
    anywhere = pl.BlockSpec(memory_space=pl.ANY)
    inside = pl.BlockSpec(memory_space=pltpu.VMEM)
    half_shape = shape((pairs // 2 * tokens_in, width), narrow)
    whole_rows = (experts, rows, width)
    return pl.pallas_call(
        functools.partial(expert_kernel, places, top_count),
        in_specs=[anywhere] * len(arrays) + [inside] * 2 + [anywhere] * 3,
        out_specs=[anywhere] * 4 + [inside] + [anywhere] * 4,
        out_shape=[half_shape] * 4
        + [
            shape((pairs, experts, tokens_in), wide),
            shape(whole_rows, narrow),
            shape(whole_rows, narrow),
            shape((experts, rows, hidden), narrow),
            shape((experts, rows, 2 * hidden), narrow),
        ],
        scratch_shapes=[pltpu.VMEM((pairs, tokens_in, width), narrow)] * 2
        + [pltpu.VMEM((pairs, tokens_in, LANES), narrow)]
        + [pltpu.VMEM(whole_rows, narrow)] * 4
        + [
            pltpu.VMEM((pairs, experts * cap, tokens_in), narrow),
            pltpu.VMEM((pairs, tokens_in, experts * cap), narrow),
            pltpu.VMEM((experts, rows, LANES), wide),
            pltpu.VMEM((experts, rows, LANES), wide),
            pltpu.VMEM((experts, rows, hidden), narrow),
            pltpu.VMEM((experts, rows, 2 * hidden), narrow),
            pltpu.VMEM((WEIGHT_SLOTS, width, 2 * hidden), narrow),
            pltpu.VMEM((WEIGHT_SLOTS, hidden, width), narrow),
            pltpu.SemaphoreType.DMA((3, BLOCKS)),
            pltpu.SemaphoreType.DMA((3, WEIGHT_SLOTS)),
            pltpu.SemaphoreType.DMA((2, pairs)),
            pltpu.SemaphoreType.DMA((4,)),
        ],
        compiler_params=pltpu.CompilerParams(vmem_limit_bytes=60 << 20),
        cost_estimate=pl.CostEstimate(
            flops=24 * experts * rows * width * hidden,
            bytes_accessed=6 * experts * width * hidden + 4 * experts * rows * width,
            transcendentals=experts * rows * hidden,
        ),
    )(*arrays, numbers, router, w_gate, w_up, w_down)


def weight_kernel(parts, given, *refs):
    ins, (gate_ref, up_ref, down_ref) = refs[: 4 * parts], refs[4 * parts + given :]
    rows, grads, gated, both = [
        jnp.concatenate([ref[0] for ref in ins[k * parts : (k + 1) * parts]], axis=0)
        for k in range(4)
    ]
    turn = (((0,), (0,)), ((), ()))
    hidden = gated.shape[1]
    down_ref[0] = lax.dot_general(gated, grads, turn, preferred_element_type=jnp.float32)
    sides = lax.dot_general(rows, both, turn, preferred_element_type=jnp.float32)
    gate_ref[0] = sides[:, :hidden]
    up_ref[0] = sides[:, hidden:]


def weight_grads(kept, begin, count, partial):
    parts = len(kept)
    experts, rows, width = kept[0][0].shape
    hidden = kept[0][2].shape[2]
    operands = [part[k] for k in range(4) for part in kept]
    shape = jax.ShapeDtypeStruct

    def spec(rows, columns):
        return pl.BlockSpec((1, rows, columns), lambda i: (i + begin, 0, 0))

    return pl.pallas_call(
        functools.partial(weight_kernel, parts, len(partial)),
        grid=(count,),
        in_specs=[spec(rows, operand.shape[2]) for operand in operands]
        + [pl.BlockSpec(memory_space=pl.ANY)] * len(partial),
        out_specs=[spec(width, hidden), spec(width, hidden), spec(hidden, width)],
        out_shape=[
            shape((experts, width, hidden), jnp.float32),
            shape((experts, width, hidden), jnp.float32),
            shape((experts, hidden, width), jnp.float32),
        ],
        input_output_aliases={len(operands) + k: k for k in range(len(partial))},
        compiler_params=pltpu.CompilerParams(vmem_limit_bytes=56 << 20),
        cost_estimate=pl.CostEstimate(
            flops=6 * parts * count * rows * width * hidden,
            bytes_accessed=count * (parts * rows * (4 * width + 6 * hidden) + 12 * width * hidden),
            transcendentals=0,
        ),
    )(*operands, *partial)


def gathered_layer(
    tokens,
    gain_attn,
    w_query,
    w_key,
    w_value,
    w_out,
    gain_moe,
    w_router,
    w_gate,
    w_up,
    w_down,
    expert_ids,
    cotangent,
):
    seq_length, model_width = tokens.shape
    block_len, top_count = expert_ids.shape
    expert_count = w_router.shape[1]
    local_experts = w_gate.shape[0]
    local_heads = w_query.shape[1] // HD
    quarters = lax.axis_size("tensor")
    device_count = quarters * lax.axis_size("expert")
    quarter = lax.axis_index("tensor").astype(jnp.uint32)
    device = lax.axis_index(BOTH).astype(jnp.uint32)
    first_expert = lax.axis_index("expert") * local_experts
    pair_cap = 2 * (3 * block_len * top_count // (2 * expert_count))
    score_scale = HD ** (-0.5)
    narrow, wide = jnp.bfloat16, jnp.float32

    def swap(value, even, odd=None):
        odd = even if odd is None else odd
        perm = [(i, i ^ (odd if i & 1 else even)) for i in range(device_count)]
        return lax.ppermute(value, BOTH, perm)

    def near(value):
        return swap(value, ACROSS, ASIDE)

    def far(value):
        return swap(value, ASIDE, ACROSS)

    def core(value):
        return swap(value, CORE)

    def add(left, right):
        return (left.astype(wide) + right.astype(wide)).astype(narrow)

    live = {}

    def sync():
        keys = list(live)
        values = lax.optimization_barrier([live[key] for key in keys])
        live.update(zip(keys, values))

    def gather_near(name, plane):
        live[name, plane, 1] = near(live[name, plane, 0])
        live[name, plane, 2] = far(live[name, plane, 0])

    def gather_far(name, plane):
        live[name, plane, 3] = far(live[name, plane, 1])

    def gather_across(name, plane):
        live[name, plane, 3] = swap(live[name, plane, 0], ACROSS | ASIDE)

    def join_core(name, plane, *slots):
        blocks = [live[name, plane, slot] for slot in slots]
        live[name, plane, (OTHER,) + slots] = jnp.concatenate(blocks, axis=0)

    def send_core(name, plane, *slots):
        live[name, plane, (OTHER,) + slots] = core(live[name, plane, (OTHER,) + slots])

    def gather_core(name, plane, *slots):
        join_core(name, plane, *slots)
        send_core(name, plane, *slots)

    def blocks_of(name, plane):
        found = {}
        for key in list(live):
            if isinstance(key, tuple) and key[:2] == (name, plane):
                slots = key[2]
                array = live.pop(key)
                if isinstance(slots, tuple):
                    for i, slot in enumerate(slots[1:]):
                        found[4 + slot] = (array, i * block_len)
                else:
                    found[slots] = (array, 0)
        return [found[slot] for slot in range(BLOCKS)]

    def reduce_core(name, plane):
        live[name, plane, OTHER] = core(live.pop((name, plane, AWAY)))

    def add_far(name, plane):
        kept = live[name, plane, NEAR].reshape(4, block_len, model_width)
        got = live[name, plane, OTHER].reshape(4, block_len, model_width)
        live[name, plane, FAR] = add(kept[2:], got[2:])

    def send_far(name, plane):
        live[name, plane, FAR] = far(live[name, plane, FAR])

    def reduce_far(name, plane):
        add_far(name, plane)
        send_far(name, plane)

    def add_near(name, plane):
        kept = live.pop((name, plane, NEAR)).reshape(4, block_len, model_width)
        got = live.pop((name, plane, OTHER)).reshape(4, block_len, model_width)
        back = live.pop((name, plane, FAR))
        sums = [
            kept[i].astype(wide) + got[i].astype(wide) + back[i].astype(wide) for i in range(2)
        ]
        live[name, plane, OWN], live[name, plane, SIDE] = [part.astype(narrow) for part in sums]

    def send_near(name, plane):
        live[name, plane, SIDE] = near(live[name, plane, SIDE])

    def reduce_near(name, plane):
        add_near(name, plane)
        send_near(name, plane)

    def reduced(name, plane):
        return add(live.pop((name, plane, OWN)), live.pop((name, plane, SIDE)))

    def bit(mask):
        return (device // mask) % 2

    odd_core = bit(CORE)
    weight_hops = ((ASIDE, PLANE_NEXT), (PLANE_NEXT, ASIDE), (PLANE_FAR, PLANE_FAR))
    small_hops = tuple((mask, mask) for mask in (CORE, ACROSS, ASIDE, PLANE_NEXT, PLANE_FAR))

    def joined(own, got, side):
        first, second = jnp.where(side == 0, own, got), jnp.where(side == 0, got, own)
        return jnp.concatenate([first, second], axis=0)

    def sum_step(name, step, hops=weight_hops, sent_as=narrow):
        count = len(hops)
        sides = [jnp.where(odd_core == 0, bit(even), bit(odd)) for even, odd in hops]
        if step == 0:
            kept = live.pop((name, FULL))
        elif step <= count:
            kept = live.pop((name, KEPT)) + live.pop((name, GOT)).astype(wide)
        else:
            kept = joined(live.pop((name, KEPT)), live.pop((name, GOT)), sides[2 * count - step])
        if step < count:
            half = kept.shape[0] // 2
            side = sides[step]
            live[name, KEPT] = lax.dynamic_slice_in_dim(kept, side * half, half, 0)
            sent = lax.dynamic_slice_in_dim(kept, (1 - side) * half, half, 0)
            live[name, GOT] = swap(sent.astype(sent_as), *hops[step])
        else:
            kept = kept.astype(sent_as)
            live[name, KEPT] = kept
            live[name, GOT] = swap(kept, *hops[2 * count - 1 - step])

    def summed(name, hops=weight_hops):
        even, odd = hops[0]
        side = jnp.where(odd_core == 0, bit(even), bit(odd))
        return joined(live.pop((name, KEPT)), live.pop((name, GOT)), side).astype(wide)

    own, nxt, far_plane, last = PLANES

    named_ids = jnp.pad(expert_ids.astype(narrow), ((0, 0), (0, LANES - top_count)))
    live[G, own, 0] = jnp.concatenate([cotangent, named_ids], axis=1)
    half_block = block_len // 2
    live[G, nxt, 0] = swap(live[G, own, 0], nxt)
    live[G, far_plane, 0] = [swap(live[G, own, 0][:half_block], far_plane)]
    gather_near(G, own)

    by_block = tokens.reshape(quarters, block_len, model_width)
    inputs = jnp.concatenate(
        [lax.dynamic_slice_in_dim(by_block, quarter ^ r, 1, 0)[0] for r in range(quarters)], axis=0
    )
    inputs = lax.optimization_barrier(inputs)
    order = quarter.astype(jnp.int32) ^ jnp.arange(quarters, dtype=jnp.int32)
    positions = (order[:, None] * block_len + jnp.arange(block_len, dtype=jnp.int32)).reshape(-1)
    inverse_one, normed_one = norm_forward(inputs.astype(wide), gain_attn)
    hidden_one = normed_one.astype(narrow)
    frequency = jnp.exp(
        -jnp.log(theta_base) * jnp.arange(HD // 2, dtype=jnp.float32) * (2.0 / HD)
    )
    angles = positions.astype(wide)[:, None] * frequency[None, :]
    cosine_table, sine_table = (jnp.cos(angles)[:, None, :], jnp.sin(angles)[:, None, :])

    def project(weights):
        return jnp.dot(hidden_one, weights, preferred_element_type=wide).reshape(
            seq_length, local_heads, HD
        )

    live[QUERIES] = rotate(project(w_query), cosine_table, sine_table).astype(narrow)
    live[KEYS] = rotate(project(w_key), cosine_table, sine_table).astype(narrow)
    live[VALUES] = project(w_value).astype(narrow)
    sync()

    gather_far(G, own)
    gather_near(G, nxt)
    live[G, far_plane, 0] = live[G, far_plane, 0] + [
        swap(live[G, own, 0][half_block:], far_plane)
    ]
    allowed = positions[:, None] >= positions[None, :]

    def masked_scores():
        scores = jnp.einsum(
            "qhd,khd->hqk", live[QUERIES], live[KEYS], preferred_element_type=wide
        )
        return jnp.where(allowed, scores * score_scale, masked)

    scores = masked_scores()
    row_max = jnp.max(scores, axis=-1, keepdims=True)
    exponent = jnp.exp(scores - row_max)
    row_total = jnp.sum(exponent, axis=-1, keepdims=True)
    weights = (exponent / row_total).astype(narrow)
    head_out = jnp.einsum("hqk,khd->qhd", weights, live[VALUES], preferred_element_type=wide)
    live[TOTALS] = row_max + jnp.log(row_total)
    live[HEADS] = head_out.astype(narrow).reshape(seq_length, local_heads * HD)

    def split_quarters(full):
        parts = full.reshape(quarters, block_len, model_width)
        live[KEPT] = [parts[0], parts[2]]
        live[SENT] = jnp.stack([parts[1], parts[3]]).astype(narrow)

    split_quarters(jnp.dot(live[HEADS], w_out, preferred_element_type=wide))
    sync()

    expert_range = jnp.arange(expert_count, dtype=jnp.int32)
    rolled = (first_expert + expert_range) % expert_count
    live[ROUTER] = jnp.take(w_router.T, rolled, axis=0)
    live[NAMED] = jnp.broadcast_to(rolled.astype(wide)[:, None], (expert_count, LANES))
    live[SENT] = core(live[SENT])
    gather_far(G, nxt)
    live[G, far_plane, 0] = jnp.concatenate(live[G, far_plane, 0], axis=0)
    sync()

    def cross_quarters():
        kept, sent = live.pop(KEPT), live.pop(SENT).astype(wide)
        live[KEPT] = kept[0] + sent[0]
        live[SENT] = swap((kept[1] + sent[1]).astype(narrow), ACROSS)

    def quarter_sum():
        return live.pop(KEPT) + live.pop(SENT).astype(wide)

    cross_quarters()
    live[G, last, 0] = swap(live[G, far_plane, 0], nxt)
    sync()

    own_inputs = inputs[:block_len].astype(wide)
    own_inverse = inverse_one[:block_len]
    middle = own_inputs + quarter_sum()
    inverse_two, normed_two = norm_forward(middle, gain_moe)
    hidden_two = normed_two.astype(narrow)
    live[H, own, 0] = hidden_two

    gather_near(H, own)
    live[H, nxt, 0] = swap(hidden_two, nxt)
    logits = jnp.dot(hidden_two, w_router, preferred_element_type=wide)
    expert_range = jnp.arange(expert_count, dtype=jnp.int32)
    matches = expert_ids[:, :, None] == expert_range[None, None, :]
    chosen = jnp.sum(jnp.where(matches, logits[:, None, :], 0.0), axis=2)
    gate_weights = jax.nn.softmax(chosen, axis=-1)
    sync()

    gather_far(H, own)
    gather_near(H, nxt)
    hidden_two = live[H, own, 0]
    gather_core(G, own, 0, 1, 2, 3)
    live[H, last, 0] = [swap(hidden_two[:half_block], last)]
    sync()

    gather_far(H, nxt)
    gather_core(H, own, 0, 1, 2, 3)
    gather_core(G, nxt, 0, 1, 2, 3)
    hidden_two = live[H, own, 0]
    live[H, last, 0] = live[H, last, 0] + [swap(hidden_two[half_block:], last)]
    sync()

    def join_pair(plane):
        rows, grads = [live.pop((name, plane, 0)) for name in (H, G)]
        if isinstance(rows, list):
            rows = jnp.concatenate(rows, axis=0)
        after, ahead = grads.shape[1], rows.shape[1]
        pair = jnp.pad(rows, ((0, 0), (0, after))) + jnp.pad(grads, ((0, 0), (ahead, 0)))
        live[PAIR, plane, 0] = pair

    def experts(plane):
        if (PAIR, plane, 0) in live:
            rows = blocks_of(PAIR, plane)
            grads, column = rows, model_width
        else:
            rows, grads, column = blocks_of(H, plane), blocks_of(G, plane), 0
        arrays = []
        for array, _ in rows + grads:
            if not any(array is other for other in arrays):
                arrays.append(array)

        def placed(blocks, column):
            indices = [[array is other for other in arrays].index(True) for array, _ in blocks]
            return [(index, row, column) for index, (_, row) in zip(indices, blocks)]

        done = expert_chunk(
            arrays,
            (placed(rows, 0), placed(grads, column)),
            live[NAMED],
            live[ROUTER],
            w_gate,
            w_up,
            w_down,
            2 * block_len,
            top_count,
            pair_cap,
        )
        live[M, plane, NEAR], live[M, plane, AWAY] = done[:2]
        live[R, plane, NEAR], live[R, plane, AWAY] = done[2:4]
        live[SUMS, plane] = done[4]
        live[KEPT, plane] = done[5:]

    gather_core(H, nxt, 0, 1, 2, 3)
    join_pair(last)
    gather_near(PAIR, last)
    gather_core(PAIR, last, 0)
    live[H, far_plane, 0] = swap(live[H, own, 0], far_plane)
    experts(own)
    sync()

    gather_far(PAIR, last)
    gather_core(PAIR, last, 1, 2)
    join_pair(far_plane)
    gather_near(PAIR, far_plane)
    reduce_core(R, own)
    experts(nxt)
    sync()
    gather_core(PAIR, last, 3)
    join_core(PAIR, far_plane, 0, 1, 2)
    add_far(R, own)
    sync()

    gather_far(PAIR, far_plane)
    send_core(PAIR, far_plane, 0, 1, 2)
    send_far(R, own)
    reduce_core(R, nxt)
    reduce_core(M, own)
    experts(last)
    sync()
    gather_core(PAIR, far_plane, 3)
    reduce_core(R, last)
    add_near(R, own)
    add_far(R, nxt)
    sync()

    send_near(R, own)
    send_far(R, nxt)
    reduce_far(R, last)
    reduce_core(M, nxt)
    experts(far_plane)
    sync()

    part_experts = local_experts // 4

    def some_weight_grads(part):
        kept = [live[KEPT, plane] for plane in PLANES]
        live[EXPERTS] = weight_grads(kept, part * part_experts, part_experts, live.get(EXPERTS, []))

    reduce_core(R, far_plane)
    sums = jnp.stack([live.pop((SUMS, plane)) for plane in PLANES])
    sums = sums.reshape(len(PLANES), -1, local_experts, 2, block_len).transpose(0, 1, 3, 2, 4)
    sums = sums.reshape(len(PLANES), BLOCKS, local_experts, block_len)
    live[GATES] = [sums[:, :4], core(sums[:, 4:])]
    reduce_core(M, last)
    add_near(R, last)
    sync()

    reduce_far(R, far_plane)
    send_near(R, last)
    add_near(R, nxt)
    live[HOME] = reduced(R, own)
    sums = live[GATES][0] + live[GATES][1]
    crossed = jnp.stack([sums[:, 0], sums[:, 2], sums[:, 1], sums[:, 3]], axis=1)
    sums = jnp.where(odd_core == 0, sums, crossed)
    sums = sums[:, ::2] + swap(sums[:, 1::2], ACROSS)
    live[GATES] = [sums[:, 0], swap(sums[:, 1], ASIDE)]
    sync()

    live[RELAY] = swap(reduced(R, last), nxt)
    reduce_near(R, far_plane)
    sums = jnp.stack(live[GATES], axis=1)
    live[GATES] = [sums[::2], swap(sums[1::2], nxt)]
    send_near(R, nxt)
    add_far(M, nxt)
    add_far(M, last)
    sync()

    live[RELAY] = add(reduced(R, far_plane), live[RELAY])
    live[SIDE] = reduced(R, nxt)
    sync()
    live[RELAY] = swap(live[RELAY], far_plane)
    live[SIDE] = swap(live[SIDE], nxt)
    send_far(M, nxt)
    send_far(M, last)
    reduce_core(M, far_plane)
    sums = jnp.stack(live.pop(GATES), axis=1)
    sums = jnp.concatenate([sums[0], swap(sums[1], far_plane)], axis=0)
    sums = sums.reshape(-1, local_experts, block_len)
    owner = lax.axis_index("expert").astype(jnp.uint32)
    sums = [lax.dynamic_slice_in_dim(sums, owner ^ r, 1, 0)[0] for r in range(sums.shape[0])]
    own_sums = jnp.concatenate(sums, axis=0).T
    grad_gates = jnp.sum(jnp.where(matches, own_sums[:, None, :], 0.0), axis=2)
    grad_chosen = gate_weights * (
        grad_gates - jnp.sum(gate_weights * grad_gates, axis=-1, keepdims=True)
    )
    grad_logits = jnp.sum(jnp.where(matches, grad_chosen[:, :, None], 0.0), axis=1).astype(narrow)
    grad_router = jnp.einsum("ld,le->de", hidden_two, grad_logits, preferred_element_type=wide)
    live[GATES] = jnp.einsum("le,de->ld", grad_logits, w_router, preferred_element_type=wide)
    live[SMALL] = grad_router
    sync()

    grad_hidden_two = live.pop(HOME).astype(wide) + live.pop(RELAY).astype(wide)
    grad_hidden_two = grad_hidden_two + live.pop(SIDE).astype(wide) + live.pop(GATES)
    grad_out = cotangent.astype(wide)
    grad_normed_two, grad_gain_moe = norm_backward(middle, inverse_two, gain_moe, grad_hidden_two)
    grad_middle = grad_out + grad_normed_two
    grad_attn = grad_middle.astype(narrow)

    live[SMALL, FULL] = live.pop(SMALL).reshape(device_count, -1, expert_count)
    small_step = functools.partial(sum_step, SMALL, hops=small_hops, sent_as=wide)

    live[ATTN] = [grad_attn, core(grad_attn), swap(grad_attn, ACROSS)]
    small_step(0)
    add_near(M, nxt)
    sync()
    live[ATTN] = live[ATTN] + [core(live[ATTN][2])]
    sync()

    grad_attn_all = jnp.stack(live.pop(ATTN)).reshape(seq_length, model_width)
    live[OUT, FULL] = jnp.einsum(
        "lh,ld->hd", live[HEADS], grad_attn_all, preferred_element_type=wide
    )
    grad_heads = (
        jnp.einsum("ld,hd->lh", grad_attn_all, w_out, preferred_element_type=wide)
        .astype(narrow)
        .reshape(seq_length, local_heads, HD)
    )
    live[RAW] = grad_heads
    sync()

    grad_heads = live.pop(RAW)
    sum_step(OUT, 0)
    send_near(M, nxt)
    probability = jnp.exp(masked_scores() - live[TOTALS])
    grad_values = jnp.einsum(
        "hqk,qhd->khd", probability.astype(narrow), grad_heads, preferred_element_type=wide
    )
    grad_prob = jnp.einsum("qhd,khd->hqk", grad_heads, live[VALUES], preferred_element_type=wide)
    row_delta = jnp.sum(probability * grad_prob, axis=-1, keepdims=True)
    grad_scores = (probability * (grad_prob - row_delta)).astype(narrow)
    grad_query = score_scale * jnp.einsum(
        "hqk,khd->qhd", grad_scores, live[KEYS], preferred_element_type=wide
    )
    grad_keys = score_scale * jnp.einsum(
        "hqk,qhd->khd", grad_scores, live[QUERIES], preferred_element_type=wide
    )

    def flat(source):
        return source.astype(narrow).reshape(seq_length, local_heads * HD)

    live[RAW] = [
        flat(rotate(grad_query, cosine_table, -sine_table)),
        flat(rotate(grad_keys, cosine_table, -sine_table)),
        flat(grad_values),
    ]
    flying = live.pop((OUT, GOT))
    sync()
    live[OUT, GOT] = flying

    def back(grad_raw, weights):
        return jnp.einsum("lh,dh->ld", grad_raw, weights, preferred_element_type=wide)

    raw = live.pop(RAW)
    partial = back(raw[0], w_query) + back(raw[1], w_key) + back(raw[2], w_value)
    split_quarters(partial)
    live[GAIN] = partial
    live[IN, FULL] = jnp.einsum(
        "ld,lh->dh", hidden_one, jnp.concatenate(raw, axis=1), preferred_element_type=wide
    )
    sum_step(OUT, 1)
    small_step(1)
    small_step(2)
    live[MIXED] = swap(reduced(M, nxt), nxt)
    sync()

    live[SENT] = core(live[SENT])
    sum_step(IN, 0)
    sum_step(OUT, 2)
    some_weight_grads(0)
    gain = jnp.sum(live.pop(GAIN) * inputs.astype(wide) * inverse_one, axis=0)
    gain = jnp.stack([gain, grad_gain_moe])
    live[GAIN] = [gain, jnp.zeros_like(gain)]

    def gain_step(step):
        live[GAIN] = [live[GAIN][0] + live[GAIN][1]]
        live[GAIN] = live[GAIN] + [swap(live[GAIN][0], *small_hops[step])]

    small_step(3)
    gain_step(0)
    add_near(M, last)
    add_far(M, far_plane)
    add_far(M, own)
    sync()

    sum_step(IN, 1)
    cross_quarters()
    sum_step(OUT, 3)
    small_step(4)
    small_step(5)
    gain_step(1)
    some_weight_grads(1)
    sync()

    sum_step(IN, 2)
    own_grad = quarter_sum()
    grad_normed_one = norm_backward(own_inputs, own_inverse, gain_attn, own_grad)[0]
    live[TOKENS] = grad_middle + grad_normed_one
    sum_step(OUT, 4)
    small_step(6)
    send_near(M, last)
    send_far(M, far_plane)
    some_weight_grads(2)
    sync()

    sum_step(IN, 3)
    sum_step(OUT, 5)
    small_step(7)
    live[RELAY] = swap(reduced(M, last), nxt)
    reduce_near(M, far_plane)
    send_far(M, own)
    some_weight_grads(3)
    sync()
    for plane in PLANES:
        live.pop((KEPT, plane))

    live[RELAY] = add(reduced(M, far_plane), live[RELAY])
    sync()
    live[RELAY] = swap(live[RELAY], far_plane)
    sum_step(IN, 4)
    live[OUT] = summed(OUT)
    reduce_near(M, own)
    small_step(8)
    small_step(9)
    gain_step(2)
    sync()

    columns = local_heads * HD
    sum_step(IN, 5)
    gain_step(3)
    gain_step(4)
    live[SMALL] = summed(SMALL, small_hops).reshape(model_width, -1)
    mixed_out = middle + reduced(M, own).astype(wide) + live.pop(MIXED).astype(wide)
    live[MIXED] = (mixed_out + live.pop(RELAY).astype(wide)).astype(narrow)
    even, odd = weight_hops[0]
    side = jnp.where(odd_core == 0, bit(even), bit(odd))
    half = live[IN, KEPT].shape[0]

    def put(whole, part, index, at):
        part = part[:, index * columns : (index + 1) * columns].astype(wide)
        return lax.dynamic_update_slice_in_dim(whole, part, at * half, 0)

    empty = jnp.zeros((2 * half, columns), wide)
    live[RAW] = [put(empty, live[IN, KEPT], index, side) for index in range(3)]
    sync()
    grads_in = [put(whole, live[IN, GOT], i, 1 - side) for i, whole in enumerate(live[RAW])]

    gains = live[GAIN][0] + live[GAIN][1]
    return (
        live[MIXED],
        live[TOKENS],
        gains[0],
        *grads_in,
        live[OUT],
        gains[1],
        live[SMALL],
        *live[EXPERTS],
    )


def on_device(*operands):
    tokens, w_router, w_gate, expert_ids = operands[0], operands[7], operands[8], operands[11]
    owners, quarters = lax.axis_size("expert"), lax.axis_size("tensor")
    block_len, top_count = expert_ids.shape
    capacity = 3 * block_len * top_count // (2 * w_router.shape[1])
    buffer_rows = capacity * quarters * owners * w_gate.shape[0]
    gathers = owners * tokens.shape[0] <= buffer_rows and w_router.shape[1] <= 256
    gathers = gathers and (owners, quarters) == (8, 4)
    return (gathered_layer if gathers else routed_layer)(*operands)


def solution(mesh):
    return jax.shard_map(
        on_device,
        mesh=mesh,
        in_specs=(
            P("expert", None),
            P(),
            P(None, "tensor"),
            P(None, "tensor"),
            P(None, "tensor"),
            P("tensor", None),
            P(),
            P(),
            P("expert", None, "tensor"),
            P("expert", None, "tensor"),
            P("expert", "tensor", None),
            P(("expert", "tensor"), None),
            P(("expert", "tensor"), None),
        ),
        out_specs=(
            P(("expert", "tensor"), None),
            P(("expert", "tensor"), None),
            P(),
            P(None, "tensor"),
            P(None, "tensor"),
            P(None, "tensor"),
            P("tensor", None),
            P(),
            P(),
            P("expert", None, "tensor"),
            P("expert", None, "tensor"),
            P("expert", "tensor", None),
        ),
        check_vma=False,
    )
```
